32 devices in a mesh: section: 4 (over y, x), dp: 8 (over z, core).
Axes of the slice: x: 2, y: 2, z: 4, core: 2. Of those that a mesh axis runs over, the one named last changes fastest.
Arguments:
- image: bfloat16 [2, 2, 32, 7, 7, 2048], P(None, None, 'dp')
- section_weights: bfloat16 [4, 9456, 512], P('section')
- section_norms: float32 [4, 3, 2048], P('section'), as said below
- queue: bfloat16 [2, 512, 128], P(None, 'dp'), may hold values from -0.5 to 0.5
- pairing: int32 [2, 32], P(None, 'dp'), may hold values from 0 to 3, as said below
Outputs:
- loss: float32 [], replicated
- grad_input: float32 [2, 2, 32, 7, 7, 2048], P(None, None, 'dp', None, None, 'section')
- grad_weights: float32 [4, 9456, 512], P('section', None, 'dp')
- grad_norms: float32 [4, 3, 2048], P('section')
The draws below stay inside these ranges and needn't reach their ends.
Inputs may be any that keep to these rules, and one draw needn't show every extreme that they name: `pairing`: each run of 4 entries of a row (the images of one index of dp) is a permutation of 0 to 3. `section_norms`: row 0 (gains) is positive.
All inputs are finite; a program needn't handle non-finite values.
Results may differ from the reference program's by a relative error of at most 0.025.
Values may be sent and summed in bfloat16 or wider, within the bound.
No kernel may reach another device: no remote copies, remote signals or barrier semaphores. Data moves between devices by JAX's collectives and lax.ppermute only.
A program may use at most 448 MiB of HBM per device.

```python
import jax
import jax.numpy as jnp
from jax import lax

D = 2048
BOTTLENECK_WIDTH = 512
PROJ = 128
PROTOS = 3000
SIDE = 7
IMAGE_CROPS = 2
IMG_DEV = 4
MICRO = 2
SECTIONS = 4
IMAGES = 32
QUEUE = 512
PARAM_ROWS = 9456


def draw_image(key, part):
    key = jax.random.fold_in(key, 11)
    shape = (MICRO, IMAGE_CROPS, IMAGES, SIDE, SIDE, D)
    order = jnp.arange(IMAGES, dtype=jnp.float32) / max(IMAGES - 1, 1)
    rising = jnp.exp(order * jnp.log(3.0)).reshape(1, 1, IMAGES, 1, 1, 1)
    return (jax.random.normal(key, shape, jnp.float32) * rising).astype(jnp.bfloat16)


def draw_section_weights(key, part):
    key = jax.random.fold_in(key, 12)
    first = D * (D // BOTTLENECK_WIDTH)
    second = first + D * PROJ // BOTTLENECK_WIDTH
    third = second + PROTOS * PROJ // BOTTLENECK_WIDTH
    row = jnp.arange(PARAM_ROWS)[None, :, None]
    relay_section = jnp.arange(SECTIONS)[:, None, None]
    scale = jnp.full((SECTIONS, PARAM_ROWS, 1), 0.02, jnp.float32)
    scale = jnp.where((relay_section == 0) & (row < D), D ** (-0.5), scale)
    scale = jnp.where((relay_section == 1) & (row < 9 * BOTTLENECK_WIDTH), (9 * BOTTLENECK_WIDTH) ** (-0.5), scale)
    scale = jnp.where((relay_section == 2) & (row < D), BOTTLENECK_WIDTH ** (-0.5), scale)
    scale = jnp.where((relay_section == 3) & (row < second), D ** (-0.5), scale)
    scale = jnp.where((relay_section == 3) & (row >= second) & (row < third), PROJ ** (-0.5), scale)
    shape = (SECTIONS, PARAM_ROWS, BOTTLENECK_WIDTH)
    return (jax.random.normal(key, shape, jnp.float32) * scale).astype(jnp.bfloat16)


def draw_section_norms(key, part):
    key = jax.random.fold_in(key, 13)
    gain = jnp.exp(jax.random.uniform(key, (SECTIONS, 1, D), jnp.float32, -0.6931472, 0.6931472))
    rest = 0.5 * jax.random.normal(jax.random.fold_in(key, 1), (SECTIONS, 2, D), jnp.float32)
    return jnp.concatenate([gain, rest], axis=1)


def draw_pairing(key, part):
    key = jax.random.fold_in(key, 14)
    blocks = MICRO * (IMAGES // IMG_DEV)
    keys = jax.random.split(key, blocks)
    perms = jax.vmap(lambda single: jax.random.permutation(single, IMG_DEV))(keys)
    return perms.reshape(MICRO, IMAGES).astype(jnp.int32)


def levels(key, extent, cuts, low, top_value):
    loudness, own = 1.0, jax.random.fold_in(key, 6)
    for dim, parts in cuts:
        draws = jnp.exp(jax.random.uniform(jax.random.fold_in(own, dim), (parts,), jnp.float32, low / len(cuts), top_value / len(cuts)))
        loudness = loudness * jnp.repeat(draws, extent[dim] // parts).reshape([-1 if axis == dim else 1 for axis in range(len(extent))])
    return loudness


def bell_draw(own_key, shape, spread, bound, pieces=(), kind=jnp.bfloat16):
    array = spread * jax.random.normal(own_key, shape, jnp.float32)
    if pieces:
        array = array * levels(own_key, shape, pieces, -0.22, 0.18)
    return jnp.clip(array, -bound, bound).astype(kind)


def setup_inputs(seed: int = 0) -> dict:
    splits = jax.random.split(jax.random.key(seed), 6)
    return {
        "image": draw_image(jax.random.fold_in(splits[5], 71), 0),
        "section_weights": draw_section_weights(jax.random.fold_in(splits[5], 71), 0),
        "section_norms": draw_section_norms(jax.random.fold_in(splits[5], 71), 0),
        "queue": bell_draw(splits[3], (IMAGE_CROPS, QUEUE, PROJ), PROJ ** -0.5, 0.5, ((1, 8),)),
        "pairing": draw_pairing(jax.random.fold_in(splits[5], 71), 0),
    }


NORM_EPS = 1e-05
UNIT_EPS = 1e-06
SINK_EPS = 0.05
TEMPER = 0.1
HIGH = lax.Precision.HIGHEST

@jax.custom_vjp
def low(v):
    return lax.optimization_barrier(v.astype(jnp.bfloat16)).astype(jnp.float32)

@jax.custom_vjp
def low_back(v):
    return v

def low_keep(v):
    return (low(v), None)

def low_pass(kept, grad):
    return (grad,)

def back_keep(v):
    return (v, None)

def back_low(kept, grad):
    return (low(grad),)
low.defvjp(low_keep, low_pass)
low_back.defvjp(back_keep, back_low)

def unpack(weights):
    first = D * (D // BOTTLENECK_WIDTH)
    second = first + D * PROJ // BOTTLENECK_WIDTH
    third = second + PROTOS * PROJ // BOTTLENECK_WIDTH
    return (weights[0, :D], weights[1, :9 * BOTTLENECK_WIDTH].reshape(9, BOTTLENECK_WIDTH, BOTTLENECK_WIDTH), weights[2, :D].reshape(BOTTLENECK_WIDTH, D), weights[3, :first].reshape(D, D), weights[3, first:second].reshape(D, PROJ), weights[3, second:third].reshape(PROTOS, PROJ))

def batch_norm(value, gain, shift, axes):
    batch_mean = lax.optimization_barrier(jnp.mean(value, axis=axes, keepdims=True))
    square = lax.optimization_barrier(jnp.mean(value * value, axis=axes, keepdims=True))
    return (value - batch_mean) * lax.rsqrt(square - batch_mean * batch_mean + NORM_EPS) * gain + shift

def conv_taps(value, kernel):
    flat = value.reshape(-1, SIDE, SIDE, BOTTLENECK_WIDTH)
    out = lax.conv_general_dilated(flat, kernel.reshape(3, 3, BOTTLENECK_WIDTH, BOTTLENECK_WIDTH), (1, 1), ((1, 1), (1, 1)), dimension_numbers=('NHWC', 'HWIO', 'NHWC'), precision=HIGH)
    return out.reshape(value.shape)

def forward(weights, norms, image_main, image_side, queue_float):
    w_reduce, w_conv, w_expand, w_head, w_proj, protos = unpack(weights)
    axes = (0, 1, 2, 3)
    queued_scores = jnp.einsum('cqp,kp->cqk', queue_float, protos, precision=HIGH)
    pre0 = low_back(jnp.einsum('cihwd,dk->cihwk', image_main, w_reduce, precision=HIGH))
    act0 = low_back(low(jax.nn.silu(batch_norm(pre0, norms[0, 0, :BOTTLENECK_WIDTH], norms[0, 1, :BOTTLENECK_WIDTH], axes))))
    pre1 = low_back(conv_taps(act0, w_conv))
    act1 = low_back(low(jax.nn.silu(batch_norm(pre1, norms[1, 0, :BOTTLENECK_WIDTH], norms[1, 1, :BOTTLENECK_WIDTH], axes))))
    pre2 = low_back(jnp.einsum('cihwk,kd->cihwd', act1, w_expand, precision=HIGH))
    out = jax.nn.silu(batch_norm(pre2, norms[2, 0], norms[2, 1], axes) + image_side)
    pooled = low_back(low(lax.optimization_barrier(jnp.mean(out, axis=(2, 3)))))
    pre3 = low_back(jnp.einsum('cid,de->cie', pooled, w_head, precision=HIGH))
    act3 = low(jax.nn.silu(batch_norm(pre3, norms[3, 0], norms[3, 1], (0, 1))))
    embed = low_back(jnp.einsum('cid,dp->cip', act3, w_proj, precision=HIGH) + norms[3, 2, :PROJ])
    unit = low(embed * lax.rsqrt(lax.optimization_barrier(jnp.sum(embed * embed, axis=-1, keepdims=True)) + UNIT_EPS))
    return (low_back(jnp.einsum('cip,kp->cik', unit, protos, precision=HIGH)), queued_scores)

def balanced_assignment(prototype_scores, queued_scores):
    mass = jnp.exp(jnp.concatenate([queued_scores, prototype_scores], axis=0) / SINK_EPS)
    for turn in range(3):
        mass = mass / lax.optimization_barrier(jnp.sum(mass, axis=0, keepdims=True))
        mass = mass / lax.optimization_barrier(jnp.sum(mass, axis=1, keepdims=True))
    return mass[queued_scores.shape[0]:]

def reference(image, section_weights, section_norms, queue, pairing):
    weights = section_weights.astype(jnp.float32)
    queue_float = queue.astype(jnp.float32)
    places = jnp.arange(IMAGES, dtype=jnp.int32)
    loss = jnp.zeros((), jnp.float32)
    grad_input = []
    grad_weights = jnp.zeros_like(weights)
    grad_norms = jnp.zeros_like(section_norms)
    for step in range(MICRO):
        image_now = image[step].astype(jnp.float32)
        (prototype_scores, queued_scores), pull = jax.vjp(forward, weights, section_norms, image_now, image_now, queue_float)
        assigned_codes = jnp.stack([balanced_assignment(prototype_scores[crop_index], queued_scores[crop_index]) for crop_index in range(IMAGE_CROPS)])
        partner = places // IMG_DEV * IMG_DEV + pairing[step].astype(jnp.int32)
        inverse = jnp.zeros((IMAGES,), jnp.int32).at[partner].set(places)
        target = jnp.stack([jnp.take(assigned_codes[1], partner, axis=0), jnp.take(assigned_codes[0], inverse, axis=0)])

        def swapped(values):
            logp = jax.nn.log_softmax(values / TEMPER, axis=-1)
            return -jnp.sum(target * logp) / (IMAGE_CROPS * IMAGES)
        value, pull_loss = jax.vjp(swapped, prototype_scores)
        grad_scores, = pull_loss(jnp.ones((), jnp.float32) / MICRO)
        d_weights, d_norms, d_main, d_side, d_queue = pull((grad_scores, jnp.zeros_like(queued_scores)))
        loss = loss + value / MICRO
        grad_weights = grad_weights + d_weights
        grad_norms = grad_norms + d_norms
        grad_input.append(low(d_main) + low(d_side))
    return (loss, jnp.stack(grad_input), grad_weights, grad_norms)
```

```python
import functools

import jax
import jax.numpy as jnp
from jax import lax
from jax.experimental import pallas as pl
from jax.experimental.pallas import tpu as pltpu
from jax.sharding import PartitionSpec as P

D = 2048
WIDTH = 512
PROJ = 128
PROTOS = 3000
SIDE = 7
CROPS = 2
SECTIONS = 4
PART = WIDTH // SECTIONS
WIDE = D // SECTIONS
QUARTER = PROTOS // 4
QUARTER_PAD = 768
PLACES = SIDE * SIDE
FIRST = D * (D // WIDTH)
SECOND = FIRST + D * PROJ // WIDTH
THIRD = SECOND + PROTOS * PROJ // WIDTH

NORM_EPS = 1e-05
UNIT_EPS = 1e-06
SINK_EPS = 0.05
TEMPER = 0.1
HIGH = lax.Precision.HIGHEST
F32 = jnp.float32
BF16 = jnp.bfloat16
NT = (((1,), (1,)), ((), ()))
TN = (((0,), (0,)), ((), ()))


def dot(a, b):
    return jnp.dot(a, b, preferred_element_type=F32)


def dot_nt(a, b):
    return lax.dot_general(a, b, NT, preferred_element_type=F32)


def dot_tn(a, b):
    return lax.dot_general(a, b, TN, preferred_element_type=F32)


def flip(value, axis, step):
    count = lax.axis_size(axis)
    return lax.ppermute(value, axis, [(source, source ^ step) for source in range(count)])


def send(value, source, target):
    return lax.ppermute(value, "section", [(source, target)])


def sum_dp(value):
    count = lax.axis_size("dp")
    value = value + flip(value, "dp", 1)
    step = 2
    while step < count:
        if 2 * step < count:
            near = value + flip(value, "dp", step)
            far = flip(value, "dp", 2 * step) + flip(value, "dp", 3 * step)
            value = near + far
            step *= 4
        else:
            value = value + flip(value, "dp", step)
            step *= 2
    return value


def gather_xor(value, axis):
    return [value] + [flip(value, axis, step) for step in range(1, lax.axis_size(axis))]


def gather_dp(value):
    count = lax.axis_size("dp")
    value = jnp.stack([value, flip(value, "dp", 1)])
    step = 2
    while step < count:
        if 2 * step < count:
            value = jnp.concatenate(
                [value] + [flip(value, "dp", step * j) for j in (1, 2, 3)]
            )
            step *= 4
        else:
            value = jnp.concatenate([value, flip(value, "dp", step)])
            step *= 2
    return value


def sigmoid(v):
    return 1.0 / (1.0 + jnp.exp(-v))


def slope(v):
    s = sigmoid(v)
    return s * (1.0 + v * (1.0 - s))


def call(kernel, out, *args, scratch=(), vmem=32):
    in_specs = []
    for a in args:
        if jnp.issubdtype(a.dtype, jnp.integer):
            in_specs.append(pl.BlockSpec(memory_space=pltpu.SMEM))
        else:
            in_specs.append(pl.BlockSpec(memory_space=pltpu.VMEM))
    return pl.pallas_call(
        kernel,
        out_shape=out,
        in_specs=in_specs,
        out_specs=jax.tree.map(lambda _: pl.BlockSpec(memory_space=pltpu.VMEM), out),
        scratch_shapes=list(scratch),
        compiler_params=pltpu.CompilerParams(vmem_limit_bytes=vmem * 2**20),
    )(*args)


def shape(dims, dtype):
    return jax.ShapeDtypeStruct(tuple(dims), dtype)


def split_sums(first, second, micro):
    width = first[0].shape[1]
    rows = [jnp.sum(v, axis=0, keepdims=True) for v in first]
    rows += [jnp.sum(v, axis=0, keepdims=True) for v in second]
    rows.append(jnp.zeros((8 - 2 * micro, width), F32))
    return jnp.concatenate(rows, axis=0)


def moments(sums, m, micro, count):
    mean = sums[m : m + 1] * (1.0 / count)
    square = sums[micro + m : micro + m + 1] * (1.0 / count)
    return mean, lax.rsqrt(square - mean * mean + NORM_EPS)


def per_micro(value, micro):
    rows = value.shape[0] // micro
    return [value[m * rows : (m + 1) * rows] for m in range(micro)]


def normalized(value, sums, micro, count):
    out = []
    for m, v in enumerate(per_micro(value, micro)):
        mean, rstd = moments(sums, m, micro, count)
        out.append(((v - mean) * rstd, rstd))
    return out


def join(parts):
    return jnp.concatenate(parts, axis=0)


def tap_valid(rows, images, tap, sign):
    row = lax.broadcasted_iota(jnp.int32, (rows, PART), 0).astype(F32)
    cell = jnp.floor((row + 0.5) * (1.0 / images))
    crop = jnp.floor((cell + 0.5) * (1.0 / PLACES))
    place = cell - crop * PLACES
    y = jnp.floor((place + 0.5) * (1.0 / SIDE))
    x = place - y * SIDE
    y = y + float(sign * (tap // 3 - 1))
    x = x + float(sign * (tap % 3 - 1))
    return (y > -0.5) & (y < SIDE - 0.5) & (x > -0.5) & (x < SIDE - 0.5)


def tap_shift(value, images, tap, sign):
    rows = value.shape[0]
    offset = sign * images * (SIDE * (tap // 3 - 1) + (tap % 3 - 1))
    moved = value if offset == 0 else pltpu.roll(value, (-offset) % rows, 0)
    if tap == 4:
        return moved
    return jnp.where(tap_valid(rows, images, tap, sign), moved, 0.0)


def reduce_kernel(micro, image, weight, pre, sums):
    value = dot(image[...], weight[...])
    pre[...] = value.astype(BF16)
    parts = per_micro(value, micro)
    sums[...] = split_sums(parts, [v * v for v in parts], micro)


def fill_active(micro, count, place, pieces, sums, norm, full, own=None):
    for k, piece in enumerate(pieces):
        lanes = pl.ds(pl.multiple_of(place[k] * PART, PART), PART)
        gain = norm[0:1, lanes]
        shift = norm[1:2, lanes]
        out = []
        for xhat, _ in normalized(piece[...].astype(F32), sums[k], micro, count):
            y = xhat * gain + shift
            out.append(y * sigmoid(y))
        value = join(out).astype(BF16)
        full[:, lanes] = value
        if k == 0 and own is not None:
            own[...] = value


def conv_kernel(micro, images, count, place, p0, p1, p2, p3, sums, norm, weight, own, pre, sums_out, full):
    fill_active(micro, count, place, (p0, p1, p2, p3), sums, norm, full, own)
    active = full[...]
    total = None
    for tap in range(9):
        part = dot(active, weight[tap * WIDTH : (tap + 1) * WIDTH, :])
        part = tap_shift(part, images, tap, 1)
        total = part if total is None else total + part
    pre[...] = total.astype(BF16)
    parts = per_micro(total, micro)
    sums_out[...] = split_sums(parts, [v * v for v in parts], micro)


def expand_kernel(micro, count, place, p0, p1, p2, p3, sums, norm, weight, active, pre, sums_out):
    fill_active(micro, count, place, (p0, p1, p2, p3), sums, norm, active)
    value = dot(active[...], weight[...])
    pre[...] = value
    parts = per_micro(value, micro)
    sums_out[...] = split_sums(parts, [v * v for v in parts], micro)


def crop_rows(rows, images, transpose=False):
    shp = (rows // PLACES, rows)
    r = lax.broadcasted_iota(jnp.int32, shp, 1).astype(F32)
    q = lax.broadcasted_iota(jnp.int32, shp, 0).astype(F32)
    cell = jnp.floor((r + 0.5) * (1.0 / images))
    crop = jnp.floor((cell + 0.5) * (1.0 / PLACES))
    image = r - cell * images
    return (jnp.abs(crop * images + image - q) < 0.5).astype(F32).astype(BF16)


def pool_kernel(micro, images, count, place, pre, sums, norm, image, pooled):
    lanes = pl.ds(pl.multiple_of(place[0] * WIDE, WIDE), WIDE)
    out = []
    for xhat, _ in normalized(pre[...], sums[...], micro, count):
        out.append(xhat * norm[0:1, :] + norm[1:2, :])
    z = join(out) + image[:, lanes].astype(F32)
    out = z * sigmoid(z)
    high = out.astype(BF16)
    low = (out - high.astype(F32)).astype(BF16)
    choose = crop_rows(pre.shape[0], images)
    pooled[...] = ((dot(choose, high) + dot(choose, low)) * (1.0 / PLACES)).astype(BF16)


def out_back_kernel(micro, images, count, place, pre, sums, norm, image, d_pooled, d_z, sums_out):
    lanes = pl.ds(pl.multiple_of(place[0] * WIDE, WIDE), WIDE)
    rows = pre.shape[0]
    spread = dot_tn(crop_rows(rows, images), d_pooled[...]) * (1.0 / PLACES)
    xhats = [x for x, _ in normalized(pre[...], sums[...], micro, count)]
    z = join([x * norm[0:1, :] + norm[1:2, :] for x in xhats]) + image[:, lanes].astype(F32)
    value = spread * slope(z)
    d_z[...] = value
    parts = per_micro(value, micro)
    sums_out[...] = split_sums([v * x for v, x in zip(parts, xhats)], parts, micro)


def norm_back(value, pre, sums, back, gain, micro, count):
    out = []
    parts = per_micro(value, micro)
    for m, (xhat, rstd) in enumerate(normalized(pre, sums, micro, count)):
        by_x = back[m : m + 1] * (1.0 / count)
        plain = back[micro + m : micro + m + 1] * (1.0 / count)
        out.append(gain * rstd * (parts[m] - plain - xhat * by_x))
    return join(out)


def expand_back_kernel(micro, count, place, pre, sums, norm, d_z, back, weight, d_pre, q0, q1, q2, q3, full):
    d_low = norm_back(d_z[...], pre[...], sums[...], back[...], norm[0:1, :], micro, count).astype(BF16)
    d_pre[...] = d_low
    full[...] = dot_nt(d_low, weight[...])
    for k, q in enumerate((q0, q1, q2, q3)):
        lanes = pl.ds(pl.multiple_of(place[k] * PART, PART), PART)
        q[...] = full[:, lanes].astype(BF16)


def silu_back_kernel(micro, count, place, q0, q1, q2, q3, pre, sums, norm, d_y, sums_out):
    total = (q0[...].astype(F32) + q1[...].astype(F32)) + (q2[...].astype(F32) + q3[...].astype(F32))
    d_active = total.astype(BF16).astype(F32)
    finish_silu(micro, count, place, d_active, pre, sums, norm, d_y, sums_out)


def finish_silu(micro, count, place, d_active, pre, sums, norm, d_y, sums_out):
    lanes = pl.ds(pl.multiple_of(place[0] * PART, PART), PART)
    gain = norm[0:1, lanes]
    shift = norm[1:2, lanes]
    values, products = [], []
    parts = per_micro(d_active, micro)
    for m, (xhat, _) in enumerate(normalized(pre[...].astype(F32), sums[0], micro, count)):
        value = parts[m] * slope(xhat * gain + shift)
        values.append(value)
        products.append(value * xhat)
    d_y[...] = join(values).astype(BF16)
    sums_out[...] = split_sums(products, values, micro)


def fill_d_pre(micro, count, place, pieces, backs, pres, sums, norm, full, grads):
    for k, piece in enumerate(pieces):
        lanes = pl.ds(pl.multiple_of(place[k] * PART, PART), PART)
        value = norm_back(
            piece[...].astype(F32), pres[k][...].astype(F32), sums[k], backs[k], norm[0:1, lanes], micro, count
        )
        full[:, lanes] = value.astype(BF16)
        back = backs[k]
        gain = back[0:1]
        shift = back[micro : micro + 1]
        for m in range(1, micro):
            gain = gain + back[m : m + 1]
            shift = shift + back[micro + m : micro + m + 1]
        grads[:, lanes] = join([gain, shift, jnp.zeros((6, PART), F32)])


def conv_back_kernel(
    micro, images, count, place, d0, d1, d2, d3, back, p0, p1, p2, p3, sums, norm, weight, pre, sums0, norm0,
    d_full, grads, d_y, sums_out,
):
    fill_d_pre(micro, count, place, (d0, d1, d2, d3), back, (p0, p1, p2, p3), sums, norm, d_full, grads)
    d_low = d_full[...]
    total = None
    for tap in range(9):
        part = dot_nt(d_low, weight[tap * PART : (tap + 1) * PART, :])
        part = tap_shift(part, images, tap, -1)
        total = part if total is None else total + part
    d_active = total.astype(BF16).astype(F32)
    finish_silu(micro, count, place, d_active, pre, sums0, norm0, d_y, sums_out)


def reduce_back_kernel(
    micro, count, place, d0, d1, d2, d3, back, p0, p1, p2, p3, sums, norm, weight, d_z, d_full, grads, grad_in
):
    fill_d_pre(micro, count, place, (d0, d1, d2, d3), back, (p0, p1, p2, p3), sums, norm, d_full, grads)
    main = dot_nt(d_full[...], weight[...]).astype(BF16).astype(F32)
    grad_in[...] = main + d_z[...].astype(BF16).astype(F32)


def taps_kernel(images, active, out):
    value = active[...].astype(F32)
    for tap in range(9):
        out[:, tap * PART : (tap + 1) * PART] = tap_shift(value, images, tap, 1).astype(BF16)


def head(pooled, w_head, w_proj, protos, norm, queue, match, micro, images, dp):
    rows = pooled.shape[0]
    group = rows // micro
    half = group // CROPS
    scale_all = 1.0 / (TEMPER * CROPS * half * micro)
    pre = dot(pooled, w_head)

    def by_micro(v):
        return v.reshape(micro, group, v.shape[-1])

    pre_m = by_micro(pre)
    mean = jnp.mean(pre_m, axis=1, keepdims=True)
    square = jnp.mean(pre_m * pre_m, axis=1, keepdims=True)
    rstd = lax.rsqrt(square - mean * mean + NORM_EPS)
    xhat = (pre_m - mean) * rstd
    y = xhat * norm[0] + norm[1]
    active = (y * sigmoid(y)).astype(BF16).reshape(rows, D)
    embed = dot(active, w_proj) + norm[2, :PROJ]
    recip = lax.rsqrt(jnp.sum(embed * embed, axis=1, keepdims=True) + UNIT_EPS)
    unit = (embed * recip).astype(BF16)
    scores = dot_nt(unit, protos)
    valid = lax.broadcasted_iota(jnp.int32, (1, 4, QUARTER_PAD), 2).reshape(1, 4 * QUARTER_PAD) < QUARTER
    own_mass = jnp.where(valid, jnp.exp(scores / SINK_EPS), 0.0).reshape(micro, CROPS, half, -1)
    queue_mass = jnp.where(valid, jnp.exp(jnp.einsum("cqp,kp->cqk", queue, protos, preferred_element_type=F32) / SINK_EPS), 0.0)
    codes = []
    for m in range(micro):
        for c in range(CROPS):
            a, b = queue_mass[c], own_mass[m, c]
            column = jnp.sum(a, axis=0, keepdims=True) + jnp.sum(b, axis=0, keepdims=True)
            once = jnp.where(valid, 1.0 / column, 0.0)
            a, b = a * once, b * once
            scale = valid.astype(F32)
            for turn in range(2):
                ra = 1.0 / jnp.sum(a * scale, axis=1, keepdims=True)
                rb = 1.0 / jnp.sum(b * scale, axis=1, keepdims=True)
                column = jnp.sum(a * ra, axis=0, keepdims=True) + jnp.sum(b * rb, axis=0, keepdims=True)
                scale = jnp.where(valid, 1.0 / column, 0.0)
            b = b * scale
            codes.append(b / jnp.sum(b, axis=1, keepdims=True))
    targets = []
    for m in range(micro):
        targets.append(jnp.dot(match[m], codes[m * CROPS + 1], precision=HIGH))
        targets.append(jnp.dot(match[m].T, codes[m * CROPS], precision=HIGH))
    target = jnp.concatenate(targets)
    logits = jnp.where(valid, scores / TEMPER, -1e30)
    logp = jax.nn.log_softmax(logits, axis=1)
    loss = -jnp.sum(jnp.where(valid, target * logp, 0.0)) * (TEMPER * scale_all)
    d_scores = ((jnp.exp(logp) * jnp.sum(target, axis=1, keepdims=True) - target) * scale_all).astype(BF16)
    d_unit = dot(d_scores, protos)
    d_embed = (
        recip * d_unit - embed * (recip * recip * recip) * jnp.sum(d_unit * embed, axis=1, keepdims=True)
    ).astype(BF16)
    d_active = dot_nt(d_embed, w_proj)
    d_y = by_micro(d_active) * slope(y)
    by_x = jnp.sum(d_y * xhat, axis=1, keepdims=True)
    plain = jnp.sum(d_y, axis=1, keepdims=True)
    d_pre = (norm[0] * rstd * (d_y - plain / group - xhat * by_x / group)).astype(BF16).reshape(rows, D)
    bias = jnp.pad(jnp.sum(d_embed.astype(F32), axis=0), (0, D - PROJ))
    grads = jnp.stack([jnp.sum(by_x, axis=(0, 1)), jnp.sum(plain, axis=(0, 1)), bias])
    return loss, grads, active, unit, d_scores, d_embed, d_pre


def interleave(width):
    row = lax.broadcasted_iota(jnp.int32, (4 * width, 4 * width), 0)
    column = lax.broadcasted_iota(jnp.int32, (4 * width, 4 * width), 1)
    return (column == 4 * (row % width) + row // width).astype(BF16)


def head_grads_kernel(pooled, active, unit, d_scores, d_embed, d_pre, choose, weave, out):
    own = choose.shape[1]
    block = PART
    parts = []
    for q in range(4):
        own_d = dot(d_pre[:, q * WIDTH : (q + 1) * WIDTH], choose[...]).astype(BF16)
        parts.append(dot_tn(own_d, pooled[...]).astype(BF16))
    for b in range(D // block):
        mixed = jnp.concatenate([p[:, b * block : (b + 1) * block] for p in parts], axis=1)
        out[:, 4 * block * b : 4 * block * (b + 1)] = dot(mixed, weave[...])
    proj = jnp.zeros((own, WIDTH), F32)
    proto = jnp.zeros((own, QUARTER_PAD), F32)
    apart = []
    for b in range(4):
        apart.append(dot_nt(active[:, b * WIDTH : (b + 1) * WIDTH], weave[...]).astype(BF16))
    for a in range(4):
        some = choose[a * PROJ : (a + 1) * PROJ, :]
        own_e = dot(d_embed[...], some).astype(BF16)
        own_u = dot(unit[...], some).astype(BF16)
        column = jnp.concatenate([v[:, a * block : (a + 1) * block] for v in apart], axis=1)
        proj = proj + dot_tn(own_e, column)
        proto = proto + dot_tn(own_u, d_scores[:, a * QUARTER_PAD : (a + 1) * QUARTER_PAD])
    out[:, FIRST:SECOND] = proj
    out[:, SECOND:] = proto[:, : out.shape[1] - SECOND]


def body(image, section_weights, section_norms, queue, pairing):
    micro, images = image.shape[0], image.shape[2]
    ndp = lax.axis_size("dp")
    t = lax.axis_index("section")
    dp = lax.axis_index("dp")
    place = jnp.stack([t ^ k for k in range(SECTIONS)]).astype(jnp.int32)
    cells = CROPS * PLACES * images
    rows = micro * cells
    count = float(cells * ndp)
    packed = section_weights[0]
    param_rows = packed.shape[0]
    flat = image.transpose(0, 1, 3, 4, 2, 5).reshape(rows, D)

    def part_rows(value):
        size = value.shape[0] // ndp
        return lax.dynamic_slice_in_dim(value, dp * size, size, 0)

    def whole(part):
        return lax.all_gather(part, "dp", axis=0, tiled=True)

    head_rows = part_rows(packed[:D])
    columns = [head_rows[:, j * PART : (j + 1) * PART] for j in range(SECTIONS)]
    got = columns[0]
    came = [send(columns[j], 0, j) for j in range(1, SECTIONS)]
    w_reduce = whole(jnp.where(t == 0, got, came[0] + came[1] + came[2]))

    conv_rows = part_rows(packed[: 9 * WIDTH])
    conv_columns = [conv_rows[:, j * PART : (j + 1) * PART] for j in range(SECTIONS)]
    expand_rows = head_rows.reshape(WIDTH // ndp, 4, WIDTH)
    expand_slices = [expand_rows[:, j] for j in range(SECTIONS)]
    came_c = [send(conv_columns[j], 1, j) for j in (0, 2, 3)]
    w_conv = whole(jnp.where(t == 1, conv_columns[1], came_c[0] + came_c[1] + came_c[2]))
    came_e = [send(expand_slices[j], 2, j) for j in (0, 1, 3)]
    w_expand = whole(jnp.where(t == 2, expand_slices[2], came_e[0] + came_e[1] + came_e[2]))
    by_input = packed[: 9 * WIDTH].reshape(9, SECTIONS, PART, WIDTH)
    back_slices = [part_rows(by_input[:, j].reshape(9 * PART, WIDTH)) for j in range(SECTIONS)]
    came_b = [send(back_slices[j], 1, j) for j in (0, 2, 3)]
    w_conv_back = whole(jnp.where(t == 1, back_slices[1], came_b[0] + came_b[1] + came_b[2]))
    reduce_slices = [part_rows(packed[j * WIDE : (j + 1) * WIDE]) for j in range(SECTIONS)]
    came_r = [send(reduce_slices[j], 0, j) for j in range(1, SECTIONS)]
    w_reduce_back = whole(jnp.where(t == 0, reduce_slices[0], came_r[0] + came_r[1] + came_r[2]))

    norms = lax.all_gather(section_norms[0], "section", axis=0)
    norm0, norm1 = norms[0, :, :WIDTH], norms[1, :, :WIDTH]
    norm2 = lax.dynamic_slice_in_dim(norms[2], t * WIDE, WIDE, 1)
    norm3 = section_norms[0]
    queue_all = lax.all_gather(queue, "dp", axis=1, tiled=True)
    pairing_all = lax.all_gather(pairing.astype(F32), "dp", axis=1, tiled=True).astype(jnp.int32)

    def piece():
        return shape((rows, PART), BF16)

    sums_of = shape((8, PART), F32)
    k = functools.partial

    def exchange(value, sums):
        sums = jnp.stack(gather_xor(sums, "section"))
        pieces = gather_xor(value, "section")
        return pieces, sum_dp(sums.reshape(SECTIONS * 8, PART)).reshape(SECTIONS, 8, PART)

    pre0, part = call(k(reduce_kernel, micro), (piece(), sums_of), flat, w_reduce)
    pre0s, sums0 = exchange(pre0, part)
    active0, pre1, part = call(
        k(conv_kernel, micro, images, count),
        (piece(), piece(), sums_of),
        place, *pre0s, sums0, norm0, w_conv,
        scratch=[pltpu.VMEM((rows, WIDTH), BF16)],
    )
    pre1s, sums1 = exchange(pre1, part)
    active1, pre2, part = call(
        k(expand_kernel, micro, count),
        (shape((rows, WIDTH), BF16), shape((rows, WIDE), F32), shape((8, WIDE), F32)),
        place, *pre1s, sums1, norm1, w_expand,
    )
    sums2 = sum_dp(part)
    pooled = call(
        k(pool_kernel, micro, images, count),
        shape((rows // PLACES, WIDE), BF16),
        place, pre2, sums2, norm2, flat,
    )

    head_order = jnp.arange(rows // PLACES * ndp, dtype=jnp.int32)
    per_dp = rows // PLACES
    block, inner = head_order // per_dp, head_order % per_dp
    group, single = inner // images, inner % images
    position = (group * ndp + (block ^ dp)) * images + single
    order = (position[None, :] == head_order[:, None]).astype(BF16)
    all_pooled = gather_dp(pooled).reshape(per_dp * ndp, WIDE)
    came_p = [send(all_pooled, j, 3) for j in range(3)]
    all_pooled = dot(order, jnp.concatenate(came_p + [all_pooled], axis=1)).astype(BF16)
    w_head = packed[:FIRST].reshape(D, D)
    w_proj = packed[FIRST:SECOND].reshape(D, PROJ)
    table = jnp.pad(packed[SECOND:THIRD], ((0, QUARTER_PAD - QUARTER), (0, 0)))
    protos = jnp.concatenate([table[:, a * PROJ : (a + 1) * PROJ] for a in range(4)], axis=0)
    half = images * ndp
    left = jnp.arange(half, dtype=jnp.int32)
    partner = left // images * images + pairing_all
    match = (partner[:, :, None] == left[None, None, :]).astype(F32)
    loss, grads3, active3, unit, d_scores, d_embed, d_pre3 = head(
        all_pooled, w_head, w_proj, protos, norm3, queue_all, match, micro, images, dp
    )
    d_pooled = dot_nt(dot_tn(order[:, :per_dp], d_pre3).astype(BF16), w_head).astype(BF16)
    parts = [d_pooled[:, j * WIDE : (j + 1) * WIDE] for j in range(SECTIONS)]
    came_d = [send(parts[j], 3, j) for j in range(3)]
    d_pooled = jnp.where(t == 3, parts[3], came_d[0] + came_d[1] + came_d[2])

    d_z, part = call(
        k(out_back_kernel, micro, images, count),
        (shape((rows, WIDE), F32), shape((8, WIDE), F32)),
        place, pre2, sums2, norm2, flat, d_pooled,
    )
    back2 = sum_dp(part)
    d_pre2, *partial = call(
        k(expand_back_kernel, micro, count),
        (shape((rows, WIDE), BF16), piece(), piece(), piece(), piece()),
        place, pre2, sums2, norm2, d_z, back2, w_expand,
        scratch=[pltpu.VMEM((rows, WIDTH), F32)],
    )
    partial = [partial[0]] + [flip(partial[j], "section", j) for j in range(1, SECTIONS)]
    d_y1, part = call(
        k(silu_back_kernel, micro, count),
        (piece(), sums_of),
        place, *partial, pre1, sums1, norm1,
    )
    d_y1s, back1 = exchange(d_y1, part)
    d_pre1, grads1, d_y0, part = call(
        k(conv_back_kernel, micro, images, count),
        (shape((rows, WIDTH), BF16), shape((8, WIDTH), F32), piece(), sums_of),
        place, *d_y1s, back1, *pre1s, sums1, norm1, w_conv_back, pre0, sums0, norm0,
    )
    d_y0s, back0 = exchange(d_y0, part)
    d_pre0, grads0, grad_in = call(
        k(reduce_back_kernel, micro, count),
        (shape((rows, WIDTH), BF16), shape((8, WIDTH), F32), shape((rows, WIDE), F32)),
        place, *d_y0s, back0, *pre0s, sums0, norm0, w_reduce_back, d_z,
    )

    def scatter(value):
        return lax.psum_scatter(value.astype(BF16), "dp", scatter_dimension=0, tiled=True)

    g_expand = scatter(dot_tn(d_pre2, active1))
    taps = call(k(taps_kernel, images), shape((rows, 9 * PART), BF16), active0)
    g_conv = scatter(dot_tn(d_pre1, taps))
    own_image = lax.dynamic_slice_in_dim(flat, t * WIDE, WIDE, 1)
    g_reduce = scatter(dot_tn(d_pre0, own_image))
    own = WIDTH // ndp
    to_conv = [send(g_conv, j, 1) for j in (0, 2, 3)]
    to_expand = [send(g_expand, j, 2) for j in (0, 1, 3)]
    to_reduce = [send(g_reduce, j, 0) for j in (1, 2, 3)]
    pick = (jnp.arange(WIDTH, dtype=jnp.int32)[:, None] == dp * own + jnp.arange(own, dtype=jnp.int32)[None, :]).astype(BF16)
    weave = interleave(PART)

    def fill(value):
        return jnp.pad(value, ((0, 0), (0, param_rows - value.shape[1])))

    def finish_reduce():
        return fill(jnp.concatenate([g_reduce] + to_reduce, axis=1).astype(F32))

    def finish_conv():
        four = [to_conv[0], g_conv, to_conv[1], to_conv[2]]
        cols = [f[:, tap * PART : (tap + 1) * PART] for tap in range(9) for f in four]
        return fill(jnp.concatenate(cols, axis=1).astype(F32))

    def finish_expand():
        four = [to_expand[0], to_expand[1], g_expand, to_expand[2]]
        cols = []
        for b in range(WIDTH // PART):
            mixed = jnp.concatenate([f[:, b * PART : (b + 1) * PART] for f in four], axis=1)
            cols.append(dot(mixed, weave))
        return fill(jnp.concatenate(cols, axis=1))

    def finish_head():
        return call(
            head_grads_kernel,
            shape((own, param_rows), F32),
            all_pooled, active3, unit, d_scores, d_embed, d_pre3, pick, weave,
        )

    weight_grads = lax.switch(t, [finish_reduce, finish_conv, finish_expand, finish_head])
    loss = jnp.where(t == 3, loss, 0.0)
    own_norm = jnp.concatenate([back2[:1] + back2[1:2], back2[micro : micro + 1] + back2[micro + 1 : micro + 2]])
    note = jnp.concatenate([own_norm, jnp.full((1, WIDE), loss), jnp.zeros((5, WIDE), F32)])
    notes = lax.all_gather(note, "section", axis=0)
    loss = jnp.sum(notes[:, 2, 0])
    grads2 = jnp.pad(notes[:, :2].transpose(1, 0, 2).reshape(2, D), ((0, 1), (0, 0)))

    def narrow(value):
        return jnp.pad(value[:3], ((0, 0), (0, D - WIDTH)))

    norm_grads = jnp.where(
        t == 0, narrow(grads0), jnp.where(t == 1, narrow(grads1), jnp.where(t == 2, grads2, grads3))
    )
    grad_in = grad_in.reshape(micro, CROPS, SIDE, SIDE, images, WIDE).transpose(0, 1, 4, 2, 3, 5)
    return (loss, grad_in, weight_grads.T[None], norm_grads[None])


def solution(mesh):
    in_specs = (
        P(None, None, "dp", None, None, None),
        P("section", None, None),
        P("section", None, None),
        P(None, "dp", None),
        P(None, "dp"),
    )
    out_specs = (
        P(),
        P(None, None, "dp", None, None, "section"),
        P("section", None, "dp"),
        P("section", None, None),
    )
    return jax.shard_map(body, mesh=mesh, in_specs=in_specs, out_specs=out_specs, check_vma=False)
```

```python
import functools

import jax
import jax.numpy as jnp
from jax import lax
from jax.experimental import pallas as pl
from jax.experimental.pallas import tpu as pltpu
from jax.sharding import PartitionSpec as P

D = 2048
WIDTH = 512
PROJ = 128
PROTOS = 3000
SIDE = 7
CROPS = 2
SECTIONS = 4
PART = WIDTH // SECTIONS
WIDE = D // SECTIONS
QUARTER = PROTOS // 4
QUARTER_PAD = 768
PLACES = SIDE * SIDE
FIRST = D * (D // WIDTH)
SECOND = FIRST + D * PROJ // WIDTH
THIRD = SECOND + PROTOS * PROJ // WIDTH

NORM_EPS = 1e-05
UNIT_EPS = 1e-06
SINK_EPS = 0.05
TEMPER = 0.1
HIGH = lax.Precision.HIGHEST
F32 = jnp.float32
BF16 = jnp.bfloat16
NT = (((1,), (1,)), ((), ()))
TN = (((0,), (0,)), ((), ()))


def dot(a, b):
    return jnp.dot(a, b, preferred_element_type=F32)


def dot_nt(a, b):
    return lax.dot_general(a, b, NT, preferred_element_type=F32)


def dot_tn(a, b):
    return lax.dot_general(a, b, TN, preferred_element_type=F32)


def flip(value, axis, step):
    count = lax.axis_size(axis)
    return lax.ppermute(value, axis, [(source, source ^ step) for source in range(count)])


def send(value, source, target):
    return lax.ppermute(value, "section", [(source, target)])


def sum_dp(value):
    count = lax.axis_size("dp")
    value = value + flip(value, "dp", 1)
    step = 2
    while step < count:
        if 2 * step < count:
            near = value + flip(value, "dp", step)
            far = flip(value, "dp", 2 * step) + flip(value, "dp", 3 * step)
            value = near + far
            step *= 4
        else:
            value = value + flip(value, "dp", step)
            step *= 2
    return value


def gather_xor(value, axis):
    return [value] + [flip(value, axis, step) for step in range(1, lax.axis_size(axis))]


def gather_dp(value):
    count = lax.axis_size("dp")
    value, offsets = value[None], [0]
    step = 2
    while step < count:
        far = (1, 2, 3) if 2 * step < count else (1,)
        value = jnp.concatenate([value] + [flip(value, "dp", step * j) for j in far])
        offsets = offsets + [o ^ (step * j) for j in far for o in offsets]
        step *= len(far) + 1
    value = jnp.concatenate([value, flip(value, "dp", 1)])
    return offsets + [o ^ 1 for o in offsets], value


def sigmoid(v):
    return 1.0 / (1.0 + jnp.exp(-v))


def slope(v):
    s = sigmoid(v)
    return s * (1.0 + v * (1.0 - s))


def call(kernel, out, *args, scratch=(), vmem=20):
    in_specs = []
    for a in args:
        if jnp.issubdtype(a.dtype, jnp.integer):
            in_specs.append(pl.BlockSpec(memory_space=pltpu.SMEM))
        else:
            in_specs.append(pl.BlockSpec(memory_space=pltpu.VMEM))
    return pl.pallas_call(
        kernel,
        out_shape=out,
        in_specs=in_specs,
        out_specs=jax.tree.map(lambda _: pl.BlockSpec(memory_space=pltpu.VMEM), out),
        scratch_shapes=list(scratch),
        compiler_params=pltpu.CompilerParams(vmem_limit_bytes=vmem * 2**20),
    )(*args)


def shape(dims, dtype):
    return jax.ShapeDtypeStruct(tuple(dims), dtype)


def split_sums(first, second, micro):
    width = first[0].shape[1]
    rows = [jnp.sum(v, axis=0, keepdims=True) for v in first]
    rows += [jnp.sum(v, axis=0, keepdims=True) for v in second]
    rows.append(jnp.zeros((8 - 2 * micro, width), F32))
    return jnp.concatenate(rows, axis=0)


def moments(sums, m, micro, count):
    mean = sums[m : m + 1] * (1.0 / count)
    square = sums[micro + m : micro + m + 1] * (1.0 / count)
    return mean, lax.rsqrt(square - mean * mean + NORM_EPS)


def per_micro(value, micro):
    rows = value.shape[0] // micro
    return [value[m * rows : (m + 1) * rows] for m in range(micro)]


def normalized(value, sums, micro, count):
    out = []
    for m, v in enumerate(per_micro(value, micro)):
        mean, rstd = moments(sums, m, micro, count)
        out.append(((v - mean) * rstd, rstd))
    return out


def join(parts):
    return jnp.concatenate(parts, axis=0)


def tap_valid(rows, images, tap, sign):
    row = lax.broadcasted_iota(jnp.int32, (rows, PART), 0).astype(F32)
    cell = jnp.floor((row + 0.5) * (1.0 / images))
    crop = jnp.floor((cell + 0.5) * (1.0 / PLACES))
    place = cell - crop * PLACES
    y = jnp.floor((place + 0.5) * (1.0 / SIDE))
    x = place - y * SIDE
    y = y + float(sign * (tap // 3 - 1))
    x = x + float(sign * (tap % 3 - 1))
    return (y > -0.5) & (y < SIDE - 0.5) & (x > -0.5) & (x < SIDE - 0.5)


def tap_shift(value, images, tap, sign):
    rows = value.shape[0]
    offset = sign * images * (SIDE * (tap // 3 - 1) + (tap % 3 - 1))
    moved = value if offset == 0 else pltpu.roll(value, (-offset) % rows, 0)
    if tap == 4:
        return moved
    return jnp.where(tap_valid(rows, images, tap, sign), moved, 0.0)


def reduce_kernel(micro, place, image, w0, w1, pre, sums):
    half = D // 2
    first = pl.ds(pl.multiple_of(place[4] * half, half), half)
    second = pl.ds(pl.multiple_of(place[5] * half, half), half)
    value = dot(image[:, first], w0[...]) + dot(image[:, second], w1[...])
    pre[...] = value
    parts = per_micro(value, micro)
    sums[...] = split_sums(parts, [v * v for v in parts], micro)


def active_kernel(micro, count, pre, sums, norm, active):
    out = []
    for xhat, _ in normalized(pre[...], sums[...], micro, count):
        y = xhat * norm[0:1, :] + norm[1:2, :]
        out.append(y * sigmoid(y))
    active[...] = join(out).astype(BF16)


def fill(place, pieces, full):
    for k, piece in enumerate(pieces):
        full[:, pl.ds(pl.multiple_of(place[k] * PART, PART), PART)] = piece[...]


def conv_kernel(micro, images, place, a0, a1, a2, a3, w0, w1, pre, sums, full):
    fill(place, (a0, a1, a2, a3), full)
    active = full[...]
    total = None
    for tap in range(9):
        part = None
        for j, w in enumerate((w0, w1)):
            half = WIDTH // 2
            lanes = pl.ds(pl.multiple_of(place[4 + j] * half, half), half)
            more = dot(full[:, lanes], w[tap * half : (tap + 1) * half, :])
            part = more if part is None else part + more
        part = tap_shift(part, images, tap, 1)
        total = part if total is None else total + part
    pre[...] = total
    parts = per_micro(total, micro)
    sums[...] = split_sums(parts, [v * v for v in parts], micro)


def expand_kernel(micro, place, a0, a1, a2, a3, w0, w1, active, pre, sums):
    fill(place, (a0, a1, a2, a3), active)
    half = WIDTH // 2
    value = None
    for j, w in enumerate((w0, w1)):
        lanes = pl.ds(pl.multiple_of(place[4 + j] * half, half), half)
        more = dot(active[:, lanes], w[...])
        value = more if value is None else value + more
    pre[...] = value
    parts = per_micro(value, micro)
    sums[...] = split_sums(parts, [v * v for v in parts], micro)


def crop_rows(rows, images, transpose=False):
    shp = (rows // PLACES, rows)
    r = lax.broadcasted_iota(jnp.int32, shp, 1).astype(F32)
    q = lax.broadcasted_iota(jnp.int32, shp, 0).astype(F32)
    cell = jnp.floor((r + 0.5) * (1.0 / images))
    crop = jnp.floor((cell + 0.5) * (1.0 / PLACES))
    image = r - cell * images
    return (jnp.abs(crop * images + image - q) < 0.5).astype(F32).astype(BF16)


def pool_kernel(micro, images, count, place, pre, sums, norm, image, pooled):
    lanes = pl.ds(pl.multiple_of(place[0] * WIDE, WIDE), WIDE)
    out = []
    for xhat, _ in normalized(pre[...], sums[...], micro, count):
        out.append(xhat * norm[0:1, :] + norm[1:2, :])
    z = join(out) + image[:, lanes].astype(F32)
    out = z * sigmoid(z)
    high = out.astype(BF16)
    low = (out - high.astype(F32)).astype(BF16)
    choose = crop_rows(pre.shape[0], images)
    pooled[...] = ((dot(choose, high) + dot(choose, low)) * (1.0 / PLACES)).astype(BF16)


def out_back_kernel(micro, images, count, place, pre, sums, norm, image, own, r0, r1, r2, d_z, sums_out):
    lanes = pl.ds(pl.multiple_of(place[0] * WIDE, WIDE), WIDE)
    rows = pre.shape[0]
    came = (r0[...].astype(F32) + r1[...].astype(F32) + r2[...].astype(F32)).astype(BF16)
    d_pooled = jnp.where(place[0] == SECTIONS - 1, own[...], came)
    spread = dot_tn(crop_rows(rows, images), d_pooled) * (1.0 / PLACES)
    xhats = [x for x, _ in normalized(pre[...], sums[...], micro, count)]
    z = join([x * norm[0:1, :] + norm[1:2, :] for x in xhats]) + image[:, lanes].astype(F32)
    value = spread * slope(z)
    d_z[...] = value
    parts = per_micro(value, micro)
    sums_out[...] = split_sums([v * x for v, x in zip(parts, xhats)], parts, micro)


def norm_back(value, pre, sums, back, gain, micro, count):
    out = []
    parts = per_micro(value, micro)
    for m, (xhat, rstd) in enumerate(normalized(pre, sums, micro, count)):
        by_x = back[m : m + 1] * (1.0 / count)
        plain = back[micro + m : micro + m + 1] * (1.0 / count)
        out.append(gain * rstd * (parts[m] - plain - xhat * by_x))
    return join(out)


def norm_back_kernel(micro, count, d_y, pre, sums, back, norm, d_pre):
    d_pre[...] = norm_back(d_y[...], pre[...], sums[...], back[...], norm[0:1, :], micro, count).astype(BF16)


def expand_back_kernel(micro, count, place, pre, sums, norm, d_z, back, w0, w1, d_pre, q0, q1, q2, q3, full):
    d_low = norm_back(d_z[...], pre[...], sums[...], back[...], norm[0:1, :], micro, count).astype(BF16)
    d_pre[...] = d_low
    half = WIDTH // 2
    for j, w in enumerate((w0, w1)):
        full[:, pl.ds(pl.multiple_of(place[4 + j] * half, half), half)] = dot_nt(d_low, w[...])
    for k, q in enumerate((q0, q1, q2, q3)):
        lanes = pl.ds(pl.multiple_of(place[k] * PART, PART), PART)
        q[...] = full[:, lanes].astype(BF16)


def finish_silu(micro, count, d_active, pre, sums, norm, d_y, sums_out):
    values, products = [], []
    parts = per_micro(d_active, micro)
    for m, (xhat, _) in enumerate(normalized(pre[...], sums[...], micro, count)):
        value = parts[m] * slope(xhat * norm[0:1, :] + norm[1:2, :])
        values.append(value)
        products.append(value * xhat)
    d_y[...] = join(values)
    sums_out[...] = split_sums(products, values, micro)


def silu_back_kernel(micro, count, q0, q1, q2, q3, pre, sums, norm, d_y, sums_out):
    total = (q0[...].astype(F32) + q1[...].astype(F32)) + (q2[...].astype(F32) + q3[...].astype(F32))
    finish_silu(micro, count, total.astype(BF16).astype(F32), pre, sums, norm, d_y, sums_out)


def conv_back_kernel(micro, images, count, place, d0, d1, d2, d3, w0, w1, pre, sums, norm, d_full, d_y, sums_out, back):
    fill(place, (d0, d1, d2, d3), d_full)
    d_low = d_full[...]
    half = PART // 2
    for j, w in enumerate((w0, w1)):
        for tap in range(9):
            at = pl.ds(pl.multiple_of(tap * PART + place[4 + j] * half, half), half)
            back[at, :] = w[tap * half : (tap + 1) * half, :]
    total = None
    for tap in range(9):
        part = dot_nt(d_low, back[tap * PART : (tap + 1) * PART, :])
        part = tap_shift(part, images, tap, -1)
        total = part if total is None else total + part
    finish_silu(micro, count, total.astype(BF16).astype(F32), pre, sums, norm, d_y, sums_out)


def reduce_back_kernel(place, d0, d1, d2, d3, w0, w1, d_z, d_full, grad_in, full):
    fill(place, (d0, d1, d2, d3), d_full)
    half = WIDE // 2
    for j, w in enumerate((w0, w1)):
        full[:, pl.ds(pl.multiple_of(place[4 + j] * half, half), half)] = dot_nt(d_full[...], w[...])
    grad_in[...] = full[...].astype(BF16).astype(F32) + d_z[...].astype(BF16).astype(F32)


def taps_kernel(images, active, out):
    value = active[...].astype(F32)
    for tap in range(9):
        out[:, tap * PART : (tap + 1) * PART] = tap_shift(value, images, tap, 1).astype(BF16)


def head(pooled, w_head, w_proj, protos, norm, queue, match, micro, images, dp):
    rows = pooled.shape[0]
    group = rows // micro
    half = group // CROPS
    scale_all = 1.0 / (TEMPER * CROPS * half * micro)
    pre = dot(pooled, w_head)

    def by_micro(v):
        return v.reshape(micro, group, v.shape[-1])

    pre_m = by_micro(pre)
    mean = jnp.mean(pre_m, axis=1, keepdims=True)
    square = jnp.mean(pre_m * pre_m, axis=1, keepdims=True)
    rstd = lax.rsqrt(square - mean * mean + NORM_EPS)
    xhat = (pre_m - mean) * rstd
    y = xhat * norm[0] + norm[1]
    active = (y * sigmoid(y)).astype(BF16).reshape(rows, D)
    embed = dot(active, w_proj) + norm[2, :PROJ]
    recip = lax.rsqrt(jnp.sum(embed * embed, axis=1, keepdims=True) + UNIT_EPS)
    unit = (embed * recip).astype(BF16)
    scores = dot_nt(unit, protos)
    valid = lax.broadcasted_iota(jnp.int32, (1, 4, QUARTER_PAD), 2).reshape(1, 4 * QUARTER_PAD) < QUARTER
    own_mass = jnp.where(valid, jnp.exp(scores / SINK_EPS), 0.0).reshape(micro, CROPS, half, -1)
    queue_mass = jnp.where(valid, jnp.exp(jnp.einsum("cqp,kp->cqk", queue, protos, preferred_element_type=F32) / SINK_EPS), 0.0)
    codes = []
    for m in range(micro):
        for c in range(CROPS):
            a, b = queue_mass[c], own_mass[m, c]
            column = jnp.sum(a, axis=0, keepdims=True) + jnp.sum(b, axis=0, keepdims=True)
            once = jnp.where(valid, 1.0 / column, 0.0)
            a, b = a * once, b * once
            scale = valid.astype(F32)
            for turn in range(2):
                ra = 1.0 / jnp.sum(a * scale, axis=1, keepdims=True)
                rb = 1.0 / jnp.sum(b * scale, axis=1, keepdims=True)
                column = jnp.sum(a * ra, axis=0, keepdims=True) + jnp.sum(b * rb, axis=0, keepdims=True)
                scale = jnp.where(valid, 1.0 / column, 0.0)
            b = b * scale
            codes.append(b / jnp.sum(b, axis=1, keepdims=True))
    targets = []
    for m in range(micro):
        targets.append(jnp.dot(match[m], codes[m * CROPS + 1], precision=HIGH))
        targets.append(jnp.dot(match[m].T, codes[m * CROPS], precision=HIGH))
    target = jnp.concatenate(targets)
    logits = jnp.where(valid, scores / TEMPER, -1e30)
    logp = jax.nn.log_softmax(logits, axis=1)
    loss = -jnp.sum(jnp.where(valid, target * logp, 0.0)) * (TEMPER * scale_all)
    d_scores = ((jnp.exp(logp) * jnp.sum(target, axis=1, keepdims=True) - target) * scale_all).astype(BF16)
    d_unit = dot(d_scores, protos)
    d_embed = (
        recip * d_unit - embed * (recip * recip * recip) * jnp.sum(d_unit * embed, axis=1, keepdims=True)
    ).astype(BF16)
    d_active = dot_nt(d_embed, w_proj)
    d_y = by_micro(d_active) * slope(y)
    by_x = jnp.sum(d_y * xhat, axis=1, keepdims=True)
    plain = jnp.sum(d_y, axis=1, keepdims=True)
    d_pre = (norm[0] * rstd * (d_y - plain / group - xhat * by_x / group)).astype(BF16).reshape(rows, D)
    bias = jnp.pad(jnp.sum(d_embed.astype(F32), axis=0), (0, D - PROJ))
    grads = jnp.stack([jnp.sum(by_x, axis=(0, 1)), jnp.sum(plain, axis=(0, 1)), bias])
    return loss, grads, active, unit, d_scores, d_embed, d_pre


def valid_lanes():
    lane = lax.broadcasted_iota(jnp.int32, (1, 4 * QUARTER_PAD), 1).astype(F32)
    block = jnp.floor((lane + 0.5) * (1.0 / QUARTER_PAD))
    return lane - block * QUARTER_PAD < QUARTER - 0.5


def mass_kernel(queue, table, mass, column):
    valid = valid_lanes()
    size = queue.shape[2]
    column[...] = jnp.zeros_like(column)
    for c in range(CROPS):
        for j in range(queue.shape[0]):
            own = queue[j, c]
            scores = jnp.concatenate(
                [dot_nt(own, table[:, a * PROJ : (a + 1) * PROJ]) for a in range(4)], axis=1
            )
            value = jnp.where(valid, jnp.exp(scores * (1.0 / SINK_EPS)), 0.0)
            mass[c, j * size : (j + 1) * size, :] = value.astype(BF16)
            column[c : c + 1, :] += jnp.sum(value, axis=0, keepdims=True)


def head_kernel(
    micro, images, ndp, pooled, order, w_head, w_proj, table, norm, mass, column, match,
    d_pooled, notes, all_pooled, active, unit, d_scores, d_embed, d_pre,
    scores, xhat_s, y_s, rstd_s, own_mass, target, total,
):
    rows = pooled.shape[0]
    group = rows // micro
    half = group // CROPS
    own = rows // ndp
    queued = mass.shape[1]
    scale_all = 1.0 / (TEMPER * CROPS * half * micro)
    chunk = WIDTH
    low = dot(order[...], pooled[...]).astype(BF16)
    all_pooled[...] = low
    for b in range(D // chunk):
        lanes = slice(b * chunk, (b + 1) * chunk)
        pre = dot(low, w_head[:, lanes])
        for m in range(micro):
            at = slice(m * group, (m + 1) * group)
            v = pre[at]
            mean = jnp.sum(v, axis=0, keepdims=True) * (1.0 / group)
            square = jnp.sum(v * v, axis=0, keepdims=True) * (1.0 / group)
            rstd = lax.rsqrt(square - mean * mean + NORM_EPS)
            xhat = (v - mean) * rstd
            y = xhat * norm[0:1, lanes] + norm[1:2, lanes]
            rstd_s[m : m + 1, lanes] = rstd
            xhat_s[at, lanes] = xhat
            y_s[at, lanes] = y
            active[at, lanes] = (y * sigmoid(y)).astype(BF16)
    embed = dot(active[...], w_proj[...]) + norm[2:3, :PROJ]
    recip = lax.rsqrt(jnp.sum(embed * embed, axis=1, keepdims=True) + UNIT_EPS)
    unit_v = (embed * recip).astype(BF16)
    unit[...] = unit_v
    valid = valid_lanes()
    for a in range(4):
        lanes = slice(a * QUARTER_PAD, (a + 1) * QUARTER_PAD)
        scores[:, lanes] = dot_nt(unit_v, table[:, a * PROJ : (a + 1) * PROJ])
    own_mass[...] = jnp.where(valid, jnp.exp(scores[...] * (1.0 / SINK_EPS)), 0.0)

    step = 32
    for c in range(CROPS):
        starts = [(m * CROPS + c) * half for m in range(micro)]
        once, scale = [], []
        for m in range(micro):
            at = slice(starts[m], starts[m] + half)
            sums = column[c : c + 1, :] + jnp.sum(own_mass[at, :], axis=0, keepdims=True)
            once.append(jnp.where(valid, 1.0 / sums, 0.0))
            own_mass[at, :] = own_mass[at, :] * once[m]
            scale.append(None)
        for turn in range(2):
            for m in range(micro):
                at = slice(starts[m], starts[m] + half)
                a = own_mass[at, :]
                if turn:
                    a = a * scale[m]
                a = a * (1.0 / jnp.sum(a, axis=1, keepdims=True))
                total[m] = jnp.sum(a.reshape(half // 8, 8, a.shape[1]), axis=0)

            def block(i, carry):
                e = mass[c, pl.ds(pl.multiple_of(i * step, step), step), :].astype(F32)
                for m in range(micro):
                    a = e * once[m]
                    if turn:
                        a = a * scale[m]
                    a = a * (1.0 / jnp.sum(a, axis=1, keepdims=True))
                    total[m] += jnp.sum(a.reshape(step // 8, 8, a.shape[1]), axis=0)
                return carry

            lax.fori_loop(0, queued // step, block, 0)
            for m in range(micro):
                more = jnp.where(valid, 1.0 / jnp.sum(total[m], axis=0, keepdims=True), 0.0)
                scale[m] = more if turn == 0 else scale[m] * more
        for m in range(micro):
            at = slice(starts[m], starts[m] + half)
            a = own_mass[at, :] * scale[m]
            own_mass[at, :] = a * (1.0 / jnp.sum(a, axis=1, keepdims=True))
    for m in range(micro):
        zero, one = (slice((m * CROPS + c) * half, (m * CROPS + c + 1) * half) for c in range(CROPS))
        target[zero, :] = jnp.dot(match[m], own_mass[one, :], precision=HIGH, preferred_element_type=F32)
        target[one, :] = lax.dot_general(match[m], own_mass[zero, :], TN, precision=HIGH, preferred_element_type=F32)
    logits = jnp.where(valid, scores[...] * (1.0 / TEMPER), -1e30)
    logits = logits - jnp.max(logits, axis=1, keepdims=True)
    power = jnp.exp(logits)
    summed = jnp.sum(power, axis=1, keepdims=True)
    goal = target[...]
    loss = jnp.sum(goal * (logits - jnp.log(summed)), axis=1, keepdims=True)
    loss = jnp.sum(loss, axis=0, keepdims=True) * (-TEMPER * scale_all)
    weight = jnp.sum(goal, axis=1, keepdims=True) / summed
    d_scores[...] = ((power * weight - goal) * scale_all).astype(BF16)
    d_unit = None
    for a in range(4):
        more = dot(d_scores[:, a * QUARTER_PAD : (a + 1) * QUARTER_PAD], table[:, a * PROJ : (a + 1) * PROJ])
        d_unit = more if d_unit is None else d_unit + more
    along = jnp.sum(d_unit * embed, axis=1, keepdims=True)
    d_low = (recip * d_unit - embed * (recip * recip * recip) * along).astype(BF16)
    d_embed[...] = d_low
    notes[...] = jnp.zeros_like(notes)
    notes[2:3, :PROJ] = jnp.sum(d_low.astype(F32), axis=0, keepdims=True)
    notes[3:4, :] = jnp.broadcast_to(loss, (1, D))
    for b in range(D // chunk):
        lanes = slice(b * chunk, (b + 1) * chunk)
        d_active = dot_nt(d_low, w_proj[lanes, :])
        for m in range(micro):
            at = slice(m * group, (m + 1) * group)
            d_y = d_active[at] * slope(y_s[at, lanes])
            xhat = xhat_s[at, lanes]
            by_x = jnp.sum(d_y * xhat, axis=0, keepdims=True)
            plain = jnp.sum(d_y, axis=0, keepdims=True)
            notes[0:1, lanes] += by_x
            notes[1:2, lanes] += plain
            value = d_y - plain * (1.0 / group) - xhat * (by_x * (1.0 / group))
            d_pre[at, lanes] = (norm[0:1, lanes] * rstd_s[m : m + 1, lanes] * value).astype(BF16)
    mine = dot_tn(order[:, :own], d_pre[...]).astype(BF16)
    d_pooled[...] = dot_nt(mine, w_head[...]).astype(BF16)


def interleave(width):
    row = lax.broadcasted_iota(jnp.int32, (4 * width, 4 * width), 0)
    column = lax.broadcasted_iota(jnp.int32, (4 * width, 4 * width), 1)
    return (column == 4 * (row % width) + row // width).astype(BF16)


def head_grads_kernel(pooled, active, unit, d_scores, d_embed, d_pre, choose, weave, out):
    own = choose.shape[1]
    block = PART
    parts = []
    for q in range(4):
        own_d = dot(d_pre[:, q * WIDTH : (q + 1) * WIDTH], choose[...]).astype(BF16)
        parts.append(dot_tn(own_d, pooled[...]).astype(BF16))
    for b in range(D // block):
        mixed = jnp.concatenate([p[:, b * block : (b + 1) * block] for p in parts], axis=1)
        out[:, 4 * block * b : 4 * block * (b + 1)] = dot(mixed, weave[...])
    proj = jnp.zeros((own, WIDTH), F32)
    proto = jnp.zeros((own, QUARTER_PAD), F32)
    apart = []
    for b in range(4):
        apart.append(dot_nt(active[:, b * WIDTH : (b + 1) * WIDTH], weave[...]).astype(BF16))
    for a in range(4):
        some = choose[a * PROJ : (a + 1) * PROJ, :]
        own_e = dot(d_embed[...], some).astype(BF16)
        own_u = dot(unit[...], some).astype(BF16)
        column = jnp.concatenate([v[:, a * block : (a + 1) * block] for v in apart], axis=1)
        proj = proj + dot_tn(own_e, column)
        proto = proto + dot_tn(own_u, d_scores[:, a * QUARTER_PAD : (a + 1) * QUARTER_PAD])
    out[:, FIRST:SECOND] = proj
    out[:, SECOND:] = proto[:, : out.shape[1] - SECOND]


def unpack_kernel(packed, out, buffer):
    rows = packed.shape[0]
    for b in range(4):
        buffer[b] = packed[:, b * PART : (b + 1) * PART].astype(F32)
    for q in range(4):
        for b in range(4):
            at = q * WIDTH + b * PART
            out[:, at : at + PART] = buffer[b, pl.ds(q, rows // 4, stride=4), :].astype(BF16)


def unpack_proj(rows):
    return rows.reshape(D, PROJ)


def unpack(packed, rows):
    step = 1024
    return pl.pallas_call(
        unpack_kernel,
        out_shape=shape((rows // 4, 4 * WIDTH), BF16),
        grid=(rows // step,),
        in_specs=[pl.BlockSpec((step, WIDTH), lambda i: (i, 0))],
        out_specs=pl.BlockSpec((step // 4, 4 * WIDTH), lambda i: (i, 0)),
        scratch_shapes=[pltpu.VMEM((4, step, PART), F32)],
        compiler_params=pltpu.CompilerParams(vmem_limit_bytes=16 * 2**20),
    )(packed)


def copy_kernel(plan, place, *refs):
    count = len(plan)
    sources, sem = refs[: -count - 1], refs[-1]
    outs = refs[-count - 1 : -1]
    copies = []
    for parts, out in zip(plan, outs):
        for source, row, rows, lane, lanes, at in parts(place):
            ref = sources[source].at[pl.ds(row, rows), pl.ds(lane, lanes)]
            copies.append(pltpu.make_async_copy(ref, out.at[pl.ds(at, rows), :], sem.at[len(copies)]))
    for copy in copies:
        copy.start()
    for copy in copies:
        copy.wait()


def copy_parts(place, sources, plan, outs):
    place_list = [place]
    n = sum(len(parts([0] * 8)) for parts in plan)
    return pl.pallas_call(
        functools.partial(copy_kernel, plan),
        out_shape=[shape(o, BF16) for o in outs],
        in_specs=[pl.BlockSpec(memory_space=pltpu.SMEM)] + [pl.BlockSpec(memory_space=pl.ANY)] * len(sources),
        out_specs=[pl.BlockSpec(memory_space=pltpu.VMEM)] * len(outs),
        scratch_shapes=[pltpu.SemaphoreType.DMA((n,))],
        compiler_params=pltpu.CompilerParams(vmem_limit_bytes=16 * 2**20),
    )(*place_list, *sources)


def multiple(value, step):
    return value if isinstance(value, int) else pl.multiple_of(value, step)


def pair_kernel(place, a, b, keep, out, full):
    full[...] = dot_tn(a[...], b[...])
    own = keep.shape[1]
    for z in range(keep.shape[0]):
        mine = (2 * z + place[4]) * own
        other = (2 * z + place[5]) * own
        keep[z] = full[pl.ds(pl.multiple_of(mine, own), own), :]
        out[z] = full[pl.ds(pl.multiple_of(other, own), own), :].astype(BF16)


def cross_kernel(place, keep, came, own, o1, o2, o3):
    for k, o in enumerate((own, o1, o2, o3)):
        z = place[6] ^ k
        o[...] = (keep[z] + came[z].astype(F32)).astype(o.dtype)


def add_kernel(own, r1, r2, r3, out):
    out[...] = ((own[...] + r1[...].astype(F32)) + (r2[...].astype(F32) + r3[...].astype(F32))).astype(BF16)


def body(image, section_weights, section_norms, queue, pairing):
    micro, images = image.shape[0], image.shape[2]
    ndp = lax.axis_size("dp")
    t = lax.axis_index("section")
    dp = lax.axis_index("dp")
    core = dp % 2
    place = jnp.stack([t ^ k for k in range(SECTIONS)] + [core, 1 - core, dp // 2, dp]).astype(jnp.int32)
    cells = CROPS * PLACES * images
    rows = micro * cells
    count = float(cells * ndp)
    packed = section_weights[0]
    param_rows = packed.shape[0]
    own = WIDTH // ndp
    k = functools.partial

    def pieces_of(width, dtype):
        return shape((rows, width), dtype)

    def from_section(pieces, source):
        return [lax.ppermute(pieces[j], "section", [(source, source ^ j)]) for j in range(1, SECTIONS)]

    def choose(source, pieces, came):
        own_piece = pieces[0]
        return jnp.where(t == source, own_piece, came[0] + came[1] + came[2])

    half = D // 2

    def reduce_part(j):
        return lambda p: [(0, multiple(p[4] * half, half), half, j * PART, PART, 0)]

    reduce_own = copy_parts(place, [packed], [reduce_part(j) for j in range(SECTIONS)], [(half, PART)] * 4)
    came_reduce = from_section(reduce_own, 0)
    packed, *reduce_own = lax.optimization_barrier((packed, *reduce_own))

    def conv_part(j):
        return lambda p: [
            (0, multiple(tap * WIDTH + p[4] * (WIDTH // 2), WIDTH // 2), WIDTH // 2, (1 ^ j) * PART, PART, tap * (WIDTH // 2))
            for tap in range(9)
        ]

    conv_own = copy_parts(place, [packed], [conv_part(j) for j in range(SECTIONS)], [(9 * WIDTH // 2, PART)] * 4)
    came_conv = from_section(conv_own, 1)
    packed, *conv_own = lax.optimization_barrier((packed, *conv_own))

    natural = unpack(packed, FIRST)

    def expand_part(j):
        return lambda p: [(0, multiple(p[4] * (WIDTH // 2), WIDTH // 2), WIDTH // 2, (2 ^ j) * WIDE, WIDE, 0)]

    expand_own = copy_parts(place, [natural], [expand_part(j) for j in range(SECTIONS)], [(WIDTH // 2, WIDE)] * 4)
    norms = jnp.stack(gather_xor(section_norms[0], "section"))
    came_expand = from_section(expand_own, 2)

    def norm_of(section, width):
        rows3 = lax.dynamic_index_in_dim(norms, t ^ section, 0, keepdims=False)
        return lax.dynamic_slice_in_dim(rows3, t * width, width, 1)

    norm0, norm1, norm2 = norm_of(0, PART), norm_of(1, PART), norm_of(2, WIDE)
    norm3 = section_norms[0]

    w_reduce = choose(0, reduce_own, came_reduce)
    w_reduce = (w_reduce, flip(w_reduce, "dp", 1))
    flat = image.transpose(0, 1, 3, 4, 2, 5).reshape(rows, D)
    sums_of = shape((8, PART), F32)
    pre0, part = call(k(reduce_kernel, micro), (pieces_of(PART, F32), sums_of), place, flat, *w_reduce)
    sums0 = sum_dp(part)
    active0 = call(k(active_kernel, micro, count), pieces_of(PART, BF16), pre0, sums0, norm0)
    actives0 = gather_xor(active0, "section")

    w_conv = choose(1, conv_own, came_conv)
    w_conv = (w_conv, flip(w_conv, "dp", 1))
    pre1, part = call(
        k(conv_kernel, micro, images),
        (pieces_of(PART, F32), sums_of),
        place, *actives0, *w_conv,
        scratch=[pltpu.VMEM((rows, WIDTH), BF16)],
    )
    sums1 = sum_dp(part)
    active1_own = call(k(active_kernel, micro, count), pieces_of(PART, BF16), pre1, sums1, norm1)
    actives1 = gather_xor(active1_own, "section")
    w_expand = choose(2, expand_own, came_expand)
    w_expand = (w_expand, flip(w_expand, "dp", 1))
    active1, pre2, part = call(
        k(expand_kernel, micro),
        (pieces_of(WIDTH, BF16), pieces_of(WIDE, F32), shape((8, WIDE), F32)),
        place, *actives1, *w_expand,
    )
    sums2 = sum_dp(part)
    pooled = call(
        k(pool_kernel, micro, images, count),
        shape((rows // PLACES, WIDE), BF16),
        place, pre2, sums2, norm2, flat,
    )

    per_dp = rows // PLACES
    came_p = [send(pooled, j, 3) for j in range(3)]
    offsets, all_pooled = gather_dp(jnp.concatenate(came_p + [pooled], axis=1))
    all_pooled = all_pooled.reshape(per_dp * ndp, D)
    head_order = jnp.arange(per_dp * ndp, dtype=jnp.int32)
    block, inner = head_order // per_dp, head_order % per_dp
    group, single = inner // images, inner % images
    offset = jnp.array(offsets, jnp.int32)
    source = offset[block] ^ dp
    position = (group * ndp + source) * images + single
    order = (position[None, :] == head_order[:, None]).astype(BF16)
    queue_size = CROPS * queue.shape[1]
    note = jnp.pad(pairing.astype(BF16), ((0, 16 - micro), (0, PROJ - images)))
    _, told = gather_dp(jnp.concatenate([queue.reshape(queue_size, PROJ), note]))
    queue_all = told[:, :queue_size].reshape(ndp, CROPS, queue.shape[1], PROJ)
    pairs = told[:, queue_size : queue_size + micro, :images].astype(jnp.int32)
    pairs_dp = (offset ^ dp)[None, :] == jnp.arange(ndp, dtype=jnp.int32)[:, None]
    pairs = jnp.sum(jnp.where(pairs_dp[:, :, None, None], pairs[None], 0), axis=1)
    left = jnp.arange(images * ndp, dtype=jnp.int32)
    pairs = pairs.transpose(1, 0, 2).reshape(micro, ndp * images)
    match = ((left // images * images + pairs)[:, :, None] == left[None, None, :]).astype(F32)
    w_head = natural
    w_proj = unpack_proj(packed[FIRST:SECOND])
    table = jnp.pad(packed[SECOND:THIRD], ((0, QUARTER_PAD - QUARTER), (0, 0)))
    head_rows = per_dp * ndp
    if head_rows <= 128 and CROPS * images * ndp >= 32 and queue.shape[1] * ndp <= 512:
        lanes = 4 * QUARTER_PAD
        mass, column = call(
            mass_kernel,
            (shape((CROPS, ndp * queue.shape[1], lanes), BF16), shape((8, lanes), F32)),
            queue_all, table,
        )
        d_pooled, notes3, all_pooled, active3, unit, d_scores, d_embed, d_pre3 = call(
            k(head_kernel, micro, images, ndp),
            (
                shape((per_dp, D), BF16), shape((8, D), F32), shape((head_rows, D), BF16), shape((head_rows, D), BF16),
                shape((head_rows, PROJ), BF16), shape((head_rows, lanes), BF16), shape((head_rows, PROJ), BF16),
                shape((head_rows, D), BF16),
            ),
            all_pooled, order, w_head, w_proj, table, norm3, mass, column, match,
            scratch=[
                pltpu.VMEM((head_rows, lanes), F32), pltpu.VMEM((head_rows, D), F32), pltpu.VMEM((head_rows, D), F32),
                pltpu.VMEM((8, D), F32), pltpu.VMEM((head_rows, lanes), F32), pltpu.VMEM((head_rows, lanes), F32),
                pltpu.VMEM((micro, 8, lanes), F32),
            ],
            vmem=48,
        )
        grads3, loss = notes3[:3], notes3[3, 0]
    else:
        all_pooled = dot(order, all_pooled).astype(BF16)
        protos = jnp.concatenate([table[:, a * PROJ : (a + 1) * PROJ] for a in range(4)], axis=0)
        queue_rows = queue_all.transpose(1, 0, 2, 3).reshape(CROPS, -1, PROJ)
        loss, grads3, active3, unit, d_scores, d_embed, d_pre3 = head(
            all_pooled, w_head, w_proj, protos, norm3, queue_rows, match, micro, images, dp
        )
        d_pooled = dot_nt(dot_tn(order[:, :per_dp], d_pre3).astype(BF16), w_head).astype(BF16)

    packed_b, _ = lax.optimization_barrier((packed, pooled))

    def conv_back_part(j):
        return lambda p: [
            (0, multiple(tap * WIDTH + (1 ^ j) * PART + p[4] * (PART // 2), PART // 2), PART // 2, 0, WIDTH, tap * (PART // 2))
            for tap in range(9)
        ]

    def reduce_back_part(j):
        return lambda p: [(0, multiple(j * WIDE + p[4] * (WIDE // 2), WIDE // 2), WIDE // 2, 0, WIDTH, 0)]

    back_own = copy_parts(
        place, [packed_b],
        [conv_back_part(j) for j in range(SECTIONS)] + [reduce_back_part(j) for j in range(SECTIONS)],
        [(9 * PART // 2, WIDTH)] * 4 + [(WIDE // 2, WIDTH)] * 4,
    )
    conv_back_own, reduce_back_own = back_own[:4], back_own[4:]
    w_conv_back = choose(1, conv_back_own, from_section(conv_back_own, 1))
    w_reduce_back = choose(0, reduce_back_own, from_section(reduce_back_own, 0))
    w_conv_back = (w_conv_back, flip(w_conv_back, "dp", 1))
    w_reduce_back = (w_reduce_back, flip(w_reduce_back, "dp", 1))

    parts = [d_pooled[:, j * WIDE : (j + 1) * WIDE] for j in range(SECTIONS)]
    came_d = [send(parts[j], 3, j) for j in range(3)]
    d_z, part = call(
        k(out_back_kernel, micro, images, count),
        (pieces_of(WIDE, F32), shape((8, WIDE), F32)),
        place, pre2, sums2, norm2, flat, parts[3], *came_d,
    )
    back2 = sum_dp(part)
    d_pre2, *partial = call(
        k(expand_back_kernel, micro, count),
        [pieces_of(WIDE, BF16)] + [pieces_of(PART, BF16)] * 4,
        place, pre2, sums2, norm2, d_z, back2, *w_expand,
        scratch=[pltpu.VMEM((rows, WIDTH), F32)],
    )
    partial = [partial[0]] + [flip(partial[j], "section", j) for j in range(1, SECTIONS)]

    def scatter_start(a, b):
        if ndp != 8:
            return dot_tn(a, b)
        width = b.shape[1]
        keep, out = call(
            pair_kernel,
            (shape((4, own, width), F32), shape((4, own, width), BF16)),
            place, a, b,
            scratch=[pltpu.VMEM((WIDTH, width), F32)],
        )
        return keep, flip(out, "dp", 1)

    def scatter_finish(started):
        if ndp != 8:
            return lax.psum_scatter(started.astype(BF16), "dp", scatter_dimension=0, tiled=True)
        keep, came = started
        dims = keep.shape[1:]
        kept, *out = call(
            cross_kernel, [shape(dims, F32)] + [shape(dims, BF16)] * 3, place, keep, came
        )
        came = [flip(out[j], "dp", 2 * (j + 1)) for j in range(3)]
        return call(add_kernel, shape(dims, BF16), kept, *came)

    g_expand = scatter_finish(scatter_start(d_pre2, active1))

    d_y1, part = call(
        k(silu_back_kernel, micro, count), (pieces_of(PART, F32), sums_of), *partial, pre1, sums1, norm1
    )
    back1 = sum_dp(part)
    d_pre1_own = call(k(norm_back_kernel, micro, count), pieces_of(PART, BF16), d_y1, pre1, sums1, back1, norm1)
    d_pre1s = gather_xor(d_pre1_own, "section")
    d_pre1, d_y0, part = call(
        k(conv_back_kernel, micro, images, count),
        (pieces_of(WIDTH, BF16), pieces_of(PART, F32), sums_of),
        place, *d_pre1s, *w_conv_back, pre0, sums0, norm0,
        scratch=[pltpu.VMEM((9 * PART, WIDTH), BF16)],
    )
    back0 = sum_dp(part)
    d_pre0_own = call(k(norm_back_kernel, micro, count), pieces_of(PART, BF16), d_y0, pre0, sums0, back0, norm0)
    taps = call(k(taps_kernel, images), pieces_of(9 * PART, BF16), active0)
    conv_started = scatter_start(d_pre1, taps)
    d_pre0s = gather_xor(d_pre0_own, "section")
    g_conv = scatter_finish(conv_started)
    d_pre0, grad_in = call(
        reduce_back_kernel,
        (pieces_of(WIDTH, BF16), pieces_of(WIDE, F32)),
        place, *d_pre0s, *w_reduce_back, d_z,
        scratch=[pltpu.VMEM((rows, WIDE), F32)],
    )
    own_image = lax.dynamic_slice_in_dim(flat, t * WIDE, WIDE, 1)
    g_reduce = scatter_finish(scatter_start(d_pre0, own_image))
    to_conv = [send(g_conv, j, 1) for j in (0, 2, 3)]
    to_expand = [send(g_expand, j, 2) for j in (0, 1, 3)]
    to_reduce = [send(g_reduce, j, 0) for j in (1, 2, 3)]
    pick = (jnp.arange(WIDTH, dtype=jnp.int32)[:, None] == dp * own + jnp.arange(own, dtype=jnp.int32)[None, :]).astype(BF16)
    weave = interleave(PART)

    def widen(value):
        return jnp.pad(value, ((0, 0), (0, param_rows - value.shape[1])))

    def finish_reduce():
        return widen(jnp.concatenate([g_reduce] + to_reduce, axis=1).astype(F32))

    def finish_conv():
        four = [to_conv[0], g_conv, to_conv[1], to_conv[2]]
        cols = [f[:, tap * PART : (tap + 1) * PART] for tap in range(9) for f in four]
        return widen(jnp.concatenate(cols, axis=1).astype(F32))

    def finish_expand():
        four = [to_expand[0], to_expand[1], g_expand, to_expand[2]]
        cols = []
        for b in range(WIDTH // PART):
            mixed = jnp.concatenate([f[:, b * PART : (b + 1) * PART] for f in four], axis=1)
            cols.append(dot(mixed, weave))
        return widen(jnp.concatenate(cols, axis=1))

    def finish_head():
        return call(
            head_grads_kernel,
            shape((own, param_rows), F32),
            all_pooled, active3, unit, d_scores, d_embed, d_pre3, pick, weave,
        )

    weight_grads = lax.switch(t, [finish_reduce, finish_conv, finish_expand, finish_head])

    def both(back):
        gain, shift = back[0:1], back[micro : micro + 1]
        for m in range(1, micro):
            gain, shift = gain + back[m : m + 1], shift + back[micro + m : micro + m + 1]
        return jnp.concatenate([gain, shift])

    lines = jnp.concatenate([both(back2), jnp.concatenate([both(back0), both(back1)], axis=1)[:, : 2 * PART]], axis=1)
    note = jnp.concatenate([lines, jnp.full((6, lines.shape[1]), jnp.where(t == 3, loss, 0.0))])
    told = jnp.stack(gather_xor(note, "section"))
    loss = (told[0, 2, 0] + told[1, 2, 0]) + (told[2, 2, 0] + told[3, 2, 0])
    told = jnp.concatenate(
        [lax.dynamic_index_in_dim(told, t ^ j, 0, keepdims=False) for j in range(SECTIONS)], axis=1
    )[:2].reshape(2, SECTIONS, WIDE + 2 * PART)

    def narrow(value):
        value = value.reshape(2, -1)
        return jnp.pad(value, ((0, 1), (0, D - value.shape[1])))

    norm_grads = jnp.where(
        t == 0,
        narrow(told[:, :, WIDE : WIDE + PART]),
        jnp.where(t == 1, narrow(told[:, :, WIDE + PART :]), jnp.where(t == 2, narrow(told[:, :, :WIDE]), grads3)),
    )
    grad_in = grad_in.reshape(micro, CROPS, SIDE, SIDE, images, WIDE).transpose(0, 1, 4, 2, 3, 5)
    return (loss, grad_in, weight_grads.T[None], norm_grads[None])


def solution(mesh):
    in_specs = (
        P(None, None, "dp", None, None, None),
        P("section", None, None),
        P("section", None, None),
        P(None, "dp", None),
        P(None, "dp"),
    )
    out_specs = (
        P(),
        P(None, None, "dp", None, None, "section"),
        P("section", None, "dp"),
        P("section", None, None),
    )
    return jax.shard_map(body, mesh=mesh, in_specs=in_specs, out_specs=out_specs, check_vma=False)
```

```python
import functools

import jax
import jax.numpy as jnp
from jax import lax
from jax.experimental import pallas as pl
from jax.experimental.pallas import tpu as pltpu
from jax.sharding import PartitionSpec as P

D = 2048
WIDTH = 512
PROJ = 128
PROTOS = 3000
SIDE = 7
CROPS = 2
SECTIONS = 4
PART = WIDTH // SECTIONS
WIDE = D // SECTIONS
QUARTER = PROTOS // 4
QUARTER_PAD = 768
PLACES = SIDE * SIDE
FIRST = D * (D // WIDTH)
SECOND = FIRST + D * PROJ // WIDTH
THIRD = SECOND + PROTOS * PROJ // WIDTH

NORM_EPS = 1e-05
UNIT_EPS = 1e-06
SINK_EPS = 0.05
TEMPER = 0.1
HIGH = lax.Precision.HIGHEST
F32 = jnp.float32
BF16 = jnp.bfloat16
NT = (((1,), (1,)), ((), ()))
TN = (((0,), (0,)), ((), ()))


def dot(a, b):
    return jnp.dot(a, b, preferred_element_type=F32)


def dot_nt(a, b):
    return lax.dot_general(a, b, NT, preferred_element_type=F32)


def dot_tn(a, b):
    return lax.dot_general(a, b, TN, preferred_element_type=F32)


def flip(value, axis, step):
    count = lax.axis_size(axis)
    return lax.ppermute(value, axis, [(source, source ^ step) for source in range(count)])


def send(value, source, target):
    return lax.ppermute(value, "section", [(source, target)])


def sum_dp(value):
    count = lax.axis_size("dp")
    value = value + flip(value, "dp", 1)
    step = 2
    while step < count:
        if 2 * step < count:
            near = value + flip(value, "dp", step)
            far = flip(value, "dp", 2 * step) + flip(value, "dp", 3 * step)
            value = near + far
            step *= 4
        else:
            value = value + flip(value, "dp", step)
            step *= 2
    return value


def gather_xor(value, axis):
    return [value] + [flip(value, axis, step) for step in range(1, lax.axis_size(axis))]


def dp_stages():
    count = lax.axis_size("dp")
    stages, step = [(1,)], 2
    while step < count:
        if 2 * step < count:
            stages.append((step, 2 * step, 3 * step))
            step *= 4
        else:
            stages.append((step,))
            step *= 2
    return stages


def gather_dp(value, stages):
    arrays, offsets = [value], [[0]]
    for steps in stages:
        if len(arrays) > 1:
            arrays, offsets = [jnp.concatenate(arrays)], [sum(offsets, [])]
        first = offsets[0]
        for step in steps:
            arrays.append(flip(arrays[0], "dp", step))
            offsets.append([o ^ step for o in first])
    return arrays, offsets


def sigmoid(v):
    return 1.0 / (1.0 + jnp.exp(-v))


def slope(v):
    s = sigmoid(v)
    return s * (1.0 + v * (1.0 - s))


def cost(us):
    return pl.CostEstimate(flops=0, bytes_accessed=int(us * 3_000_000), transcendentals=0)


def call(kernel, out, *args, scratch=(), vmem=12, us=1.0):
    in_specs = []
    for a in args:
        if jnp.issubdtype(a.dtype, jnp.integer):
            in_specs.append(pl.BlockSpec(memory_space=pltpu.SMEM))
        else:
            in_specs.append(pl.BlockSpec(memory_space=pltpu.VMEM))
    return pl.pallas_call(
        kernel,
        out_shape=out,
        in_specs=in_specs,
        out_specs=jax.tree.map(lambda _: pl.BlockSpec(memory_space=pltpu.VMEM), out),
        scratch_shapes=list(scratch),
        compiler_params=pltpu.CompilerParams(vmem_limit_bytes=vmem * 2**20),
        cost_estimate=cost(us),
    )(*args)


def shape(dims, dtype):
    return jax.ShapeDtypeStruct(tuple(dims), dtype)


def split_sums(first, second, micro):
    width = first[0].shape[1]
    rows = [jnp.sum(v, axis=0, keepdims=True) for v in first]
    rows += [jnp.sum(v, axis=0, keepdims=True) for v in second]
    rows.append(jnp.zeros((8 - 2 * micro, width), F32))
    return jnp.concatenate(rows, axis=0)


def moments(sums, m, micro, count):
    mean = sums[m : m + 1] * (1.0 / count)
    square = sums[micro + m : micro + m + 1] * (1.0 / count)
    return mean, lax.rsqrt(square - mean * mean + NORM_EPS)


def per_micro(value, micro):
    rows = value.shape[0] // micro
    return [value[m * rows : (m + 1) * rows] for m in range(micro)]


def normalized(value, sums, micro, count):
    out = []
    for m, v in enumerate(per_micro(value, micro)):
        mean, rstd = moments(sums, m, micro, count)
        out.append(((v - mean) * rstd, rstd))
    return out


def join(parts):
    return jnp.concatenate(parts, axis=0)


def tap_valid(rows, images, tap, sign):
    row = lax.broadcasted_iota(jnp.int32, (rows, PART), 0).astype(F32)
    cell = jnp.floor((row + 0.5) * (1.0 / images))
    crop = jnp.floor((cell + 0.5) * (1.0 / PLACES))
    place = cell - crop * PLACES
    y = jnp.floor((place + 0.5) * (1.0 / SIDE))
    x = place - y * SIDE
    y = y + float(sign * (tap // 3 - 1))
    x = x + float(sign * (tap % 3 - 1))
    return (y > -0.5) & (y < SIDE - 0.5) & (x > -0.5) & (x < SIDE - 0.5)


def tap_shift(value, images, tap, sign):
    rows = value.shape[0]
    offset = sign * images * (SIDE * (tap // 3 - 1) + (tap % 3 - 1))
    moved = value if offset == 0 else pltpu.roll(value, (-offset) % rows, 0)
    if tap == 4:
        return moved
    return jnp.where(tap_valid(rows, images, tap, sign), moved, 0.0)


def told_norm(message, at):
    rows = message[at : at + 16, :].astype(F32)
    return rows[0:1] + rows[1:2] + rows[2:3], rows[3:4] + rows[4:5] + rows[5:6]


def tell_norm(rows):
    out = []
    for r in range(2):
        left = rows[r : r + 1]
        for _ in range(3):
            term = left.astype(BF16).astype(F32)
            out.append(term)
            left = left - term
    out.append(jnp.zeros((10, rows.shape[1]), F32))
    return jnp.concatenate(out, axis=0).astype(BF16)


def reduce_kernel(micro, place, image, w0, w1, pre, sums):
    half = D // 2
    first = pl.ds(pl.multiple_of(place[4] * half, half), half)
    second = pl.ds(pl.multiple_of(place[5] * half, half), half)
    value = dot(image[:, first], w0[:half, :]) + dot(image[:, second], w1[:half, :])
    pre[...] = value
    parts = per_micro(value, micro)
    sums[...] = split_sums(parts, [v * v for v in parts], micro)


def active_kernel(micro, count, at, pre, sums, told, active):
    gain, shift = told_norm(told, at)
    out = []
    for xhat, _ in normalized(pre[...], sums[...], micro, count):
        y = xhat * gain + shift
        out.append(y * sigmoid(y))
    active[...] = join(out).astype(BF16)


def fill(place, pieces, full):
    for k, piece in enumerate(pieces):
        full[:, pl.ds(pl.multiple_of(place[k] * PART, PART), PART)] = piece[...]


def conv_kernel(micro, images, place, a0, a1, a2, a3, w0, w1, pre, sums, full):
    fill(place, (a0, a1, a2, a3), full)
    half = WIDTH // 2
    total = None
    for first in range(0, 9, 2):
        taps = [tap for tap in (first, first + 1) if tap < 9]
        part = None
        for j, w in enumerate((w0, w1)):
            lanes = pl.ds(pl.multiple_of(place[4 + j] * half, half), half)
            weight = jnp.concatenate([w[tap * half : (tap + 1) * half, :] for tap in taps], axis=1)
            more = dot(full[:, lanes], weight)
            part = more if part is None else part + more
        for j, tap in enumerate(taps):
            moved = tap_shift(part[:, j * PART : (j + 1) * PART], images, tap, 1)
            total = moved if total is None else total + moved
    pre[...] = total
    parts = per_micro(total, micro)
    sums[...] = split_sums(parts, [v * v for v in parts], micro)


def expand_kernel(micro, place, a0, a1, a2, a3, w0, w1, active, pre, sums):
    fill(place, (a0, a1, a2, a3), active)
    half = WIDTH // 2
    value = None
    for j, w in enumerate((w0, w1)):
        lanes = pl.ds(pl.multiple_of(place[4 + j] * half, half), half)
        more = dot(active[:, lanes], w[:half, :])
        value = more if value is None else value + more
    pre[...] = value
    parts = per_micro(value, micro)
    sums[...] = split_sums(parts, [v * v for v in parts], micro)


def crop_rows(rows, images, transpose=False):
    shp = (rows // PLACES, rows)
    r = lax.broadcasted_iota(jnp.int32, shp, 1).astype(F32)
    q = lax.broadcasted_iota(jnp.int32, shp, 0).astype(F32)
    cell = jnp.floor((r + 0.5) * (1.0 / images))
    crop = jnp.floor((cell + 0.5) * (1.0 / PLACES))
    image = r - cell * images
    return (jnp.abs(crop * images + image - q) < 0.5).astype(F32).astype(BF16)


def pool_kernel(micro, images, count, place, pre, sums, told, image, pooled):
    lanes = pl.ds(pl.multiple_of(place[0] * WIDE, WIDE), WIDE)
    gain, shift = told_norm(told, WIDTH // 2)
    out = []
    for xhat, _ in normalized(pre[...], sums[...], micro, count):
        out.append(xhat * gain + shift)
    z = join(out) + image[:, lanes].astype(F32)
    out = z * sigmoid(z)
    high = out.astype(BF16)
    low = (out - high.astype(F32)).astype(BF16)
    choose = crop_rows(pre.shape[0], images)
    pooled[...] = ((dot(choose, high) + dot(choose, low)) * (1.0 / PLACES)).astype(BF16)


def out_back_kernel(micro, images, count, place, pre, sums, told, image, own, r0, r1, r2, d_z, sums_out):
    lanes = pl.ds(pl.multiple_of(place[0] * WIDE, WIDE), WIDE)
    rows = pre.shape[0]
    gain, shift = told_norm(told, WIDTH // 2)
    came = (r0[...].astype(F32) + r1[...].astype(F32) + r2[...].astype(F32)).astype(BF16)
    d_pooled = jnp.where(place[0] == SECTIONS - 1, own[...], came)
    spread = dot_tn(crop_rows(rows, images), d_pooled) * (1.0 / PLACES)
    xhats = [x for x, _ in normalized(pre[...], sums[...], micro, count)]
    z = join([x * gain + shift for x in xhats]) + image[:, lanes].astype(F32)
    value = spread * slope(z)
    d_z[...] = value
    parts = per_micro(value, micro)
    sums_out[...] = split_sums([v * x for v, x in zip(parts, xhats)], parts, micro)


def norm_back(value, pre, sums, back, gain, micro, count):
    out = []
    parts = per_micro(value, micro)
    for m, (xhat, rstd) in enumerate(normalized(pre, sums, micro, count)):
        by_x = back[m : m + 1] * (1.0 / count)
        plain = back[micro + m : micro + m + 1] * (1.0 / count)
        out.append(gain * rstd * (parts[m] - plain - xhat * by_x))
    return join(out)


def norm_back_kernel(micro, count, at, d_y, pre, sums, back, told, d_pre):
    gain, _ = told_norm(told, at)
    d_pre[...] = norm_back(d_y[...], pre[...], sums[...], back[...], gain, micro, count).astype(BF16)


def expand_back_kernel(micro, count, place, pre, sums, d_z, back, w0, w1, d_pre, q0, q1, q2, q3, full):
    half = WIDTH // 2
    gain, _ = told_norm(w0, half)
    d_low = norm_back(d_z[...], pre[...], sums[...], back[...], gain, micro, count).astype(BF16)
    d_pre[...] = d_low
    for j, w in enumerate((w0, w1)):
        full[:, pl.ds(pl.multiple_of(place[4 + j] * half, half), half)] = dot_nt(d_low, w[:half, :])
    for k, q in enumerate((q0, q1, q2, q3)):
        lanes = pl.ds(pl.multiple_of(place[k] * PART, PART), PART)
        q[...] = full[:, lanes].astype(BF16)


def finish_silu(micro, count, d_active, pre, sums, norm, d_y, sums_out):
    gain, shift = norm
    values, products = [], []
    parts = per_micro(d_active, micro)
    for m, (xhat, _) in enumerate(normalized(pre[...], sums[...], micro, count)):
        value = parts[m] * slope(xhat * gain + shift)
        values.append(value)
        products.append(value * xhat)
    d_y[...] = join(values)
    sums_out[...] = split_sums(products, values, micro)


def silu_back_kernel(micro, count, at, q0, q1, q2, q3, pre, sums, told, d_y, sums_out):
    total = (q0[...].astype(F32) + q1[...].astype(F32)) + (q2[...].astype(F32) + q3[...].astype(F32))
    d_active = total.astype(BF16).astype(F32)
    finish_silu(micro, count, d_active, pre, sums, told_norm(told, at), d_y, sums_out)


def conv_back_kernel(
    micro, images, count, at, place, d0, d1, d2, d3, back0, back1, pre, sums, told, d_full, d_y, sums_out, weight
):
    fill(place, (d0, d1, d2, d3), d_full)
    d_low = d_full[...]
    half = PART // 2
    for j, back in enumerate((back0, back1)):
        for k in range(SECTIONS):
            lanes = pl.ds(pl.multiple_of(place[k] * PART, PART), PART)
            for tap in range(9):
                rows = pl.ds(pl.multiple_of(tap * PART + place[4 + j] * half, half), half)
                weight[rows, lanes] = back[k, tap * half : (tap + 1) * half, :]
    total = None
    for first in range(0, 9, 2):
        taps = [tap for tap in (first, first + 1) if tap < 9]
        part = dot_nt(d_low, weight[first * PART : (taps[-1] + 1) * PART, :])
        for j, tap in enumerate(taps):
            moved = tap_shift(part[:, j * PART : (j + 1) * PART], images, tap, -1)
            total = moved if total is None else total + moved
    d_active = total.astype(BF16).astype(F32)
    finish_silu(micro, count, d_active, pre, sums, told_norm(told, at), d_y, sums_out)


def reduce_back_kernel(place, d0, d1, d2, d3, back0, back1, d_z, d_full, grad_in, weight):
    fill(place, (d0, d1, d2, d3), d_full)
    half = WIDE // 2
    first = 9 * PART // 2
    for j, back in enumerate((back0, back1)):
        rows = pl.ds(pl.multiple_of(place[4 + j] * half, half), half)
        for k in range(SECTIONS):
            lanes = pl.ds(pl.multiple_of(place[k] * PART, PART), PART)
            weight[rows, lanes] = back[k, first : first + half, :]
    main = dot_nt(d_full[...], weight[...]).astype(BF16).astype(F32)
    grad_in[...] = main + d_z[...].astype(BF16).astype(F32)


def back_parts_kernel(place, conv0, conv1, reduce0, reduce1, *outs):
    half = PART // 2
    wide = WIDE // 2
    first = 9 * half
    for k, out in enumerate(outs):
        u = place[k]
        high = u // 2
        low = u - 2 * high
        for j, (conv, reduce) in enumerate(((conv0, reduce0), (conv1, reduce1))):

            @pl.when(high == place[4 + j])
            def _():
                for tap in range(9):
                    at = pl.multiple_of(tap * WIDTH // 2 + low * PART + place[4] * half, half)
                    out[tap * half : (tap + 1) * half, :] = conv[pl.ds(at, half), :]
                at = pl.multiple_of(low * WIDE + place[4] * wide, wide)
                out[first : first + wide, :] = reduce[pl.ds(at, wide), :]


def stack_kernel(*refs):
    out = refs[-1]
    rows = refs[0].shape[0]
    for j, ref in enumerate(refs[:-1]):
        if len(out.shape) == 3:
            out[j] = ref[...]
        else:
            out[j * rows : (j + 1) * rows, :] = ref[...]


def pick_kernel(source, place, p0, p1, p2, p3, out):
    for j, p in enumerate((p0, p1, p2, p3)):

        @pl.when(place[0] == source ^ j)
        def _():
            out[...] = p[...]


def taps_kernel(images, active, out):
    value = active[...].astype(F32)
    for tap in range(9):
        out[:, tap * PART : (tap + 1) * PART] = tap_shift(value, images, tap, 1).astype(BF16)


def head(pooled, w_head, w_proj, protos, norm, queue, match, micro, images, dp):
    rows = pooled.shape[0]
    group = rows // micro
    half = group // CROPS
    scale_all = 1.0 / (TEMPER * CROPS * half * micro)
    pre = dot(pooled, w_head)

    def by_micro(v):
        return v.reshape(micro, group, v.shape[-1])

    pre_m = by_micro(pre)
    mean = jnp.mean(pre_m, axis=1, keepdims=True)
    square = jnp.mean(pre_m * pre_m, axis=1, keepdims=True)
    rstd = lax.rsqrt(square - mean * mean + NORM_EPS)
    xhat = (pre_m - mean) * rstd
    y = xhat * norm[0] + norm[1]
    active = (y * sigmoid(y)).astype(BF16).reshape(rows, D)
    embed = dot(active, w_proj) + norm[2, :PROJ]
    recip = lax.rsqrt(jnp.sum(embed * embed, axis=1, keepdims=True) + UNIT_EPS)
    unit = (embed * recip).astype(BF16)
    scores = dot_nt(unit, protos)
    valid = lax.broadcasted_iota(jnp.int32, (1, 4, QUARTER_PAD), 2).reshape(1, 4 * QUARTER_PAD) < QUARTER
    own_mass = jnp.where(valid, jnp.exp(scores / SINK_EPS), 0.0).reshape(micro, CROPS, half, -1)
    queue_mass = jnp.where(valid, jnp.exp(jnp.einsum("cqp,kp->cqk", queue, protos, preferred_element_type=F32) / SINK_EPS), 0.0)
    codes = []
    for m in range(micro):
        for c in range(CROPS):
            a, b = queue_mass[c], own_mass[m, c]
            column = jnp.sum(a, axis=0, keepdims=True) + jnp.sum(b, axis=0, keepdims=True)
            once = jnp.where(valid, 1.0 / column, 0.0)
            a, b = a * once, b * once
            scale = valid.astype(F32)
            for turn in range(2):
                ra = 1.0 / jnp.sum(a * scale, axis=1, keepdims=True)
                rb = 1.0 / jnp.sum(b * scale, axis=1, keepdims=True)
                column = jnp.sum(a * ra, axis=0, keepdims=True) + jnp.sum(b * rb, axis=0, keepdims=True)
                scale = jnp.where(valid, 1.0 / column, 0.0)
            b = b * scale
            codes.append(b / jnp.sum(b, axis=1, keepdims=True))
    targets = []
    for m in range(micro):
        targets.append(jnp.dot(match[m], codes[m * CROPS + 1], precision=HIGH))
        targets.append(jnp.dot(match[m].T, codes[m * CROPS], precision=HIGH))
    target = jnp.concatenate(targets)
    logits = jnp.where(valid, scores / TEMPER, -1e30)
    logp = jax.nn.log_softmax(logits, axis=1)
    loss = -jnp.sum(jnp.where(valid, target * logp, 0.0)) * (TEMPER * scale_all)
    d_scores = ((jnp.exp(logp) * jnp.sum(target, axis=1, keepdims=True) - target) * scale_all).astype(BF16)
    d_unit = dot(d_scores, protos)
    d_embed = (
        recip * d_unit - embed * (recip * recip * recip) * jnp.sum(d_unit * embed, axis=1, keepdims=True)
    ).astype(BF16)
    d_active = dot_nt(d_embed, w_proj)
    d_y = by_micro(d_active) * slope(y)
    by_x = jnp.sum(d_y * xhat, axis=1, keepdims=True)
    plain = jnp.sum(d_y, axis=1, keepdims=True)
    d_pre = (norm[0] * rstd * (d_y - plain / group - xhat * by_x / group)).astype(BF16).reshape(rows, D)
    bias = jnp.pad(jnp.sum(d_embed.astype(F32), axis=0), (0, D - PROJ))
    grads = jnp.stack([jnp.sum(by_x, axis=(0, 1)), jnp.sum(plain, axis=(0, 1)), bias])
    return loss, grads, active, unit, d_scores, d_embed, d_pre


def valid_lanes():
    lane = lax.broadcasted_iota(jnp.int32, (1, 4 * QUARTER_PAD), 1).astype(F32)
    block = jnp.floor((lane + 0.5) * (1.0 / QUARTER_PAD))
    return lane - block * QUARTER_PAD < QUARTER - 0.5


def mass_kernel(parts, table, *refs):
    mass, column = refs[-2:]
    valid = valid_lanes()
    size = mass.shape[1] // parts
    column[...] = jnp.zeros_like(column)
    at = 0
    for ref in refs[:-2]:
        rows = CROPS * size + 16
        for j in range(ref.shape[0] // rows):
            for c in range(CROPS):
                own = ref[j * rows + c * size : j * rows + (c + 1) * size, :]
                scores = jnp.concatenate(
                    [dot_nt(own, table[:, a * PROJ : (a + 1) * PROJ]) for a in range(4)], axis=1
                )
                value = jnp.where(valid, jnp.exp(scores * (1.0 / SINK_EPS)), 0.0)
                mass[c, at : at + size, :] = value.astype(BF16)
                column[c : c + 1, :] += jnp.sum(value, axis=0, keepdims=True)
            at += size


def tables_kernel(packed, proj, table, rows, buffer, sem):
    size = THIRD - FIRST + 2
    copy = pltpu.make_async_copy(packed.at[pl.ds(FIRST, size), :], rows, sem)
    copy.start()
    copy.wait()
    wide = SECOND - FIRST
    for a in range(4):
        buffer[pl.ds(a, wide, stride=4), :] = rows[:wide, a * PROJ : (a + 1) * PROJ].astype(F32)
    proj[...] = buffer[...].astype(BF16)
    row = lax.broadcasted_iota(jnp.int32, (size - wide, WIDTH), 0)
    kept = jnp.where(row < QUARTER, rows[wide:, :].astype(F32), 0.0).astype(BF16)
    table[: size - wide, :] = kept
    table[size - wide :, :] = jnp.zeros((QUARTER_PAD - (size - wide), WIDTH), BF16)


def head_kernel(
    micro, images, ndp, pooled, order, w_head, w_proj, table, norm, mass, column, match,
    d_pooled, notes, all_pooled, active, unit, d_scores, d_embed, d_pre,
    scores, xhat_s, y_s, rstd_s, own_mass, target, total,
):
    rows = pooled.shape[0]
    group = rows // micro
    half = group // CROPS
    own = rows // ndp
    queued = mass.shape[1]
    scale_all = 1.0 / (TEMPER * CROPS * half * micro)
    chunk = WIDTH
    low = dot(order[...], pooled[...]).astype(BF16)
    all_pooled[...] = low
    for b in range(D // chunk):
        lanes = slice(b * chunk, (b + 1) * chunk)
        pre = dot(low, w_head[:, lanes])
        for m in range(micro):
            at = slice(m * group, (m + 1) * group)
            v = pre[at]
            mean = jnp.sum(v, axis=0, keepdims=True) * (1.0 / group)
            square = jnp.sum(v * v, axis=0, keepdims=True) * (1.0 / group)
            rstd = lax.rsqrt(square - mean * mean + NORM_EPS)
            xhat = (v - mean) * rstd
            y = xhat * norm[0:1, lanes] + norm[1:2, lanes]
            rstd_s[m : m + 1, lanes] = rstd
            xhat_s[at, lanes] = xhat
            y_s[at, lanes] = y
            active[at, lanes] = (y * sigmoid(y)).astype(BF16)
    embed = dot(active[...], w_proj[...]) + norm[2:3, :PROJ]
    recip = lax.rsqrt(jnp.sum(embed * embed, axis=1, keepdims=True) + UNIT_EPS)
    unit_v = (embed * recip).astype(BF16)
    unit[...] = unit_v
    valid = valid_lanes()
    for a in range(4):
        lanes = slice(a * QUARTER_PAD, (a + 1) * QUARTER_PAD)
        scores[:, lanes] = dot_nt(unit_v, table[:, a * PROJ : (a + 1) * PROJ])
    own_mass[...] = jnp.where(valid, jnp.exp(scores[...] * (1.0 / SINK_EPS)), 0.0)

    step = 32
    for c in range(CROPS):
        starts = [(m * CROPS + c) * half for m in range(micro)]
        once, scale = [], []
        for m in range(micro):
            at = slice(starts[m], starts[m] + half)
            sums = column[c : c + 1, :] + jnp.sum(own_mass[at, :], axis=0, keepdims=True)
            once.append(jnp.where(valid, 1.0 / sums, 0.0))
            own_mass[at, :] = own_mass[at, :] * once[m]
            scale.append(None)
        for turn in range(2):
            for m in range(micro):
                at = slice(starts[m], starts[m] + half)
                a = own_mass[at, :]
                if turn:
                    a = a * scale[m]
                a = a * (1.0 / jnp.sum(a, axis=1, keepdims=True))
                total[m] = jnp.sum(a.reshape(half // 8, 8, a.shape[1]), axis=0)

            def block(i, carry):
                e = mass[c, pl.ds(pl.multiple_of(i * step, step), step), :].astype(F32)
                for m in range(micro):
                    a = e * once[m]
                    if turn:
                        a = a * scale[m]
                    a = a * (1.0 / jnp.sum(a, axis=1, keepdims=True))
                    total[m] += jnp.sum(a.reshape(step // 8, 8, a.shape[1]), axis=0)
                return carry

            lax.fori_loop(0, queued // step, block, 0)
            for m in range(micro):
                more = jnp.where(valid, 1.0 / jnp.sum(total[m], axis=0, keepdims=True), 0.0)
                scale[m] = more if turn == 0 else scale[m] * more
        for m in range(micro):
            at = slice(starts[m], starts[m] + half)
            a = own_mass[at, :] * scale[m]
            own_mass[at, :] = a * (1.0 / jnp.sum(a, axis=1, keepdims=True))
    for m in range(micro):
        zero, one = (slice((m * CROPS + c) * half, (m * CROPS + c + 1) * half) for c in range(CROPS))
        target[zero, :] = jnp.dot(match[m], own_mass[one, :], precision=HIGH, preferred_element_type=F32)
        target[one, :] = lax.dot_general(match[m], own_mass[zero, :], TN, precision=HIGH, preferred_element_type=F32)
    logits = jnp.where(valid, scores[...] * (1.0 / TEMPER), -1e30)
    logits = logits - jnp.max(logits, axis=1, keepdims=True)
    power = jnp.exp(logits)
    summed = jnp.sum(power, axis=1, keepdims=True)
    goal = target[...]
    loss = jnp.sum(goal * (logits - jnp.log(summed)), axis=1, keepdims=True)
    loss = jnp.sum(loss, axis=0, keepdims=True) * (-TEMPER * scale_all)
    weight = jnp.sum(goal, axis=1, keepdims=True) / summed
    d_scores[...] = ((power * weight - goal) * scale_all).astype(BF16)
    d_unit = None
    for a in range(4):
        more = dot(d_scores[:, a * QUARTER_PAD : (a + 1) * QUARTER_PAD], table[:, a * PROJ : (a + 1) * PROJ])
        d_unit = more if d_unit is None else d_unit + more
    along = jnp.sum(d_unit * embed, axis=1, keepdims=True)
    d_low = (recip * d_unit - embed * (recip * recip * recip) * along).astype(BF16)
    d_embed[...] = d_low
    notes[...] = jnp.zeros_like(notes)
    notes[2:3, :PROJ] = jnp.sum(d_low.astype(F32), axis=0, keepdims=True)
    notes[3:4, :] = jnp.broadcast_to(loss, (1, D))
    for b in range(D // chunk):
        lanes = slice(b * chunk, (b + 1) * chunk)
        d_active = dot_nt(d_low, w_proj[lanes, :])
        for m in range(micro):
            at = slice(m * group, (m + 1) * group)
            d_y = d_active[at] * slope(y_s[at, lanes])
            xhat = xhat_s[at, lanes]
            by_x = jnp.sum(d_y * xhat, axis=0, keepdims=True)
            plain = jnp.sum(d_y, axis=0, keepdims=True)
            notes[0:1, lanes] += by_x
            notes[1:2, lanes] += plain
            value = d_y - plain * (1.0 / group) - xhat * (by_x * (1.0 / group))
            d_pre[at, lanes] = (norm[0:1, lanes] * rstd_s[m : m + 1, lanes] * value).astype(BF16)
    mine = dot_tn(order[:, :own], d_pre[...]).astype(BF16)
    d_pooled[...] = dot_nt(mine, w_head[...]).astype(BF16)


def interleave(width):
    row = lax.broadcasted_iota(jnp.int32, (4 * width, 4 * width), 0)
    column = lax.broadcasted_iota(jnp.int32, (4 * width, 4 * width), 1)
    return (column == 4 * (row % width) + row // width).astype(BF16)


def head_grads_kernel(place, pooled, active, unit, d_scores, d_embed, d_pre, choose, weave, out):
    @pl.when(place[0] != SECTIONS - 1)
    def _():
        out[...] = jnp.zeros_like(out)

    @pl.when(place[0] == SECTIONS - 1)
    def _():
        own = choose.shape[1]
        block = PART
        parts = []
        for q in range(4):
            own_d = dot(d_pre[:, q * WIDTH : (q + 1) * WIDTH], choose[...]).astype(BF16)
            parts.append(dot_tn(own_d, pooled[...]).astype(BF16))
        for b in range(D // block):
            mixed = jnp.concatenate([p[:, b * block : (b + 1) * block] for p in parts], axis=1)
            out[:, 4 * block * b : 4 * block * (b + 1)] = dot(mixed, weave[...])
        proj = jnp.zeros((own, WIDTH), F32)
        proto = jnp.zeros((own, QUARTER_PAD), F32)
        apart = []
        for b in range(4):
            apart.append(dot_nt(active[:, b * WIDTH : (b + 1) * WIDTH], weave[...]).astype(BF16))
        for a in range(4):
            some = choose[a * PROJ : (a + 1) * PROJ, :]
            own_e = dot(d_embed[...], some).astype(BF16)
            own_u = dot(unit[...], some).astype(BF16)
            column = jnp.concatenate([v[:, a * block : (a + 1) * block] for v in apart], axis=1)
            proj = proj + dot_tn(own_e, column)
            proto = proto + dot_tn(own_u, d_scores[:, a * QUARTER_PAD : (a + 1) * QUARTER_PAD])
        out[:, FIRST:SECOND] = proj
        out[:, SECOND:] = proto[:, : out.shape[1] - SECOND]


def finish_kernel(place, base, reduce, expand, m1, m2, m3, conv, c1, c2, c3, weave, out, buffer, sem):
    mixed = (None, m1, m2, m3)
    t = place[0]

    def write(lanes):
        copy = pltpu.make_async_copy(buffer.at[:, pl.ds(0, lanes)], out.at[:, pl.ds(0, lanes)], sem)
        copy.start()
        copy.wait()

    @pl.when(t == 0)
    def _():
        for u in range(SECTIONS):
            piece = reduce if u == 0 else mixed[u]
            buffer[:, u * WIDE : (u + 1) * WIDE] = piece[...].astype(F32)
        write(D)

    @pl.when(t == 1)
    def _():
        for u in range(SECTIONS):
            piece = (conv, c1, c2, c3)[u ^ 1]
            for tap in range(9):
                at = tap * WIDTH + u * PART
                buffer[:, at : at + PART] = piece[:, tap * PART : (tap + 1) * PART].astype(F32)
        write(9 * WIDTH)

    @pl.when(t == 2)
    def _():
        four = [expand if u == 2 else mixed[u ^ 2] for u in range(SECTIONS)]
        for b in range(WIDTH // PART):
            lanes = slice(b * PART, (b + 1) * PART)
            row = jnp.concatenate([f[:, lanes] for f in four], axis=1)
            buffer[:, 4 * b * PART : 4 * (b + 1) * PART] = dot(row, weave[...])
        write(D)


def unpack_kernel(packed, out, buffer):
    rows = packed.shape[0]
    for b in range(4):
        buffer[b] = packed[:, b * PART : (b + 1) * PART].astype(F32)
    for q in range(4):
        for b in range(4):
            at = q * WIDTH + b * PART
            out[:, at : at + PART] = buffer[b, pl.ds(q, rows // 4, stride=4), :].astype(BF16)


def unpack(packed, rows):
    step = 1024
    return pl.pallas_call(
        unpack_kernel,
        out_shape=shape((rows // 4, 4 * WIDTH), BF16),
        grid=(rows // step,),
        in_specs=[pl.BlockSpec((step, WIDTH), lambda i: (i, 0))],
        out_specs=pl.BlockSpec((step // 4, 4 * WIDTH), lambda i: (i, 0)),
        scratch_shapes=[pltpu.VMEM((4, step, PART), F32)],
        compiler_params=pltpu.CompilerParams(vmem_limit_bytes=16 * 2**20),
        cost_estimate=cost(4),
    )(packed)


def pack_kernel(parts, lanes_of, place, source, norm, *refs):
    outs, sem = refs[:-1], refs[-1]
    copies = []
    for j, out in enumerate(outs):
        lane, lanes = lanes_of[j]
        for row, rows, at in parts(place):
            ref = source.at[pl.ds(row, rows), pl.ds(lane, lanes)]
            copies.append(pltpu.make_async_copy(ref, out.at[pl.ds(at, rows), :], sem.at[len(copies)]))
    for copy in copies:
        copy.start()
    for j, out in enumerate(outs):
        lane, lanes = lanes_of[j]
        out[out.shape[0] - 16 :, :] = tell_norm(norm[:, lane : lane + lanes])
    for copy in copies:
        copy.wait()


def pack(place, source, norm, parts, lanes_of, rows):
    count = len(parts([0] * 8))
    return pl.pallas_call(
        functools.partial(pack_kernel, parts, lanes_of),
        out_shape=[shape((rows + 16, lanes), BF16) for _, lanes in lanes_of],
        in_specs=[
            pl.BlockSpec(memory_space=pltpu.SMEM),
            pl.BlockSpec(memory_space=pltpu.HBM),
            pl.BlockSpec(memory_space=pltpu.VMEM),
        ],
        out_specs=[pl.BlockSpec(memory_space=pltpu.VMEM)] * len(lanes_of),
        scratch_shapes=[pltpu.SemaphoreType.DMA((count * len(lanes_of),))],
        compiler_params=pltpu.CompilerParams(vmem_limit_bytes=12 * 2**20),
        cost_estimate=cost(1.5),
    )(place, source, norm)


def multiple(value, step):
    return value if isinstance(value, int) else pl.multiple_of(value, step)


def pair_kernel(place, a, b, keep, out, full):
    full[...] = dot_tn(a[...], b[...])
    own = keep.shape[1]
    for z in range(keep.shape[0]):
        mine = (2 * z + place[4]) * own
        other = (2 * z + place[5]) * own
        keep[z] = full[pl.ds(pl.multiple_of(mine, own), own), :]
        out[z] = full[pl.ds(pl.multiple_of(other, own), own), :].astype(BF16)


def image_pair_kernel(place, a, image, keep, out, full):
    lanes = pl.ds(pl.multiple_of(place[0] * WIDE, WIDE), WIDE)
    pair_kernel(place, a, image.at[:, lanes], keep, out, full)


def cross_kernel(place, keep, came, own, o1, o2, o3):
    for k, o in enumerate((own, o1, o2, o3)):
        z = place[6] ^ k
        o[...] = (keep[z] + came[z].astype(F32)).astype(o.dtype)


def add_kernel(own, r1, r2, r3, out):
    out[...] = ((own[...] + r1[...].astype(F32)) + (r2[...].astype(F32) + r3[...].astype(F32))).astype(BF16)


def after(value, *others):
    return lax.optimization_barrier((value, *others))[0]


def body(image, section_weights, section_norms, queue, pairing):
    micro, images = image.shape[0], image.shape[2]
    ndp = lax.axis_size("dp")
    t = lax.axis_index("section")
    dp = lax.axis_index("dp")
    core = dp % 2
    place = jnp.stack([t ^ k for k in range(SECTIONS)] + [core, 1 - core, dp // 2, dp]).astype(jnp.int32)
    cells = CROPS * PLACES * images
    rows = micro * cells
    count = float(cells * ndp)
    packed = section_weights[0]
    norm3 = section_norms[0]
    param_rows = packed.shape[0]
    own = WIDTH // ndp
    k = functools.partial

    def pieces_of(width, dtype):
        return shape((rows, width), dtype)

    def from_section(pieces, source):
        return [pieces[0]] + [lax.ppermute(pieces[j], "section", [(source, source ^ j)]) for j in range(1, SECTIONS)]

    def both_halves(came, source, us):
        half = call(k(pick_kernel, source), shape(came[0].shape, BF16), place, *came, us=us)
        return half, flip(half, "dp", 1)

    half = D // 2
    reduce_came = from_section(
        pack(
            place, packed, norm3,
            lambda p: [(multiple(p[4] * half, half), half, 0)],
            [(j * PART, PART) for j in range(SECTIONS)],
            half,
        ),
        0,
    )
    quarter = WIDTH // 2
    conv_own = pack(
        place, after(packed, *reduce_came[:1]), norm3,
        lambda p: [(multiple(tap * WIDTH + p[4] * quarter, quarter), quarter, tap * quarter) for tap in range(9)],
        [((1 ^ j) * PART, PART) for j in range(SECTIONS)],
        9 * quarter,
    )
    conv_came = from_section(conv_own, 1)
    natural = unpack(after(packed, *conv_own[:1]), FIRST)
    expand_own = pack(
        place, natural, norm3,
        lambda p: [(multiple(p[4] * quarter, quarter), quarter, 0)],
        [((2 ^ j) * WIDE, WIDE) for j in range(SECTIONS)],
        quarter,
    )
    expand_came = from_section(expand_own, 2)
    flat = image.transpose(0, 1, 3, 4, 2, 5).reshape(rows, D)

    queue_size = CROPS * queue.shape[1]
    note = jnp.pad(pairing.astype(BF16), ((0, 16 - micro), (0, PROJ - images)))
    note = jnp.concatenate([queue.reshape(queue_size, PROJ), note])
    told, told_offsets = gather_dp(note, dp_stages())

    w_reduce = both_halves(reduce_came, 0, 0.5)
    sums_of = shape((8, PART), F32)
    pre0, part = call(k(reduce_kernel, micro), (pieces_of(PART, F32), sums_of), place, flat, *w_reduce, us=2)
    sums0 = sum_dp(part)
    active0 = call(
        k(active_kernel, micro, count, half), pieces_of(PART, BF16), pre0, sums0, w_reduce[0], us=1
    )
    actives0 = gather_xor(active0, "section")

    w_conv = both_halves(conv_came, 1, 0.6)
    w_proj, table = pl.pallas_call(
        tables_kernel,
        out_shape=(shape((D, PROJ), BF16), shape((QUARTER_PAD, WIDTH), BF16)),
        in_specs=[pl.BlockSpec(memory_space=pltpu.HBM)],
        out_specs=(pl.BlockSpec(memory_space=pltpu.VMEM), pl.BlockSpec(memory_space=pltpu.VMEM)),
        scratch_shapes=[
            pltpu.VMEM((THIRD - FIRST + 2, WIDTH), BF16), pltpu.VMEM((D, PROJ), F32), pltpu.SemaphoreType.DMA,
        ],
        compiler_params=pltpu.CompilerParams(vmem_limit_bytes=12 * 2**20),
        cost_estimate=cost(1.5),
    )(after(packed, *expand_own[:1]))
    head_rows = rows // PLACES * ndp
    lanes = 4 * QUARTER_PAD
    small = head_rows <= 128 and images * ndp >= 32 and queue.shape[1] * ndp <= 512
    if small:
        mass, column = call(
            k(mass_kernel, ndp),
            (shape((CROPS, ndp * queue.shape[1], lanes), BF16), shape((8, lanes), F32)),
            after(table, active0), *[v.reshape(-1, PROJ) for v in told],
            vmem=16, us=5,
        )
        actives0 = lax.optimization_barrier((*actives0, mass))[:4]

    pre1, part = call(
        k(conv_kernel, micro, images),
        (pieces_of(PART, F32), sums_of),
        place, *actives0, *w_conv,
        scratch=[pltpu.VMEM((rows, WIDTH), BF16)],
        us=3,
    )
    sums1 = sum_dp(part)
    active1_own = call(
        k(active_kernel, micro, count, 9 * quarter), pieces_of(PART, BF16), pre1, sums1, w_conv[0], us=1
    )
    actives1 = gather_xor(active1_own, "section")
    w_expand = both_halves(expand_came, 2, 0.5)
    active1, pre2, part = call(
        k(expand_kernel, micro),
        (pieces_of(WIDTH, BF16), pieces_of(WIDE, F32), shape((8, WIDE), F32)),
        place, *actives1, *w_expand,
        us=2,
    )
    back_rows = 9 * PART // 2 + WIDE // 2
    back_own = call(
        back_parts_kernel, [shape((back_rows, PART), BF16)] * 4, place, *w_conv, *w_reduce, us=1
    )
    back_own = lax.optimization_barrier((*back_own, part))[:4]
    back_came = [back_own[0]] + [flip(back_own[j], "section", j) for j in range(1, SECTIONS)]

    sums2 = sum_dp(part)
    pooled = call(
        k(pool_kernel, micro, images, count),
        shape((rows // PLACES, WIDE), BF16),
        place, pre2, sums2, w_expand[0], flat,
        us=1.6,
    )

    per_dp = rows // PLACES
    came_p = [send(pooled, j, 3) for j in range(3)]
    pooled_here = jnp.concatenate(came_p + [pooled], axis=1)
    stages = dp_stages()
    parts, offsets = gather_dp(pooled_here, stages[1:] + stages[:1])
    all_pooled = jnp.concatenate(parts)
    offset = jnp.array(sum(offsets, []), jnp.int32)
    head_order = jnp.arange(head_rows, dtype=jnp.int32)
    block, inner = head_order // per_dp, head_order % per_dp
    group, single = inner // images, inner % images
    position = (group * ndp + (offset[block] ^ dp)) * images + single
    order = (position[None, :] == head_order[:, None]).astype(BF16)
    told = [v.reshape(-1, queue_size + 16, PROJ) for v in told]
    pairs = jnp.concatenate([v[:, queue_size : queue_size + micro, :images] for v in told]).astype(jnp.int32)
    told_offset = jnp.array(sum(told_offsets, []), jnp.int32)
    pairs_dp = (told_offset ^ dp)[None, :] == jnp.arange(ndp, dtype=jnp.int32)[:, None]
    pairs = jnp.sum(jnp.where(pairs_dp[:, :, None, None], pairs[None], 0), axis=1)
    left = jnp.arange(images * ndp, dtype=jnp.int32)
    pairs = pairs.transpose(1, 0, 2).reshape(micro, ndp * images)
    match = ((left // images * images + pairs)[:, :, None] == left[None, None, :]).astype(F32)
    if small:
        order, match, all_pooled = lax.optimization_barrier((order, match, all_pooled))
        d_pooled, notes3, all_pooled, active3, unit, d_scores, d_embed, d_pre3 = call(
            k(head_kernel, micro, images, ndp),
            (
                shape((per_dp, D), BF16), shape((8, D), F32), shape((head_rows, D), BF16), shape((head_rows, D), BF16),
                shape((head_rows, PROJ), BF16), shape((head_rows, lanes), BF16), shape((head_rows, PROJ), BF16),
                shape((head_rows, D), BF16),
            ),
            all_pooled, order, natural, w_proj, table, norm3, mass, column, match,
            scratch=[
                pltpu.VMEM((head_rows, lanes), F32), pltpu.VMEM((head_rows, D), F32), pltpu.VMEM((head_rows, D), F32),
                pltpu.VMEM((8, D), F32), pltpu.VMEM((head_rows, lanes), F32), pltpu.VMEM((head_rows, lanes), F32),
                pltpu.VMEM((micro, 8, lanes), F32),
            ],
            vmem=30, us=27,
        )
        grads3, loss = notes3[:3], notes3[3:4, :1]
    else:
        all_pooled = dot(order, all_pooled).astype(BF16)
        protos = jnp.concatenate([table[:, a * PROJ : (a + 1) * PROJ] for a in range(4)], axis=0)
        queue_all = jnp.concatenate(told)[:, :queue_size].reshape(ndp, CROPS, queue.shape[1], PROJ)
        queue_rows = queue_all.transpose(1, 0, 2, 3).reshape(CROPS, -1, PROJ)
        loss, grads3, active3, unit, d_scores, d_embed, d_pre3 = head(
            all_pooled, natural, w_proj, protos, norm3, queue_rows, match, micro, images, dp
        )
        loss = loss.reshape(1, 1)
        d_pooled = dot_nt(dot_tn(order[:, :per_dp], d_pre3).astype(BF16), natural).astype(BF16)

    parts = [d_pooled[:, j * WIDE : (j + 1) * WIDE] for j in range(SECTIONS)]
    came_d = [send(parts[j], 3, j) for j in range(3)]
    back_half = call(stack_kernel, shape((SECTIONS, back_rows, PART), BF16), *back_came, us=0.6)
    back_halves = (back_half, flip(back_half, "dp", 1))
    d_z, part = call(
        k(out_back_kernel, micro, images, count),
        (pieces_of(WIDE, F32), shape((8, WIDE), F32)),
        place, pre2, sums2, w_expand[0], flat, parts[3], *came_d,
        us=1.8,
    )
    back2 = sum_dp(part)
    d_pre2, *partial = call(
        k(expand_back_kernel, micro, count),
        [pieces_of(WIDE, BF16)] + [pieces_of(PART, BF16)] * 4,
        place, pre2, sums2, d_z, back2, *w_expand,
        scratch=[pltpu.VMEM((rows, WIDTH), F32)],
        us=2,
    )
    partial = [partial[0]] + [flip(partial[j], "section", j) for j in range(1, SECTIONS)]

    def scatter_start(kernel, a, b, width):
        if ndp != 8:
            if kernel is image_pair_kernel:
                b = lax.dynamic_slice_in_dim(b, t * WIDE, WIDE, 1)
            return dot_tn(a, b)
        keep, out = call(
            kernel,
            (shape((4, own, width), F32), shape((4, own, width), BF16)),
            place, a, b,
            scratch=[pltpu.VMEM((WIDTH, width), F32)],
            us=2.5,
        )
        return keep, flip(out, "dp", 1)

    def scatter_cross(started, *others):
        if ndp != 8:
            return lax.psum_scatter(started.astype(BF16), "dp", scatter_dimension=0, tiled=True)
        keep, came = started
        if others:
            keep = after(keep, *others)
        dims = keep.shape[1:]
        kept, *out = call(
            cross_kernel, [shape(dims, F32)] + [shape(dims, BF16)] * 3, place, keep, came
        )
        return [kept] + [flip(out[j], "dp", 2 * (j + 1)) for j in range(3)]

    def scatter_finish(crossed):
        if ndp != 8:
            return crossed
        return call(add_kernel, shape(crossed[0].shape, BF16), *crossed)

    expand_started = scatter_start(pair_kernel, d_pre2, active1, WIDTH)
    choose = (jnp.arange(WIDTH, dtype=jnp.int32)[:, None] == dp * own + jnp.arange(own, dtype=jnp.int32)[None, :])
    choose = choose.astype(BF16)
    weave = interleave(PART)
    base = call(
        head_grads_kernel,
        shape((own, param_rows), F32),
        place, after(all_pooled, d_pre2), active3, unit, d_scores, d_embed, d_pre3, choose, weave,
        us=7,
    )
    partial = lax.optimization_barrier((*partial, base))[:4]

    d_y1, part = call(
        k(silu_back_kernel, micro, count, 9 * quarter),
        (pieces_of(PART, F32), sums_of),
        *partial, pre1, sums1, w_conv[0],
    )
    back1 = sum_dp(part)
    d_pre1_own = call(
        k(norm_back_kernel, micro, count, 9 * quarter), pieces_of(PART, BF16), d_y1, pre1, sums1, back1, w_conv[0]
    )
    d_pre1s = gather_xor(d_pre1_own, "section")
    expand_crossed = scatter_cross(expand_started, d_pre1_own)
    taps = call(k(taps_kernel, images), pieces_of(9 * PART, BF16), after(active0, d_pre1_own), us=1.3)
    *d_pre1s, taps = lax.optimization_barrier((*d_pre1s, taps))
    d_pre1, d_y0, part = call(
        k(conv_back_kernel, micro, images, count, half),
        (pieces_of(WIDTH, BF16), pieces_of(PART, F32), sums_of),
        place, *d_pre1s, *back_halves, pre0, sums0, w_reduce[0],
        scratch=[pltpu.VMEM((9 * PART, WIDTH), BF16)],
        us=3.5,
    )
    back0 = sum_dp(part)
    conv_started = scatter_start(pair_kernel, after(d_pre1, part), taps, 9 * PART)
    d_pre0_own = call(
        k(norm_back_kernel, micro, count, half), pieces_of(PART, BF16), d_y0, pre0, sums0, back0, w_reduce[0]
    )
    d_pre0s = gather_xor(d_pre0_own, "section")
    g_expand = scatter_finish(expand_crossed)
    conv_crossed = scatter_cross(conv_started, d_pre0_own)

    def both(back):
        gain, shift = back[0:1], back[micro : micro + 1]
        for m in range(1, micro):
            gain, shift = gain + back[m : m + 1], shift + back[micro + m : micro + m + 1]
        return jnp.concatenate([gain, shift])

    lines = jnp.concatenate([both(back2), both(back0), both(back1)], axis=1)
    note = jnp.concatenate([lines, jnp.broadcast_to(jnp.where(t == 3, loss, 0.0), (6, lines.shape[1]))])
    notes = jnp.stack(gather_xor(note, "section"))
    d_pre0, grad_in = call(
        reduce_back_kernel,
        (pieces_of(WIDTH, BF16), pieces_of(WIDE, F32)),
        place, *d_pre0s, *back_halves, d_z,
        scratch=[pltpu.VMEM((WIDE, WIDTH), BF16)],
        us=2,
    )
    reduce_started = scatter_start(image_pair_kernel, d_pre0, flat, WIDE)
    reduce_crossed = scatter_cross(reduce_started)
    g_conv = scatter_finish(conv_crossed)
    conv_here = [g_conv] + [send(g_conv, 1 ^ j, 1) for j in range(1, SECTIONS)]
    g_reduce = scatter_finish(reduce_crossed)
    mixed = []
    for j in range(1, SECTIONS):
        value = jnp.where((t ^ j) == 0, g_reduce, g_expand)
        mixed.append(lax.ppermute(value, "section", [(j, 0), (2 ^ j, 2)]))
    weight_grads = pl.pallas_call(
        finish_kernel,
        out_shape=shape((own, param_rows), F32),
        in_specs=[pl.BlockSpec(memory_space=pltpu.SMEM), pl.BlockSpec(memory_space=pltpu.HBM)]
        + [pl.BlockSpec(memory_space=pltpu.VMEM)] * 10,
        out_specs=pl.BlockSpec(memory_space=pltpu.HBM),
        scratch_shapes=[pltpu.VMEM((own, 9 * WIDTH), F32), pltpu.SemaphoreType.DMA],
        input_output_aliases={1: 0},
        compiler_params=pltpu.CompilerParams(vmem_limit_bytes=12 * 2**20),
        cost_estimate=cost(2),
    )(place, base, g_reduce, g_expand, *mixed, *conv_here, weave)

    loss = ((notes[0, 2:3, :1] + notes[1, 2:3, :1]) + (notes[2, 2:3, :1] + notes[3, 2:3, :1])).reshape(())
    notes = jnp.concatenate(
        [lax.dynamic_index_in_dim(notes, t ^ j, 0, keepdims=False) for j in range(SECTIONS)], axis=1
    )[:2].reshape(2, SECTIONS, WIDE + 2 * PART)

    def narrow(value):
        value = value.reshape(2, -1)
        return jnp.pad(value, ((0, 1), (0, D - value.shape[1])))

    norm_grads = jnp.where(
        t == 0,
        narrow(notes[:, :, WIDE : WIDE + PART]),
        jnp.where(t == 1, narrow(notes[:, :, WIDE + PART :]), jnp.where(t == 2, narrow(notes[:, :, :WIDE]), grads3)),
    )
    grad_in = grad_in.reshape(micro, CROPS, SIDE, SIDE, images, WIDE).transpose(0, 1, 4, 2, 3, 5)
    return (loss, grad_in, weight_grads.T[None], norm_grads[None])


def solution(mesh):
    in_specs = (
        P(None, None, "dp", None, None, None),
        P("section", None, None),
        P("section", None, None),
        P(None, "dp", None),
        P(None, "dp"),
    )
    out_specs = (
        P(),
        P(None, None, "dp", None, None, "section"),
        P("section", None, "dp"),
        P("section", None, None),
    )
    return jax.shard_map(body, mesh=mesh, in_specs=in_specs, out_specs=out_specs, check_vma=False)
```

```python
import functools

import jax
import jax.numpy as jnp
from jax import lax
from jax.experimental import pallas as pl
from jax.experimental.pallas import tpu as pltpu
from jax.sharding import PartitionSpec as P

D = 2048
WIDTH = 512
PROJ = 128
PROTOS = 3000
SIDE = 7
CROPS = 2
SECTIONS = 4
PART = WIDTH // SECTIONS
WIDE = D // SECTIONS
QUARTER = PROTOS // 4
QUARTER_PAD = 768
PLACES = SIDE * SIDE
FIRST = D * (D // WIDTH)
SECOND = FIRST + D * PROJ // WIDTH
THIRD = SECOND + PROTOS * PROJ // WIDTH

NORM_EPS = 1e-05
UNIT_EPS = 1e-06
SINK_EPS = 0.05
TEMPER = 0.1
HIGH = lax.Precision.HIGHEST
F32 = jnp.float32
BF16 = jnp.bfloat16
NT = (((1,), (1,)), ((), ()))
TN = (((0,), (0,)), ((), ()))


def dot(a, b):
    return jnp.dot(a, b, preferred_element_type=F32)


def dot_nt(a, b):
    return lax.dot_general(a, b, NT, preferred_element_type=F32)


def dot_tn(a, b):
    return lax.dot_general(a, b, TN, preferred_element_type=F32)


def flip(value, axis, step):
    count = lax.axis_size(axis)
    return lax.ppermute(value, axis, [(source, source ^ step) for source in range(count)])


def send(value, source, target):
    return lax.ppermute(value, "section", [(source, target)])


def sum_dp(value):
    count = lax.axis_size("dp")
    value = value + flip(value, "dp", 1)
    step = 2
    while step < count:
        if 2 * step < count:
            near = value + flip(value, "dp", step)
            far = flip(value, "dp", 2 * step) + flip(value, "dp", 3 * step)
            value = near + far
            step *= 4
        else:
            value = value + flip(value, "dp", step)
            step *= 2
    return value


def gather_xor(value, axis):
    return [value] + [flip(value, axis, step) for step in range(1, lax.axis_size(axis))]


def dp_stages():
    count = lax.axis_size("dp")
    stages, step = [(1,)], 2
    while step < count:
        if 2 * step < count:
            stages.append((step, 2 * step, 3 * step))
            step *= 4
        else:
            stages.append((step,))
            step *= 2
    return stages


def gather_dp(value, stages):
    arrays, offsets = [value], [[0]]
    for steps in stages:
        if len(arrays) > 1:
            arrays, offsets = [rows_of(arrays)], [sum(offsets, [])]
        first = offsets[0]
        for step in steps:
            arrays.append(flip(arrays[0], "dp", step))
            offsets.append([o ^ step for o in first])
    return arrays, offsets


def sigmoid(v):
    return 1.0 / (1.0 + jnp.exp(-v))


def slope(v):
    s = sigmoid(v)
    return s * (1.0 + v * (1.0 - s))


def cost(us):
    return pl.CostEstimate(flops=0, bytes_accessed=int(us * 3_000_000), transcendentals=0)


def hbm(value):
    return pltpu.with_memory_space_constraint(value, pltpu.HBM)


def call(kernel, out, *args, scratch=(), vmem=12, us=1.0, in_hbm=()):
    in_specs, ins = [], []
    for j, a in enumerate(args):
        space = pltpu.VMEM
        if jnp.issubdtype(a.dtype, jnp.integer):
            space = pltpu.SMEM
        elif j in in_hbm:
            space = pltpu.HBM
            a = hbm(a)
        in_specs.append(pl.BlockSpec(memory_space=space))
        ins.append(a)
    return pl.pallas_call(
        kernel,
        out_shape=out,
        in_specs=in_specs,
        out_specs=jax.tree.map(lambda _: pl.BlockSpec(memory_space=pltpu.VMEM), out),
        scratch_shapes=list(scratch),
        compiler_params=pltpu.CompilerParams(vmem_limit_bytes=vmem * 2**20),
        cost_estimate=cost(us),
    )(*ins)


def shape(dims, dtype):
    return jax.ShapeDtypeStruct(tuple(dims), dtype)


def retile_kernel(image, flat):
    flat[...] = image[...].reshape(flat.shape)


def note_kernel(pairing, queue, out):
    size = queue.shape[1]
    for c in range(CROPS):
        out[c * size : (c + 1) * size, :] = queue[c]
    row = lax.broadcasted_iota(jnp.int32, (16, PROJ), 0)
    lane = lax.broadcasted_iota(jnp.int32, (16, PROJ), 1)
    value = jnp.zeros((16, PROJ), F32)
    for m in range(pairing.shape[0]):
        for i in range(pairing.shape[1]):
            value = jnp.where((row == m) & (lane == i), pairing[m, i].astype(F32), value)
    out[CROPS * size :, :] = value.astype(BF16)


def rows_kernel(*refs):
    out, at = refs[-1], 0
    for ref in refs[:-1]:
        out[at : at + ref.shape[0], :] = ref[...]
        at += ref.shape[0]


def lanes_kernel(*refs):
    out, at = refs[-1], 0
    for ref in refs[:-1]:
        out[:, at : at + ref.shape[1]] = ref[...]
        at += ref.shape[1]


def rows_of(values, us=0.5):
    rows = sum(v.shape[0] for v in values)
    return call(rows_kernel, shape((rows, values[0].shape[1]), values[0].dtype), *values, us=us)


def split_sums(first, second, micro):
    width = first[0].shape[1]
    rows = [jnp.sum(v, axis=0, keepdims=True) for v in first]
    rows += [jnp.sum(v, axis=0, keepdims=True) for v in second]
    rows.append(jnp.zeros((8 - 2 * micro, width), F32))
    return jnp.concatenate(rows, axis=0)


def moments(sums, m, micro, count):
    mean = sums[m : m + 1] * (1.0 / count)
    square = sums[micro + m : micro + m + 1] * (1.0 / count)
    return mean, lax.rsqrt(square - mean * mean + NORM_EPS)


def per_micro(value, micro):
    rows = value.shape[0] // micro
    return [value[m * rows : (m + 1) * rows] for m in range(micro)]


def normalized(value, sums, micro, count):
    out = []
    for m, v in enumerate(per_micro(value, micro)):
        mean, rstd = moments(sums, m, micro, count)
        out.append(((v - mean) * rstd, rstd))
    return out


def join(parts):
    return jnp.concatenate(parts, axis=0)


def tap_valid(rows, images, tap, sign):
    row = lax.broadcasted_iota(jnp.int32, (rows, PART), 0).astype(F32)
    cell = jnp.floor((row + 0.5) * (1.0 / images))
    crop = jnp.floor((cell + 0.5) * (1.0 / PLACES))
    place = cell - crop * PLACES
    y = jnp.floor((place + 0.5) * (1.0 / SIDE))
    x = place - y * SIDE
    y = y + float(sign * (tap // 3 - 1))
    x = x + float(sign * (tap % 3 - 1))
    return (y > -0.5) & (y < SIDE - 0.5) & (x > -0.5) & (x < SIDE - 0.5)


def tap_shift(value, images, tap, sign):
    rows = value.shape[0]
    offset = sign * images * (SIDE * (tap // 3 - 1) + (tap % 3 - 1))
    moved = value if offset == 0 else pltpu.roll(value, (-offset) % rows, 0)
    if tap == 4:
        return moved
    return jnp.where(tap_valid(rows, images, tap, sign), moved, 0.0)


def told_norm(message, at):
    rows = message[at : at + 16, :].astype(F32)
    return rows[0:1] + rows[1:2] + rows[2:3], rows[3:4] + rows[4:5] + rows[5:6]


def tell_norm(rows):
    out = []
    for r in range(2):
        left = rows[r : r + 1]
        for _ in range(3):
            term = left.astype(BF16).astype(F32)
            out.append(term)
            left = left - term
    out.append(jnp.zeros((10, rows.shape[1]), F32))
    return jnp.concatenate(out, axis=0).astype(BF16)


def reduce_kernel(micro, place, image, w0, w1, pre, sums):
    half = D // 2
    first = pl.ds(pl.multiple_of(place[4] * half, half), half)
    second = pl.ds(pl.multiple_of(place[5] * half, half), half)
    value = dot(image[:, first], w0[:half, :]) + dot(image[:, second], w1[:half, :])
    pre[...] = value
    parts = per_micro(value, micro)
    sums[...] = split_sums(parts, [v * v for v in parts], micro)


def active_kernel(micro, count, at, pre, sums, told, active):
    gain, shift = told_norm(told, at)
    out = []
    for xhat, _ in normalized(pre[...], sums[...], micro, count):
        y = xhat * gain + shift
        out.append(y * sigmoid(y))
    active[...] = join(out).astype(BF16)


def fill(place, pieces, full):
    for k, piece in enumerate(pieces):
        full[:, pl.ds(pl.multiple_of(place[k] * PART, PART), PART)] = piece[...]


def quarter_of(place, j):
    return place[8] ^ (0, 2, 1, 3)[j]


def conv_kernel(micro, images, place, a0, a1, a2, a3, wa, wb, pre, sums, full, weight):
    fill(place, (a0, a1, a2, a3), full)
    quarter = WIDTH // 4
    step = 9 * quarter + 16
    for j in range(4):
        w = (wa, wb)[j // 2]
        at = pl.multiple_of(quarter_of(place, j) * quarter, quarter)
        for tap in range(9):
            lanes = slice(tap * PART, (tap + 1) * PART)
            first = (j % 2) * step + tap * quarter
            weight[pl.ds(at, quarter), lanes] = w[first : first + quarter, :]
    total = None
    for first in range(0, 9, 2):
        taps = [tap for tap in (first, first + 1) if tap < 9]
        part = dot(full[...], weight[:, first * PART : (taps[-1] + 1) * PART])
        for j, tap in enumerate(taps):
            moved = tap_shift(part[:, j * PART : (j + 1) * PART], images, tap, 1)
            total = moved if total is None else total + moved
    pre[...] = total
    parts = per_micro(total, micro)
    sums[...] = split_sums(parts, [v * v for v in parts], micro)


def expand_kernel(micro, place, a0, a1, a2, a3, w0, w1, active, pre, sums):
    fill(place, (a0, a1, a2, a3), active)
    half = WIDTH // 2
    value = None
    for j, w in enumerate((w0, w1)):
        lanes = pl.ds(pl.multiple_of(place[4 + j] * half, half), half)
        more = dot(active[:, lanes], w[:half, :])
        value = more if value is None else value + more
    pre[...] = value
    parts = per_micro(value, micro)
    sums[...] = split_sums(parts, [v * v for v in parts], micro)


def crop_rows(rows, images, transpose=False):
    shp = (rows // PLACES, rows)
    r = lax.broadcasted_iota(jnp.int32, shp, 1).astype(F32)
    q = lax.broadcasted_iota(jnp.int32, shp, 0).astype(F32)
    cell = jnp.floor((r + 0.5) * (1.0 / images))
    crop = jnp.floor((cell + 0.5) * (1.0 / PLACES))
    image = r - cell * images
    return (jnp.abs(crop * images + image - q) < 0.5).astype(F32).astype(BF16)


def pool_kernel(micro, images, count, place, pre, sums, told, image, pooled):
    lanes = pl.ds(pl.multiple_of(place[0] * WIDE, WIDE), WIDE)
    gain, shift = told_norm(told, WIDTH // 2)
    out = []
    for xhat, _ in normalized(pre[...], sums[...], micro, count):
        out.append(xhat * gain + shift)
    z = join(out) + image[:, lanes].astype(F32)
    out = z * sigmoid(z)
    high = out.astype(BF16)
    low = (out - high.astype(F32)).astype(BF16)
    choose = crop_rows(pre.shape[0], images)
    pooled[...] = ((dot(choose, high) + dot(choose, low)) * (1.0 / PLACES)).astype(BF16)


def out_back_kernel(micro, images, count, place, pre, sums, told, image, own, r0, r1, r2, d_z, sums_out):
    lanes = pl.ds(pl.multiple_of(place[0] * WIDE, WIDE), WIDE)
    rows = pre.shape[0]
    gain, shift = told_norm(told, WIDTH // 2)
    came = (r0[...].astype(F32) + r1[...].astype(F32) + r2[...].astype(F32)).astype(BF16)
    d_pooled = jnp.where(place[0] == SECTIONS - 1, own[...], came)
    spread = dot_tn(crop_rows(rows, images), d_pooled) * (1.0 / PLACES)
    xhats = [x for x, _ in normalized(pre[...], sums[...], micro, count)]
    z = join([x * gain + shift for x in xhats]) + image[:, lanes].astype(F32)
    value = spread * slope(z)
    d_z[...] = value
    parts = per_micro(value, micro)
    sums_out[...] = split_sums([v * x for v, x in zip(parts, xhats)], parts, micro)


def norm_back(value, pre, sums, back, gain, micro, count):
    out = []
    parts = per_micro(value, micro)
    for m, (xhat, rstd) in enumerate(normalized(pre, sums, micro, count)):
        by_x = back[m : m + 1] * (1.0 / count)
        plain = back[micro + m : micro + m + 1] * (1.0 / count)
        out.append(gain * rstd * (parts[m] - plain - xhat * by_x))
    return join(out)


def norm_back_kernel(micro, count, at, d_y, pre, sums, back, told, d_pre):
    gain, _ = told_norm(told, at)
    d_pre[...] = norm_back(d_y[...], pre[...], sums[...], back[...], gain, micro, count).astype(BF16)


def expand_back_kernel(micro, count, place, pre, sums, d_z, back, w0, w1, d_pre, q0, q1, q2, q3, full):
    half = WIDTH // 2
    gain, _ = told_norm(w0, half)
    d_low = norm_back(d_z[...], pre[...], sums[...], back[...], gain, micro, count).astype(BF16)
    d_pre[...] = d_low
    for j, w in enumerate((w0, w1)):
        full[:, pl.ds(pl.multiple_of(place[4 + j] * half, half), half)] = dot_nt(d_low, w[:half, :])
    for k, q in enumerate((q0, q1, q2, q3)):
        lanes = pl.ds(pl.multiple_of(place[k] * PART, PART), PART)
        q[...] = full[:, lanes].astype(BF16)


def finish_silu(micro, count, d_active, pre, sums, norm, d_y, sums_out):
    gain, shift = norm
    values, products = [], []
    parts = per_micro(d_active, micro)
    for m, (xhat, _) in enumerate(normalized(pre[...], sums[...], micro, count)):
        value = parts[m] * slope(xhat * gain + shift)
        values.append(value)
        products.append(value * xhat)
    d_y[...] = join(values)
    sums_out[...] = split_sums(products, values, micro)


def silu_back_kernel(micro, count, at, q0, q1, q2, q3, pre, sums, told, d_y, sums_out):
    total = (q0[...].astype(F32) + q1[...].astype(F32)) + (q2[...].astype(F32) + q3[...].astype(F32))
    d_active = total.astype(BF16).astype(F32)
    finish_silu(micro, count, d_active, pre, sums, told_norm(told, at), d_y, sums_out)


def conv_back_kernel(
    micro, images, count, at, place, d0, d1, d2, d3, back0, back1, pre, sums, told, d_full, d_y, sums_out, weight
):
    fill(place, (d0, d1, d2, d3), d_full)
    d_low = d_full[...]
    half = PART // 2
    for j, back in enumerate((back0, back1)):
        for k in range(SECTIONS):
            lanes = pl.ds(pl.multiple_of(place[k] * PART, PART), PART)
            for tap in range(9):
                rows = pl.ds(pl.multiple_of(tap * PART + place[4 + j] * half, half), half)
                weight[rows, lanes] = back[k, tap * half : (tap + 1) * half, :]
    total = None
    for first in range(0, 9, 2):
        taps = [tap for tap in (first, first + 1) if tap < 9]
        part = dot_nt(d_low, weight[first * PART : (taps[-1] + 1) * PART, :])
        for j, tap in enumerate(taps):
            moved = tap_shift(part[:, j * PART : (j + 1) * PART], images, tap, -1)
            total = moved if total is None else total + moved
    d_active = total.astype(BF16).astype(F32)
    finish_silu(micro, count, d_active, pre, sums, told_norm(told, at), d_y, sums_out)


def reduce_back_kernel(place, d_full, back0, back1, d_z, grad_in, weight):
    half = WIDE // 2
    first = 9 * PART // 2
    for j, back in enumerate((back0, back1)):
        rows = pl.ds(pl.multiple_of(place[4 + j] * half, half), half)
        for k in range(SECTIONS):
            lanes = pl.ds(pl.multiple_of(place[k] * PART, PART), PART)
            weight[rows, lanes] = back[k, first : first + half, :]
    main = dot_nt(d_full[...], weight[...]).astype(BF16).astype(F32)
    value = main + d_z[...].astype(BF16).astype(F32)
    grad_in[...] = value.reshape(grad_in.shape)


def back_parts_kernel(place, conv_a, conv_b, reduce0, reduce1, *outs):
    half = PART // 2
    wide = WIDE // 2
    first = 9 * half
    quarter = WIDTH // 4
    step = 9 * quarter + 16
    for k, out in enumerate(outs):
        u = place[k]
        high = u // 2
        low = u - 2 * high
        for j in range(4):
            conv = (conv_a, conv_b)[j // 2]

            @pl.when(u == quarter_of(place, j))
            def _():
                for tap in range(9):
                    at = pl.multiple_of((j % 2) * step + tap * quarter + place[4] * half, half)
                    out[tap * half : (tap + 1) * half, :] = conv[pl.ds(at, half), :]

        for j, reduce in enumerate((reduce0, reduce1)):

            @pl.when(high == place[4 + j])
            def _():
                at = pl.multiple_of(low * WIDE + place[4] * wide, wide)
                out[first : first + wide, :] = reduce[pl.ds(at, wide), :]


def stack_kernel(*refs):
    out = refs[-1]
    rows = refs[0].shape[0]
    for j, ref in enumerate(refs[:-1]):
        if len(out.shape) == 3:
            out[j] = ref[...]
        else:
            out[j * rows : (j + 1) * rows, :] = ref[...]


def mixed_kernel(place, reduce, expand, *outs):
    for k, out in enumerate(outs):
        out[...] = jnp.where(place[k + 1] == 0, reduce[...], expand[...])


def tell_kernel(micro, place, back2, back0, back1, notes, out):
    at = 0
    out[...] = jnp.zeros_like(out)
    for back in (back2, back0, back1):
        lanes = slice(at, at + back.shape[1])
        at += back.shape[1]
        for r in range(2):
            row = back[r * micro : r * micro + 1, :]
            for m in range(1, micro):
                row = row + back[r * micro + m : r * micro + m + 1, :]
            out[r : r + 1, lanes] = row
    loss = jnp.where(place[0] == SECTIONS - 1, notes[3:4, :PROJ], 0.0)
    out[2:3, :PROJ] = loss


def told_kernel(place, n0, n1, n2, n3, notes, out, loss):
    loss[...] = jnp.zeros_like(loss)
    loss[0:1, :] = (n0[2:3, :PROJ] + n1[2:3, :PROJ]) + (n2[2:3, :PROJ] + n3[2:3, :PROJ])
    t = place[0]
    out[...] = jnp.zeros_like(out)

    @pl.when(t == SECTIONS - 1)
    def _():
        out[...] = notes[:3, :]

    for k, note in enumerate((n0, n1, n2, n3)):
        u = place[k]

        @pl.when(t == 2)
        def _():
            out[:2, pl.ds(pl.multiple_of(u * WIDE, WIDE), WIDE)] = note[:2, :WIDE]

        for section in range(2):

            @pl.when(t == section)
            def _():
                lanes = slice(WIDE + section * PART, WIDE + (section + 1) * PART)
                out[:2, pl.ds(pl.multiple_of(u * PART, PART), PART)] = note[:2, lanes]


def pick_kernel(source, place, p0, p1, p2, p3, out):
    for j, p in enumerate((p0, p1, p2, p3)):

        @pl.when(place[0] == source ^ j)
        def _():
            out[...] = p[...]


def taps_kernel(images, active, out):
    value = active[...].astype(F32)
    for tap in range(9):
        out[:, tap * PART : (tap + 1) * PART] = tap_shift(value, images, tap, 1).astype(BF16)


def head(pooled, w_head, w_proj, protos, norm, queue, match, micro, images, dp):
    rows = pooled.shape[0]
    group = rows // micro
    half = group // CROPS
    scale_all = 1.0 / (TEMPER * CROPS * half * micro)
    pre = dot(pooled, w_head)

    def by_micro(v):
        return v.reshape(micro, group, v.shape[-1])

    pre_m = by_micro(pre)
    mean = jnp.mean(pre_m, axis=1, keepdims=True)
    square = jnp.mean(pre_m * pre_m, axis=1, keepdims=True)
    rstd = lax.rsqrt(square - mean * mean + NORM_EPS)
    xhat = (pre_m - mean) * rstd
    y = xhat * norm[0] + norm[1]
    active = (y * sigmoid(y)).astype(BF16).reshape(rows, D)
    embed = dot(active, w_proj) + norm[2, :PROJ]
    recip = lax.rsqrt(jnp.sum(embed * embed, axis=1, keepdims=True) + UNIT_EPS)
    unit = (embed * recip).astype(BF16)
    scores = dot_nt(unit, protos)
    valid = lax.broadcasted_iota(jnp.int32, (1, 4, QUARTER_PAD), 2).reshape(1, 4 * QUARTER_PAD) < QUARTER
    own_mass = jnp.where(valid, jnp.exp(scores / SINK_EPS), 0.0).reshape(micro, CROPS, half, -1)
    queue_mass = jnp.where(valid, jnp.exp(jnp.einsum("cqp,kp->cqk", queue, protos, preferred_element_type=F32) / SINK_EPS), 0.0)
    codes = []
    for m in range(micro):
        for c in range(CROPS):
            a, b = queue_mass[c], own_mass[m, c]
            column = jnp.sum(a, axis=0, keepdims=True) + jnp.sum(b, axis=0, keepdims=True)
            once = jnp.where(valid, 1.0 / column, 0.0)
            a, b = a * once, b * once
            scale = valid.astype(F32)
            for turn in range(2):
                ra = 1.0 / jnp.sum(a * scale, axis=1, keepdims=True)
                rb = 1.0 / jnp.sum(b * scale, axis=1, keepdims=True)
                column = jnp.sum(a * ra, axis=0, keepdims=True) + jnp.sum(b * rb, axis=0, keepdims=True)
                scale = jnp.where(valid, 1.0 / column, 0.0)
            b = b * scale
            codes.append(b / jnp.sum(b, axis=1, keepdims=True))
    targets = []
    for m in range(micro):
        targets.append(jnp.dot(match[m], codes[m * CROPS + 1], precision=HIGH))
        targets.append(jnp.dot(match[m].T, codes[m * CROPS], precision=HIGH))
    target = jnp.concatenate(targets)
    logits = jnp.where(valid, scores / TEMPER, -1e30)
    logp = jax.nn.log_softmax(logits, axis=1)
    loss = -jnp.sum(jnp.where(valid, target * logp, 0.0)) * (TEMPER * scale_all)
    d_scores = ((jnp.exp(logp) * jnp.sum(target, axis=1, keepdims=True) - target) * scale_all).astype(BF16)
    d_unit = dot(d_scores, protos)
    d_embed = (
        recip * d_unit - embed * (recip * recip * recip) * jnp.sum(d_unit * embed, axis=1, keepdims=True)
    ).astype(BF16)
    d_active = dot_nt(d_embed, w_proj)
    d_y = by_micro(d_active) * slope(y)
    by_x = jnp.sum(d_y * xhat, axis=1, keepdims=True)
    plain = jnp.sum(d_y, axis=1, keepdims=True)
    d_pre = (norm[0] * rstd * (d_y - plain / group - xhat * by_x / group)).astype(BF16).reshape(rows, D)
    bias = jnp.pad(jnp.sum(d_embed.astype(F32), axis=0), (0, D - PROJ))
    grads = jnp.stack([jnp.sum(by_x, axis=(0, 1)), jnp.sum(plain, axis=(0, 1)), bias])
    return loss, grads, active, unit, d_scores, d_embed, d_pre


def valid_lanes():
    lane = lax.broadcasted_iota(jnp.int32, (1, 4 * QUARTER_PAD), 1).astype(F32)
    block = jnp.floor((lane + 0.5) * (1.0 / QUARTER_PAD))
    return lane - block * QUARTER_PAD < QUARTER - 0.5


def mass_kernel(micro, images, offsets, told_offsets, place, table, *refs):
    mass, column, order, match = refs[-4:]
    ndp = len(offsets)
    valid = valid_lanes()
    size = mass.shape[1] // ndp
    half = images * ndp
    column[...] = jnp.zeros_like(column)
    at, said = 0, jnp.zeros((16, half), F32)
    row = lax.broadcasted_iota(jnp.int32, (PROJ, half), 0)
    lane = lax.broadcasted_iota(jnp.int32, (PROJ, half), 1)
    for ref in refs[:-4]:
        rows = CROPS * size + 16
        for j in range(ref.shape[0] // rows):
            for c in range(CROPS):
                own = ref[j * rows + c * size : j * rows + (c + 1) * size, :]
                scores = jnp.concatenate(
                    [dot_nt(own, table[:, a * PROJ : (a + 1) * PROJ]) for a in range(4)], axis=1
                )
                value = jnp.where(valid, jnp.exp(scores * (1.0 / SINK_EPS)), 0.0)
                mass[c, at * size : (at + 1) * size, :] = value.astype(BF16)
                column[c : c + 1, :] += jnp.sum(value, axis=0, keepdims=True)
            pairs = ref[(j + 1) * rows - 16 : (j + 1) * rows, :]
            first = (place[7] ^ told_offsets[at]) * images
            spot = ((row < images) & (lane == row + first)).astype(F32).astype(BF16)
            said = said + dot(pairs, spot)
            at += 1

    def over(value, by):
        return jnp.floor((value + 0.5) * (1.0 / by))

    row = lax.broadcasted_iota(jnp.int32, (half, half), 0).astype(F32)
    lane = lax.broadcasted_iota(jnp.int32, (half, half), 1).astype(F32)
    block = over(row, images)
    for m in range(micro):
        same = (jnp.abs(block - over(lane, images)) < 0.5) & (jnp.abs(row - block * images - said[m : m + 1, :]) < 0.5)
        match[m] = same.astype(F32)
    total = order.shape[0]
    per_dp = total // ndp
    row = lax.broadcasted_iota(jnp.int32, (total, total), 0).astype(F32)
    lane = lax.broadcasted_iota(jnp.int32, (total, total), 1).astype(F32)
    block = over(lane, per_dp)
    source = jnp.zeros((total, total), F32)
    for j, offset in enumerate(offsets):
        source = jnp.where(jnp.abs(block - j) < 0.5, (place[7] ^ offset).astype(F32), source)
    inner = lane - block * per_dp
    group = over(inner, images)
    position = (group * ndp + source) * images + (inner - group * images)
    order[...] = (jnp.abs(position - row) < 0.5).astype(F32).astype(BF16)


def tables_kernel(packed, proj, table, rows, buffer, sem):
    size = THIRD - FIRST + 2
    copy = pltpu.make_async_copy(packed.at[pl.ds(FIRST, size), :], rows, sem)
    copy.start()
    copy.wait()
    wide = SECOND - FIRST
    for a in range(4):
        buffer[pl.ds(a, wide, stride=4), :] = rows[:wide, a * PROJ : (a + 1) * PROJ].astype(F32)
    proj[...] = buffer[...].astype(BF16)
    row = lax.broadcasted_iota(jnp.int32, (size - wide, WIDTH), 0)
    kept = jnp.where(row < QUARTER, rows[wide:, :].astype(F32), 0.0).astype(BF16)
    table[: size - wide, :] = kept
    table[size - wide :, :] = jnp.zeros((QUARTER_PAD - (size - wide), WIDTH), BF16)


def head_kernel(
    micro, images, ndp, pooled, pooled_b, order, w_head, w_proj, table, norm, mass, column, match,
    d0, d1, d2, d3, notes, all_pooled, active, unit, d_scores, d_embed, d_pre,
    scores, xhat_s, y_s, rstd_s, own_mass, target, total,
):
    rows = order.shape[0]
    group = rows // micro
    half = group // CROPS
    own = rows // ndp
    queued = mass.shape[1]
    scale_all = 1.0 / (TEMPER * CROPS * half * micro)
    chunk = WIDTH
    part = rows // 2
    low = (dot(order[:, :part], pooled[...]) + dot(order[:, part:], pooled_b[...])).astype(BF16)
    all_pooled[...] = low
    for b in range(D // chunk):
        lanes = slice(b * chunk, (b + 1) * chunk)
        pre = dot(low, w_head[:, lanes])
        for m in range(micro):
            at = slice(m * group, (m + 1) * group)
            v = pre[at]
            mean = jnp.sum(v, axis=0, keepdims=True) * (1.0 / group)
            square = jnp.sum(v * v, axis=0, keepdims=True) * (1.0 / group)
            rstd = lax.rsqrt(square - mean * mean + NORM_EPS)
            xhat = (v - mean) * rstd
            y = xhat * norm[0:1, lanes] + norm[1:2, lanes]
            rstd_s[m : m + 1, lanes] = rstd
            xhat_s[at, lanes] = xhat
            y_s[at, lanes] = y
            active[at, lanes] = (y * sigmoid(y)).astype(BF16)
    embed = dot(active[...], w_proj[...]) + norm[2:3, :PROJ]
    recip = lax.rsqrt(jnp.sum(embed * embed, axis=1, keepdims=True) + UNIT_EPS)
    unit_v = (embed * recip).astype(BF16)
    unit[...] = unit_v
    valid = valid_lanes()
    for a in range(4):
        lanes = slice(a * QUARTER_PAD, (a + 1) * QUARTER_PAD)
        scores[:, lanes] = dot_nt(unit_v, table[:, a * PROJ : (a + 1) * PROJ])
    own_mass[...] = jnp.where(valid, jnp.exp(scores[...] * (1.0 / SINK_EPS)), 0.0)

    step = 32
    for c in range(CROPS):
        starts = [(m * CROPS + c) * half for m in range(micro)]
        once, scale = [], []
        for m in range(micro):
            at = slice(starts[m], starts[m] + half)
            sums = column[c : c + 1, :] + jnp.sum(own_mass[at, :], axis=0, keepdims=True)
            once.append(jnp.where(valid, 1.0 / sums, 0.0))
            own_mass[at, :] = own_mass[at, :] * once[m]
            scale.append(None)
        for turn in range(2):
            for m in range(micro):
                at = slice(starts[m], starts[m] + half)
                a = own_mass[at, :]
                if turn:
                    a = a * scale[m]
                a = a * (1.0 / jnp.sum(a, axis=1, keepdims=True))
                total[m] = jnp.sum(a.reshape(half // 8, 8, a.shape[1]), axis=0)

            def block(i, carry):
                e = mass[c, pl.ds(pl.multiple_of(i * step, step), step), :].astype(F32)
                for m in range(micro):
                    a = e * once[m]
                    if turn:
                        a = a * scale[m]
                    a = a * (1.0 / jnp.sum(a, axis=1, keepdims=True))
                    total[m] += jnp.sum(a.reshape(step // 8, 8, a.shape[1]), axis=0)
                return carry

            lax.fori_loop(0, queued // step, block, 0)
            for m in range(micro):
                more = jnp.where(valid, 1.0 / jnp.sum(total[m], axis=0, keepdims=True), 0.0)
                scale[m] = more if turn == 0 else scale[m] * more
        for m in range(micro):
            at = slice(starts[m], starts[m] + half)
            a = own_mass[at, :] * scale[m]
            own_mass[at, :] = a * (1.0 / jnp.sum(a, axis=1, keepdims=True))
    for m in range(micro):
        zero, one = (slice((m * CROPS + c) * half, (m * CROPS + c + 1) * half) for c in range(CROPS))
        target[zero, :] = lax.dot_general(match[m], own_mass[one, :], TN, precision=HIGH, preferred_element_type=F32)
        target[one, :] = jnp.dot(match[m], own_mass[zero, :], precision=HIGH, preferred_element_type=F32)
    logits = jnp.where(valid, scores[...] * (1.0 / TEMPER), -1e30)
    logits = logits - jnp.max(logits, axis=1, keepdims=True)
    power = jnp.exp(logits)
    summed = jnp.sum(power, axis=1, keepdims=True)
    goal = target[...]
    loss = jnp.sum(goal * (logits - jnp.log(summed)), axis=1, keepdims=True)
    loss = jnp.sum(loss, axis=0, keepdims=True) * (-TEMPER * scale_all)
    weight = jnp.sum(goal, axis=1, keepdims=True) / summed
    d_scores[...] = ((power * weight - goal) * scale_all).astype(BF16)
    d_unit = None
    for a in range(4):
        more = dot(d_scores[:, a * QUARTER_PAD : (a + 1) * QUARTER_PAD], table[:, a * PROJ : (a + 1) * PROJ])
        d_unit = more if d_unit is None else d_unit + more
    along = jnp.sum(d_unit * embed, axis=1, keepdims=True)
    d_low = (recip * d_unit - embed * (recip * recip * recip) * along).astype(BF16)
    d_embed[...] = d_low
    notes[...] = jnp.zeros_like(notes)
    notes[2:3, :PROJ] = jnp.sum(d_low.astype(F32), axis=0, keepdims=True)
    notes[3:4, :] = jnp.broadcast_to(loss, (1, D))
    for b in range(D // chunk):
        lanes = slice(b * chunk, (b + 1) * chunk)
        d_active = dot_nt(d_low, w_proj[lanes, :])
        for m in range(micro):
            at = slice(m * group, (m + 1) * group)
            d_y = d_active[at] * slope(y_s[at, lanes])
            xhat = xhat_s[at, lanes]
            by_x = jnp.sum(d_y * xhat, axis=0, keepdims=True)
            plain = jnp.sum(d_y, axis=0, keepdims=True)
            notes[0:1, lanes] += by_x
            notes[1:2, lanes] += plain
            value = d_y - plain * (1.0 / group) - xhat * (by_x * (1.0 / group))
            d_pre[at, lanes] = (norm[0:1, lanes] * rstd_s[m : m + 1, lanes] * value).astype(BF16)
    mine = dot_tn(order[:, :own], d_pre[...]).astype(BF16)
    for j, out in enumerate((d0, d1, d2, d3)):
        out[...] = dot_nt(mine, w_head[j * WIDE : (j + 1) * WIDE, :]).astype(BF16)


def interleave(width):
    row = lax.broadcasted_iota(jnp.int32, (4 * width, 4 * width), 0)
    column = lax.broadcasted_iota(jnp.int32, (4 * width, 4 * width), 1)
    return (column == 4 * (row & (width - 1)) + (row >> (width.bit_length() - 1))).astype(F32).astype(BF16)


def own_columns(place, own):
    row = lax.broadcasted_iota(jnp.int32, (WIDTH, own), 0)
    lane = lax.broadcasted_iota(jnp.int32, (WIDTH, own), 1)
    return (row == lane + place[7] * own).astype(F32).astype(BF16)


def head_grads_kernel(place, pooled, active, unit, d_scores, d_embed, d_pre, out):
    @pl.when(place[0] != SECTIONS - 1)
    def _():
        out[...] = jnp.zeros_like(out)

    @pl.when(place[0] == SECTIONS - 1)
    def _():
        own = out.shape[0]
        choose = own_columns(place, own)
        weave = interleave(PART)
        block = PART
        parts = []
        for q in range(4):
            own_d = dot(d_pre[:, q * WIDTH : (q + 1) * WIDTH], choose).astype(BF16)
            parts.append(dot_tn(own_d, pooled[...]).astype(BF16))
        for b in range(D // block):
            mixed = jnp.concatenate([p[:, b * block : (b + 1) * block] for p in parts], axis=1)
            out[:, 4 * block * b : 4 * block * (b + 1)] = dot(mixed, weave)
        proj = jnp.zeros((own, WIDTH), F32)
        proto = jnp.zeros((own, QUARTER_PAD), F32)
        apart = []
        for b in range(4):
            apart.append(dot_nt(active[:, b * WIDTH : (b + 1) * WIDTH], weave).astype(BF16))
        for a in range(4):
            some = choose[a * PROJ : (a + 1) * PROJ, :]
            own_e = dot(d_embed[...], some).astype(BF16)
            own_u = dot(unit[...], some).astype(BF16)
            column = jnp.concatenate([v[:, a * block : (a + 1) * block] for v in apart], axis=1)
            proj = proj + dot_tn(own_e, column)
            proto = proto + dot_tn(own_u, d_scores[:, a * QUARTER_PAD : (a + 1) * QUARTER_PAD])
        out[:, FIRST:SECOND] = proj
        out[:, SECOND:] = proto[:, : out.shape[1] - SECOND]


def finish_kernel(place, base, reduce, expand, m1, m2, m3, conv, c1, c2, c3, out, buffer, sem):
    mixed = (None, m1, m2, m3)
    t = place[0]

    def write(lanes):
        copy = pltpu.make_async_copy(buffer.at[:, pl.ds(0, lanes)], out.at[:, pl.ds(0, lanes)], sem)
        copy.start()
        copy.wait()

    @pl.when(t == 0)
    def _():
        for u in range(SECTIONS):
            piece = reduce if u == 0 else mixed[u]
            buffer[:, u * WIDE : (u + 1) * WIDE] = piece[...].astype(F32)
        write(D)

    @pl.when(t == 1)
    def _():
        for u in range(SECTIONS):
            piece = (conv, c1, c2, c3)[u ^ 1]
            for tap in range(9):
                at = tap * WIDTH + u * PART
                buffer[:, at : at + PART] = piece[:, tap * PART : (tap + 1) * PART].astype(F32)
        write(9 * WIDTH)

    @pl.when(t == 2)
    def _():
        four = [expand if u == 2 else mixed[u ^ 2] for u in range(SECTIONS)]
        weave = interleave(PART)
        for b in range(WIDTH // PART):
            lanes = slice(b * PART, (b + 1) * PART)
            row = jnp.concatenate([f[:, lanes] for f in four], axis=1)
            buffer[:, 4 * b * PART : 4 * (b + 1) * PART] = dot(row, weave)
        write(D)


def unpack_kernel(packed, out, buffer):
    rows = packed.shape[0]
    for b in range(4):
        buffer[b] = packed[:, b * PART : (b + 1) * PART].astype(F32)
    for q in range(4):
        for b in range(4):
            at = q * WIDTH + b * PART
            out[:, at : at + PART] = buffer[b, pl.ds(q, rows // 4, stride=4), :].astype(BF16)


def unpack(packed, rows):
    step = 1024
    return pl.pallas_call(
        unpack_kernel,
        out_shape=shape((rows // 4, 4 * WIDTH), BF16),
        grid=(rows // step,),
        in_specs=[pl.BlockSpec((step, WIDTH), lambda i: (i, 0))],
        out_specs=pl.BlockSpec((step // 4, 4 * WIDTH), lambda i: (i, 0)),
        scratch_shapes=[pltpu.VMEM((4, step, PART), F32)],
        compiler_params=pltpu.CompilerParams(vmem_limit_bytes=16 * 2**20),
        cost_estimate=cost(4),
    )(packed)


def pack_kernel(parts, lanes_of, place, source, norm, *refs):
    outs, sem = refs[:-1], refs[-1]
    copies = []
    for j, out in enumerate(outs):
        lane, lanes = lanes_of[j]
        for row, rows, at in parts(place):
            ref = source.at[pl.ds(row, rows), pl.ds(lane, lanes)]
            copies.append(pltpu.make_async_copy(ref, out.at[pl.ds(at, rows), :], sem.at[len(copies)]))
    for copy in copies:
        copy.start()
    for j, out in enumerate(outs):
        lane, lanes = lanes_of[j]
        out[out.shape[0] - 16 :, :] = tell_norm(norm[:, lane : lane + lanes])
    for copy in copies:
        copy.wait()


def pack(place, source, norm, parts, lanes_of, rows):
    count = len(parts([0] * 9))
    return pl.pallas_call(
        functools.partial(pack_kernel, parts, lanes_of),
        out_shape=[shape((rows + 16, lanes), BF16) for _, lanes in lanes_of],
        in_specs=[
            pl.BlockSpec(memory_space=pltpu.SMEM),
            pl.BlockSpec(memory_space=pltpu.HBM),
            pl.BlockSpec(memory_space=pltpu.VMEM),
        ],
        out_specs=[pl.BlockSpec(memory_space=pltpu.VMEM)] * len(lanes_of),
        scratch_shapes=[pltpu.SemaphoreType.DMA((count * len(lanes_of),))],
        compiler_params=pltpu.CompilerParams(vmem_limit_bytes=12 * 2**20),
        cost_estimate=cost(1.5),
    )(place, hbm(source), norm)


def multiple(value, step):
    return value if isinstance(value, int) else pl.multiple_of(value, step)


def pair_kernel(place, a, b, keep, out, full):
    full[...] = dot_tn(a[...], b[...])
    own = keep.shape[1]
    for z in range(keep.shape[0]):
        mine = (2 * z + place[4]) * own
        other = (2 * z + place[5]) * own
        keep[z] = full[pl.ds(pl.multiple_of(mine, own), own), :]
        out[z] = full[pl.ds(pl.multiple_of(other, own), own), :].astype(BF16)


def image_pair_kernel(place, d0, d1, d2, d3, image, keep, out, d_full, full):
    fill(place, (d0, d1, d2, d3), d_full)
    lanes = pl.ds(pl.multiple_of(place[0] * WIDE, WIDE), WIDE)
    pair_kernel(place, d_full, image.at[:, lanes], keep, out, full)


def cross_kernel(place, keep, came, own, o1, o2, o3):
    for k, o in enumerate((own, o1, o2, o3)):
        z = place[6] ^ k
        o[...] = (keep[z] + came[z].astype(F32)).astype(o.dtype)


def add_kernel(own, r1, r2, r3, out):
    out[...] = ((own[...] + r1[...].astype(F32)) + (r2[...].astype(F32) + r3[...].astype(F32))).astype(BF16)


def after(value, *others):
    return lax.optimization_barrier((value, *others))[0]


def body(image, section_weights, section_norms, queue, pairing):
    micro, images = image.shape[0], image.shape[2]
    ndp = lax.axis_size("dp")
    t = lax.axis_index("section")
    dp = lax.axis_index("dp")
    core = dp % 2
    place = jnp.stack([t ^ k for k in range(SECTIONS)] + [core, 1 - core, dp // 2, dp, dp % 4]).astype(jnp.int32)
    cells = CROPS * PLACES * images
    rows = micro * cells
    count = float(cells * ndp)
    packed = section_weights[0]
    norm3 = section_norms[0]
    param_rows = packed.shape[0]
    own = WIDTH // ndp
    k = functools.partial

    def pieces_of(width, dtype):
        return shape((rows, width), dtype)

    def from_section(pieces, source):
        return [pieces[0]] + [lax.ppermute(pieces[j], "section", [(source, source ^ j)]) for j in range(1, SECTIONS)]

    def both_halves(came, source, us):
        half = call(k(pick_kernel, source), shape(came[0].shape, BF16), place, *came, us=us)
        return half, flip(half, "dp", 1)

    half = D // 2
    reduce_came = from_section(
        pack(
            place, packed, norm3,
            lambda p: [(multiple(p[4] * half, half), half, 0)],
            [(j * PART, PART) for j in range(SECTIONS)],
            half,
        ),
        0,
    )
    quarter = WIDTH // 4
    conv_rows = 9 * quarter
    conv_own = pack(
        place, after(packed, *reduce_came[:1]), norm3,
        lambda p: [(multiple(tap * WIDTH + p[8] * quarter, quarter), quarter, tap * quarter) for tap in range(9)],
        [((1 ^ j) * PART, PART) for j in range(SECTIONS)],
        conv_rows,
    )
    conv_came = from_section(conv_own, 1)
    flat = call(
        retile_kernel, shape((rows, D), BF16),
        image.transpose(0, 1, 3, 4, 2, 5).reshape(rows // images, images, D),
        us=2,
    )

    queue_size = CROPS * queue.shape[1]
    note = call(note_kernel, shape((queue_size + 16, PROJ), BF16), pairing, queue, us=0.5)
    told, told_offsets = gather_dp(note, dp_stages())
    reduce_came = lax.optimization_barrier((*reduce_came, flat, *told))[:4]

    w_reduce = both_halves(reduce_came, 0, 0.5)
    sums_of = shape((8, PART), F32)
    pre0, part = call(k(reduce_kernel, micro), (pieces_of(PART, F32), sums_of), place, flat, *w_reduce, us=2)
    sums0 = sum_dp(part)
    active0 = call(
        k(active_kernel, micro, count, half), pieces_of(PART, BF16), pre0, sums0, w_reduce[0], us=1
    )
    actives0 = gather_xor(active0, "section")

    conv_came = lax.optimization_barrier((*conv_came, active0))[:4]
    conv_part = call(k(pick_kernel, 1), shape(conv_came[0].shape, BF16), place, *conv_came, us=0.6)
    conv_part = rows_of([conv_part, flip(conv_part, "dp", 2)])
    w_conv = (conv_part, flip(conv_part, "dp", 1))
    natural = unpack(after(packed, active0), FIRST)
    half_expand = WIDTH // 2
    expand_own = pack(
        place, natural, norm3,
        lambda p: [(multiple(p[4] * half_expand, half_expand), half_expand, 0)],
        [((2 ^ j) * WIDE, WIDE) for j in range(SECTIONS)],
        half_expand,
    )
    *actives0, expand_own0 = lax.optimization_barrier((*actives0, expand_own[0]))
    pre1, part = call(
        k(conv_kernel, micro, images),
        (pieces_of(PART, F32), sums_of),
        place, *actives0, *w_conv,
        scratch=[pltpu.VMEM((rows, WIDTH), BF16), pltpu.VMEM((WIDTH, 9 * PART), BF16)],
        us=3,
    )
    expand_own = lax.optimization_barrier((expand_own0, *expand_own[1:], part))[:4]
    expand_came = from_section(expand_own, 2)
    sums1 = sum_dp(part)
    active1_own = call(
        k(active_kernel, micro, count, conv_rows), pieces_of(PART, BF16), pre1, sums1, w_conv[0], us=1
    )
    actives1 = gather_xor(active1_own, "section")

    w_expand = both_halves(expand_came, 2, 0.5)
    w_proj, table = pl.pallas_call(
        tables_kernel,
        out_shape=(shape((D, PROJ), BF16), shape((QUARTER_PAD, WIDTH), BF16)),
        in_specs=[pl.BlockSpec(memory_space=pltpu.HBM)],
        out_specs=(pl.BlockSpec(memory_space=pltpu.VMEM), pl.BlockSpec(memory_space=pltpu.VMEM)),
        scratch_shapes=[
            pltpu.VMEM((THIRD - FIRST + 2, WIDTH), BF16), pltpu.VMEM((D, PROJ), F32), pltpu.SemaphoreType.DMA,
        ],
        compiler_params=pltpu.CompilerParams(vmem_limit_bytes=12 * 2**20),
        cost_estimate=cost(1.5),
    )(hbm(after(packed, active1_own)))
    head_rows = rows // PLACES * ndp
    lanes = 4 * QUARTER_PAD
    stages = dp_stages()
    head_stages = stages[1:] + stages[:1]
    offsets = [0]
    for steps in head_stages:
        offsets = offsets + [o ^ step for step in steps for o in offsets]
    small = head_rows <= 128 and images * ndp == 32 and queue.shape[1] * ndp <= 512
    if small:
        mass, column, order, match = call(
            k(mass_kernel, micro, images, offsets, sum(told_offsets, [])),
            (
                shape((CROPS, ndp * queue.shape[1], lanes), BF16), shape((8, lanes), F32),
                shape((head_rows, head_rows), BF16), shape((micro, images * ndp, images * ndp), F32),
            ),
            place, table, *told,
            vmem=16, us=5,
        )
        actives1 = lax.optimization_barrier((*actives1, mass))[:4]
    active1, pre2, part = call(
        k(expand_kernel, micro),
        (pieces_of(WIDTH, BF16), pieces_of(WIDE, F32), shape((8, WIDE), F32)),
        place, *actives1, *w_expand,
        us=2,
    )
    back_rows = 9 * PART // 2 + WIDE // 2
    back_own = call(
        back_parts_kernel, [shape((back_rows, PART), BF16)] * 4, place, *w_conv, *w_reduce, us=1
    )
    back_own = lax.optimization_barrier((*back_own, part))[:4]
    back_came = [back_own[0]] + [flip(back_own[j], "section", j) for j in range(1, SECTIONS)]

    sums2 = sum_dp(part)
    pooled = call(
        k(pool_kernel, micro, images, count),
        shape((rows // PLACES, WIDE), BF16),
        place, pre2, sums2, w_expand[0], flat,
        us=1.6,
    )

    per_dp = rows // PLACES
    came_p = [send(pooled, j, 3) for j in range(3)]
    pooled_here = call(lanes_kernel, shape((per_dp, D), BF16), *came_p, pooled, us=0.3)
    parts, _ = gather_dp(pooled_here, head_stages)
    if small:
        *d_pooled, notes3, all_pooled, active3, unit, d_scores, d_embed, d_pre3 = call(
            k(head_kernel, micro, images, ndp),
            [shape((per_dp, WIDE), BF16)] * 4
            + [
                shape((8, D), F32), shape((head_rows, D), BF16), shape((head_rows, D), BF16),
                shape((head_rows, PROJ), BF16), shape((head_rows, lanes), BF16), shape((head_rows, PROJ), BF16),
                shape((head_rows, D), BF16),
            ],
            *parts, order, natural, w_proj, table, norm3, mass, column, match,
            scratch=[
                pltpu.VMEM((head_rows, lanes), F32), pltpu.VMEM((head_rows, D), F32), pltpu.VMEM((head_rows, D), F32),
                pltpu.VMEM((8, D), F32), pltpu.VMEM((head_rows, lanes), F32), pltpu.VMEM((head_rows, lanes), F32),
                pltpu.VMEM((micro, 8, lanes), F32),
            ],
            vmem=30, us=22,
        )
    else:
        all_pooled = jnp.concatenate(parts)
        offset = jnp.array(offsets, jnp.int32)
        head_order = jnp.arange(head_rows, dtype=jnp.int32)
        block, inner = head_order // per_dp, head_order % per_dp
        group, single = inner // images, inner % images
        position = (group * ndp + (offset[block] ^ dp)) * images + single
        order = (position[None, :] == head_order[:, None]).astype(BF16)
        told = jnp.concatenate(told).reshape(ndp, queue_size + 16, PROJ)
        pairs = told[:, queue_size : queue_size + micro, :images].astype(jnp.int32)
        told_offset = jnp.array(sum(told_offsets, []), jnp.int32)
        pairs_dp = (told_offset ^ dp)[None, :] == jnp.arange(ndp, dtype=jnp.int32)[:, None]
        pairs = jnp.sum(jnp.where(pairs_dp[:, :, None, None], pairs[None], 0), axis=1)
        left = jnp.arange(images * ndp, dtype=jnp.int32)
        pairs = pairs.transpose(1, 0, 2).reshape(micro, ndp * images)
        match = ((left // images * images + pairs)[:, :, None] == left[None, None, :]).astype(F32)
        all_pooled = dot(order, all_pooled).astype(BF16)
        protos = jnp.concatenate([table[:, a * PROJ : (a + 1) * PROJ] for a in range(4)], axis=0)
        queue_all = told[:, :queue_size].reshape(ndp, CROPS, queue.shape[1], PROJ)
        queue_rows = queue_all.transpose(1, 0, 2, 3).reshape(CROPS, -1, PROJ)
        loss, grads3, active3, unit, d_scores, d_embed, d_pre3 = head(
            all_pooled, natural, w_proj, protos, norm3, queue_rows, match, micro, images, dp
        )
        notes3 = jnp.concatenate([grads3, jnp.full((5, D), loss)])
        d_pooled = dot_nt(dot_tn(order[:, :per_dp], d_pre3).astype(BF16), natural).astype(BF16)
        d_pooled = [d_pooled[:, j * WIDE : (j + 1) * WIDE] for j in range(SECTIONS)]

    came_d = [send(d_pooled[j], 3, j) for j in range(3)]
    back_half = call(stack_kernel, shape((SECTIONS, back_rows, PART), BF16), *back_came, us=0.6)
    back_halves = (back_half, flip(back_half, "dp", 1))
    d_z, part = call(
        k(out_back_kernel, micro, images, count),
        (pieces_of(WIDE, F32), shape((8, WIDE), F32)),
        place, pre2, sums2, w_expand[0], flat, d_pooled[3], *came_d,
        us=1.8,
    )
    back2 = sum_dp(part)
    d_pre2, *partial = call(
        k(expand_back_kernel, micro, count),
        [pieces_of(WIDE, BF16)] + [pieces_of(PART, BF16)] * 4,
        place, pre2, sums2, d_z, back2, *w_expand,
        scratch=[pltpu.VMEM((rows, WIDTH), F32)],
        us=2,
    )
    partial = [partial[0]] + [flip(partial[j], "section", j) for j in range(1, SECTIONS)]

    def scatter_start(a, b, width):
        if ndp != 8:
            return dot_tn(a, b)
        keep, out = call(
            pair_kernel,
            (shape((4, own, width), F32), shape((4, own, width), BF16)),
            place, a, b,
            scratch=[pltpu.VMEM((WIDTH, width), F32)],
            us=2.5,
        )
        return keep, flip(out, "dp", 1)

    def scatter_cross(started, *others):
        if ndp != 8:
            return [lax.psum_scatter(started.astype(BF16), "dp", scatter_dimension=0, tiled=True)]
        keep, came = started
        if others:
            keep = after(keep, *others)
        dims = keep.shape[1:]
        kept, *out = call(
            cross_kernel, [shape(dims, F32)] + [shape(dims, BF16)] * 3, place, keep, came
        )
        return [kept] + [flip(out[j], "dp", 2 * (j + 1)) for j in range(3)]

    def scatter_finish(crossed):
        if ndp != 8:
            return crossed[0]
        return call(add_kernel, shape(crossed[0].shape, BF16), *crossed, us=0.6)

    expand_started = scatter_start(d_pre2, active1, WIDTH)
    base = call(
        head_grads_kernel,
        shape((own, param_rows), F32),
        place, after(all_pooled, d_pre2), active3, unit, d_scores, d_embed, d_pre3,
        us=6,
    )
    partial = lax.optimization_barrier((*partial, base))[:4]

    d_y1, part = call(
        k(silu_back_kernel, micro, count, conv_rows),
        (pieces_of(PART, F32), sums_of),
        *partial, pre1, sums1, w_conv[0],
    )
    back1 = sum_dp(part)
    d_pre1_own = call(
        k(norm_back_kernel, micro, count, conv_rows), pieces_of(PART, BF16), d_y1, pre1, sums1, back1, w_conv[0]
    )
    d_pre1s = gather_xor(d_pre1_own, "section")
    expand_crossed = scatter_cross(expand_started, d_pre1_own)
    taps = call(k(taps_kernel, images), pieces_of(9 * PART, BF16), after(active0, d_pre1_own), us=1.3)
    *d_pre1s, taps = lax.optimization_barrier((*d_pre1s, taps))
    d_pre1, d_y0, part = call(
        k(conv_back_kernel, micro, images, count, half),
        (pieces_of(WIDTH, BF16), pieces_of(PART, F32), sums_of),
        place, *d_pre1s, *back_halves, pre0, sums0, w_reduce[0],
        scratch=[pltpu.VMEM((9 * PART, WIDTH), BF16)],
        us=3.5,
    )
    back0 = sum_dp(part)
    conv_started = scatter_start(after(d_pre1, part), taps, 9 * PART)
    d_pre0_own = call(
        k(norm_back_kernel, micro, count, half), pieces_of(PART, BF16), d_y0, pre0, sums0, back0, w_reduce[0]
    )
    d_pre0s = gather_xor(d_pre0_own, "section")
    g_expand = scatter_finish(expand_crossed)
    conv_crossed = scatter_cross(conv_started, d_pre0_own)

    note = call(
        k(tell_kernel, micro), shape((8, WIDE + 2 * PART), F32), place, back2, back0, back1, notes3, us=0.5
    )
    notes = gather_xor(note, "section")
    *d_pre0s, conv_crossed[0] = lax.optimization_barrier((*d_pre0s, *conv_crossed))[:5]

    if ndp == 8:
        keep, out, d_pre0 = call(
            image_pair_kernel,
            (shape((4, own, WIDE), F32), shape((4, own, WIDE), BF16), pieces_of(WIDTH, BF16)),
            place, *d_pre0s, flat,
            scratch=[pltpu.VMEM((WIDTH, WIDE), F32)],
            us=2.5,
        )
        reduce_started = keep, flip(out, "dp", 1)
    else:
        d_pre0 = jnp.stack(d_pre0s)[place[:SECTIONS]].transpose(1, 0, 2).reshape(rows, WIDTH)
        reduce_started = dot_tn(d_pre0, lax.dynamic_slice_in_dim(flat, t * WIDE, WIDE, 1))
    reduce_crossed = scatter_cross(reduce_started)
    grad_in = call(
        reduce_back_kernel,
        shape((rows // images, images, WIDE), F32),
        place, d_pre0, *back_halves, d_z,
        scratch=[pltpu.VMEM((WIDE, WIDTH), BF16)],
        us=2,
    )
    g_conv = scatter_finish(conv_crossed)
    conv_here = [g_conv] + [send(g_conv, 1 ^ j, 1) for j in range(1, SECTIONS)]
    norm_grads, loss = call(
        told_kernel, (shape((3, D), F32), shape((8, PROJ), F32)), place, *notes, notes3, us=0.5
    )
    reduce_crossed = lax.optimization_barrier((*reduce_crossed, grad_in, norm_grads))[:len(reduce_crossed)]
    g_reduce = scatter_finish(reduce_crossed)
    mixed = call(mixed_kernel, [shape(g_reduce.shape, BF16)] * 3, place, g_reduce, g_expand, us=0.3)
    mixed = [lax.ppermute(mixed[j - 1], "section", [(j, 0), (2 ^ j, 2)]) for j in range(1, SECTIONS)]
    weight_grads = pl.pallas_call(
        finish_kernel,
        out_shape=shape((own, param_rows), F32),
        in_specs=[pl.BlockSpec(memory_space=pltpu.SMEM), pl.BlockSpec(memory_space=pltpu.HBM)]
        + [pl.BlockSpec(memory_space=pltpu.VMEM)] * 9,
        out_specs=pl.BlockSpec(memory_space=pltpu.HBM),
        scratch_shapes=[pltpu.VMEM((own, 9 * WIDTH), F32), pltpu.SemaphoreType.DMA],
        input_output_aliases={1: 0},
        compiler_params=pltpu.CompilerParams(vmem_limit_bytes=12 * 2**20),
        cost_estimate=cost(2),
    )(place, base, g_reduce, g_expand, *mixed, *conv_here)
    grad_in = grad_in.reshape(micro, CROPS, SIDE, SIDE, images, WIDE).transpose(0, 1, 4, 2, 3, 5)
    return (loss[0, 0], grad_in, weight_grads.T[None], norm_grads[None])


def solution(mesh):
    in_specs = (
        P(None, None, "dp", None, None, None),
        P("section", None, None),
        P("section", None, None),
        P(None, "dp", None),
        P(None, "dp"),
    )
    out_specs = (
        P(),
        P(None, None, "dp", None, None, "section"),
        P("section", None, "dp"),
        P("section", None, None),
    )
    return jax.shard_map(body, mesh=mesh, in_specs=in_specs, out_specs=out_specs, check_vma=False)
```

```python
import functools

import jax
import jax.numpy as jnp
from jax import lax
from jax.experimental import pallas as pl
from jax.experimental.pallas import tpu as pltpu
from jax.sharding import PartitionSpec as P

D = 2048
WIDTH = 512
PROJ = 128
PROTOS = 3000
SIDE = 7
CROPS = 2
SECTIONS = 4
PART = WIDTH // SECTIONS
WIDE = D // SECTIONS
QUARTER = PROTOS // 4
QUARTER_PAD = 768
PLACES = SIDE * SIDE
FIRST = D * (D // WIDTH)
SECOND = FIRST + D * PROJ // WIDTH
THIRD = SECOND + PROTOS * PROJ // WIDTH
HALF_REDUCE = 16 + D // 2
HALF_EXPAND = 16 + WIDTH // 2
QUARTER_CONV = 16 + 9 * WIDTH // 4
NOTE_ROWS = 48

NORM_EPS = 1e-05
UNIT_EPS = 1e-06
SINK_EPS = 0.05
TEMPER = 0.1
HIGH = lax.Precision.HIGHEST
F32 = jnp.float32
BF16 = jnp.bfloat16
NT = (((1,), (1,)), ((), ()))
TN = (((0,), (0,)), ((), ()))


def dot(a, b):
    return jnp.dot(a, b, preferred_element_type=F32)


def dot_nt(a, b):
    return lax.dot_general(a, b, NT, preferred_element_type=F32)


def dot_tn(a, b):
    return lax.dot_general(a, b, TN, preferred_element_type=F32)


def flip(value, axis, step):
    count = lax.axis_size(axis)
    return lax.ppermute(value, axis, [(source, source ^ step) for source in range(count)])


def send(value, source, target):
    return lax.ppermute(value, "section", [(source, target)])


def sum_dp_steps(value):
    count = lax.axis_size("dp")
    value = pair = value + flip(value, "dp", 1)
    step = 2
    while step < count:
        if 2 * step < count:
            near = value + flip(value, "dp", step)
            far = flip(value, "dp", 2 * step) + flip(value, "dp", 3 * step)
            value = near + far
            step *= 4
        else:
            value = value + flip(value, "dp", step)
            step *= 2
    return value, pair


def sum_dp(value):
    return sum_dp_steps(value)[0]


def gather_xor(value, axis):
    return [value] + [flip(value, axis, step) for step in range(1, lax.axis_size(axis))]


def dp_stages():
    count = lax.axis_size("dp")
    stages, step = [(1,)], 2
    while step < count:
        if 2 * step < count:
            stages.append((step, 2 * step, 3 * step))
            step *= 4
        else:
            stages.append((step,))
            step *= 2
    return stages


def gather_dp(value, stages):
    arrays, offsets = [value], [[0]]
    for steps in stages:
        if len(arrays) > 1:
            arrays, offsets = [rows_of(arrays)], [sum(offsets, [])]
        first = offsets[0]
        for step in steps:
            arrays.append(flip(arrays[0], "dp", step))
            offsets.append([o ^ step for o in first])
    return arrays, offsets


def sigmoid(v):
    return 1.0 / (1.0 + jnp.exp(-v))


def slope(v):
    s = sigmoid(v)
    return s * (1.0 + v * (1.0 - s))


def cost(us):
    return pl.CostEstimate(flops=0, bytes_accessed=int(us * 3_000_000), transcendentals=0)


def hbm(value):
    return pltpu.with_memory_space_constraint(value, pltpu.HBM)


def call(kernel, out, *args, scratch=(), vmem=12, us=1.0, in_hbm=()):
    in_specs, ins = [], []
    for j, a in enumerate(args):
        space = pltpu.VMEM
        if jnp.issubdtype(a.dtype, jnp.integer):
            space = pltpu.SMEM
        elif j in in_hbm:
            space = pltpu.HBM
            a = hbm(a)
        in_specs.append(pl.BlockSpec(memory_space=space))
        ins.append(a)
    return pl.pallas_call(
        kernel,
        name=getattr(kernel, 'func', kernel).__name__,
        out_shape=out,
        in_specs=in_specs,
        out_specs=jax.tree.map(lambda _: pl.BlockSpec(memory_space=pltpu.VMEM), out),
        scratch_shapes=list(scratch),
        compiler_params=pltpu.CompilerParams(vmem_limit_bytes=vmem * 2**20),
        cost_estimate=cost(us),
    )(*ins)


def shape(dims, dtype):
    return jax.ShapeDtypeStruct(tuple(dims), dtype)


def retile_kernel(image, flat):
    flat[...] = image[...].reshape(flat.shape)


def note_kernel(pairing, queue, out):
    size = queue.shape[1]
    for c in range(CROPS):
        out[c * size : (c + 1) * size, :] = queue[c]
    row = lax.broadcasted_iota(jnp.int32, (16, PROJ), 0)
    lane = lax.broadcasted_iota(jnp.int32, (16, PROJ), 1)
    value = jnp.zeros((16, PROJ), F32)
    for m in range(pairing.shape[0]):
        for i in range(pairing.shape[1]):
            value = jnp.where((row == m) & (lane == i), pairing[m, i].astype(F32), value)
    out[CROPS * size :, :] = value.astype(BF16)


def rows_kernel(*refs):
    out, at = refs[-1], 0
    for ref in refs[:-1]:
        out[at : at + ref.shape[0], :] = ref[...]
        at += ref.shape[0]


def lanes_kernel(*refs):
    out, at = refs[-1], 0
    for ref in refs[:-1]:
        out[:, at : at + ref.shape[1]] = ref[...]
        at += ref.shape[1]


def rows_of(values, us=0.5):
    rows = sum(v.shape[0] for v in values)
    return call(rows_kernel, shape((rows, values[0].shape[1]), values[0].dtype), *values, us=us)


def split_sums(first, second, micro):
    width = first[0].shape[1]
    rows = [jnp.sum(v, axis=0, keepdims=True) for v in first]
    rows += [jnp.sum(v, axis=0, keepdims=True) for v in second]
    rows.append(jnp.zeros((8 - 2 * micro, width), F32))
    return jnp.concatenate(rows, axis=0)


def moments(sums, m, micro, count):
    mean = sums[m : m + 1] * (1.0 / count)
    square = sums[micro + m : micro + m + 1] * (1.0 / count)
    return mean, lax.rsqrt(square - mean * mean + NORM_EPS)


def per_micro(value, micro):
    rows = value.shape[0] // micro
    return [value[m * rows : (m + 1) * rows] for m in range(micro)]


def normalized(value, sums, micro, count):
    out = []
    for m, v in enumerate(per_micro(value, micro)):
        mean, rstd = moments(sums, m, micro, count)
        out.append(((v - mean) * rstd, rstd))
    return out


def join(parts):
    return jnp.concatenate(parts, axis=0)


def tap_valid(rows, images, tap, sign):
    row = lax.broadcasted_iota(jnp.int32, (rows, PART), 0).astype(F32)
    cell = jnp.floor((row + 0.5) * (1.0 / images))
    crop = jnp.floor((cell + 0.5) * (1.0 / PLACES))
    place = cell - crop * PLACES
    y = jnp.floor((place + 0.5) * (1.0 / SIDE))
    x = place - y * SIDE
    y = y + float(sign * (tap // 3 - 1))
    x = x + float(sign * (tap % 3 - 1))
    return (y > -0.5) & (y < SIDE - 0.5) & (x > -0.5) & (x < SIDE - 0.5)


def tap_shift(value, images, tap, sign):
    rows = value.shape[0]
    offset = sign * images * (SIDE * (tap // 3 - 1) + (tap % 3 - 1))
    moved = value if offset == 0 else pltpu.roll(value, (-offset) % rows, 0)
    if tap == 4:
        return moved
    return jnp.where(tap_valid(rows, images, tap, sign), moved, 0.0)


def told_norm(message, at=0):
    rows = message[at : at + 16, :].astype(F32)
    return rows[0:1] + rows[1:2] + rows[2:3], rows[3:4] + rows[4:5] + rows[5:6]


def told_wide(message):
    parts = [told_norm(message, HALF_REDUCE + b * HALF_EXPAND) for b in range(4)]
    return tuple(jnp.concatenate(p, axis=1) for p in zip(*parts))


def terms(row):
    out = []
    for _ in range(3):
        term = row.astype(BF16).astype(F32)
        out.append(term)
        row = row - term
    return out


def tell_norm(rows):
    out = terms(rows[0:1]) + terms(rows[1:2])
    out.append(jnp.zeros((10, rows.shape[1]), F32))
    return jnp.concatenate(out, axis=0).astype(BF16)


def reduce_kernel(micro, place, image, w0, w1, pre, sums):
    half = D // 2
    first = pl.ds(pl.multiple_of(place[4] * half, half), half)
    second = pl.ds(pl.multiple_of(place[5] * half, half), half)
    value = dot(image[:, first], w0[16 : 16 + half, :]) + dot(image[:, second], w1[16 : 16 + half, :])
    pre[...] = value
    parts = per_micro(value, micro)
    sums[...] = split_sums(parts, [v * v for v in parts], micro)


def active_kernel(micro, count, pre, sums, told, active):
    gain, shift = told_norm(told)
    out = []
    for xhat, _ in normalized(pre[...], sums[...], micro, count):
        y = xhat * gain + shift
        out.append(y * sigmoid(y))
    active[...] = join(out).astype(BF16)


def fill(place, pieces, full):
    for k, piece in enumerate(pieces):
        full[:, pl.ds(pl.multiple_of(place[k] * PART, PART), PART)] = piece[: full.shape[0], :]


def quarter_of(place, j):
    return place[8] ^ (0, 2, 1, 3)[j]


def conv_kernel(micro, images, place, a0, a1, a2, a3, wa, wb, pre, sums, full, weight):
    fill(place, (a0, a1, a2, a3), full)
    quarter = WIDTH // 4
    for j in range(4):
        w = (wa, wb)[j // 2]
        at = pl.multiple_of(quarter_of(place, j) * quarter, quarter)
        for tap in range(9):
            lanes = slice(tap * PART, (tap + 1) * PART)
            first = (j % 2) * QUARTER_CONV + 16 + tap * quarter
            weight[pl.ds(at, quarter), lanes] = w[first : first + quarter, :]
    total = None
    for first in range(0, 9, 2):
        taps = [tap for tap in (first, first + 1) if tap < 9]
        part = dot(full[...], weight[:, first * PART : (taps[-1] + 1) * PART])
        for j, tap in enumerate(taps):
            moved = tap_shift(part[:, j * PART : (j + 1) * PART], images, tap, 1)
            total = moved if total is None else total + moved
    pre[...] = total
    parts = per_micro(total, micro)
    sums[...] = split_sums(parts, [v * v for v in parts], micro)


def expand_kernel(micro, place, a0, a1, a2, a3, w0, w1, active, pre, sums, weight):
    fill(place, (a0, a1, a2, a3), active)
    half = WIDTH // 2
    for j, w in enumerate((w0, w1)):
        rows = pl.ds(pl.multiple_of(place[4 + j] * half, half), half)
        for b in range(4):
            at = HALF_REDUCE + b * HALF_EXPAND + 16
            weight[rows, b * PART : (b + 1) * PART] = w[at : at + half, :]
    value = dot(active[...], weight[...])
    pre[...] = value
    parts = per_micro(value, micro)
    sums[...] = split_sums(parts, [v * v for v in parts], micro)


def crop_rows(rows, images, transpose=False):
    shp = (rows // PLACES, rows)
    r = lax.broadcasted_iota(jnp.int32, shp, 1).astype(F32)
    q = lax.broadcasted_iota(jnp.int32, shp, 0).astype(F32)
    cell = jnp.floor((r + 0.5) * (1.0 / images))
    crop = jnp.floor((cell + 0.5) * (1.0 / PLACES))
    image = r - cell * images
    return (jnp.abs(crop * images + image - q) < 0.5).astype(F32).astype(BF16)


def pool_kernel(micro, images, count, place, pre, sums, told, image, pooled):
    lanes = pl.ds(pl.multiple_of(place[0] * WIDE, WIDE), WIDE)
    gain, shift = told_wide(told)
    out = []
    for xhat, _ in normalized(pre[...], sums[...], micro, count):
        out.append(xhat * gain + shift)
    z = join(out) + image[:, lanes].astype(F32)
    out = z * sigmoid(z)
    high = out.astype(BF16)
    low = (out - high.astype(F32)).astype(BF16)
    choose = crop_rows(pre.shape[0], images)
    pooled[...] = ((dot(choose, high) + dot(choose, low)) * (1.0 / PLACES)).astype(BF16)


def out_back_kernel(micro, images, count, place, pre, sums, told, image, own, r0, r1, r2, d_z, sums_out):
    lanes = pl.ds(pl.multiple_of(place[0] * WIDE, WIDE), WIDE)
    rows = pre.shape[0]
    gain, shift = told_wide(told)
    came = (r0[...].astype(F32) + r1[...].astype(F32) + r2[...].astype(F32)).astype(BF16)
    d_pooled = jnp.where(place[0] == SECTIONS - 1, own[...], came)
    spread = dot_tn(crop_rows(rows, images), d_pooled) * (1.0 / PLACES)
    xhats = [x for x, _ in normalized(pre[...], sums[...], micro, count)]
    z = join([x * gain + shift for x in xhats]) + image[:, lanes].astype(F32)
    value = spread * slope(z)
    d_z[...] = value
    parts = per_micro(value, micro)
    sums_out[...] = split_sums([v * x for v, x in zip(parts, xhats)], parts, micro)


def norm_back(value, pre, sums, back, gain, micro, count):
    out = []
    parts = per_micro(value, micro)
    for m, (xhat, rstd) in enumerate(normalized(pre, sums, micro, count)):
        by_x = back[m : m + 1] * (1.0 / count)
        plain = back[micro + m : micro + m + 1] * (1.0 / count)
        out.append(gain * rstd * (parts[m] - plain - xhat * by_x))
    return join(out)


def norm_back_kernel(micro, count, d_y, pre, sums, back, told, d_pre):
    gain, _ = told_norm(told)
    d_pre[...] = norm_back(d_y[...], pre[...], sums[...], back[...], gain, micro, count).astype(BF16)


def over_micro(back, micro):
    out = []
    for r in range(2):
        row = back[r * micro : r * micro + 1, :]
        for m in range(1, micro):
            row = row + back[r * micro + m : r * micro + m + 1, :]
        out.append(row)
    return out


def last_norm_back_kernel(micro, count, place, d_y, pre, sums, back, told, back2, back1, notes, d_pre):
    gain, _ = told_norm(told)
    rows = d_y.shape[0]
    d_pre[:rows, :] = norm_back(d_y[...], pre[...], sums[...], back[...], gain, micro, count).astype(BF16)
    said = []
    for row in over_micro(back2, micro):
        said += [row[:, b * PART : (b + 1) * PART] for b in range(4)]
    said += over_micro(back1, micro) + over_micro(back, micro)
    said.append(jnp.where(place[0] == SECTIONS - 1, notes[3:4, :PART], 0.0))
    said = sum([terms(row) for row in said], [])
    said.append(jnp.zeros((NOTE_ROWS - len(said), PART), F32))
    d_pre[rows:, :] = jnp.concatenate(said, axis=0).astype(BF16)


def expand_back_kernel(micro, count, place, pre, sums, d_z, back, told, weight, d_pre, q0, q1, q2, q3, full):
    gain, _ = told_wide(told)
    d_low = norm_back(d_z[...], pre[...], sums[...], back[...], gain, micro, count).astype(BF16)
    d_pre[...] = d_low
    full[...] = dot_nt(d_low, weight[...])
    for k, q in enumerate((q0, q1, q2, q3)):
        lanes = pl.ds(pl.multiple_of(place[k] * PART, PART), PART)
        q[...] = full[:, lanes].astype(BF16)


def finish_silu(micro, count, d_active, pre, sums, norm, d_y, sums_out):
    gain, shift = norm
    values, products = [], []
    parts = per_micro(d_active, micro)
    for m, (xhat, _) in enumerate(normalized(pre[...], sums[...], micro, count)):
        value = parts[m] * slope(xhat * gain + shift)
        values.append(value)
        products.append(value * xhat)
    d_y[...] = join(values)
    sums_out[...] = split_sums(products, values, micro)


def silu_back_kernel(micro, count, q0, q1, q2, q3, pre, sums, told, d_y, sums_out):
    total = (q0[...].astype(F32) + q1[...].astype(F32)) + (q2[...].astype(F32) + q3[...].astype(F32))
    d_active = total.astype(BF16).astype(F32)
    finish_silu(micro, count, d_active, pre, sums, told_norm(told), d_y, sums_out)


def conv_back_kernel(
    micro, images, count, place, d0, d1, d2, d3, back0, back1, pre, sums, told, d_full, d_y, sums_out, weight
):
    fill(place, (d0, d1, d2, d3), d_full)
    d_low = d_full[...]
    half = PART // 2
    for j, back in enumerate((back0, back1)):
        for k in range(SECTIONS):
            lanes = pl.ds(pl.multiple_of(place[k] * PART, PART), PART)
            for tap in range(9):
                rows = pl.ds(pl.multiple_of(tap * PART + place[4 + j] * half, half), half)
                weight[rows, lanes] = back[k, tap * half : (tap + 1) * half, :]
    total = None
    for first in range(0, 9, 2):
        taps = [tap for tap in (first, first + 1) if tap < 9]
        part = dot_nt(d_low, weight[first * PART : (taps[-1] + 1) * PART, :])
        for j, tap in enumerate(taps):
            moved = tap_shift(part[:, j * PART : (j + 1) * PART], images, tap, -1)
            total = moved if total is None else total + moved
    d_active = total.astype(BF16).astype(F32)
    finish_silu(micro, count, d_active, pre, sums, told_norm(told), d_y, sums_out)


def reduce_back_kernel(place, d_full, back0, back1, d_z, grad_in, weight):
    half = WIDE // 2
    first = 9 * PART // 2
    for j, back in enumerate((back0, back1)):
        rows = pl.ds(pl.multiple_of(place[4 + j] * half, half), half)
        for k in range(SECTIONS):
            lanes = pl.ds(pl.multiple_of(place[k] * PART, PART), PART)
            weight[rows, lanes] = back[k, first : first + half, :]
    main = dot_nt(d_full[...], weight[...]).astype(BF16).astype(F32)
    value = main + d_z[...].astype(BF16).astype(F32)
    grad_in[...] = value.reshape(grad_in.shape)


def back_parts_kernel(place, conv_a, conv_b, reduce0, reduce1, *outs):
    half = PART // 2
    wide = WIDE // 2
    first = 9 * half
    quarter = WIDTH // 4
    for k, out in enumerate(outs):
        for core in range(2):
            for j in range(4):
                conv = (conv_a, conv_b)[j // 2]

                @pl.when((place[k] == quarter_of(place, j)) & (place[4] == core))
                def _():
                    for tap in range(9):
                        at = (j % 2) * QUARTER_CONV + 16 + tap * quarter + core * half
                        out[tap * half : (tap + 1) * half, :] = conv[at : at + half, :]

            for u in range(SECTIONS):
                reduce = (reduce0, reduce1)[core ^ (u // 2)]

                @pl.when((place[k] == u) & (place[4] == core))
                def _():
                    at = 16 + (u % 2) * WIDE + core * wide
                    out[first : first + wide, :] = reduce[at : at + wide, :]


def stack_kernel(*refs):
    out = refs[-1]
    rows = refs[0].shape[0]
    for j, ref in enumerate(refs[:-1]):
        if len(out.shape) == 3:
            out[j] = ref[...]
        else:
            out[j * rows : (j + 1) * rows, :] = ref[...]


def mixed_kernel(place, reduce, conv, expand, *outs):
    for k, out in enumerate(outs):
        target = place[k + 1]

        @pl.when(target == 0)
        def _():
            out[:, :WIDE] = reduce[...]

        @pl.when(target == 1)
        def _():
            out[...] = conv[...]

        @pl.when(target == 2)
        def _():
            out[:, :WIDE] = expand[...]


def told_kernel(place, n0, n1, n2, n3, notes, out, loss):
    t = place[0]
    out[...] = jnp.zeros_like(out)

    @pl.when(t == SECTIONS - 1)
    def _():
        out[...] = notes[:3, :]

    total = None
    for k, note in enumerate((n0, n1, n2, n3)):
        u = place[k]
        rows = note[note.shape[0] - NOTE_ROWS :, :].astype(F32)

        def said(i):
            return (rows[3 * i : 3 * i + 1] + rows[3 * i + 1 : 3 * i + 2]) + rows[3 * i + 2 : 3 * i + 3]

        total = said(12) if total is None else total + said(12)

        @pl.when(t == 2)
        def _():
            for r in range(2):
                for b in range(4):
                    lanes = pl.ds(pl.multiple_of(u * WIDE + b * PART, PART), PART)
                    out[r : r + 1, lanes] = said(4 * r + b)

        for section in range(2):

            @pl.when(t == section)
            def _():
                for r in range(2):
                    lanes = pl.ds(pl.multiple_of(u * PART, PART), PART)
                    out[r : r + 1, lanes] = said((10, 8)[section] + r)

    loss[...] = jnp.broadcast_to(total, loss.shape)


def pick_kernel(place, p0, p1, p2, p3, conv, pair):
    for j, p in enumerate((p0, p1, p2, p3)):

        @pl.when(place[0] == j)
        def _():
            pair[:HALF_REDUCE, :] = p[:HALF_REDUCE, :]

        @pl.when(place[1] == j)
        def _():
            conv[...] = p[...]

        @pl.when(place[2] == j)
        def _():
            pair[HALF_REDUCE:, :] = p[: 4 * HALF_EXPAND, :]


def taps_kernel(images, active, out):
    value = active[...].astype(F32)
    for tap in range(9):
        out[:, tap * PART : (tap + 1) * PART] = tap_shift(value, images, tap, 1).astype(BF16)


def head(pooled, w_head, w_proj, protos, norm, queue, match, micro, images, dp):
    rows = pooled.shape[0]
    group = rows // micro
    half = group // CROPS
    scale_all = 1.0 / (TEMPER * CROPS * half * micro)
    pre = dot(pooled, w_head)

    def by_micro(v):
        return v.reshape(micro, group, v.shape[-1])

    pre_m = by_micro(pre)
    mean = jnp.mean(pre_m, axis=1, keepdims=True)
    square = jnp.mean(pre_m * pre_m, axis=1, keepdims=True)
    rstd = lax.rsqrt(square - mean * mean + NORM_EPS)
    xhat = (pre_m - mean) * rstd
    y = xhat * norm[0] + norm[1]
    active = (y * sigmoid(y)).astype(BF16).reshape(rows, D)
    embed = dot(active, w_proj) + norm[2, :PROJ]
    recip = lax.rsqrt(jnp.sum(embed * embed, axis=1, keepdims=True) + UNIT_EPS)
    unit = (embed * recip).astype(BF16)
    scores = dot_nt(unit, protos)
    valid = lax.broadcasted_iota(jnp.int32, (1, 4, QUARTER_PAD), 2).reshape(1, 4 * QUARTER_PAD) < QUARTER
    own_mass = jnp.where(valid, jnp.exp(scores / SINK_EPS), 0.0).reshape(micro, CROPS, half, -1)
    queue_mass = jnp.where(valid, jnp.exp(jnp.einsum("cqp,kp->cqk", queue, protos, preferred_element_type=F32) / SINK_EPS), 0.0)
    codes = []
    for m in range(micro):
        for c in range(CROPS):
            a, b = queue_mass[c], own_mass[m, c]
            column = jnp.sum(a, axis=0, keepdims=True) + jnp.sum(b, axis=0, keepdims=True)
            once = jnp.where(valid, 1.0 / column, 0.0)
            a, b = a * once, b * once
            scale = valid.astype(F32)
            for turn in range(2):
                ra = 1.0 / jnp.sum(a * scale, axis=1, keepdims=True)
                rb = 1.0 / jnp.sum(b * scale, axis=1, keepdims=True)
                column = jnp.sum(a * ra, axis=0, keepdims=True) + jnp.sum(b * rb, axis=0, keepdims=True)
                scale = jnp.where(valid, 1.0 / column, 0.0)
            b = b * scale
            codes.append(b / jnp.sum(b, axis=1, keepdims=True))
    targets = []
    for m in range(micro):
        targets.append(jnp.dot(match[m], codes[m * CROPS + 1], precision=HIGH))
        targets.append(jnp.dot(match[m].T, codes[m * CROPS], precision=HIGH))
    target = jnp.concatenate(targets)
    logits = jnp.where(valid, scores / TEMPER, -1e30)
    logp = jax.nn.log_softmax(logits, axis=1)
    loss = -jnp.sum(jnp.where(valid, target * logp, 0.0)) * (TEMPER * scale_all)
    d_scores = ((jnp.exp(logp) * jnp.sum(target, axis=1, keepdims=True) - target) * scale_all).astype(BF16)
    d_unit = dot(d_scores, protos)
    d_embed = (
        recip * d_unit - embed * (recip * recip * recip) * jnp.sum(d_unit * embed, axis=1, keepdims=True)
    ).astype(BF16)
    d_active = dot_nt(d_embed, w_proj)
    d_y = by_micro(d_active) * slope(y)
    by_x = jnp.sum(d_y * xhat, axis=1, keepdims=True)
    plain = jnp.sum(d_y, axis=1, keepdims=True)
    d_pre = (norm[0] * rstd * (d_y - plain / group - xhat * by_x / group)).astype(BF16).reshape(rows, D)
    bias = jnp.pad(jnp.sum(d_embed.astype(F32), axis=0), (0, D - PROJ))
    grads = jnp.stack([jnp.sum(by_x, axis=(0, 1)), jnp.sum(plain, axis=(0, 1)), bias])
    return loss, grads, active, unit, d_scores, d_embed, d_pre


def valid_lanes():
    lane = lax.broadcasted_iota(jnp.int32, (1, 4 * QUARTER_PAD), 1).astype(F32)
    block = jnp.floor((lane + 0.5) * (1.0 / QUARTER_PAD))
    return lane - block * QUARTER_PAD < QUARTER - 0.5


def lanes_at(b, size):
    return pl.ds(pl.multiple_of(b * size, size), size)


def lanes_at(b, size):
    return pl.ds(pl.multiple_of(b * size, size), size)


def mass_kernel(micro, images, told_offsets, place, table, *refs):
    mass, column, match, rows_s, exps = refs[-5:]
    ndp = len(told_offsets)
    valid = valid_lanes()
    size = mass.shape[0] // ndp
    half = images * ndp
    at, said = 0, jnp.zeros((16, half), F32)
    row = lax.broadcasted_iota(jnp.int32, (PROJ, half), 0)
    lane = lax.broadcasted_iota(jnp.int32, (PROJ, half), 1)
    for ref in refs[:-5]:
        rows = CROPS * size + 16
        for j in range(ref.shape[0] // rows):
            mine = pl.ds(pl.multiple_of(j * rows + place[4] * size, 16), size)
            rows_s[lanes_at(place[7] ^ told_offsets[at], size), :] = ref[mine, :]
            pairs = ref[(j + 1) * rows - 16 : (j + 1) * rows, :]
            spot_at = (place[7] ^ told_offsets[at]) * images
            spot = ((row < images) & (lane == row + spot_at)).astype(F32).astype(BF16)
            said = said + dot(pairs, spot)
            at += 1
    step = 128
    steps = mass.shape[0] // step

    def scored(i, sums):
        own = rows_s[lanes_at(i, step), :]
        out = []
        for a in range(4):
            lanes = slice(a * QUARTER_PAD, (a + 1) * QUARTER_PAD)
            value = jnp.exp(dot_nt(own, table[:, a * PROJ : (a + 1) * PROJ]) * (1.0 / SINK_EPS))
            value = jnp.where(valid[:, lanes], value, 0.0)
            exps[lanes_at(i, step), lanes] = value
            out.append(jnp.sum(value, axis=0, keepdims=True))
        return sums + jnp.concatenate(out, axis=1)

    sums = lax.fori_loop(0, steps, scored, jnp.zeros((1, 4 * QUARTER_PAD), F32))
    column[...] = jnp.broadcast_to(sums, column.shape)
    factor = jnp.where(valid, 1.0 / sums, 0.0)

    def divide(i, carry):
        mass[lanes_at(i, step), :] = (exps[lanes_at(i, step), :] * factor).astype(BF16)
        return carry

    lax.fori_loop(0, steps, divide, 0)

    def over(value, by):
        return jnp.floor((value + 0.5) * (1.0 / by))

    row = lax.broadcasted_iota(jnp.int32, (half, half), 0).astype(F32)
    lane = lax.broadcasted_iota(jnp.int32, (half, half), 1).astype(F32)
    block = over(row, images)
    for m in range(micro):
        same = (jnp.abs(block - over(lane, images)) < 0.5) & (jnp.abs(row - block * images - said[m : m + 1, :]) < 0.5)
        there = same.astype(F32)
        match[m] = jnp.where(place[4] == 0, there, there.T).astype(BF16)


def tables_kernel(packed, proj, table, rows, buffer, sem):
    size = THIRD - FIRST + 2
    copy = pltpu.make_async_copy(packed.at[pl.ds(FIRST, size), :], rows, sem)
    copy.start()
    copy.wait()
    wide = SECOND - FIRST
    for a in range(4):
        buffer[pl.ds(a, wide, stride=4), :] = rows[:wide, a * PROJ : (a + 1) * PROJ].astype(F32)
    proj[...] = buffer[...].astype(BF16)
    row = lax.broadcasted_iota(jnp.int32, (size - wide, WIDTH), 0)
    kept = jnp.where(row < QUARTER, rows[wide:, :].astype(F32), 0.0).astype(BF16)
    table[: size - wide, :] = kept
    table[size - wide :, :] = jnp.zeros((QUARTER_PAD - (size - wide), WIDTH), BF16)


def exact_dot(choose, value):
    parts, left = [], value
    for _ in range(3):
        term = left.astype(BF16)
        left = left - term.astype(F32)
        parts.append(term)
    return dot(jnp.concatenate([choose] * 3, axis=1), jnp.concatenate(parts, axis=0))


def by_micro_rows(value, ndp, micro):
    return value.reshape(ndp, micro, value.shape[0] // (ndp * micro), value.shape[1])


def total_of(value):
    return jnp.sum(jnp.sum(value, axis=0), axis=0, keepdims=True)


def regroup(rows, own, images, to_groups):
    ndp = rows // own
    row = lax.broadcasted_iota(jnp.int32, (rows, rows), 0).astype(F32)
    lane = lax.broadcasted_iota(jnp.int32, (rows, rows), 1).astype(F32)
    source, target = (lane, row) if to_groups else (row, lane)
    block = jnp.floor((source + 0.5) * (1.0 / own))
    inner = source - block * own
    part = jnp.floor((inner + 0.5) * (1.0 / images))
    moved = (part * ndp + block) * images + inner - part * images
    return (jnp.abs(moved - target) < 0.5).astype(F32).astype(BF16)


def head_kernel(
    micro, images, offsets, place, pooled_a, pooled_b, w_head, w_proj, table, norm, mass, column, match,
    pooled, active, unit, d_scores, embed, xhat_s, y_s, rstd_s, said,
    scores, own_mass, total, factor,
):
    ndp = len(offsets)
    rows = pooled.shape[0]
    group = rows // micro
    half = group // CROPS
    own = rows // ndp
    queued = mass.shape[0]
    scale_all = 1.0 / (TEMPER * CROPS * half * micro)
    chunk = WIDTH
    chunks = D // chunk
    core = place[4]
    for j, offset in enumerate(offsets):
        source = (pooled_a, pooled_b)[j * own // pooled_a.shape[0]]
        at = j * own % pooled_a.shape[0]
        pooled[lanes_at(place[7] ^ offset, own), :] = source[at : at + own, :]
    low = pooled[...]

    def forward(b, carry):
        lanes = lanes_at(b, chunk)
        pre = by_micro_rows(dot(low, w_head[:, lanes]), ndp, micro)
        gain, shift = norm[0:1, lanes], norm[1:2, lanes]
        xhats, ys = [], []
        for m in range(micro):
            v = pre[:, m]
            mean = total_of(v) * (1.0 / group)
            square = total_of(v * v) * (1.0 / group)
            rstd = lax.rsqrt(square - mean * mean + NORM_EPS)
            xhat = (v - mean) * rstd
            rstd_s[m : m + 1, lanes] = rstd
            xhats.append(xhat)
            ys.append(xhat * gain + shift)
        xhat_s[:, lanes] = jnp.stack(xhats, axis=1).reshape(rows, chunk)
        y = jnp.stack(ys, axis=1).reshape(rows, chunk)
        y_s[:, lanes] = y
        active[:, lanes] = (y * sigmoid(y)).astype(BF16)
        return carry

    lax.fori_loop(0, chunks, forward, 0)
    value = dot(active[...], w_proj[...]) + norm[2:3, :PROJ]
    embed[...] = value
    recip = lax.rsqrt(jnp.sum(value * value, axis=1, keepdims=True) + UNIT_EPS)
    unit_v = dot(regroup(rows, own, images, True), (value * recip).astype(BF16)).astype(BF16)
    unit[...] = unit_v
    valid = valid_lanes()
    for a in range(4):
        lanes = slice(a * QUARTER_PAD, (a + 1) * QUARTER_PAD)
        scores[:, lanes] = dot_nt(unit_v, table[:, a * PROJ : (a + 1) * PROJ])

    step = 128

    def divided(a):
        return a * (1.0 / jnp.sum(a, axis=1, keepdims=True))

    def folded(a):
        return jnp.sum(a.reshape(a.shape[0] // 8, 8, a.shape[1]), axis=0)

    def own_rows(m):
        return slice(m * half, (m + 1) * half)

    queue_sum = column[0:1, :]
    for m in range(micro):
        a = scores[lanes_at(m * CROPS + core, half), :]
        a = jnp.where(valid, jnp.exp(a * (1.0 / SINK_EPS)), 0.0)
        inverse = jnp.where(valid, 1.0 / (queue_sum + jnp.sum(a, axis=0, keepdims=True)), 0.0)
        factor[m : m + 1, :] = queue_sum * inverse
        factor[micro + m : micro + m + 1, :] = jnp.ones_like(inverse)
        own_mass[own_rows(m), :] = a * inverse

    def turn(i, carry):
        def block(i, carry):
            at = lanes_at(i, step)
            e_of = [mass[at, b * PART : (b + 1) * PART].astype(F32) for b in range(4 * QUARTER_PAD // PART)]
            rows_by = []
            for m in range(micro):
                sums = None
                for b, e in enumerate(e_of):
                    more = e * factor[m : m + 1, b * PART : (b + 1) * PART]
                    sums = more if sums is None else sums + more
                rows_by.append(1.0 / jnp.sum(sums, axis=1, keepdims=True))
            for b in range(4 * QUARTER_PAD // PART):
                lanes = slice(b * PART, (b + 1) * PART)
                e = mass[at, lanes].astype(F32)
                for m in range(micro):
                    total[m, :, lanes] += folded(e * rows_by[m])
            return carry

        total[...] = jnp.zeros_like(total)
        lax.fori_loop(0, queued // step, block, 0)
        for m in range(micro):
            scale = factor[micro + m : micro + m + 1, :]
            a = divided(own_mass[own_rows(m), :] * scale)
            sums = jnp.sum(total[m], axis=0, keepdims=True) * factor[m : m + 1, :]
            more = jnp.where(valid, 1.0 / (sums + jnp.sum(a, axis=0, keepdims=True)), 0.0)
            factor[m : m + 1, :] = factor[m : m + 1, :] * more
            factor[micro + m : micro + m + 1, :] = scale * more
        return carry

    lax.fori_loop(0, 2, turn, 0)

    def losses(m, loss):
        mine, there = lanes_at(m, half), lanes_at(m * CROPS + 1 - core, half)
        codes = divided(own_mass[mine, :] * factor[pl.ds(micro + m, 1), :])
        goal = exact_dot(match[m], codes)
        logits = jnp.where(valid, scores[there, :] * (1.0 / TEMPER), -1e30)
        logits = logits - jnp.max(logits, axis=1, keepdims=True)
        power = jnp.exp(logits)
        summed = jnp.sum(power, axis=1, keepdims=True)
        weight = jnp.sum(goal, axis=1, keepdims=True) / summed
        d_low = ((power * weight - goal) * scale_all).astype(BF16)
        d_scores[mine, :] = d_low
        d_unit = None
        for a in range(4):
            more = dot(d_low[:, a * QUARTER_PAD : (a + 1) * QUARTER_PAD], table[:, a * PROJ : (a + 1) * PROJ])
            d_unit = more if d_unit is None else d_unit + more
        said[mine, :] = d_unit
        return loss + jnp.sum(goal * (logits - jnp.log(summed)), axis=1, keepdims=True)

    loss = lax.fori_loop(0, micro, losses, jnp.zeros((half, 1), F32))
    loss = jnp.sum(loss, axis=0, keepdims=True) * (-TEMPER * scale_all)
    said[micro * half :, :] = jnp.broadcast_to(loss, (8, PROJ))


def head_back_kernel(
    micro, images, ndp, place, here, there, embed, w_proj, w_head, norm, xhat_s, y_s, rstd_s,
    d0, d1, d2, d3, notes, d_embed, d_pre, d_unit, d_own,
):
    rows = embed.shape[0]
    group = rows // micro
    half = group // CROPS
    own = rows // ndp
    chunk = WIDTH
    chunks = D // chunk
    for m in range(micro):
        d_unit[lanes_at(m * CROPS + place[5], half), :] = here[m * half : (m + 1) * half, :]
        d_unit[lanes_at(m * CROPS + place[4], half), :] = there[m * half : (m + 1) * half, :]
    value = embed[...]
    recip = lax.rsqrt(jnp.sum(value * value, axis=1, keepdims=True) + UNIT_EPS)
    d_back = exact_dot(regroup(rows, own, images, False), d_unit[...])
    along = jnp.sum(d_back * value, axis=1, keepdims=True)
    d_low = (recip * d_back - value * (recip * recip * recip) * along).astype(BF16)
    d_embed[...] = d_low
    notes[...] = jnp.zeros_like(notes)
    notes[2:3, :PROJ] = jnp.sum(d_low.astype(F32), axis=0, keepdims=True)
    loss = here[micro * half : micro * half + 1, :] + there[micro * half : micro * half + 1, :]
    notes[3:4, :PROJ] = loss

    def backward(b, carry):
        lanes = lanes_at(b, chunk)
        d_y = by_micro_rows(dot_nt(d_low, w_proj[lanes, :]) * slope(y_s[:, lanes]), ndp, micro)
        xhat = by_micro_rows(xhat_s[:, lanes], ndp, micro)
        gain = norm[0:1, lanes]
        values, by_xs, plains = [], None, None
        for m in range(micro):
            by_x = total_of(d_y[:, m] * xhat[:, m])
            plain = total_of(d_y[:, m])
            by_xs = by_x if by_xs is None else by_xs + by_x
            plains = plain if plains is None else plains + plain
            value = d_y[:, m] - plain * (1.0 / group) - xhat[:, m] * (by_x * (1.0 / group))
            values.append(gain * rstd_s[m : m + 1, lanes] * value)
        notes[0:1, lanes] = by_xs
        notes[1:2, lanes] = plains
        d_pre[:, lanes] = jnp.stack(values, axis=1).reshape(rows, chunk).astype(BF16)
        return carry

    lax.fori_loop(0, chunks, backward, 0)
    mine = d_pre[lanes_at(place[7], own), :]

    def to_pooled(b, carry):
        d_own[:, lanes_at(b, chunk)] = dot_nt(mine, w_head[lanes_at(b, chunk), :]).astype(BF16)
        return carry

    lax.fori_loop(0, chunks, to_pooled, 0)
    for j, out in enumerate((d0, d1, d2, d3)):
        out[...] = d_own[:, j * WIDE : (j + 1) * WIDE]


def interleave(width):
    row = lax.broadcasted_iota(jnp.int32, (4 * width, 4 * width), 0)
    column = lax.broadcasted_iota(jnp.int32, (4 * width, 4 * width), 1)
    return (column == 4 * (row & (width - 1)) + (row >> (width.bit_length() - 1))).astype(F32).astype(BF16)


def own_columns(place, own):
    row = lax.broadcasted_iota(jnp.int32, (WIDTH, own), 0)
    lane = lax.broadcasted_iota(jnp.int32, (WIDTH, own), 1)
    return (row == lane + place[7] * own).astype(F32).astype(BF16)


def head_grads_kernel(place, pooled, active, unit, d_here, d_there, d_embed, d_pre, out, parts, apart):
    @pl.when(place[0] != SECTIONS - 1)
    def _():
        out[...] = jnp.zeros_like(out)

    @pl.when(place[0] == SECTIONS - 1)
    def _():
        own = out.shape[0]
        choose = own_columns(place, own)
        weave = interleave(PART)
        block = PART

        def product(q, carry):
            own_d = dot(d_pre[:, lanes_at(q, WIDTH)], choose).astype(BF16)
            parts[q] = dot_tn(own_d, pooled[...]).astype(BF16)
            return carry

        lax.fori_loop(0, 4, product, 0)

        def mix(b, carry):
            mixed = jnp.concatenate([parts[q, :, lanes_at(b, block)] for q in range(4)], axis=1)
            out[:, lanes_at(b, 4 * block)] = dot(mixed, weave)
            return carry

        lax.fori_loop(0, D // block, mix, 0)

        def part(b, carry):
            apart[b] = dot_nt(active[:, lanes_at(b, WIDTH)], weave).astype(BF16)
            return carry

        lax.fori_loop(0, 4, part, 0)
        half = d_here.shape[0] // 2
        units = []
        for core in (place[5], place[4]):
            units.append(jnp.concatenate([unit[lanes_at(m * CROPS + core, half), :] for m in range(2)], axis=0))
        proj = jnp.zeros((own, WIDTH), F32)
        proto = jnp.zeros((own, QUARTER_PAD), F32)
        for a in range(4):
            some = choose[a * PROJ : (a + 1) * PROJ, :]
            own_e = dot(d_embed[...], some).astype(BF16)
            column = jnp.concatenate([apart[b, :, a * block : (a + 1) * block] for b in range(4)], axis=1)
            proj = proj + dot_tn(own_e, column)
            for own_unit, d_scores in zip(units, (d_here, d_there)):
                own_u = dot(own_unit, some).astype(BF16)
                proto = proto + dot_tn(own_u, d_scores[:, a * QUARTER_PAD : (a + 1) * QUARTER_PAD])
        out[:, FIRST:SECOND] = proj
        out[:, SECOND:] = proto[:, : out.shape[1] - SECOND]


def finish_kernel(place, base, reduce, conv, expand, m1, m2, m3, out, buffer, sem):
    mixed = (None, m1, m2, m3)
    t = place[0]

    def write(lanes):
        copy = pltpu.make_async_copy(buffer.at[:, pl.ds(0, lanes)], out.at[:, pl.ds(0, lanes)], sem)
        copy.start()
        copy.wait()

    @pl.when(t == 0)
    def _():
        for u in range(SECTIONS):
            piece = reduce if u == 0 else mixed[u]
            buffer[:, u * WIDE : (u + 1) * WIDE] = piece[:, :WIDE].astype(F32)
        write(D)

    @pl.when(t == 1)
    def _():
        for u in range(SECTIONS):
            piece = conv if u == 1 else mixed[u ^ 1]
            for tap in range(9):
                at = tap * WIDTH + u * PART
                buffer[:, at : at + PART] = piece[:, tap * PART : (tap + 1) * PART].astype(F32)
        write(9 * WIDTH)

    @pl.when(t == 2)
    def _():
        four = [expand if u == 2 else mixed[u ^ 2] for u in range(SECTIONS)]
        weave = interleave(PART)
        for b in range(WIDTH // PART):
            lanes = slice(b * PART, (b + 1) * PART)
            row = jnp.concatenate([f[:, lanes] for f in four], axis=1)
            buffer[:, 4 * b * PART : 4 * (b + 1) * PART] = dot(row, weave)
        write(D)


def unpack_kernel(packed, out, buffer):
    rows = packed.shape[0]
    for b in range(4):
        buffer[b] = packed[:, b * PART : (b + 1) * PART].astype(F32)
    for q in range(4):
        for b in range(4):
            at = q * WIDTH + b * PART
            out[:, at : at + PART] = buffer[b, pl.ds(q, rows // 4, stride=4), :].astype(BF16)


def unpack(packed, rows):
    step = 1024
    return pl.pallas_call(
        unpack_kernel,
        name="unpack",
        out_shape=shape((rows // 4, 4 * WIDTH), BF16),
        grid=(rows // step,),
        in_specs=[pl.BlockSpec((step, WIDTH), lambda i: (i, 0))],
        out_specs=pl.BlockSpec((step // 4, 4 * WIDTH), lambda i: (i, 0)),
        scratch_shapes=[pltpu.VMEM((4, step, PART), F32)],
        compiler_params=pltpu.CompilerParams(vmem_limit_bytes=16 * 2**20),
        cost_estimate=cost(4),
    )(packed)


def pack_kernel(place, packed, norm, o0, o1, o2, o3, rows, buffer, sem):
    outs = (o0, o1, o2, o3)
    t, core = place[0], place[4]

    def run(copies):
        for copy in copies:
            copy.start()
        return copies

    def lanes_of(target, lanes):
        return pl.ds(target * lanes, lanes)

    @pl.when(t == 0)
    def _():
        half = D // 2
        copies = []
        for k, out in enumerate(outs):
            source = packed.at[pl.ds(pl.multiple_of(core * half, half), half), lanes_of(k, PART)]
            copies.append(pltpu.make_async_copy(source, out.at[pl.ds(16, half), :], sem.at[k]))
        run(copies)
        for k, out in enumerate(outs):
            out[:16, :] = tell_norm(norm[:, k * PART : (k + 1) * PART])
        for copy in copies:
            copy.wait()

    @pl.when(t == 1)
    def _():
        quarter = WIDTH // 4
        copies = []
        for k, out in enumerate(outs):
            for tap in range(9):
                at = pl.multiple_of(tap * WIDTH + place[8] * quarter, quarter)
                source = packed.at[pl.ds(at, quarter), lanes_of(1 ^ k, PART)]
                target = out.at[pl.ds(16 + tap * quarter, quarter), :]
                copies.append(pltpu.make_async_copy(source, target, sem.at[9 * k + tap]))
        run(copies)
        for k, out in enumerate(outs):
            out[:16, :] = tell_norm(norm[:, (1 ^ k) * PART : ((1 ^ k) + 1) * PART])
        for copy in copies:
            copy.wait()

    @pl.when(t == 2)
    def _():
        size = rows.shape[0]
        copy = pltpu.make_async_copy(packed.at[pl.ds(pl.multiple_of(core * size, size), size), :], rows, sem.at[0])
        copy.start()
        copy.wait()
        for b in range(4):
            buffer[b] = rows[:, b * PART : (b + 1) * PART].astype(F32)
        for k, out in enumerate(outs):
            u = 2 ^ k
            for b in range(4):
                at = b * HALF_EXPAND
                lane = u * WIDE + b * PART
                out[at : at + 16, :] = tell_norm(norm[:, lane : lane + PART])
                out[at + 16 : at + HALF_EXPAND, :] = buffer[b, pl.ds(u, size // 4, stride=4), :].astype(BF16)


def pack(place, packed, norm):
    rows = 4 * (WIDTH // 2)
    return pl.pallas_call(
        pack_kernel,
        name="pack",
        out_shape=[shape((QUARTER_CONV, PART), BF16)] * 4,
        in_specs=[
            pl.BlockSpec(memory_space=pltpu.SMEM),
            pl.BlockSpec(memory_space=pltpu.HBM),
            pl.BlockSpec(memory_space=pltpu.VMEM),
        ],
        out_specs=[pl.BlockSpec(memory_space=pltpu.VMEM)] * 4,
        scratch_shapes=[
            pltpu.VMEM((rows, WIDTH), BF16), pltpu.VMEM((4, rows, PART), F32), pltpu.SemaphoreType.DMA((36,)),
        ],
        compiler_params=pltpu.CompilerParams(vmem_limit_bytes=12 * 2**20),
        cost_estimate=cost(2),
    )(place, hbm(packed), norm)


def multiple(value, step):
    return value if isinstance(value, int) else pl.multiple_of(value, step)


def pair_kernel(place, a, b, keep, out, full):
    full[...] = dot_tn(a[...], b[...])
    own = keep.shape[1]
    for z in range(keep.shape[0]):
        mine = (2 * z + place[4]) * own
        other = (2 * z + place[5]) * own
        keep[z] = full[pl.ds(pl.multiple_of(mine, own), own), :]
        out[z] = full[pl.ds(pl.multiple_of(other, own), own), :].astype(BF16)


def image_pair_kernel(place, d0, d1, d2, d3, image, keep, out, d_full, full):
    fill(place, (d0, d1, d2, d3), d_full)
    lanes = pl.ds(pl.multiple_of(place[0] * WIDE, WIDE), WIDE)
    pair_kernel(place, d_full, image.at[:, lanes], keep, out, full)


def cross_kernel(place, keep, came, own, o1, o2, o3):
    for k, o in enumerate((own, o1, o2, o3)):
        z = place[6] ^ k
        o[...] = (keep[z] + came[z].astype(F32)).astype(o.dtype)


def add_kernel(own, r1, r2, r3, out):
    out[...] = ((own[...] + r1[...].astype(F32)) + (r2[...].astype(F32) + r3[...].astype(F32))).astype(BF16)


def after(value, *others):
    return lax.optimization_barrier((value, *others))[0]


def body(image, section_weights, section_norms, queue, pairing):
    micro, images = image.shape[0], image.shape[2]
    ndp = lax.axis_size("dp")
    t = lax.axis_index("section")
    dp = lax.axis_index("dp")
    core = dp % 2
    place = jnp.stack([t ^ k for k in range(SECTIONS)] + [core, 1 - core, dp // 2, dp, dp % 4]).astype(jnp.int32)
    cells = CROPS * PLACES * images
    rows = micro * cells
    count = float(cells * ndp)
    packed = section_weights[0]
    norm3 = section_norms[0]
    param_rows = packed.shape[0]
    own = WIDTH // ndp
    k = functools.partial

    def pieces_of(width, dtype):
        return shape((rows, width), dtype)

    own_message, *messages = pack(place, packed, norm3)
    came = [own_message]
    for j in range(1, SECTIONS):
        came.append(lax.ppermute(messages[j - 1], "section", [(u, u ^ j) for u in range(3)]))
    flat = call(
        retile_kernel, shape((rows, D), BF16),
        image.transpose(0, 1, 3, 4, 2, 5).reshape(rows // images, images, D),
        us=2,
    )
    queue_size = CROPS * queue.shape[1]
    note = call(note_kernel, shape((queue_size + 16, PROJ), BF16), pairing, queue, us=0.5)
    told, told_offsets = gather_dp(note, dp_stages())
    *came, flat, told[0] = lax.optimization_barrier((*came, flat, *told))[:6]
    conv_part, pair_part = call(
        pick_kernel,
        (shape((QUARTER_CONV, PART), BF16), shape((HALF_REDUCE + 4 * HALF_EXPAND, PART), BF16)),
        place, *came,
    )
    pair_parts = (pair_part, flip(pair_part, "dp", 1))
    conv_near = flip(conv_part, "dp", 2)
    sums_of = shape((8, PART), F32)
    pre0, part = call(
        k(reduce_kernel, micro), (pieces_of(PART, F32), sums_of), place, flat, *pair_parts, us=2
    )
    sums0 = sum_dp(part)
    active0 = call(k(active_kernel, micro, count), pieces_of(PART, BF16), pre0, sums0, pair_part, us=1)
    actives0 = gather_xor(active0, "section")

    conv_part = rows_of([conv_part, after(conv_near, active0)])
    w_conv = (conv_part, flip(conv_part, "dp", 1))
    w_proj, table = pl.pallas_call(
        tables_kernel,
        name="tables",
        out_shape=(shape((D, PROJ), BF16), shape((QUARTER_PAD, WIDTH), BF16)),
        in_specs=[pl.BlockSpec(memory_space=pltpu.HBM)],
        out_specs=(pl.BlockSpec(memory_space=pltpu.VMEM), pl.BlockSpec(memory_space=pltpu.VMEM)),
        scratch_shapes=[
            pltpu.VMEM((THIRD - FIRST + 2, WIDTH), BF16), pltpu.VMEM((D, PROJ), F32), pltpu.SemaphoreType.DMA,
        ],
        compiler_params=pltpu.CompilerParams(vmem_limit_bytes=12 * 2**20),
        cost_estimate=cost(1.5),
    )(hbm(after(packed, active0)))
    head_rows = rows // PLACES * ndp
    lanes = 4 * QUARTER_PAD
    stages = dp_stages()
    head_stages = stages[1:] + stages[:1]
    offsets = [0]
    for steps in head_stages:
        offsets = offsets + [o ^ step for step in steps for o in offsets]
    small = head_rows <= 128 and images * ndp == 32 and queue.shape[1] * ndp <= 512
    if small:
        queued = ndp * queue.shape[1]
        mass, column, match = call(
            k(mass_kernel, micro, images, sum(told_offsets, [])),
            (
                shape((queued, lanes), BF16), shape((8, lanes), F32),
                shape((micro, images * ndp, images * ndp), BF16),
            ),
            place, table, *told,
            scratch=[pltpu.VMEM((queued, PROJ), BF16), pltpu.VMEM((queued, lanes), F32)],
            vmem=16, us=5,
        )
        *actives0, mass = lax.optimization_barrier((*actives0, mass))
    pre1, part = call(
        k(conv_kernel, micro, images),
        (pieces_of(PART, F32), sums_of),
        place, *actives0, *w_conv,
        scratch=[pltpu.VMEM((rows, WIDTH), BF16), pltpu.VMEM((WIDTH, 9 * PART), BF16)],
        us=3,
    )
    sums1 = sum_dp(part)
    active1_own = call(k(active_kernel, micro, count), pieces_of(PART, BF16), pre1, sums1, conv_part, us=1)
    actives1 = gather_xor(active1_own, "section")
    natural = unpack(after(packed, active1_own), FIRST)
    taps = call(k(taps_kernel, images), pieces_of(9 * PART, BF16), after(active0, active1_own), us=1.3)
    *actives1, natural, taps = lax.optimization_barrier((*actives1, natural, taps))
    active1, pre2, part, w_expand = call(
        k(expand_kernel, micro),
        (pieces_of(WIDTH, BF16), pieces_of(WIDE, F32), shape((8, WIDE), F32), shape((WIDTH, WIDE), BF16)),
        place, *actives1, *pair_parts,
        us=2,
    )
    back_rows = 9 * PART // 2 + WIDE // 2
    back_own = call(
        back_parts_kernel, [shape((back_rows, PART), BF16)] * 4, place, *w_conv, *pair_parts, us=1
    )
    back_own = lax.optimization_barrier((*back_own, part))[:4]
    back_came = [back_own[0]] + [flip(back_own[j], "section", j) for j in range(1, SECTIONS)]

    sums2 = sum_dp(part)
    pooled = call(
        k(pool_kernel, micro, images, count),
        shape((rows // PLACES, WIDE), BF16),
        place, pre2, sums2, pair_part, flat,
        us=1.6,
    )

    per_dp = rows // PLACES
    came_p = gather_xor(pooled, "section")[::-1]
    pooled_here = call(lanes_kernel, shape((per_dp, D), BF16), *came_p, us=0.3)
    parts, _ = gather_dp(pooled_here, head_stages)
    if small:
        all_pooled, active3, unit, d_scores, embed, *kept, said = call(
            k(head_kernel, micro, images, offsets),
            [
                shape((head_rows, D), BF16), shape((head_rows, D), BF16), shape((head_rows, PROJ), BF16),
                shape((head_rows // 2, lanes), BF16), shape((head_rows, PROJ), F32), shape((head_rows, D), F32),
                shape((head_rows, D), F32), shape((8, D), F32), shape((head_rows // 2 + 8, PROJ), F32),
            ],
            place, *parts, natural, w_proj, table, norm3, mass, column, match,
            scratch=[
                pltpu.VMEM((head_rows, lanes), F32), pltpu.VMEM((head_rows // 2, lanes), F32),
                pltpu.VMEM((micro, 8, lanes), F32), pltpu.VMEM((8, lanes), F32),
            ],
            vmem=15, us=12,
        )
        *d_pooled, notes3, d_embed, d_pre3 = call(
            k(head_back_kernel, micro, images, ndp),
            [shape((per_dp, WIDE), BF16)] * 4
            + [shape((8, D), F32), shape((head_rows, PROJ), BF16), shape((head_rows, D), BF16)],
            place, said, flip(said, "dp", 1), embed, w_proj, natural, norm3, *kept,
            scratch=[pltpu.VMEM((head_rows, PROJ), F32), pltpu.VMEM((per_dp, D), BF16)],
            us=5,
        )
    else:
        all_pooled = jnp.concatenate(parts)
        offset = jnp.array(offsets, jnp.int32)
        head_order = jnp.arange(head_rows, dtype=jnp.int32)
        block, inner = head_order // per_dp, head_order % per_dp
        group, single = inner // images, inner % images
        position = (group * ndp + (offset[block] ^ dp)) * images + single
        order = (position[None, :] == head_order[:, None]).astype(BF16)
        told = jnp.concatenate(told).reshape(ndp, queue_size + 16, PROJ)
        pairs = told[:, queue_size : queue_size + micro, :images].astype(jnp.int32)
        told_offset = jnp.array(sum(told_offsets, []), jnp.int32)
        pairs_dp = (told_offset ^ dp)[None, :] == jnp.arange(ndp, dtype=jnp.int32)[:, None]
        pairs = jnp.sum(jnp.where(pairs_dp[:, :, None, None], pairs[None], 0), axis=1)
        left = jnp.arange(images * ndp, dtype=jnp.int32)
        pairs = pairs.transpose(1, 0, 2).reshape(micro, ndp * images)
        match = ((left // images * images + pairs)[:, :, None] == left[None, None, :]).astype(F32)
        all_pooled = dot(order, all_pooled).astype(BF16)
        protos = jnp.concatenate([table[:, a * PROJ : (a + 1) * PROJ] for a in range(4)], axis=0)
        queue_all = told[:, :queue_size].reshape(ndp, CROPS, queue.shape[1], PROJ)
        queue_rows = queue_all.transpose(1, 0, 2, 3).reshape(CROPS, -1, PROJ)
        loss, grads3, active3, unit, d_scores, d_embed, d_pre3 = head(
            all_pooled, natural, w_proj, protos, norm3, queue_rows, match, micro, images, dp
        )
        notes3 = jnp.concatenate([grads3, jnp.full((5, D), loss)])
        d_pooled = dot_nt(dot_tn(order[:, :per_dp], d_pre3).astype(BF16), natural).astype(BF16)
        d_pooled = [d_pooled[:, j * WIDE : (j + 1) * WIDE] for j in range(SECTIONS)]
        d_scores = d_scores.reshape(micro, CROPS, head_rows // 4, lanes)
        d_scores = lax.dynamic_index_in_dim(d_scores, 1 - core, 1, keepdims=False).reshape(-1, lanes)

    came_d = [send(d_pooled[j], 3, j) for j in range(3)]
    back_half = call(stack_kernel, shape((SECTIONS, back_rows, PART), BF16), *back_came, us=0.6)
    back_halves = (back_half, flip(back_half, "dp", 1))
    d_z, part = call(
        k(out_back_kernel, micro, images, count),
        (pieces_of(WIDE, F32), shape((8, WIDE), F32)),
        place, pre2, sums2, pair_part, flat, d_pooled[3], *came_d,
        us=1.8,
    )
    back2 = sum_dp(part)
    d_pre2, *partial = call(
        k(expand_back_kernel, micro, count),
        [pieces_of(WIDE, BF16)] + [pieces_of(PART, BF16)] * 4,
        place, pre2, sums2, d_z, back2, pair_part, w_expand,
        scratch=[pltpu.VMEM((rows, WIDTH), F32)],
        us=2,
    )
    partial = [partial[0]] + [flip(partial[j], "section", j) for j in range(1, SECTIONS)]

    def scatter_start(a, b, width):
        if ndp != 8:
            return dot_tn(a, b)
        keep, out = call(
            pair_kernel,
            (shape((4, own, width), F32), shape((4, own, width), BF16)),
            place, a, b,
            scratch=[pltpu.VMEM((WIDTH, width), F32)],
            us=2.5,
        )
        return keep, flip(out, "dp", 1)

    def scatter_cross(started, *others):
        if ndp != 8:
            return [lax.psum_scatter(started.astype(BF16), "dp", scatter_dimension=0, tiled=True)]
        keep, came = started
        if others:
            keep = after(keep, *others)
        dims = keep.shape[1:]
        kept, *out = call(
            cross_kernel, [shape(dims, F32)] + [shape(dims, BF16)] * 3, place, keep, came
        )
        return [kept] + [flip(out[j], "dp", 2 * (j + 1)) for j in range(3)]

    def scatter_finish(crossed):
        if ndp != 8:
            return crossed[0].astype(BF16)
        return call(add_kernel, shape(crossed[0].shape, BF16), *crossed, us=0.6)

    expand_started = scatter_start(d_pre2, active1, WIDTH)
    base = call(
        head_grads_kernel,
        shape((own, param_rows), F32),
        place, after(all_pooled, d_pre2), active3, unit, d_scores, flip(d_scores, "dp", 1), d_embed, d_pre3,
        scratch=[pltpu.VMEM((4, own, D), BF16), pltpu.VMEM((4, all_pooled.shape[0], WIDTH), BF16)],
        us=6,
    )
    partial = lax.optimization_barrier((*partial, base))[:4]

    d_y1, part = call(
        k(silu_back_kernel, micro, count),
        (pieces_of(PART, F32), sums_of),
        *partial, pre1, sums1, conv_part,
    )
    back1 = sum_dp(part)
    d_pre1_own = call(
        k(norm_back_kernel, micro, count), pieces_of(PART, BF16), d_y1, pre1, sums1, back1, conv_part
    )
    d_pre1s = gather_xor(d_pre1_own, "section")
    expand_crossed = scatter_cross(expand_started, d_pre1_own)
    joined = lax.optimization_barrier((*d_pre1s, *expand_crossed))
    d_pre1s, expand_crossed = joined[:SECTIONS], joined[SECTIONS:]
    d_pre1, d_y0, part = call(
        k(conv_back_kernel, micro, images, count),
        (pieces_of(WIDTH, BF16), pieces_of(PART, F32), sums_of),
        place, *d_pre1s, *back_halves, pre0, sums0, pair_part,
        scratch=[pltpu.VMEM((9 * PART, WIDTH), BF16)],
        us=3.5,
    )
    back0, paired = sum_dp_steps(part)
    conv_started = scatter_start(after(d_pre1, paired), taps, 9 * PART)
    d_pre0_own = call(
        k(last_norm_back_kernel, micro, count),
        shape((rows + NOTE_ROWS, PART), BF16),
        place, d_y0, pre0, sums0, back0, pair_part, back2, back1, notes3,
    )
    d_pre0s = gather_xor(d_pre0_own, "section")
    conv_crossed = scatter_cross(conv_started, d_pre0_own)
    joined = lax.optimization_barrier((*d_pre0s, *conv_crossed))
    d_pre0s, conv_crossed = joined[:SECTIONS], joined[SECTIONS:]

    if ndp == 8:
        keep, out, d_pre0 = call(
            image_pair_kernel,
            (shape((4, own, WIDE), F32), shape((4, own, WIDE), BF16), pieces_of(WIDTH, BF16)),
            place, *d_pre0s, flat,
            scratch=[pltpu.VMEM((WIDTH, WIDE), F32)],
            us=2.5,
        )
        reduce_started = keep, flip(out, "dp", 1)
    else:
        d_pre0 = jnp.stack(d_pre0s)[place[:SECTIONS], :rows].transpose(1, 0, 2).reshape(rows, WIDTH)
        reduce_started = dot_tn(d_pre0, lax.dynamic_slice_in_dim(flat, t * WIDE, WIDE, 1))
    reduce_crossed = scatter_cross(reduce_started)
    grad_in = call(
        reduce_back_kernel,
        shape((rows // images, images, WIDE), F32),
        place, d_pre0, *back_halves, d_z,
        scratch=[pltpu.VMEM((WIDE, WIDTH), BF16)],
        us=2,
    )
    norm_grads, loss = call(
        told_kernel, (shape((3, D), F32), shape((8, PROJ), F32)), place, *d_pre0s, notes3, us=0.5
    )
    g_conv = scatter_finish(conv_crossed)
    g_expand = scatter_finish(expand_crossed)
    joined = lax.optimization_barrier((*reduce_crossed, grad_in, norm_grads, g_conv, g_expand))
    *reduce_crossed, grad_in, norm_grads, g_conv, g_expand = joined
    g_reduce = scatter_finish(reduce_crossed)
    mixed = call(mixed_kernel, [shape(g_conv.shape, BF16)] * 3, place, g_reduce, g_conv, g_expand, us=0.3)
    mixed = [
        lax.ppermute(mixed[j - 1], "section", [(u ^ j, u) for u in range(3)]) for j in range(1, SECTIONS)
    ]
    weight_grads = pl.pallas_call(
        finish_kernel,
        name="finish",
        out_shape=shape((own, param_rows), F32),
        in_specs=[pl.BlockSpec(memory_space=pltpu.SMEM), pl.BlockSpec(memory_space=pltpu.HBM)]
        + [pl.BlockSpec(memory_space=pltpu.VMEM)] * 6,
        out_specs=pl.BlockSpec(memory_space=pltpu.HBM),
        scratch_shapes=[pltpu.VMEM((own, 9 * WIDTH), F32), pltpu.SemaphoreType.DMA],
        input_output_aliases={1: 0},
        compiler_params=pltpu.CompilerParams(vmem_limit_bytes=12 * 2**20),
        cost_estimate=cost(2),
    )(place, base, g_reduce, g_conv, g_expand, *mixed)
    grad_in = grad_in.reshape(micro, CROPS, SIDE, SIDE, images, WIDE).transpose(0, 1, 4, 2, 3, 5)
    return (loss[0, 0], grad_in, weight_grads.T[None], norm_grads[None])


def solution(mesh):
    in_specs = (
        P(None, None, "dp", None, None, None),
        P("section", None, None),
        P("section", None, None),
        P(None, "dp", None),
        P(None, "dp"),
    )
    out_specs = (
        P(),
        P(None, None, "dp", None, None, "section"),
        P("section", None, "dp"),
        P("section", None, None),
    )
    return jax.shard_map(body, mesh=mesh, in_specs=in_specs, out_specs=out_specs, check_vma=False)
```

```python
import functools

import jax
import jax.numpy as jnp
from jax import lax
from jax.experimental import pallas as pl
from jax.experimental.pallas import tpu as pltpu
from jax.sharding import PartitionSpec as P

D = 2048
WIDTH = 512
PROJ = 128
PROTOS = 3000
SIDE = 7
CROPS = 2
SECTIONS = 4
PART = WIDTH // SECTIONS
WIDE = D // SECTIONS
QUARTER = PROTOS // 4
QUARTER_PAD = 768
PLACES = SIDE * SIDE
FIRST = D * (D // WIDTH)
SECOND = FIRST + D * PROJ // WIDTH
THIRD = SECOND + PROTOS * PROJ // WIDTH
HALF_REDUCE = 16 + D // 2
HALF_EXPAND = 16 + WIDTH // 2
QUARTER_CONV = 16 + 9 * WIDTH // 4
NOTE_ROWS = 48

NORM_EPS = 1e-05
UNIT_EPS = 1e-06
SINK_EPS = 0.05
TEMPER = 0.1
HIGH = lax.Precision.HIGHEST
F32 = jnp.float32
BF16 = jnp.bfloat16
NT = (((1,), (1,)), ((), ()))
TN = (((0,), (0,)), ((), ()))


def dot(a, b):
    return jnp.dot(a, b, preferred_element_type=F32)


def dot_nt(a, b):
    return lax.dot_general(a, b, NT, preferred_element_type=F32)


def dot_tn(a, b):
    return lax.dot_general(a, b, TN, preferred_element_type=F32)


def flip(value, axis, step):
    count = lax.axis_size(axis)
    return lax.ppermute(value, axis, [(source, source ^ step) for source in range(count)])


def send(value, source, target):
    return lax.ppermute(value, "section", [(source, target)])


def sum_dp_steps(value):
    count = lax.axis_size("dp")
    value = pair = value + flip(value, "dp", 1)
    step = 2
    while step < count:
        if 2 * step < count:
            near = value + flip(value, "dp", step)
            far = flip(value, "dp", 2 * step) + flip(value, "dp", 3 * step)
            value = near + far
            step *= 4
        else:
            value = value + flip(value, "dp", step)
            step *= 2
    return value, pair


def sum_dp(value):
    return sum_dp_steps(value)[0]


def gather_xor(value, axis):
    return [value] + [flip(value, axis, step) for step in range(1, lax.axis_size(axis))]


def dp_stages():
    count = lax.axis_size("dp")
    stages, step = [(1,)], 2
    while step < count:
        if 2 * step < count:
            stages.append((step, 2 * step, 3 * step))
            step *= 4
        else:
            stages.append((step,))
            step *= 2
    return stages


def gather_dp(value, stages):
    arrays, offsets = [value], [[0]]
    for steps in stages:
        if len(arrays) > 1:
            arrays, offsets = [rows_of(arrays)], [sum(offsets, [])]
        first = offsets[0]
        for step in steps:
            arrays.append(flip(arrays[0], "dp", step))
            offsets.append([o ^ step for o in first])
    return arrays, offsets


def sigmoid(v):
    return 1.0 / (1.0 + jnp.exp(-v))


def slope(v):
    s = sigmoid(v)
    return s * (1.0 + v * (1.0 - s))


def cost(us):
    return pl.CostEstimate(flops=0, bytes_accessed=int(us * 3_000_000), transcendentals=0)


def hbm(value):
    return pltpu.with_memory_space_constraint(value, pltpu.HBM)


def call(kernel, out, *args, scratch=(), vmem=12, us=1.0, in_hbm=()):
    in_specs, ins = [], []
    for j, a in enumerate(args):
        space = pltpu.VMEM
        if jnp.issubdtype(a.dtype, jnp.integer):
            space = pltpu.SMEM
        elif j in in_hbm:
            space = pltpu.HBM
            a = hbm(a)
        in_specs.append(pl.BlockSpec(memory_space=space))
        ins.append(a)
    return pl.pallas_call(
        kernel,
        name=getattr(kernel, 'func', kernel).__name__,
        out_shape=out,
        in_specs=in_specs,
        out_specs=jax.tree.map(lambda _: pl.BlockSpec(memory_space=pltpu.VMEM), out),
        scratch_shapes=list(scratch),
        compiler_params=pltpu.CompilerParams(vmem_limit_bytes=vmem * 2**20),
        cost_estimate=cost(us),
    )(*ins)


def shape(dims, dtype):
    return jax.ShapeDtypeStruct(tuple(dims), dtype)


def retile_kernel(image, flat):
    flat[...] = image[...].reshape(flat.shape)


def note_kernel(pairing, queue, out):
    size = queue.shape[1]
    for c in range(CROPS):
        out[c * size : (c + 1) * size, :] = queue[c]
    row = lax.broadcasted_iota(jnp.int32, (16, PROJ), 0)
    lane = lax.broadcasted_iota(jnp.int32, (16, PROJ), 1)
    value = jnp.zeros((16, PROJ), F32)
    for m in range(pairing.shape[0]):
        for i in range(pairing.shape[1]):
            value = jnp.where((row == m) & (lane == i), pairing[m, i].astype(F32), value)
    out[CROPS * size :, :] = value.astype(BF16)


def rows_kernel(*refs):
    out, at = refs[-1], 0
    for ref in refs[:-1]:
        out[at : at + ref.shape[0], :] = ref[...]
        at += ref.shape[0]


def lanes_kernel(*refs):
    out, at = refs[-1], 0
    for ref in refs[:-1]:
        out[:, at : at + ref.shape[1]] = ref[...]
        at += ref.shape[1]


def rows_of(values, us=0.5):
    rows = sum(v.shape[0] for v in values)
    return call(rows_kernel, shape((rows, values[0].shape[1]), values[0].dtype), *values, us=us)


def split_sums(first, second, micro):
    width = first[0].shape[1]
    rows = [jnp.sum(v, axis=0, keepdims=True) for v in first]
    rows += [jnp.sum(v, axis=0, keepdims=True) for v in second]
    rows.append(jnp.zeros((8 - 2 * micro, width), F32))
    return jnp.concatenate(rows, axis=0)


def moments(sums, m, micro, count):
    mean = sums[m : m + 1] * (1.0 / count)
    square = sums[micro + m : micro + m + 1] * (1.0 / count)
    return mean, lax.rsqrt(square - mean * mean + NORM_EPS)


def per_micro(value, micro):
    rows = value.shape[0] // micro
    return [value[m * rows : (m + 1) * rows] for m in range(micro)]


def normalized(value, sums, micro, count):
    out = []
    for m, v in enumerate(per_micro(value, micro)):
        mean, rstd = moments(sums, m, micro, count)
        out.append(((v - mean) * rstd, rstd))
    return out


def join(parts):
    return jnp.concatenate(parts, axis=0)


def tap_valid(rows, images, tap, sign):
    row = lax.broadcasted_iota(jnp.int32, (rows, PART), 0).astype(F32)
    cell = jnp.floor((row + 0.5) * (1.0 / images))
    crop = jnp.floor((cell + 0.5) * (1.0 / PLACES))
    place = cell - crop * PLACES
    y = jnp.floor((place + 0.5) * (1.0 / SIDE))
    x = place - y * SIDE
    y = y + float(sign * (tap // 3 - 1))
    x = x + float(sign * (tap % 3 - 1))
    return (y > -0.5) & (y < SIDE - 0.5) & (x > -0.5) & (x < SIDE - 0.5)


def tap_shift(value, images, tap, sign):
    rows = value.shape[0]
    offset = sign * images * (SIDE * (tap // 3 - 1) + (tap % 3 - 1))
    moved = value if offset == 0 else pltpu.roll(value, (-offset) % rows, 0)
    if tap == 4:
        return moved
    return jnp.where(tap_valid(rows, images, tap, sign), moved, 0.0)


def told_norm(message, at=0):
    rows = message[at : at + 16, :].astype(F32)
    return rows[0:1] + rows[1:2] + rows[2:3], rows[3:4] + rows[4:5] + rows[5:6]


def told_wide(message):
    parts = [told_norm(message, HALF_REDUCE + b * HALF_EXPAND) for b in range(4)]
    return tuple(jnp.concatenate(p, axis=1) for p in zip(*parts))


def terms(row):
    out = []
    for _ in range(3):
        term = row.astype(BF16).astype(F32)
        out.append(term)
        row = row - term
    return out


def tell_norm(rows):
    out = terms(rows[0:1]) + terms(rows[1:2])
    out.append(jnp.zeros((10, rows.shape[1]), F32))
    return jnp.concatenate(out, axis=0).astype(BF16)


def reduce_kernel(micro, place, image, w0, w1, pre, sums):
    half = D // 2
    first = pl.ds(pl.multiple_of(place[4] * half, half), half)
    second = pl.ds(pl.multiple_of(place[5] * half, half), half)
    value = dot(image[:, first], w0[16 : 16 + half, :]) + dot(image[:, second], w1[16 : 16 + half, :])
    pre[...] = value
    parts = per_micro(value, micro)
    sums[...] = split_sums(parts, [v * v for v in parts], micro)


def active_kernel(micro, count, pre, sums, told, active):
    gain, shift = told_norm(told)
    out = []
    for xhat, _ in normalized(pre[...], sums[...], micro, count):
        y = xhat * gain + shift
        out.append(y * sigmoid(y))
    active[...] = join(out).astype(BF16)


def fill(place, pieces, full):
    for k, piece in enumerate(pieces):
        full[:, pl.ds(pl.multiple_of(place[k] * PART, PART), PART)] = piece[: full.shape[0], :]


def quarter_of(place, j):
    return place[8] ^ (0, 2, 1, 3)[j]


def conv_kernel(micro, images, place, a0, a1, a2, a3, wa, wb, pre, sums, full, weight):
    fill(place, (a0, a1, a2, a3), full)
    quarter = WIDTH // 4
    for j in range(4):
        w = (wa, wb)[j // 2]
        at = pl.multiple_of(quarter_of(place, j) * quarter, quarter)
        for tap in range(9):
            lanes = slice(tap * PART, (tap + 1) * PART)
            first = (j % 2) * QUARTER_CONV + 16 + tap * quarter
            weight[pl.ds(at, quarter), lanes] = w[first : first + quarter, :]
    total = None
    for first in range(0, 9, 2):
        taps = [tap for tap in (first, first + 1) if tap < 9]
        part = dot(full[...], weight[:, first * PART : (taps[-1] + 1) * PART])
        for j, tap in enumerate(taps):
            moved = tap_shift(part[:, j * PART : (j + 1) * PART], images, tap, 1)
            total = moved if total is None else total + moved
    pre[...] = total
    parts = per_micro(total, micro)
    sums[...] = split_sums(parts, [v * v for v in parts], micro)


def expand_kernel(micro, place, a0, a1, a2, a3, w0, w1, active, pre, sums, weight):
    fill(place, (a0, a1, a2, a3), active)
    half = WIDTH // 2
    for j, w in enumerate((w0, w1)):
        rows = pl.ds(pl.multiple_of(place[4 + j] * half, half), half)
        for b in range(4):
            at = HALF_REDUCE + b * HALF_EXPAND + 16
            weight[rows, b * PART : (b + 1) * PART] = w[at : at + half, :]
    value = dot(active[...], weight[...])
    pre[...] = value
    parts = per_micro(value, micro)
    sums[...] = split_sums(parts, [v * v for v in parts], micro)


def crop_rows(rows, images, transpose=False):
    shp = (rows // PLACES, rows)
    r = lax.broadcasted_iota(jnp.int32, shp, 1).astype(F32)
    q = lax.broadcasted_iota(jnp.int32, shp, 0).astype(F32)
    cell = jnp.floor((r + 0.5) * (1.0 / images))
    crop = jnp.floor((cell + 0.5) * (1.0 / PLACES))
    image = r - cell * images
    return (jnp.abs(crop * images + image - q) < 0.5).astype(F32).astype(BF16)


def pool_kernel(micro, images, count, place, pre, sums, told, image, pooled):
    lanes = pl.ds(pl.multiple_of(place[0] * WIDE, WIDE), WIDE)
    gain, shift = told_wide(told)
    out = []
    for xhat, _ in normalized(pre[...], sums[...], micro, count):
        out.append(xhat * gain + shift)
    z = join(out) + image[:, lanes].astype(F32)
    out = z * sigmoid(z)
    high = out.astype(BF16)
    low = (out - high.astype(F32)).astype(BF16)
    choose = crop_rows(pre.shape[0], images)
    pooled[...] = ((dot(choose, high) + dot(choose, low)) * (1.0 / PLACES)).astype(BF16)


def out_back_kernel(micro, images, count, place, pre, sums, told, image, own, r0, r1, r2, d_z, sums_out):
    lanes = pl.ds(pl.multiple_of(place[0] * WIDE, WIDE), WIDE)
    rows = pre.shape[0]
    gain, shift = told_wide(told)
    d_pooled = own[...].astype(F32)
    for k, came in enumerate((r0, r1, r2)):
        d_pooled = jnp.where(place[k + 1] == SECTIONS - 1, came[...].astype(F32), d_pooled)
    d_pooled = d_pooled.astype(BF16)
    spread = dot_tn(crop_rows(rows, images), d_pooled) * (1.0 / PLACES)
    xhats = [x for x, _ in normalized(pre[...], sums[...], micro, count)]
    z = join([x * gain + shift for x in xhats]) + image[:, lanes].astype(F32)
    value = spread * slope(z)
    d_z[...] = value
    parts = per_micro(value, micro)
    sums_out[...] = split_sums([v * x for v, x in zip(parts, xhats)], parts, micro)


def norm_back(value, pre, sums, back, gain, micro, count):
    out = []
    parts = per_micro(value, micro)
    for m, (xhat, rstd) in enumerate(normalized(pre, sums, micro, count)):
        by_x = back[m : m + 1] * (1.0 / count)
        plain = back[micro + m : micro + m + 1] * (1.0 / count)
        out.append(gain * rstd * (parts[m] - plain - xhat * by_x))
    return join(out)


def norm_back_kernel(micro, count, d_y, pre, sums, back, told, d_pre):
    gain, _ = told_norm(told)
    d_pre[...] = norm_back(d_y[...], pre[...], sums[...], back[...], gain, micro, count).astype(BF16)


def over_micro(back, micro):
    out = []
    for r in range(2):
        row = back[r * micro : r * micro + 1, :]
        for m in range(1, micro):
            row = row + back[r * micro + m : r * micro + m + 1, :]
        out.append(row)
    return out


def last_norm_back_kernel(micro, count, place, d_y, pre, sums, back, told, back2, back1, notes, d_pre):
    gain, _ = told_norm(told)
    rows = d_y.shape[0]
    d_pre[:rows, :] = norm_back(d_y[...], pre[...], sums[...], back[...], gain, micro, count).astype(BF16)
    said = []
    for row in over_micro(back2, micro):
        said += [row[:, b * PART : (b + 1) * PART] for b in range(4)]
    said += over_micro(back1, micro) + over_micro(back, micro)
    said.append(jnp.where(place[0] == SECTIONS - 1, notes[3:4, :PART], 0.0))
    said = sum([terms(row) for row in said], [])
    said.append(jnp.zeros((NOTE_ROWS - len(said), PART), F32))
    d_pre[rows:, :] = jnp.concatenate(said, axis=0).astype(BF16)


def expand_back_kernel(micro, count, place, pre, sums, d_z, back, told, weight, d_pre, q0, q1, q2, q3, full):
    gain, _ = told_wide(told)
    d_low = norm_back(d_z[...], pre[...], sums[...], back[...], gain, micro, count).astype(BF16)
    d_pre[...] = d_low
    full[...] = dot_nt(d_low, weight[...])
    for k, q in enumerate((q0, q1, q2, q3)):
        lanes = pl.ds(pl.multiple_of(place[k] * PART, PART), PART)
        q[...] = full[:, lanes].astype(BF16)


def finish_silu(micro, count, d_active, pre, sums, norm, d_y, sums_out):
    gain, shift = norm
    values, products = [], []
    parts = per_micro(d_active, micro)
    for m, (xhat, _) in enumerate(normalized(pre[...], sums[...], micro, count)):
        value = parts[m] * slope(xhat * gain + shift)
        values.append(value)
        products.append(value * xhat)
    d_y[...] = join(values)
    sums_out[...] = split_sums(products, values, micro)


def silu_back_kernel(micro, count, q0, q1, q2, q3, pre, sums, told, d_y, sums_out):
    total = (q0[...].astype(F32) + q1[...].astype(F32)) + (q2[...].astype(F32) + q3[...].astype(F32))
    d_active = total.astype(BF16).astype(F32)
    finish_silu(micro, count, d_active, pre, sums, told_norm(told), d_y, sums_out)


def conv_back_kernel(
    micro, images, count, place, d0, d1, d2, d3, back0, back1, pre, sums, told, d_full, d_y, sums_out, weight
):
    fill(place, (d0, d1, d2, d3), d_full)
    d_low = d_full[...]
    half = PART // 2
    for j, back in enumerate((back0, back1)):
        for k in range(SECTIONS):
            lanes = pl.ds(pl.multiple_of(place[k] * PART, PART), PART)
            for tap in range(9):
                rows = pl.ds(pl.multiple_of(tap * PART + place[4 + j] * half, half), half)
                weight[rows, lanes] = back[k, tap * half : (tap + 1) * half, :]
    total = None
    for first in range(0, 9, 2):
        taps = [tap for tap in (first, first + 1) if tap < 9]
        part = dot_nt(d_low, weight[first * PART : (taps[-1] + 1) * PART, :])
        for j, tap in enumerate(taps):
            moved = tap_shift(part[:, j * PART : (j + 1) * PART], images, tap, -1)
            total = moved if total is None else total + moved
    d_active = total.astype(BF16).astype(F32)
    finish_silu(micro, count, d_active, pre, sums, told_norm(told), d_y, sums_out)


def reduce_back_kernel(place, d_full, back0, back1, d_z, grad_in, weight):
    half = WIDE // 2
    first = 9 * PART // 2
    for j, back in enumerate((back0, back1)):
        rows = pl.ds(pl.multiple_of(place[4 + j] * half, half), half)
        for k in range(SECTIONS):
            lanes = pl.ds(pl.multiple_of(place[k] * PART, PART), PART)
            weight[rows, lanes] = back[k, first : first + half, :]
    main = dot_nt(d_full[...], weight[...]).astype(BF16).astype(F32)
    value = main + d_z[...].astype(BF16).astype(F32)
    grad_in[...] = value.reshape(grad_in.shape)


def back_parts_kernel(place, conv_a, conv_b, reduce0, reduce1, *outs):
    half = PART // 2
    wide = WIDE // 2
    first = 9 * half
    quarter = WIDTH // 4
    for k, out in enumerate(outs):
        for core in range(2):
            for j in range(4):
                conv = (conv_a, conv_b)[j // 2]

                @pl.when((place[k] == quarter_of(place, j)) & (place[4] == core))
                def _():
                    for tap in range(9):
                        at = (j % 2) * QUARTER_CONV + 16 + tap * quarter + core * half
                        out[tap * half : (tap + 1) * half, :] = conv[at : at + half, :]

            for u in range(SECTIONS):
                reduce = (reduce0, reduce1)[core ^ (u // 2)]

                @pl.when((place[k] == u) & (place[4] == core))
                def _():
                    at = 16 + (u % 2) * WIDE + core * wide
                    out[first : first + wide, :] = reduce[at : at + wide, :]


def stack_kernel(*refs):
    out = refs[-1]
    rows = refs[0].shape[0]
    for j, ref in enumerate(refs[:-1]):
        if len(out.shape) == 3:
            out[j] = ref[...]
        else:
            out[j * rows : (j + 1) * rows, :] = ref[...]


def mixed_kernel(place, reduce, conv, expand, *outs):
    for k, out in enumerate(outs):
        target = place[k + 1]

        @pl.when(target == 0)
        def _():
            out[:, :WIDE] = reduce[...]

        @pl.when(target == 1)
        def _():
            out[...] = conv[...]

        @pl.when(target == 2)
        def _():
            out[:, :WIDE] = expand[...]


def told_kernel(place, n0, n1, n2, n3, notes, out, loss):
    t = place[0]
    out[...] = jnp.zeros_like(out)

    @pl.when(t == SECTIONS - 1)
    def _():
        out[...] = notes[:3, :]

    total = None
    for k, note in enumerate((n0, n1, n2, n3)):
        u = place[k]
        rows = note[note.shape[0] - NOTE_ROWS :, :].astype(F32)

        def said(i):
            return (rows[3 * i : 3 * i + 1] + rows[3 * i + 1 : 3 * i + 2]) + rows[3 * i + 2 : 3 * i + 3]

        total = said(12) if total is None else total + said(12)

        @pl.when(t == 2)
        def _():
            for r in range(2):
                for b in range(4):
                    lanes = pl.ds(pl.multiple_of(u * WIDE + b * PART, PART), PART)
                    out[r : r + 1, lanes] = said(4 * r + b)

        for section in range(2):

            @pl.when(t == section)
            def _():
                for r in range(2):
                    lanes = pl.ds(pl.multiple_of(u * PART, PART), PART)
                    out[r : r + 1, lanes] = said((10, 8)[section] + r)

    loss[...] = jnp.broadcast_to(total, loss.shape)


def pick_kernel(place, p0, p1, p2, p3, conv, pair):
    for j, p in enumerate((p0, p1, p2, p3)):

        @pl.when(place[0] == j)
        def _():
            pair[:HALF_REDUCE, :] = p[:HALF_REDUCE, :]

        @pl.when(place[1] == j)
        def _():
            conv[...] = p[...]

        @pl.when(place[2] == j)
        def _():
            pair[HALF_REDUCE:, :] = p[: 4 * HALF_EXPAND, :]


def taps_kernel(images, active, out):
    value = active[...].astype(F32)
    for tap in range(9):
        out[:, tap * PART : (tap + 1) * PART] = tap_shift(value, images, tap, 1).astype(BF16)


def head(pooled, w_head, w_proj, protos, norm, queue, match, micro, images, dp):
    rows = pooled.shape[0]
    group = rows // micro
    half = group // CROPS
    scale_all = 1.0 / (TEMPER * CROPS * half * micro)
    pre = dot(pooled, w_head)

    def by_micro(v):
        return v.reshape(micro, group, v.shape[-1])

    pre_m = by_micro(pre)
    mean = jnp.mean(pre_m, axis=1, keepdims=True)
    square = jnp.mean(pre_m * pre_m, axis=1, keepdims=True)
    rstd = lax.rsqrt(square - mean * mean + NORM_EPS)
    xhat = (pre_m - mean) * rstd
    y = xhat * norm[0] + norm[1]
    active = (y * sigmoid(y)).astype(BF16).reshape(rows, D)
    embed = dot(active, w_proj) + norm[2, :PROJ]
    recip = lax.rsqrt(jnp.sum(embed * embed, axis=1, keepdims=True) + UNIT_EPS)
    unit = (embed * recip).astype(BF16)
    scores = dot_nt(unit, protos)
    valid = lax.broadcasted_iota(jnp.int32, (1, 4, QUARTER_PAD), 2).reshape(1, 4 * QUARTER_PAD) < QUARTER
    own_mass = jnp.where(valid, jnp.exp(scores / SINK_EPS), 0.0).reshape(micro, CROPS, half, -1)
    queue_mass = jnp.where(valid, jnp.exp(jnp.einsum("cqp,kp->cqk", queue, protos, preferred_element_type=F32) / SINK_EPS), 0.0)
    codes = []
    for m in range(micro):
        for c in range(CROPS):
            a, b = queue_mass[c], own_mass[m, c]
            column = jnp.sum(a, axis=0, keepdims=True) + jnp.sum(b, axis=0, keepdims=True)
            once = jnp.where(valid, 1.0 / column, 0.0)
            a, b = a * once, b * once
            scale = valid.astype(F32)
            for turn in range(2):
                ra = 1.0 / jnp.sum(a * scale, axis=1, keepdims=True)
                rb = 1.0 / jnp.sum(b * scale, axis=1, keepdims=True)
                column = jnp.sum(a * ra, axis=0, keepdims=True) + jnp.sum(b * rb, axis=0, keepdims=True)
                scale = jnp.where(valid, 1.0 / column, 0.0)
            b = b * scale
            codes.append(b / jnp.sum(b, axis=1, keepdims=True))
    targets = []
    for m in range(micro):
        targets.append(jnp.dot(match[m], codes[m * CROPS + 1], precision=HIGH))
        targets.append(jnp.dot(match[m].T, codes[m * CROPS], precision=HIGH))
    target = jnp.concatenate(targets)
    logits = jnp.where(valid, scores / TEMPER, -1e30)
    logp = jax.nn.log_softmax(logits, axis=1)
    loss = -jnp.sum(jnp.where(valid, target * logp, 0.0)) * (TEMPER * scale_all)
    d_scores = ((jnp.exp(logp) * jnp.sum(target, axis=1, keepdims=True) - target) * scale_all).astype(BF16)
    d_unit = dot(d_scores, protos)
    d_embed = (
        recip * d_unit - embed * (recip * recip * recip) * jnp.sum(d_unit * embed, axis=1, keepdims=True)
    ).astype(BF16)
    d_active = dot_nt(d_embed, w_proj)
    d_y = by_micro(d_active) * slope(y)
    by_x = jnp.sum(d_y * xhat, axis=1, keepdims=True)
    plain = jnp.sum(d_y, axis=1, keepdims=True)
    d_pre = (norm[0] * rstd * (d_y - plain / group - xhat * by_x / group)).astype(BF16).reshape(rows, D)
    bias = jnp.pad(jnp.sum(d_embed.astype(F32), axis=0), (0, D - PROJ))
    grads = jnp.stack([jnp.sum(by_x, axis=(0, 1)), jnp.sum(plain, axis=(0, 1)), bias])
    return loss, grads, active, unit, d_scores, d_embed, d_pre


def valid_lanes():
    lane = lax.broadcasted_iota(jnp.int32, (1, 4 * QUARTER_PAD), 1).astype(F32)
    block = jnp.floor((lane + 0.5) * (1.0 / QUARTER_PAD))
    return lane - block * QUARTER_PAD < QUARTER - 0.5


def lanes_at(b, size):
    return pl.ds(pl.multiple_of(b * size, size), size)


def lanes_at(b, size):
    return pl.ds(pl.multiple_of(b * size, size), size)


def mass_kernel(micro, images, told_offsets, place, table, *refs):
    mass, column, match, rows_s, exps = refs[-5:]
    ndp = len(told_offsets)
    valid = valid_lanes()
    size = mass.shape[0] // ndp
    half = images * ndp
    at, said = 0, jnp.zeros((16, half), F32)
    row = lax.broadcasted_iota(jnp.int32, (PROJ, half), 0)
    lane = lax.broadcasted_iota(jnp.int32, (PROJ, half), 1)
    for ref in refs[:-5]:
        rows = CROPS * size + 16
        for j in range(ref.shape[0] // rows):
            mine = pl.ds(pl.multiple_of(j * rows + place[4] * size, 16), size)
            rows_s[lanes_at(place[7] ^ told_offsets[at], size), :] = ref[mine, :]
            pairs = ref[(j + 1) * rows - 16 : (j + 1) * rows, :]
            spot_at = (place[7] ^ told_offsets[at]) * images
            spot = ((row < images) & (lane == row + spot_at)).astype(F32).astype(BF16)
            said = said + dot(pairs, spot)
            at += 1
    step = 128
    steps = mass.shape[0] // step

    def scored(i, sums):
        own = rows_s[lanes_at(i, step), :]
        out = []
        for a in range(4):
            lanes = slice(a * QUARTER_PAD, (a + 1) * QUARTER_PAD)
            value = jnp.exp(dot_nt(own, table[:, a * PROJ : (a + 1) * PROJ]) * (1.0 / SINK_EPS))
            value = jnp.where(valid[:, lanes], value, 0.0)
            exps[lanes_at(i, step), lanes] = value
            out.append(jnp.sum(value, axis=0, keepdims=True))
        return sums + jnp.concatenate(out, axis=1)

    sums = lax.fori_loop(0, steps, scored, jnp.zeros((1, 4 * QUARTER_PAD), F32))
    column[...] = jnp.broadcast_to(sums, column.shape)
    factor = jnp.where(valid, 1.0 / sums, 0.0)

    def divide(i, carry):
        mass[lanes_at(i, step), :] = (exps[lanes_at(i, step), :] * factor).astype(BF16)
        return carry

    lax.fori_loop(0, steps, divide, 0)

    def over(value, by):
        return jnp.floor((value + 0.5) * (1.0 / by))

    row = lax.broadcasted_iota(jnp.int32, (half, half), 0).astype(F32)
    lane = lax.broadcasted_iota(jnp.int32, (half, half), 1).astype(F32)
    block = over(row, images)
    for m in range(micro):
        same = (jnp.abs(block - over(lane, images)) < 0.5) & (jnp.abs(row - block * images - said[m : m + 1, :]) < 0.5)
        there = same.astype(F32)
        match[m] = jnp.where(place[4] == 0, there, there.T).astype(BF16)


def tables_kernel(packed, proj, table, rows, buffer, sem):
    size = THIRD - FIRST + 2
    copy = pltpu.make_async_copy(packed.at[pl.ds(FIRST, size), :], rows, sem)
    copy.start()
    copy.wait()
    wide = SECOND - FIRST
    for a in range(4):
        buffer[pl.ds(a, wide, stride=4), :] = rows[:wide, a * PROJ : (a + 1) * PROJ].astype(F32)
    proj[...] = buffer[...].astype(BF16)
    row = lax.broadcasted_iota(jnp.int32, (size - wide, WIDTH), 0)
    kept = jnp.where(row < QUARTER, rows[wide:, :].astype(F32), 0.0).astype(BF16)
    table[: size - wide, :] = kept
    table[size - wide :, :] = jnp.zeros((QUARTER_PAD - (size - wide), WIDTH), BF16)


def exact_dot(choose, value):
    parts, left = [], value
    for _ in range(3):
        term = left.astype(BF16)
        left = left - term.astype(F32)
        parts.append(term)
    return dot(jnp.concatenate([choose] * 3, axis=1), jnp.concatenate(parts, axis=0))


def by_micro_rows(value, ndp, micro):
    return value.reshape(ndp, micro, value.shape[0] // (ndp * micro), value.shape[1])


def total_of(value):
    return jnp.sum(jnp.sum(value, axis=0), axis=0, keepdims=True)


def regroup(rows, own, images, to_groups):
    ndp = rows // own
    row = lax.broadcasted_iota(jnp.int32, (rows, rows), 0).astype(F32)
    lane = lax.broadcasted_iota(jnp.int32, (rows, rows), 1).astype(F32)
    source, target = (lane, row) if to_groups else (row, lane)
    block = jnp.floor((source + 0.5) * (1.0 / own))
    inner = source - block * own
    part = jnp.floor((inner + 0.5) * (1.0 / images))
    moved = (part * ndp + block) * images + inner - part * images
    return (jnp.abs(moved - target) < 0.5).astype(F32).astype(BF16)


def head_kernel(
    micro, images, offsets, place, pooled_a, pooled_b, w_head, w_proj, table, norm, mass, column, match,
    pooled, active, unit, d_scores, embed, xhat_s, y_s, rstd_s, said,
    scores, own_mass, total, factor,
):
    ndp = len(offsets)
    rows = pooled.shape[0]
    group = rows // micro
    half = group // CROPS
    own = rows // ndp
    queued = mass.shape[0]
    scale_all = 1.0 / (TEMPER * CROPS * half * micro)
    chunk = WIDTH
    chunks = D // chunk
    core = place[4]
    for j, offset in enumerate(offsets):
        source = (pooled_a, pooled_b)[j * own // pooled_a.shape[0]]
        at = j * own % pooled_a.shape[0]
        pooled[lanes_at(place[7] ^ offset, own), :] = source[at : at + own, :]
    low = pooled[...]

    def forward(b, carry):
        lanes = lanes_at(b, chunk)
        pre = by_micro_rows(dot(low, w_head[:, lanes]), ndp, micro)
        gain, shift = norm[0:1, lanes], norm[1:2, lanes]
        xhats, ys = [], []
        for m in range(micro):
            v = pre[:, m]
            mean = total_of(v) * (1.0 / group)
            square = total_of(v * v) * (1.0 / group)
            rstd = lax.rsqrt(square - mean * mean + NORM_EPS)
            xhat = (v - mean) * rstd
            rstd_s[m : m + 1, lanes] = rstd
            xhats.append(xhat)
            ys.append(xhat * gain + shift)
        xhat_s[:, lanes] = jnp.stack(xhats, axis=1).reshape(rows, chunk)
        y = jnp.stack(ys, axis=1).reshape(rows, chunk)
        y_s[:, lanes] = y
        active[:, lanes] = (y * sigmoid(y)).astype(BF16)
        return carry

    lax.fori_loop(0, chunks, forward, 0)
    value = dot(active[...], w_proj[...]) + norm[2:3, :PROJ]
    embed[...] = value
    recip = lax.rsqrt(jnp.sum(value * value, axis=1, keepdims=True) + UNIT_EPS)
    unit_v = dot(regroup(rows, own, images, True), (value * recip).astype(BF16)).astype(BF16)
    unit[...] = unit_v
    valid = valid_lanes()
    for a in range(4):
        lanes = slice(a * QUARTER_PAD, (a + 1) * QUARTER_PAD)
        scores[:, lanes] = dot_nt(unit_v, table[:, a * PROJ : (a + 1) * PROJ])

    step = 128

    def divided(a):
        return a * (1.0 / jnp.sum(a, axis=1, keepdims=True))

    def folded(a):
        return jnp.sum(a.reshape(a.shape[0] // 8, 8, a.shape[1]), axis=0)

    def own_rows(m):
        return slice(m * half, (m + 1) * half)

    queue_sum = column[0:1, :]
    for m in range(micro):
        a = scores[lanes_at(m * CROPS + core, half), :]
        a = jnp.where(valid, jnp.exp(a * (1.0 / SINK_EPS)), 0.0)
        inverse = jnp.where(valid, 1.0 / (queue_sum + jnp.sum(a, axis=0, keepdims=True)), 0.0)
        factor[m : m + 1, :] = queue_sum * inverse
        factor[micro + m : micro + m + 1, :] = jnp.ones_like(inverse)
        own_mass[own_rows(m), :] = a * inverse

    def turn(i, carry):
        def block(i, carry):
            at = lanes_at(i, step)
            e_of = [mass[at, b * PART : (b + 1) * PART].astype(F32) for b in range(4 * QUARTER_PAD // PART)]
            rows_by = []
            for m in range(micro):
                sums = None
                for b, e in enumerate(e_of):
                    more = e * factor[m : m + 1, b * PART : (b + 1) * PART]
                    sums = more if sums is None else sums + more
                rows_by.append(1.0 / jnp.sum(sums, axis=1, keepdims=True))
            for b in range(4 * QUARTER_PAD // PART):
                lanes = slice(b * PART, (b + 1) * PART)
                e = mass[at, lanes].astype(F32)
                for m in range(micro):
                    total[m, :, lanes] += folded(e * rows_by[m])
            return carry

        total[...] = jnp.zeros_like(total)
        lax.fori_loop(0, queued // step, block, 0)
        for m in range(micro):
            scale = factor[micro + m : micro + m + 1, :]
            a = divided(own_mass[own_rows(m), :] * scale)
            sums = jnp.sum(total[m], axis=0, keepdims=True) * factor[m : m + 1, :]
            more = jnp.where(valid, 1.0 / (sums + jnp.sum(a, axis=0, keepdims=True)), 0.0)
            factor[m : m + 1, :] = factor[m : m + 1, :] * more
            factor[micro + m : micro + m + 1, :] = scale * more
        return carry

    lax.fori_loop(0, 2, turn, 0)

    def losses(m, loss):
        mine, there = lanes_at(m, half), lanes_at(m * CROPS + 1 - core, half)
        codes = divided(own_mass[mine, :] * factor[pl.ds(micro + m, 1), :])
        goal = exact_dot(match[m], codes)
        logits = jnp.where(valid, scores[there, :] * (1.0 / TEMPER), -1e30)
        logits = logits - jnp.max(logits, axis=1, keepdims=True)
        power = jnp.exp(logits)
        summed = jnp.sum(power, axis=1, keepdims=True)
        weight = jnp.sum(goal, axis=1, keepdims=True) / summed
        d_low = ((power * weight - goal) * scale_all).astype(BF16)
        d_scores[mine, :] = d_low
        d_unit = None
        for a in range(4):
            more = dot(d_low[:, a * QUARTER_PAD : (a + 1) * QUARTER_PAD], table[:, a * PROJ : (a + 1) * PROJ])
            d_unit = more if d_unit is None else d_unit + more
        said[mine, :] = d_unit
        return loss + jnp.sum(goal * (logits - jnp.log(summed)), axis=1, keepdims=True)

    loss = lax.fori_loop(0, micro, losses, jnp.zeros((half, 1), F32))
    loss = jnp.sum(loss, axis=0, keepdims=True) * (-TEMPER * scale_all)
    said[micro * half :, :] = jnp.broadcast_to(loss, (8, PROJ))


def head_back_kernel(
    micro, images, ndp, place, here, there, embed, w_proj, w_head, norm, xhat_s, y_s, rstd_s,
    d0, d1, d2, d3, notes, d_embed, d_pre, d_unit, d_own,
):
    rows = embed.shape[0]
    group = rows // micro
    half = group // CROPS
    own = rows // ndp
    chunk = WIDTH
    chunks = D // chunk
    for m in range(micro):
        d_unit[lanes_at(m * CROPS + place[5], half), :] = here[m * half : (m + 1) * half, :]
        d_unit[lanes_at(m * CROPS + place[4], half), :] = there[m * half : (m + 1) * half, :]
    value = embed[...]
    recip = lax.rsqrt(jnp.sum(value * value, axis=1, keepdims=True) + UNIT_EPS)
    d_back = exact_dot(regroup(rows, own, images, False), d_unit[...])
    along = jnp.sum(d_back * value, axis=1, keepdims=True)
    d_low = (recip * d_back - value * (recip * recip * recip) * along).astype(BF16)
    d_embed[...] = d_low
    notes[...] = jnp.zeros_like(notes)
    notes[2:3, :PROJ] = jnp.sum(d_low.astype(F32), axis=0, keepdims=True)
    loss = here[micro * half : micro * half + 1, :] + there[micro * half : micro * half + 1, :]
    notes[3:4, :PROJ] = loss

    def backward(b, carry):
        lanes = lanes_at(b, chunk)
        d_y = by_micro_rows(dot_nt(d_low, w_proj[lanes, :]) * slope(y_s[:, lanes]), ndp, micro)
        xhat = by_micro_rows(xhat_s[:, lanes], ndp, micro)
        gain = norm[0:1, lanes]
        values, by_xs, plains = [], None, None
        for m in range(micro):
            by_x = total_of(d_y[:, m] * xhat[:, m])
            plain = total_of(d_y[:, m])
            by_xs = by_x if by_xs is None else by_xs + by_x
            plains = plain if plains is None else plains + plain
            value = d_y[:, m] - plain * (1.0 / group) - xhat[:, m] * (by_x * (1.0 / group))
            values.append(gain * rstd_s[m : m + 1, lanes] * value)
        notes[0:1, lanes] = by_xs
        notes[1:2, lanes] = plains
        d_pre[:, lanes] = jnp.stack(values, axis=1).reshape(rows, chunk).astype(BF16)
        return carry

    lax.fori_loop(0, chunks, backward, 0)
    mine = d_pre[lanes_at(place[7], own), :]

    def to_pooled(b, carry):
        d_own[:, lanes_at(b, chunk)] = dot_nt(mine, w_head[lanes_at(b, chunk), :]).astype(BF16)
        return carry

    lax.fori_loop(0, chunks, to_pooled, 0)
    for j, out in enumerate((d0, d1, d2, d3)):
        out[...] = d_own[:, j * WIDE : (j + 1) * WIDE]


def interleave(width):
    row = lax.broadcasted_iota(jnp.int32, (4 * width, 4 * width), 0)
    column = lax.broadcasted_iota(jnp.int32, (4 * width, 4 * width), 1)
    return (column == 4 * (row & (width - 1)) + (row >> (width.bit_length() - 1))).astype(F32).astype(BF16)


def own_columns(place, own):
    row = lax.broadcasted_iota(jnp.int32, (WIDTH, own), 0)
    lane = lax.broadcasted_iota(jnp.int32, (WIDTH, own), 1)
    return (row == lane + place[7] * own).astype(F32).astype(BF16)


def head_grads_kernel(place, pooled, active, unit, d_here, d_there, d_embed, d_pre, out, parts):
    @pl.when(place[0] != SECTIONS - 1)
    def _():
        out[...] = jnp.zeros_like(out)

    @pl.when(place[0] == SECTIONS - 1)
    def _():
        own = out.shape[0]
        choose = own_columns(place, own)
        weave = interleave(PART)
        own_d = [dot(d_pre[:, q * WIDTH : (q + 1) * WIDTH], choose).astype(BF16) for q in range(4)]
        own_d = jnp.concatenate(own_d, axis=1)

        def product(b, carry):
            parts[:, lanes_at(b, WIDTH)] = dot_tn(own_d, pooled[:, lanes_at(b, WIDTH)]).astype(BF16)
            return carry

        lax.fori_loop(0, 4, product, 0)

        def mix(b, carry):
            mixed = []
            for j in range(4):
                lanes = pl.ds(pl.multiple_of(b * WIDTH + j * PART, PART), PART)
                four = [parts[q * own : (q + 1) * own, lanes] for q in range(4)]
                mixed.append(jnp.concatenate(four, axis=1))
            mixed = dot(jnp.concatenate(mixed, axis=0), weave)
            for j in range(4):
                lanes = pl.ds(pl.multiple_of((4 * b + j) * WIDTH, WIDTH), WIDTH)
                out[:, lanes] = mixed[j * own : (j + 1) * own, :]
            return carry

        lax.fori_loop(0, 4, mix, 0)
        rows = active.shape[0]
        wide = jnp.concatenate([active[:, b * WIDTH : (b + 1) * WIDTH] for b in range(4)], axis=0)
        wide = dot_nt(wide, weave).astype(BF16)
        half = d_here.shape[0] // 2
        units = []
        for core in (place[5], place[4]):
            units.append(jnp.concatenate([unit[lanes_at(m * CROPS + core, half), :] for m in range(2)], axis=0))
        proj = jnp.zeros((own, WIDTH), F32)
        proto = jnp.zeros((own, QUARTER_PAD), F32)
        for a in range(4):
            some = choose[a * PROJ : (a + 1) * PROJ, :]
            own_e = dot(d_embed[...], some).astype(BF16)
            column = [wide[b * rows : (b + 1) * rows, a * PART : (a + 1) * PART] for b in range(4)]
            proj = proj + dot_tn(own_e, jnp.concatenate(column, axis=1))
            for own_unit, d_scores in zip(units, (d_here, d_there)):
                own_u = dot(own_unit, some).astype(BF16)
                proto = proto + dot_tn(own_u, d_scores[:, a * QUARTER_PAD : (a + 1) * QUARTER_PAD])
        out[:, FIRST:SECOND] = proj
        out[:, SECOND:] = proto[:, : out.shape[1] - SECOND]


def finish_kernel(place, base, reduce, conv, expand, m1, m2, m3, out, buffer, sem):
    mixed = (None, m1, m2, m3)
    t = place[0]

    def write(lanes):
        copy = pltpu.make_async_copy(buffer.at[:, pl.ds(0, lanes)], out.at[:, pl.ds(0, lanes)], sem)
        copy.start()
        copy.wait()

    @pl.when(t == 0)
    def _():
        for u in range(SECTIONS):
            piece = reduce if u == 0 else mixed[u]
            buffer[:, u * WIDE : (u + 1) * WIDE] = piece[:, :WIDE].astype(F32)
        write(D)

    @pl.when(t == 1)
    def _():
        for u in range(SECTIONS):
            piece = conv if u == 1 else mixed[u ^ 1]
            for tap in range(9):
                at = tap * WIDTH + u * PART
                buffer[:, at : at + PART] = piece[:, tap * PART : (tap + 1) * PART].astype(F32)
        write(9 * WIDTH)

    @pl.when(t == 2)
    def _():
        four = [expand if u == 2 else mixed[u ^ 2] for u in range(SECTIONS)]
        weave = interleave(PART)
        for b in range(WIDTH // PART):
            lanes = slice(b * PART, (b + 1) * PART)
            row = jnp.concatenate([f[:, lanes] for f in four], axis=1)
            buffer[:, 4 * b * PART : 4 * (b + 1) * PART] = dot(row, weave)
        write(D)


def unpack_kernel(packed, out, buffer):
    rows = packed.shape[0]
    for b in range(4):
        buffer[b] = packed[:, b * PART : (b + 1) * PART].astype(F32)
    for q in range(4):
        for b in range(4):
            at = q * WIDTH + b * PART
            out[:, at : at + PART] = buffer[b, pl.ds(q, rows // 4, stride=4), :].astype(BF16)


def unpack(packed, rows):
    step = 1024
    return pl.pallas_call(
        unpack_kernel,
        name="unpack",
        out_shape=shape((rows // 4, 4 * WIDTH), BF16),
        grid=(rows // step,),
        in_specs=[pl.BlockSpec((step, WIDTH), lambda i: (i, 0))],
        out_specs=pl.BlockSpec((step // 4, 4 * WIDTH), lambda i: (i, 0)),
        scratch_shapes=[pltpu.VMEM((4, step, PART), F32)],
        compiler_params=pltpu.CompilerParams(vmem_limit_bytes=16 * 2**20),
        cost_estimate=cost(4),
    )(packed)


def pack_kernel(place, packed, norm, o0, o1, o2, o3, rows, buffer, sem):
    outs = (o0, o1, o2, o3)
    t, core = place[0], place[4]

    def run(copies):
        for copy in copies:
            copy.start()
        return copies

    def lanes_of(target, lanes):
        return pl.ds(target * lanes, lanes)

    @pl.when(t == 0)
    def _():
        half = D // 2
        copies = []
        for k, out in enumerate(outs):
            source = packed.at[pl.ds(pl.multiple_of(core * half, half), half), lanes_of(k, PART)]
            copies.append(pltpu.make_async_copy(source, out.at[pl.ds(16, half), :], sem.at[k]))
        run(copies)
        for k, out in enumerate(outs):
            out[:16, :] = tell_norm(norm[:, k * PART : (k + 1) * PART])
        for copy in copies:
            copy.wait()

    @pl.when(t == 1)
    def _():
        quarter = WIDTH // 4
        copies = []
        for k, out in enumerate(outs):
            for tap in range(9):
                at = pl.multiple_of(tap * WIDTH + place[8] * quarter, quarter)
                source = packed.at[pl.ds(at, quarter), lanes_of(1 ^ k, PART)]
                target = out.at[pl.ds(16 + tap * quarter, quarter), :]
                copies.append(pltpu.make_async_copy(source, target, sem.at[9 * k + tap]))
        run(copies)
        for k, out in enumerate(outs):
            out[:16, :] = tell_norm(norm[:, (1 ^ k) * PART : ((1 ^ k) + 1) * PART])
        for copy in copies:
            copy.wait()

    @pl.when(t == 2)
    def _():
        size = rows.shape[0]
        copy = pltpu.make_async_copy(packed.at[pl.ds(pl.multiple_of(core * size, size), size), :], rows, sem.at[0])
        copy.start()
        copy.wait()
        for b in range(4):
            buffer[b] = rows[:, b * PART : (b + 1) * PART].astype(F32)
        for k, out in enumerate(outs):
            u = 2 ^ k
            for b in range(4):
                at = b * HALF_EXPAND
                lane = u * WIDE + b * PART
                out[at : at + 16, :] = tell_norm(norm[:, lane : lane + PART])
                out[at + 16 : at + HALF_EXPAND, :] = buffer[b, pl.ds(u, size // 4, stride=4), :].astype(BF16)


def pack(place, packed, norm):
    rows = 4 * (WIDTH // 2)
    return pl.pallas_call(
        pack_kernel,
        name="pack",
        out_shape=[shape((QUARTER_CONV, PART), BF16)] * 4,
        in_specs=[
            pl.BlockSpec(memory_space=pltpu.SMEM),
            pl.BlockSpec(memory_space=pltpu.HBM),
            pl.BlockSpec(memory_space=pltpu.VMEM),
        ],
        out_specs=[pl.BlockSpec(memory_space=pltpu.VMEM)] * 4,
        scratch_shapes=[
            pltpu.VMEM((rows, WIDTH), BF16), pltpu.VMEM((4, rows, PART), F32), pltpu.SemaphoreType.DMA((36,)),
        ],
        compiler_params=pltpu.CompilerParams(vmem_limit_bytes=12 * 2**20),
        cost_estimate=cost(2),
    )(place, hbm(packed), norm)


def multiple(value, step):
    return value if isinstance(value, int) else pl.multiple_of(value, step)


def pair_kernel(place, a, b, keep, out, full):
    full[...] = dot_tn(a[...], b[...])
    own = keep.shape[1]
    for z in range(keep.shape[0]):
        mine = (2 * z + place[4]) * own
        other = (2 * z + place[5]) * own
        keep[z] = full[pl.ds(pl.multiple_of(mine, own), own), :]
        out[z] = full[pl.ds(pl.multiple_of(other, own), own), :].astype(BF16)


def image_pair_kernel(place, d0, d1, d2, d3, image, keep, out, d_full, full):
    fill(place, (d0, d1, d2, d3), d_full)
    lanes = pl.ds(pl.multiple_of(place[0] * WIDE, WIDE), WIDE)
    pair_kernel(place, d_full, image.at[:, lanes], keep, out, full)


def cross_kernel(place, keep, came, own, o1, o2, o3):
    for k, o in enumerate((own, o1, o2, o3)):
        z = place[6] ^ k
        o[...] = (keep[z] + came[z].astype(F32)).astype(o.dtype)


def near_kernel(place, keep, came, kept, out):
    for j in range(2):
        mine, other = place[6] ^ (2 * j), place[6] ^ (2 * j + 1)
        kept[j] = keep[mine] + came[mine].astype(F32)
        out[j] = (keep[other] + came[other].astype(F32)).astype(BF16)


def far_kernel(keep, came, kept, out):
    kept[...] = keep[0] + came[0].astype(F32)
    out[...] = (keep[1] + came[1].astype(F32)).astype(BF16)


def last_kernel(keep, came, out):
    out[...] = (keep[...] + came[...].astype(F32)).astype(BF16)


def add_kernel(own, r1, r2, r3, out):
    out[...] = ((own[...] + r1[...].astype(F32)) + (r2[...].astype(F32) + r3[...].astype(F32))).astype(BF16)


def after(value, *others):
    return lax.optimization_barrier((value, *others))[0]


def body(image, section_weights, section_norms, queue, pairing):
    micro, images = image.shape[0], image.shape[2]
    ndp = lax.axis_size("dp")
    t = lax.axis_index("section")
    dp = lax.axis_index("dp")
    core = dp % 2
    place = jnp.stack([t ^ k for k in range(SECTIONS)] + [core, 1 - core, dp // 2, dp, dp % 4]).astype(jnp.int32)
    cells = CROPS * PLACES * images
    rows = micro * cells
    count = float(cells * ndp)
    packed = section_weights[0]
    norm3 = section_norms[0]
    param_rows = packed.shape[0]
    own = WIDTH // ndp
    k = functools.partial

    def pieces_of(width, dtype):
        return shape((rows, width), dtype)

    own_message, *messages = pack(place, packed, norm3)
    came = [own_message]
    for j in range(1, SECTIONS):
        came.append(lax.ppermute(messages[j - 1], "section", [(u, u ^ j) for u in range(3)]))
    flat = call(
        retile_kernel, shape((rows, D), BF16),
        image.transpose(0, 1, 3, 4, 2, 5).reshape(rows // images, images, D),
        us=2,
    )
    queue_size = CROPS * queue.shape[1]
    note = call(note_kernel, shape((queue_size + 16, PROJ), BF16), pairing, queue, us=0.5)
    told, told_offsets = gather_dp(note, dp_stages())
    *came, flat, told[0] = lax.optimization_barrier((*came, flat, *told))[:6]
    conv_part, pair_part = call(
        pick_kernel,
        (shape((QUARTER_CONV, PART), BF16), shape((HALF_REDUCE + 4 * HALF_EXPAND, PART), BF16)),
        place, *came,
    )
    pair_parts = (pair_part, flip(pair_part, "dp", 1))
    conv_near = flip(conv_part, "dp", 2)
    sums_of = shape((8, PART), F32)
    pre0, part = call(
        k(reduce_kernel, micro), (pieces_of(PART, F32), sums_of), place, flat, *pair_parts, us=2
    )
    sums0 = sum_dp(part)
    active0 = call(k(active_kernel, micro, count), pieces_of(PART, BF16), pre0, sums0, pair_part, us=1)
    actives0 = gather_xor(active0, "section")

    conv_part = rows_of([conv_part, after(conv_near, active0)])
    w_conv = (conv_part, flip(conv_part, "dp", 1))
    w_proj, table = pl.pallas_call(
        tables_kernel,
        name="tables",
        out_shape=(shape((D, PROJ), BF16), shape((QUARTER_PAD, WIDTH), BF16)),
        in_specs=[pl.BlockSpec(memory_space=pltpu.HBM)],
        out_specs=(pl.BlockSpec(memory_space=pltpu.VMEM), pl.BlockSpec(memory_space=pltpu.VMEM)),
        scratch_shapes=[
            pltpu.VMEM((THIRD - FIRST + 2, WIDTH), BF16), pltpu.VMEM((D, PROJ), F32), pltpu.SemaphoreType.DMA,
        ],
        compiler_params=pltpu.CompilerParams(vmem_limit_bytes=12 * 2**20),
        cost_estimate=cost(1.5),
    )(hbm(after(packed, active0)))
    head_rows = rows // PLACES * ndp
    lanes = 4 * QUARTER_PAD
    stages = dp_stages()
    head_stages = stages[1:] + stages[:1]
    offsets = [0]
    for steps in head_stages:
        offsets = offsets + [o ^ step for step in steps for o in offsets]
    small = head_rows <= 128 and images * ndp == 32 and queue.shape[1] * ndp <= 512
    if small:
        queued = ndp * queue.shape[1]
        mass, column, match = call(
            k(mass_kernel, micro, images, sum(told_offsets, [])),
            (
                shape((queued, lanes), BF16), shape((8, lanes), F32),
                shape((micro, images * ndp, images * ndp), BF16),
            ),
            place, table, *told,
            scratch=[pltpu.VMEM((queued, PROJ), BF16), pltpu.VMEM((queued, lanes), F32)],
            vmem=16, us=5,
        )
        *actives0, mass = lax.optimization_barrier((*actives0, mass))
    pre1, part = call(
        k(conv_kernel, micro, images),
        (pieces_of(PART, F32), sums_of),
        place, *actives0, *w_conv,
        scratch=[pltpu.VMEM((rows, WIDTH), BF16), pltpu.VMEM((WIDTH, 9 * PART), BF16)],
        us=3,
    )
    sums1 = sum_dp(part)
    active1_own = call(k(active_kernel, micro, count), pieces_of(PART, BF16), pre1, sums1, conv_part, us=1)
    actives1 = gather_xor(active1_own, "section")
    natural = unpack(after(packed, active1_own), FIRST)
    taps = call(k(taps_kernel, images), pieces_of(9 * PART, BF16), after(active0, active1_own), us=1.3)
    back_rows = 9 * PART // 2 + WIDE // 2
    back_own = call(
        back_parts_kernel, [shape((back_rows, PART), BF16)] * 4, place, *w_conv, *pair_parts, us=1
    )
    joined = lax.optimization_barrier((*actives1, natural, taps, *back_own))
    actives1, natural, taps, back_own = joined[:4], joined[4], joined[5], joined[6:]
    active1, pre2, part, w_expand = call(
        k(expand_kernel, micro),
        (pieces_of(WIDTH, BF16), pieces_of(WIDE, F32), shape((8, WIDE), F32), shape((WIDTH, WIDE), BF16)),
        place, *actives1, *pair_parts,
        us=2,
    )
    back_own = lax.optimization_barrier((*back_own, part))[:4]
    back_came = [back_own[0]] + [flip(back_own[j], "section", j) for j in range(1, SECTIONS)]

    sums2 = sum_dp(part)
    pooled = call(
        k(pool_kernel, micro, images, count),
        shape((rows // PLACES, WIDE), BF16),
        place, pre2, sums2, pair_part, flat,
        us=1.6,
    )

    per_dp = rows // PLACES
    came_p = gather_xor(pooled, "section")[::-1]
    pooled_here = call(lanes_kernel, shape((per_dp, D), BF16), *came_p, us=0.3)
    parts, _ = gather_dp(pooled_here, head_stages)
    if small:
        all_pooled, active3, unit, d_scores, embed, *kept, said = call(
            k(head_kernel, micro, images, offsets),
            [
                shape((head_rows, D), BF16), shape((head_rows, D), BF16), shape((head_rows, PROJ), BF16),
                shape((head_rows // 2, lanes), BF16), shape((head_rows, PROJ), F32), shape((head_rows, D), F32),
                shape((head_rows, D), F32), shape((8, D), F32), shape((head_rows // 2 + 8, PROJ), F32),
            ],
            place, *parts, natural, w_proj, table, norm3, mass, column, match,
            scratch=[
                pltpu.VMEM((head_rows, lanes), F32), pltpu.VMEM((head_rows // 2, lanes), F32),
                pltpu.VMEM((micro, 8, lanes), F32), pltpu.VMEM((8, lanes), F32),
            ],
            vmem=15, us=12,
        )
        *d_pooled, notes3, d_embed, d_pre3 = call(
            k(head_back_kernel, micro, images, ndp),
            [shape((per_dp, WIDE), BF16)] * 4
            + [shape((8, D), F32), shape((head_rows, PROJ), BF16), shape((head_rows, D), BF16)],
            place, said, flip(said, "dp", 1), embed, w_proj, natural, norm3, *kept,
            scratch=[pltpu.VMEM((head_rows, PROJ), F32), pltpu.VMEM((per_dp, D), BF16)],
            us=5,
        )
    else:
        all_pooled = jnp.concatenate(parts)
        offset = jnp.array(offsets, jnp.int32)
        head_order = jnp.arange(head_rows, dtype=jnp.int32)
        block, inner = head_order // per_dp, head_order % per_dp
        group, single = inner // images, inner % images
        position = (group * ndp + (offset[block] ^ dp)) * images + single
        order = (position[None, :] == head_order[:, None]).astype(BF16)
        told = jnp.concatenate(told).reshape(ndp, queue_size + 16, PROJ)
        pairs = told[:, queue_size : queue_size + micro, :images].astype(jnp.int32)
        told_offset = jnp.array(sum(told_offsets, []), jnp.int32)
        pairs_dp = (told_offset ^ dp)[None, :] == jnp.arange(ndp, dtype=jnp.int32)[:, None]
        pairs = jnp.sum(jnp.where(pairs_dp[:, :, None, None], pairs[None], 0), axis=1)
        left = jnp.arange(images * ndp, dtype=jnp.int32)
        pairs = pairs.transpose(1, 0, 2).reshape(micro, ndp * images)
        match = ((left // images * images + pairs)[:, :, None] == left[None, None, :]).astype(F32)
        all_pooled = dot(order, all_pooled).astype(BF16)
        protos = jnp.concatenate([table[:, a * PROJ : (a + 1) * PROJ] for a in range(4)], axis=0)
        queue_all = told[:, :queue_size].reshape(ndp, CROPS, queue.shape[1], PROJ)
        queue_rows = queue_all.transpose(1, 0, 2, 3).reshape(CROPS, -1, PROJ)
        loss, grads3, active3, unit, d_scores, d_embed, d_pre3 = head(
            all_pooled, natural, w_proj, protos, norm3, queue_rows, match, micro, images, dp
        )
        notes3 = jnp.concatenate([grads3, jnp.full((5, D), loss)])
        d_pooled = dot_nt(dot_tn(order[:, :per_dp], d_pre3).astype(BF16), natural).astype(BF16)
        d_pooled = [d_pooled[:, j * WIDE : (j + 1) * WIDE] for j in range(SECTIONS)]
        d_scores = d_scores.reshape(micro, CROPS, head_rows // 4, lanes)
        d_scores = lax.dynamic_index_in_dim(d_scores, 1 - core, 1, keepdims=False).reshape(-1, lanes)

    joined = lax.optimization_barrier((*d_pooled, *back_came))
    d_pooled, back_came = joined[:SECTIONS], joined[SECTIONS:]
    came_d = [flip(d_pooled[3 ^ j], "section", j) for j in range(1, SECTIONS)]
    back_half = call(stack_kernel, shape((SECTIONS, back_rows, PART), BF16), *back_came, us=0.6)
    back_halves = (back_half, flip(back_half, "dp", 1))
    d_z, part = call(
        k(out_back_kernel, micro, images, count),
        (pieces_of(WIDE, F32), shape((8, WIDE), F32)),
        place, pre2, sums2, pair_part, flat, d_pooled[3], *came_d,
        us=1.8,
    )
    back2 = sum_dp(part)
    d_pre2, *partial = call(
        k(expand_back_kernel, micro, count),
        [pieces_of(WIDE, BF16)] + [pieces_of(PART, BF16)] * 4,
        place, pre2, sums2, d_z, back2, pair_part, w_expand,
        scratch=[pltpu.VMEM((rows, WIDTH), F32)],
        us=2,
    )
    partial = [partial[0]] + [flip(partial[j], "section", j) for j in range(1, SECTIONS)]

    def scatter_start(a, b, width):
        if ndp != 8:
            return dot_tn(a, b)
        keep, out = call(
            pair_kernel,
            (shape((4, own, width), F32), shape((4, own, width), BF16)),
            place, a, b,
            scratch=[pltpu.VMEM((WIDTH, width), F32)],
            us=2.5,
        )
        return keep, flip(out, "dp", 1)

    def scatter_cross(started, *others):
        if ndp != 8:
            return [lax.psum_scatter(started.astype(BF16), "dp", scatter_dimension=0, tiled=True)]
        keep, came = started
        if others:
            keep = after(keep, *others)
        dims = keep.shape[1:]
        kept, *out = call(
            cross_kernel, [shape(dims, F32)] + [shape(dims, BF16)] * 3, place, keep, came
        )
        return [kept] + [flip(out[j], "dp", 2 * (j + 1)) for j in range(3)]

    def scatter_near(started, *others):
        if ndp != 8:
            return lax.psum_scatter(started.astype(BF16), "dp", scatter_dimension=0, tiled=True), None
        keep, came = started
        if others:
            keep = after(keep, *others)
        dims = (2, *keep.shape[1:])
        kept, out = call(near_kernel, (shape(dims, F32), shape(dims, BF16)), place, keep, came, us=0.7)
        return kept, flip(out, "dp", 2)

    def scatter_far(started, *others):
        if ndp != 8:
            return started
        keep, came = started
        if others:
            keep = after(keep, *others)
        dims = keep.shape[1:]
        kept, out = call(far_kernel, (shape(dims, F32), shape(dims, BF16)), keep, came, us=0.5)
        return kept, flip(out, "dp", 4)

    def scatter_last(started):
        if ndp != 8:
            return started[0].astype(BF16)
        return call(last_kernel, shape(started[0].shape, BF16), *started, us=0.4)

    def scatter_finish(crossed):
        if ndp != 8:
            return crossed[0].astype(BF16)
        return call(add_kernel, shape(crossed[0].shape, BF16), *crossed, us=0.6)

    expand_near = scatter_near(scatter_start(d_pre2, active1, WIDTH))
    base = call(
        head_grads_kernel,
        shape((own, param_rows), F32),
        place, after(all_pooled, d_pre2), active3, unit, d_scores, flip(d_scores, "dp", 1), d_embed, d_pre3,
        scratch=[pltpu.VMEM((4 * own, D), BF16)],
        us=6,
    )
    joined = lax.optimization_barrier((*partial, base, *expand_near[: 2 if ndp == 8 else 1]))
    partial, base, expand_near = joined[:SECTIONS], joined[SECTIONS], joined[SECTIONS + 1 :]

    d_y1, part = call(
        k(silu_back_kernel, micro, count),
        (pieces_of(PART, F32), sums_of),
        *partial, pre1, sums1, conv_part,
    )
    back1 = sum_dp(part)
    d_pre1_own = call(
        k(norm_back_kernel, micro, count), pieces_of(PART, BF16), d_y1, pre1, sums1, back1, conv_part
    )
    d_pre1s = gather_xor(d_pre1_own, "section")
    expand_far = scatter_far(expand_near, d_pre1_own)
    joined = lax.optimization_barrier((*d_pre1s, *expand_far))
    d_pre1s, expand_far = joined[:SECTIONS], joined[SECTIONS:]
    d_pre1, d_y0, part = call(
        k(conv_back_kernel, micro, images, count),
        (pieces_of(WIDTH, BF16), pieces_of(PART, F32), sums_of),
        place, *d_pre1s, *back_halves, pre0, sums0, pair_part,
        scratch=[pltpu.VMEM((9 * PART, WIDTH), BF16)],
        us=3.5,
    )
    back0 = sum_dp(part)
    d_pre0_own = call(
        k(last_norm_back_kernel, micro, count),
        shape((rows + NOTE_ROWS, PART), BF16),
        place, d_y0, pre0, sums0, back0, pair_part, back2, back1, notes3,
    )
    d_pre0s = gather_xor(d_pre0_own, "section")
    conv_near_sum = scatter_near(scatter_start(after(d_pre1, d_pre0_own), taps, 9 * PART))
    joined = lax.optimization_barrier((*d_pre0s, conv_near_sum[0]))
    d_pre0s, conv_near_sum = joined[:SECTIONS], (joined[SECTIONS], conv_near_sum[1])
    conv_far = scatter_far(conv_near_sum)

    if ndp == 8:
        keep, out, d_pre0 = call(
            image_pair_kernel,
            (shape((4, own, WIDE), F32), shape((4, own, WIDE), BF16), pieces_of(WIDTH, BF16)),
            place, *d_pre0s, flat,
            scratch=[pltpu.VMEM((WIDTH, WIDE), F32)],
            us=2.5,
        )
        reduce_started = keep, flip(out, "dp", 1)
    else:
        d_pre0 = jnp.stack(d_pre0s)[place[:SECTIONS], :rows].transpose(1, 0, 2).reshape(rows, WIDTH)
        reduce_started = dot_tn(d_pre0, lax.dynamic_slice_in_dim(flat, t * WIDE, WIDE, 1))
    reduce_crossed = scatter_cross(reduce_started)
    grad_in = call(
        reduce_back_kernel,
        shape((rows // images, images, WIDE), F32),
        place, d_pre0, *back_halves, d_z,
        scratch=[pltpu.VMEM((WIDE, WIDTH), BF16)],
        us=2,
    )
    norm_grads, loss = call(
        told_kernel, (shape((3, D), F32), shape((8, PROJ), F32)), place, *d_pre0s, notes3, us=0.5
    )
    g_conv = scatter_last(conv_far)
    g_expand = scatter_last(expand_far)
    joined = lax.optimization_barrier((*reduce_crossed, grad_in, norm_grads, g_conv, g_expand))
    *reduce_crossed, grad_in, norm_grads, g_conv, g_expand = joined
    g_reduce = scatter_finish(reduce_crossed)
    mixed = call(mixed_kernel, [shape(g_conv.shape, BF16)] * 3, place, g_reduce, g_conv, g_expand, us=0.3)
    mixed = [
        lax.ppermute(mixed[j - 1], "section", [(u ^ j, u) for u in range(3)]) for j in range(1, SECTIONS)
    ]
    weight_grads = pl.pallas_call(
        finish_kernel,
        name="finish",
        out_shape=shape((own, param_rows), F32),
        in_specs=[pl.BlockSpec(memory_space=pltpu.SMEM), pl.BlockSpec(memory_space=pltpu.HBM)]
        + [pl.BlockSpec(memory_space=pltpu.VMEM)] * 6,
        out_specs=pl.BlockSpec(memory_space=pltpu.HBM),
        scratch_shapes=[pltpu.VMEM((own, 9 * WIDTH), F32), pltpu.SemaphoreType.DMA],
        input_output_aliases={1: 0},
        compiler_params=pltpu.CompilerParams(vmem_limit_bytes=12 * 2**20),
        cost_estimate=cost(2),
    )(place, base, g_reduce, g_conv, g_expand, *mixed)
    grad_in = grad_in.reshape(micro, CROPS, SIDE, SIDE, images, WIDE).transpose(0, 1, 4, 2, 3, 5)
    return (loss[0, 0], grad_in, weight_grads.T[None], norm_grads[None])


def solution(mesh):
    in_specs = (
        P(None, None, "dp", None, None, None),
        P("section", None, None),
        P("section", None, None),
        P(None, "dp", None),
        P(None, "dp"),
    )
    out_specs = (
        P(),
        P(None, None, "dp", None, None, "section"),
        P("section", None, "dp"),
        P("section", None, None),
    )
    return jax.shard_map(body, mesh=mesh, in_specs=in_specs, out_specs=out_specs, check_vma=False)
```

```python
import functools

import jax
import jax.numpy as jnp
from jax import lax
from jax.experimental import pallas as pl
from jax.experimental.pallas import tpu as pltpu
from jax.sharding import PartitionSpec as P

D = 2048
WIDTH = 512
PROJ = 128
PROTOS = 3000
SIDE = 7
CROPS = 2
SECTIONS = 4
PART = WIDTH // SECTIONS
WIDE = D // SECTIONS
QUARTER = PROTOS // 4
QUARTER_PAD = 768
PLACES = SIDE * SIDE
FIRST = D * (D // WIDTH)
SECOND = FIRST + D * PROJ // WIDTH
THIRD = SECOND + PROTOS * PROJ // WIDTH
HALF_REDUCE = 16 + D // 2
HALF_EXPAND = 16 + WIDTH // 2
QUARTER_CONV = 16 + 9 * WIDTH // 4
NOTE_ROWS = 48

NORM_EPS = 1e-05
UNIT_EPS = 1e-06
SINK_EPS = 0.05
TEMPER = 0.1
HIGH = lax.Precision.HIGHEST
F32 = jnp.float32
BF16 = jnp.bfloat16
NT = (((1,), (1,)), ((), ()))
TN = (((0,), (0,)), ((), ()))


def dot(a, b):
    return jnp.dot(a, b, preferred_element_type=F32)


def dot_nt(a, b):
    return lax.dot_general(a, b, NT, preferred_element_type=F32)


def dot_tn(a, b):
    return lax.dot_general(a, b, TN, preferred_element_type=F32)


def flip(value, axis, step):
    count = lax.axis_size(axis)
    return lax.ppermute(value, axis, [(source, source ^ step) for source in range(count)])


def send(value, source, target):
    return lax.ppermute(value, "section", [(source, target)])


def sum_dp_steps(value):
    count = lax.axis_size("dp")
    value = pair = value + flip(value, "dp", 1)
    step = 2
    while step < count:
        if 2 * step < count:
            near = value + flip(value, "dp", step)
            far = flip(value, "dp", 2 * step) + flip(value, "dp", 3 * step)
            value = near + far
            step *= 4
        else:
            value = value + flip(value, "dp", step)
            step *= 2
    return value, pair


def sum_dp(value):
    return sum_dp_steps(value)[0]


def gather_xor(value, axis):
    return [value] + [flip(value, axis, step) for step in range(1, lax.axis_size(axis))]


def dp_stages():
    count = lax.axis_size("dp")
    stages, step = [(1,)], 2
    while step < count:
        if 2 * step < count:
            stages.append((step, 2 * step, 3 * step))
            step *= 4
        else:
            stages.append((step,))
            step *= 2
    return stages


def gather_dp(value, stages):
    arrays, offsets = [value], [[0]]
    for steps in stages:
        if len(arrays) > 1:
            arrays, offsets = [rows_of(arrays)], [sum(offsets, [])]
        first = offsets[0]
        for step in steps:
            arrays.append(flip(arrays[0], "dp", step))
            offsets.append([o ^ step for o in first])
    return arrays, offsets


def sigmoid(v):
    return 0.5 * jnp.tanh(0.5 * v) + 0.5


def slope(v):
    s = sigmoid(v)
    return s * (1.0 + v * (1.0 - s))


def cost(us):
    return pl.CostEstimate(flops=0, bytes_accessed=int(us * 3_000_000), transcendentals=0)


def hbm(value):
    return pltpu.with_memory_space_constraint(value, pltpu.HBM)


def call(kernel, out, *args, scratch=(), vmem=12, us=1.0, in_hbm=()):
    in_specs, ins = [], []
    for j, a in enumerate(args):
        space = pltpu.VMEM
        if jnp.issubdtype(a.dtype, jnp.integer):
            space = pltpu.SMEM
        elif j in in_hbm:
            space = pltpu.HBM
            a = hbm(a)
        in_specs.append(pl.BlockSpec(memory_space=space))
        ins.append(a)
    return pl.pallas_call(
        kernel,
        name=getattr(kernel, 'func', kernel).__name__,
        out_shape=out,
        in_specs=in_specs,
        out_specs=jax.tree.map(lambda _: pl.BlockSpec(memory_space=pltpu.VMEM), out),
        scratch_shapes=list(scratch),
        compiler_params=pltpu.CompilerParams(vmem_limit_bytes=vmem * 2**20),
        cost_estimate=cost(us),
    )(*ins)


def shape(dims, dtype):
    return jax.ShapeDtypeStruct(tuple(dims), dtype)


def retile_kernel(image, flat):
    flat[...] = image[...].reshape(flat.shape)


def note_kernel(pairing, queue, out):
    size = queue.shape[1]
    for c in range(CROPS):
        out[c * size : (c + 1) * size, :] = queue[c]
    row = lax.broadcasted_iota(jnp.int32, (16, PROJ), 0)
    lane = lax.broadcasted_iota(jnp.int32, (16, PROJ), 1)
    value = jnp.zeros((16, PROJ), F32)
    for m in range(pairing.shape[0]):
        for i in range(pairing.shape[1]):
            value = jnp.where((row == m) & (lane == i), pairing[m, i].astype(F32), value)
    out[CROPS * size :, :] = value.astype(BF16)


def rows_kernel(*refs):
    out, at = refs[-1], 0
    for ref in refs[:-1]:
        out[at : at + ref.shape[0], :] = ref[...]
        at += ref.shape[0]


def lanes_kernel(*refs):
    out, at = refs[-1], 0
    for ref in refs[:-1]:
        out[:, at : at + ref.shape[1]] = ref[...]
        at += ref.shape[1]


def rows_of(values, us=0.5):
    rows = sum(v.shape[0] for v in values)
    return call(rows_kernel, shape((rows, values[0].shape[1]), values[0].dtype), *values, us=us)


def split_sums(first, second, micro):
    width = first[0].shape[1]
    rows = [jnp.sum(v, axis=0, keepdims=True) for v in first]
    rows += [jnp.sum(v, axis=0, keepdims=True) for v in second]
    rows.append(jnp.zeros((8 - 2 * micro, width), F32))
    return jnp.concatenate(rows, axis=0)


def moments(sums, m, micro, count):
    mean = sums[m : m + 1] * (1.0 / count)
    square = sums[micro + m : micro + m + 1] * (1.0 / count)
    return mean, lax.rsqrt(square - mean * mean + NORM_EPS)


def per_micro(value, micro):
    rows = value.shape[0] // micro
    return [value[m * rows : (m + 1) * rows] for m in range(micro)]


def normalized(value, sums, micro, count):
    out = []
    for m, v in enumerate(per_micro(value, micro)):
        mean, rstd = moments(sums, m, micro, count)
        out.append(((v - mean) * rstd, rstd))
    return out


def join(parts):
    return jnp.concatenate(parts, axis=0)


def map_places(rows, images):
    row = lax.broadcasted_iota(jnp.int32, (rows, PART), 0).astype(F32)
    cell = jnp.floor((row + 0.5) * (1.0 / images))
    crop = jnp.floor((cell + 0.5) * (1.0 / PLACES))
    place = cell - crop * PLACES
    y = jnp.floor((place + 0.5) * (1.0 / SIDE))
    return y, place - y * SIDE


def tap_shift(value, images, tap, sign, y, x):
    rows = value.shape[0]
    down, right = sign * (tap // 3 - 1), sign * (tap % 3 - 1)
    offset = images * (SIDE * down + right)
    moved = value if offset == 0 else pltpu.roll(value, (-offset) % rows, 0)
    for step, at in ((down, y), (right, x)):
        if step < 0:
            moved = jnp.where(at > 0.5, moved, 0.0)
        elif step > 0:
            moved = jnp.where(at < SIDE - 1.5, moved, 0.0)
    return moved


def told_norm(message, at=0):
    rows = message[at : at + 16, :].astype(F32)
    return rows[0:1] + rows[1:2] + rows[2:3], rows[3:4] + rows[4:5] + rows[5:6]


def told_wide(message):
    parts = [told_norm(message, HALF_REDUCE + b * HALF_EXPAND) for b in range(4)]
    return tuple(jnp.concatenate(p, axis=1) for p in zip(*parts))


def terms(row):
    out = []
    for _ in range(3):
        term = row.astype(BF16).astype(F32)
        out.append(term)
        row = row - term
    return out


def tell_norm(norm, lane):
    out = []
    for r in range(2):
        out += terms(norm[r, :, lane : lane + PART])
    out.append(jnp.zeros((10, PART), F32))
    return jnp.concatenate(out, axis=0).astype(BF16)


def reduce_kernel(micro, place, image, w0, w1, pre, sums):
    half = D // 2
    first = pl.ds(pl.multiple_of(place[4] * half, half), half)
    second = pl.ds(pl.multiple_of(place[5] * half, half), half)
    value = dot(image[:, first], w0[16 : 16 + half, :]) + dot(image[:, second], w1[16 : 16 + half, :])
    pre[...] = value
    parts = per_micro(value, micro)
    sums[...] = split_sums(parts, [v * v for v in parts], micro)


def active_kernel(micro, count, pre, sums, told, active):
    gain, shift = told_norm(told)
    out = []
    for xhat, _ in normalized(pre[...], sums[...], micro, count):
        y = xhat * gain + shift
        out.append(y * sigmoid(y))
    active[...] = join(out).astype(BF16)


def fill(place, pieces, full):
    for k, piece in enumerate(pieces):
        full[:, pl.ds(pl.multiple_of(place[k] * PART, PART), PART)] = piece[: full.shape[0], :]


def quarter_of(place, j):
    return place[8] ^ (0, 2, 1, 3)[j]


def conv_kernel(micro, images, place, a0, a1, a2, a3, wa, wb, pre, sums, full, weight):
    fill(place, (a0, a1, a2, a3), full)
    quarter = WIDTH // 4
    for j in range(4):
        w = (wa, wb)[j // 2]
        at = pl.multiple_of(quarter_of(place, j) * quarter, quarter)
        for tap in range(9):
            lanes = slice(tap * PART, (tap + 1) * PART)
            first = (j % 2) * QUARTER_CONV + 16 + tap * quarter
            weight[pl.ds(at, quarter), lanes] = w[first : first + quarter, :]
    total = None
    y, x = map_places(full.shape[0], images)
    for first in range(0, 9, 2):
        taps = [tap for tap in (first, first + 1) if tap < 9]
        part = dot(full[...], weight[:, first * PART : (taps[-1] + 1) * PART])
        for j, tap in enumerate(taps):
            moved = tap_shift(part[:, j * PART : (j + 1) * PART], images, tap, 1, y, x)
            total = moved if total is None else total + moved
    pre[...] = total
    parts = per_micro(total, micro)
    sums[...] = split_sums(parts, [v * v for v in parts], micro)


def expand_kernel(micro, place, a0, a1, a2, a3, w0, w1, active, pre, sums, weight):
    fill(place, (a0, a1, a2, a3), active)
    half = WIDTH // 2
    for j, w in enumerate((w0, w1)):
        rows = pl.ds(pl.multiple_of(place[4 + j] * half, half), half)
        for b in range(4):
            at = HALF_REDUCE + b * HALF_EXPAND + 16
            weight[rows, b * PART : (b + 1) * PART] = w[at : at + half, :]
    value = dot(active[...], weight[...])
    pre[...] = value
    parts = per_micro(value, micro)
    sums[...] = split_sums(parts, [v * v for v in parts], micro)


def crop_rows(rows, images, transpose=False):
    shp = (rows // PLACES, rows)
    r = lax.broadcasted_iota(jnp.int32, shp, 1).astype(F32)
    q = lax.broadcasted_iota(jnp.int32, shp, 0).astype(F32)
    cell = jnp.floor((r + 0.5) * (1.0 / images))
    crop = jnp.floor((cell + 0.5) * (1.0 / PLACES))
    image = r - cell * images
    return (jnp.abs(crop * images + image - q) < 0.5).astype(F32).astype(BF16)


def pool_kernel(micro, images, count, place, pre, sums, told, image, pooled):
    lanes = pl.ds(pl.multiple_of(place[0] * WIDE, WIDE), WIDE)
    gain, shift = told_wide(told)
    out = []
    for xhat, _ in normalized(pre[...], sums[...], micro, count):
        out.append(xhat * gain + shift)
    z = join(out) + image[:, lanes].astype(F32)
    out = z * sigmoid(z)
    high = out.astype(BF16)
    low = (out - high.astype(F32)).astype(BF16)
    choose = crop_rows(pre.shape[0], images)
    pooled[...] = ((dot(choose, high) + dot(choose, low)) * (1.0 / PLACES)).astype(BF16)


def out_back_kernel(micro, images, count, place, pre, sums, told, image, own, r0, r1, r2, d_z, sums_out):
    lanes = pl.ds(pl.multiple_of(place[0] * WIDE, WIDE), WIDE)
    rows = pre.shape[0]
    gain, shift = told_wide(told)
    d_pooled = own[...].astype(F32)
    for k, came in enumerate((r0, r1, r2)):
        d_pooled = jnp.where(place[k + 1] == SECTIONS - 1, came[...].astype(F32), d_pooled)
    d_pooled = d_pooled.astype(BF16)
    spread = dot_tn(crop_rows(rows, images), d_pooled) * (1.0 / PLACES)
    xhats = [x for x, _ in normalized(pre[...], sums[...], micro, count)]
    z = join([x * gain + shift for x in xhats]) + image[:, lanes].astype(F32)
    value = spread * slope(z)
    d_z[...] = value
    parts = per_micro(value, micro)
    sums_out[...] = split_sums([v * x for v, x in zip(parts, xhats)], parts, micro)


def norm_back(value, pre, sums, back, gain, micro, count):
    out = []
    parts = per_micro(value, micro)
    for m, (xhat, rstd) in enumerate(normalized(pre, sums, micro, count)):
        by_x = back[m : m + 1] * (1.0 / count)
        plain = back[micro + m : micro + m + 1] * (1.0 / count)
        out.append(gain * rstd * (parts[m] - plain - xhat * by_x))
    return join(out)


def norm_back_kernel(micro, count, d_y, pre, sums, back, told, d_pre):
    gain, _ = told_norm(told)
    d_pre[...] = norm_back(d_y[...], pre[...], sums[...], back[...], gain, micro, count).astype(BF16)


def over_micro(back, micro):
    out = []
    for r in range(2):
        row = back[r * micro : r * micro + 1, :]
        for m in range(1, micro):
            row = row + back[r * micro + m : r * micro + m + 1, :]
        out.append(row)
    return out


def last_norm_back_kernel(micro, count, place, d_y, pre, sums, back, told, back2, back1, notes, d_pre):
    gain, _ = told_norm(told)
    rows = d_y.shape[0]
    d_pre[:rows, :] = norm_back(d_y[...], pre[...], sums[...], back[...], gain, micro, count).astype(BF16)
    said = []
    for row in over_micro(back2, micro):
        said += [row[:, b * PART : (b + 1) * PART] for b in range(4)]
    said += over_micro(back1, micro) + over_micro(back, micro)
    said.append(jnp.where(place[0] == SECTIONS - 1, notes[3:4, :PART], 0.0))
    said = sum([terms(row) for row in said], [])
    said.append(jnp.zeros((NOTE_ROWS - len(said), PART), F32))
    d_pre[rows:, :] = jnp.concatenate(said, axis=0).astype(BF16)


def expand_back_kernel(micro, count, place, pre, sums, d_z, back, told, weight, d_pre, q0, q1, q2, q3, full):
    gain, _ = told_wide(told)
    d_low = norm_back(d_z[...], pre[...], sums[...], back[...], gain, micro, count).astype(BF16)
    d_pre[...] = d_low
    full[...] = dot_nt(d_low, weight[...])
    for k, q in enumerate((q0, q1, q2, q3)):
        lanes = pl.ds(pl.multiple_of(place[k] * PART, PART), PART)
        q[...] = full[:, lanes].astype(BF16)


def finish_silu(micro, count, d_active, pre, sums, norm, d_y, sums_out):
    gain, shift = norm
    values, products = [], []
    parts = per_micro(d_active, micro)
    for m, (xhat, _) in enumerate(normalized(pre[...], sums[...], micro, count)):
        value = parts[m] * slope(xhat * gain + shift)
        values.append(value)
        products.append(value * xhat)
    d_y[...] = join(values)
    sums_out[...] = split_sums(products, values, micro)


def silu_back_kernel(micro, count, q0, q1, q2, q3, pre, sums, told, d_y, sums_out):
    total = (q0[...].astype(F32) + q1[...].astype(F32)) + (q2[...].astype(F32) + q3[...].astype(F32))
    d_active = total.astype(BF16).astype(F32)
    finish_silu(micro, count, d_active, pre, sums, told_norm(told), d_y, sums_out)


def conv_back_kernel(
    micro, images, count, place, d0, d1, d2, d3, back0, back1, pre, sums, told, d_full, d_y, sums_out, weight
):
    fill(place, (d0, d1, d2, d3), d_full)
    d_low = d_full[...]
    half = PART // 2
    for j, back in enumerate((back0, back1)):
        for k in range(SECTIONS):
            lanes = pl.ds(pl.multiple_of(place[k] * PART, PART), PART)
            for tap in range(9):
                rows = pl.ds(pl.multiple_of(tap * PART + place[4 + j] * half, half), half)
                weight[rows, lanes] = back[k, tap * half : (tap + 1) * half, :]
    total = None
    y, x = map_places(d_low.shape[0], images)
    for first in range(0, 9, 2):
        taps = [tap for tap in (first, first + 1) if tap < 9]
        part = dot_nt(d_low, weight[first * PART : (taps[-1] + 1) * PART, :])
        for j, tap in enumerate(taps):
            moved = tap_shift(part[:, j * PART : (j + 1) * PART], images, tap, -1, y, x)
            total = moved if total is None else total + moved
    d_active = total.astype(BF16).astype(F32)
    finish_silu(micro, count, d_active, pre, sums, told_norm(told), d_y, sums_out)


def reduce_back_kernel(place, d_full, back0, back1, d_z, grad_in, weight):
    half = WIDE // 2
    first = 9 * PART // 2
    for j, back in enumerate((back0, back1)):
        rows = pl.ds(pl.multiple_of(place[4 + j] * half, half), half)
        for k in range(SECTIONS):
            lanes = pl.ds(pl.multiple_of(place[k] * PART, PART), PART)
            weight[rows, lanes] = back[k, first : first + half, :]
    main = dot_nt(d_full[...], weight[...]).astype(BF16).astype(F32)
    value = main + d_z[...].astype(BF16).astype(F32)
    grad_in[...] = value.reshape(grad_in.shape)


def back_parts_kernel(place, conv_a, conv_b, reduce0, reduce1, *outs):
    half = PART // 2
    wide = WIDE // 2
    first = 9 * half
    quarter = WIDTH // 4
    for k, out in enumerate(outs):
        for core in range(2):
            for j in range(4):
                conv = (conv_a, conv_b)[j // 2]

                @pl.when((place[k] == quarter_of(place, j)) & (place[4] == core))
                def _():
                    for tap in range(9):
                        at = (j % 2) * QUARTER_CONV + 16 + tap * quarter + core * half
                        out[tap * half : (tap + 1) * half, :] = conv[at : at + half, :]

            for u in range(SECTIONS):
                reduce = (reduce0, reduce1)[core ^ (u // 2)]

                @pl.when((place[k] == u) & (place[4] == core))
                def _():
                    at = 16 + (u % 2) * WIDE + core * wide
                    out[first : first + wide, :] = reduce[at : at + wide, :]


def stack_kernel(*refs):
    out = refs[-1]
    rows = refs[0].shape[0]
    for j, ref in enumerate(refs[:-1]):
        if len(out.shape) == 3:
            out[j] = ref[...]
        else:
            out[j * rows : (j + 1) * rows, :] = ref[...]


def mixed_kernel(place, reduce, conv, expand, *outs):
    for k, out in enumerate(outs):
        target = place[k + 1]

        @pl.when(target == 0)
        def _():
            out[:, :WIDE] = reduce[...]

        @pl.when(target == 1)
        def _():
            out[...] = conv[...]

        @pl.when(target == 2)
        def _():
            out[:, :WIDE] = expand[...]


def told_kernel(place, n0, n1, n2, n3, notes, out, loss):
    t = place[0]
    out[...] = jnp.zeros_like(out)

    @pl.when(t == SECTIONS - 1)
    def _():
        for r in range(3):
            out[r] = notes[r : r + 1, :]

    total = None
    for k, note in enumerate((n0, n1, n2, n3)):
        u = place[k]
        rows = note[note.shape[0] - NOTE_ROWS :, :].astype(F32)

        def said(i):
            return (rows[3 * i : 3 * i + 1] + rows[3 * i + 1 : 3 * i + 2]) + rows[3 * i + 2 : 3 * i + 3]

        total = said(12) if total is None else total + said(12)

        @pl.when(t == 2)
        def _():
            for r in range(2):
                for b in range(4):
                    lanes = pl.ds(pl.multiple_of(u * WIDE + b * PART, PART), PART)
                    out[r, :, lanes] = said(4 * r + b)

        for section in range(2):

            @pl.when(t == section)
            def _():
                for r in range(2):
                    lanes = pl.ds(pl.multiple_of(u * PART, PART), PART)
                    out[r, :, lanes] = said((10, 8)[section] + r)

    loss[...] = jnp.broadcast_to(total, loss.shape)


def pick_kernel(place, p0, p1, p2, p3, conv, pair):
    for j, p in enumerate((p0, p1, p2, p3)):

        @pl.when(place[0] == j)
        def _():
            pair[:HALF_REDUCE, :] = p[:HALF_REDUCE, :]

        @pl.when(place[1] == j)
        def _():
            conv[...] = p[...]

        @pl.when(place[2] == j)
        def _():
            pair[HALF_REDUCE:, :] = p[: 4 * HALF_EXPAND, :]


def taps_kernel(images, active, out):
    value = active[...].astype(F32)
    y, x = map_places(value.shape[0], images)
    for tap in range(9):
        out[:, tap * PART : (tap + 1) * PART] = tap_shift(value, images, tap, 1, y, x).astype(BF16)


def head(pooled, w_head, w_proj, protos, norm, queue, match, micro, images, dp):
    rows = pooled.shape[0]
    group = rows // micro
    half = group // CROPS
    scale_all = 1.0 / (TEMPER * CROPS * half * micro)
    pre = dot(pooled, w_head)

    def by_micro(v):
        return v.reshape(micro, group, v.shape[-1])

    pre_m = by_micro(pre)
    mean = jnp.mean(pre_m, axis=1, keepdims=True)
    square = jnp.mean(pre_m * pre_m, axis=1, keepdims=True)
    rstd = lax.rsqrt(square - mean * mean + NORM_EPS)
    xhat = (pre_m - mean) * rstd
    y = xhat * norm[0] + norm[1]
    active = (y * sigmoid(y)).astype(BF16).reshape(rows, D)
    embed = dot(active, w_proj) + norm[2, :PROJ]
    recip = lax.rsqrt(jnp.sum(embed * embed, axis=1, keepdims=True) + UNIT_EPS)
    unit = (embed * recip).astype(BF16)
    scores = dot_nt(unit, protos)
    valid = lax.broadcasted_iota(jnp.int32, (1, 4, QUARTER_PAD), 2).reshape(1, 4 * QUARTER_PAD) < QUARTER
    own_mass = jnp.where(valid, jnp.exp(scores / SINK_EPS), 0.0).reshape(micro, CROPS, half, -1)
    queue_mass = jnp.where(valid, jnp.exp(jnp.einsum("cqp,kp->cqk", queue, protos, preferred_element_type=F32) / SINK_EPS), 0.0)
    codes = []
    for m in range(micro):
        for c in range(CROPS):
            a, b = queue_mass[c], own_mass[m, c]
            column = jnp.sum(a, axis=0, keepdims=True) + jnp.sum(b, axis=0, keepdims=True)
            once = jnp.where(valid, 1.0 / column, 0.0)
            a, b = a * once, b * once
            scale = valid.astype(F32)
            for turn in range(2):
                ra = 1.0 / jnp.sum(a * scale, axis=1, keepdims=True)
                rb = 1.0 / jnp.sum(b * scale, axis=1, keepdims=True)
                column = jnp.sum(a * ra, axis=0, keepdims=True) + jnp.sum(b * rb, axis=0, keepdims=True)
                scale = jnp.where(valid, 1.0 / column, 0.0)
            b = b * scale
            codes.append(b / jnp.sum(b, axis=1, keepdims=True))
    targets = []
    for m in range(micro):
        targets.append(jnp.dot(match[m], codes[m * CROPS + 1], precision=HIGH))
        targets.append(jnp.dot(match[m].T, codes[m * CROPS], precision=HIGH))
    target = jnp.concatenate(targets)
    logits = jnp.where(valid, scores / TEMPER, -1e30)
    logp = jax.nn.log_softmax(logits, axis=1)
    loss = -jnp.sum(jnp.where(valid, target * logp, 0.0)) * (TEMPER * scale_all)
    d_scores = ((jnp.exp(logp) * jnp.sum(target, axis=1, keepdims=True) - target) * scale_all).astype(BF16)
    d_unit = dot(d_scores, protos)
    d_embed = (
        recip * d_unit - embed * (recip * recip * recip) * jnp.sum(d_unit * embed, axis=1, keepdims=True)
    ).astype(BF16)
    d_active = dot_nt(d_embed, w_proj)
    d_y = by_micro(d_active) * slope(y)
    by_x = jnp.sum(d_y * xhat, axis=1, keepdims=True)
    plain = jnp.sum(d_y, axis=1, keepdims=True)
    d_pre = (norm[0] * rstd * (d_y - plain / group - xhat * by_x / group)).astype(BF16).reshape(rows, D)
    bias = jnp.pad(jnp.sum(d_embed.astype(F32), axis=0), (0, D - PROJ))
    grads = jnp.stack([jnp.sum(by_x, axis=(0, 1)), jnp.sum(plain, axis=(0, 1)), bias])
    return loss, grads, active, unit, d_scores, d_embed, d_pre


def valid_lanes():
    lane = lax.broadcasted_iota(jnp.int32, (1, 4 * QUARTER_PAD), 1).astype(F32)
    block = jnp.floor((lane + 0.5) * (1.0 / QUARTER_PAD))
    return lane - block * QUARTER_PAD < QUARTER - 0.5


def lanes_at(b, size):
    return pl.ds(pl.multiple_of(b * size, size), size)


def lanes_at(b, size):
    return pl.ds(pl.multiple_of(b * size, size), size)


def mass_kernel(micro, images, told_offsets, place, table, *refs):
    mass, column, match, rows_s, exps = refs[-5:]
    ndp = len(told_offsets)
    valid = valid_lanes()
    size = mass.shape[0] // ndp
    half = images * ndp
    at, said = 0, jnp.zeros((16, half), F32)
    row = lax.broadcasted_iota(jnp.int32, (PROJ, half), 0)
    lane = lax.broadcasted_iota(jnp.int32, (PROJ, half), 1)
    for ref in refs[:-5]:
        rows = CROPS * size + 16
        for j in range(ref.shape[0] // rows):
            mine = pl.ds(pl.multiple_of(j * rows + place[4] * size, 16), size)
            rows_s[lanes_at(place[7] ^ told_offsets[at], size), :] = ref[mine, :]
            pairs = ref[(j + 1) * rows - 16 : (j + 1) * rows, :]
            spot_at = (place[7] ^ told_offsets[at]) * images
            spot = ((row < images) & (lane == row + spot_at)).astype(F32).astype(BF16)
            said = said + dot(pairs, spot)
            at += 1
    step = 128
    steps = mass.shape[0] // step

    def scored(i, sums):
        own = rows_s[lanes_at(i, step), :]
        out = []
        for a in range(4):
            lanes = slice(a * QUARTER_PAD, (a + 1) * QUARTER_PAD)
            value = jnp.exp(dot_nt(own, table[:, a * PROJ : (a + 1) * PROJ]) * (1.0 / SINK_EPS))
            value = jnp.where(valid[:, lanes], value, 0.0)
            exps[lanes_at(i, step), lanes] = value
            out.append(jnp.sum(value, axis=0, keepdims=True))
        return sums + jnp.concatenate(out, axis=1)

    sums = lax.fori_loop(0, steps, scored, jnp.zeros((1, 4 * QUARTER_PAD), F32))
    column[...] = jnp.broadcast_to(sums, column.shape)
    factor = jnp.where(valid, 1.0 / sums, 0.0)

    def divide(i, carry):
        mass[lanes_at(i, step), :] = (exps[lanes_at(i, step), :] * factor).astype(BF16)
        return carry

    lax.fori_loop(0, steps, divide, 0)

    def over(value, by):
        return jnp.floor((value + 0.5) * (1.0 / by))

    row = lax.broadcasted_iota(jnp.int32, (half, half), 0).astype(F32)
    lane = lax.broadcasted_iota(jnp.int32, (half, half), 1).astype(F32)
    block = over(row, images)
    for m in range(micro):
        same = (jnp.abs(block - over(lane, images)) < 0.5) & (jnp.abs(row - block * images - said[m : m + 1, :]) < 0.5)
        there = same.astype(F32)
        match[m] = jnp.where(place[4] == 0, there, there.T).astype(BF16)


def tables_kernel(packed, proj, table, rows, buffer, sem):
    size = THIRD - FIRST + 2
    copy = pltpu.make_async_copy(packed.at[pl.ds(FIRST, size), :], rows, sem)
    copy.start()
    copy.wait()
    wide = SECOND - FIRST
    for a in range(4):
        buffer[pl.ds(a, wide, stride=4), :] = rows[:wide, a * PROJ : (a + 1) * PROJ].astype(F32)
    proj[...] = buffer[...].astype(BF16)
    row = lax.broadcasted_iota(jnp.int32, (size - wide, WIDTH), 0)
    kept = jnp.where(row < QUARTER, rows[wide:, :].astype(F32), 0.0).astype(BF16)
    table[: size - wide, :] = kept
    table[size - wide :, :] = jnp.zeros((QUARTER_PAD - (size - wide), WIDTH), BF16)


def exact_dot(choose, value):
    parts, left = [], value
    for _ in range(3):
        term = left.astype(BF16)
        left = left - term.astype(F32)
        parts.append(term)
    return dot(jnp.concatenate([choose] * 3, axis=1), jnp.concatenate(parts, axis=0))


def by_micro_rows(value, ndp, micro):
    return value.reshape(ndp, micro, value.shape[0] // (ndp * micro), value.shape[1])


def total_of(value):
    return jnp.sum(jnp.sum(value, axis=0), axis=0, keepdims=True)


def regroup(rows, own, images, to_groups):
    ndp = rows // own
    row = lax.broadcasted_iota(jnp.int32, (rows, rows), 0).astype(F32)
    lane = lax.broadcasted_iota(jnp.int32, (rows, rows), 1).astype(F32)
    source, target = (lane, row) if to_groups else (row, lane)
    block = jnp.floor((source + 0.5) * (1.0 / own))
    inner = source - block * own
    part = jnp.floor((inner + 0.5) * (1.0 / images))
    moved = (part * ndp + block) * images + inner - part * images
    return (jnp.abs(moved - target) < 0.5).astype(F32).astype(BF16)


def head_kernel(
    micro, images, offsets, place, pooled_a, pooled_b, w_head, w_proj, table, norm, mass, column, match,
    pooled, active, unit, d_scores, embed, xhat_s, y_s, rstd_s, said,
    scores, own_mass, total, factor,
):
    ndp = len(offsets)
    rows = pooled.shape[0]
    group = rows // micro
    half = group // CROPS
    own = rows // ndp
    queued = mass.shape[0]
    scale_all = 1.0 / (TEMPER * CROPS * half * micro)
    chunk = WIDTH
    chunks = D // chunk
    core = place[4]
    for j, offset in enumerate(offsets):
        source = (pooled_a, pooled_b)[j * own // pooled_a.shape[0]]
        at = j * own % pooled_a.shape[0]
        pooled[lanes_at(place[7] ^ offset, own), :] = source[at : at + own, :]
    low = pooled[...]

    def forward(b, carry):
        lanes = lanes_at(b, chunk)
        pre = by_micro_rows(dot(low, w_head[:, lanes]), ndp, micro)
        gain, shift = norm[0, :, lanes], norm[1, :, lanes]
        xhats, ys = [], []
        for m in range(micro):
            v = pre[:, m]
            mean = total_of(v) * (1.0 / group)
            square = total_of(v * v) * (1.0 / group)
            rstd = lax.rsqrt(square - mean * mean + NORM_EPS)
            xhat = (v - mean) * rstd
            rstd_s[m : m + 1, lanes] = rstd
            xhats.append(xhat)
            ys.append(xhat * gain + shift)
        xhat_s[:, lanes] = jnp.stack(xhats, axis=1).reshape(rows, chunk)
        y = jnp.stack(ys, axis=1).reshape(rows, chunk)
        y_s[:, lanes] = y
        active[:, lanes] = (y * sigmoid(y)).astype(BF16)
        return carry

    lax.fori_loop(0, chunks, forward, 0)
    value = dot(active[...], w_proj[...]) + norm[2, :, :PROJ]
    embed[...] = value
    recip = lax.rsqrt(jnp.sum(value * value, axis=1, keepdims=True) + UNIT_EPS)
    unit_v = dot(regroup(rows, own, images, True), (value * recip).astype(BF16)).astype(BF16)
    unit[...] = unit_v
    valid = valid_lanes()
    for a in range(4):
        lanes = slice(a * QUARTER_PAD, (a + 1) * QUARTER_PAD)
        scores[:, lanes] = dot_nt(unit_v, table[:, a * PROJ : (a + 1) * PROJ])

    step = 128

    def divided(a):
        return a * (1.0 / jnp.sum(a, axis=1, keepdims=True))

    def folded(a):
        return jnp.sum(a.reshape(a.shape[0] // 8, 8, a.shape[1]), axis=0)

    def own_rows(m):
        return slice(m * half, (m + 1) * half)

    queue_sum = column[0:1, :]
    for m in range(micro):
        a = scores[lanes_at(m * CROPS + core, half), :]
        a = jnp.where(valid, jnp.exp(a * (1.0 / SINK_EPS)), 0.0)
        inverse = jnp.where(valid, 1.0 / (queue_sum + jnp.sum(a, axis=0, keepdims=True)), 0.0)
        factor[m : m + 1, :] = queue_sum * inverse
        factor[micro + m : micro + m + 1, :] = jnp.ones_like(inverse)
        own_mass[own_rows(m), :] = a * inverse

    def turn(i, carry):
        def block(i, carry):
            at = lanes_at(i, step)
            e_of = [mass[at, b * PART : (b + 1) * PART].astype(F32) for b in range(4 * QUARTER_PAD // PART)]
            rows_by = []
            for m in range(micro):
                sums = None
                for b, e in enumerate(e_of):
                    more = e * factor[m : m + 1, b * PART : (b + 1) * PART]
                    sums = more if sums is None else sums + more
                rows_by.append(1.0 / jnp.sum(sums, axis=1, keepdims=True))
            for b in range(4 * QUARTER_PAD // PART):
                lanes = slice(b * PART, (b + 1) * PART)
                e = mass[at, lanes].astype(F32)
                for m in range(micro):
                    total[m, :, lanes] += folded(e * rows_by[m])
            return carry

        total[...] = jnp.zeros_like(total)
        lax.fori_loop(0, queued // step, block, 0)
        for m in range(micro):
            scale = factor[micro + m : micro + m + 1, :]
            a = divided(own_mass[own_rows(m), :] * scale)
            sums = jnp.sum(total[m], axis=0, keepdims=True) * factor[m : m + 1, :]
            more = jnp.where(valid, 1.0 / (sums + jnp.sum(a, axis=0, keepdims=True)), 0.0)
            factor[m : m + 1, :] = factor[m : m + 1, :] * more
            factor[micro + m : micro + m + 1, :] = scale * more
        return carry

    lax.fori_loop(0, 2, turn, 0)

    def losses(m, loss):
        mine, there = lanes_at(m, half), lanes_at(m * CROPS + 1 - core, half)
        codes = divided(own_mass[mine, :] * factor[pl.ds(micro + m, 1), :])
        goal = exact_dot(match[m], codes)
        logits = jnp.where(valid, scores[there, :] * (1.0 / TEMPER), -1e30)
        logits = logits - jnp.max(logits, axis=1, keepdims=True)
        power = jnp.exp(logits)
        summed = jnp.sum(power, axis=1, keepdims=True)
        weight = jnp.sum(goal, axis=1, keepdims=True) / summed
        d_low = ((power * weight - goal) * scale_all).astype(BF16)
        d_scores[mine, :] = d_low
        d_unit = None
        for a in range(4):
            more = dot(d_low[:, a * QUARTER_PAD : (a + 1) * QUARTER_PAD], table[:, a * PROJ : (a + 1) * PROJ])
            d_unit = more if d_unit is None else d_unit + more
        said[mine, :] = d_unit
        return loss + jnp.sum(goal * (logits - jnp.log(summed)), axis=1, keepdims=True)

    loss = lax.fori_loop(0, micro, losses, jnp.zeros((half, 1), F32))
    loss = jnp.sum(loss, axis=0, keepdims=True) * (-TEMPER * scale_all)
    said[micro * half :, :] = jnp.broadcast_to(loss, (8, PROJ))


def head_back_kernel(
    micro, images, ndp, place, here, there, embed, w_proj, w_head, norm, xhat_s, y_s, rstd_s,
    d0, d1, d2, d3, notes, d_embed, d_pre, d_unit, d_own,
):
    rows = embed.shape[0]
    group = rows // micro
    half = group // CROPS
    own = rows // ndp
    chunk = WIDTH
    chunks = D // chunk
    for m in range(micro):
        d_unit[lanes_at(m * CROPS + place[5], half), :] = here[m * half : (m + 1) * half, :]
        d_unit[lanes_at(m * CROPS + place[4], half), :] = there[m * half : (m + 1) * half, :]
    value = embed[...]
    recip = lax.rsqrt(jnp.sum(value * value, axis=1, keepdims=True) + UNIT_EPS)
    d_back = exact_dot(regroup(rows, own, images, False), d_unit[...])
    along = jnp.sum(d_back * value, axis=1, keepdims=True)
    d_low = (recip * d_back - value * (recip * recip * recip) * along).astype(BF16)
    d_embed[...] = d_low
    notes[...] = jnp.zeros_like(notes)
    notes[2:3, :PROJ] = jnp.sum(d_low.astype(F32), axis=0, keepdims=True)
    loss = here[micro * half : micro * half + 1, :] + there[micro * half : micro * half + 1, :]
    notes[3:4, :PROJ] = loss

    def backward(b, carry):
        lanes = lanes_at(b, chunk)
        d_y = by_micro_rows(dot_nt(d_low, w_proj[lanes, :]) * slope(y_s[:, lanes]), ndp, micro)
        xhat = by_micro_rows(xhat_s[:, lanes], ndp, micro)
        gain = norm[0, :, lanes]
        values, by_xs, plains = [], None, None
        for m in range(micro):
            by_x = total_of(d_y[:, m] * xhat[:, m])
            plain = total_of(d_y[:, m])
            by_xs = by_x if by_xs is None else by_xs + by_x
            plains = plain if plains is None else plains + plain
            value = d_y[:, m] - plain * (1.0 / group) - xhat[:, m] * (by_x * (1.0 / group))
            values.append(gain * rstd_s[m : m + 1, lanes] * value)
        notes[0:1, lanes] = by_xs
        notes[1:2, lanes] = plains
        d_pre[:, lanes] = jnp.stack(values, axis=1).reshape(rows, chunk).astype(BF16)
        return carry

    lax.fori_loop(0, chunks, backward, 0)
    mine = d_pre[lanes_at(place[7], own), :]

    def to_pooled(b, carry):
        d_own[:, lanes_at(b, chunk)] = dot_nt(mine, w_head[lanes_at(b, chunk), :]).astype(BF16)
        return carry

    lax.fori_loop(0, chunks, to_pooled, 0)
    for j, out in enumerate((d0, d1, d2, d3)):
        out[...] = d_own[:, j * WIDE : (j + 1) * WIDE]


def interleave(width):
    row = lax.broadcasted_iota(jnp.int32, (4 * width, 4 * width), 0)
    column = lax.broadcasted_iota(jnp.int32, (4 * width, 4 * width), 1)
    return (column == 4 * (row & (width - 1)) + (row >> (width.bit_length() - 1))).astype(F32).astype(BF16)


def own_columns(place, own):
    row = lax.broadcasted_iota(jnp.int32, (WIDTH, own), 0)
    lane = lax.broadcasted_iota(jnp.int32, (WIDTH, own), 1)
    return (row == lane + place[7] * own).astype(F32).astype(BF16)


def tail_grads_kernel(place, active, unit, d_here, d_there, d_embed, out):
    @pl.when(place[0] == SECTIONS - 1)
    def _():
        own = out.shape[0]
        choose = own_columns(place, own)
        rows = active.shape[0]
        wide = jnp.concatenate([active[:, b * WIDTH : (b + 1) * WIDTH] for b in range(4)], axis=0)
        wide = dot_nt(wide, interleave(PART)).astype(BF16)
        half = d_here.shape[0] // 2
        units = []
        for core in (place[5], place[4]):
            units.append(jnp.concatenate([unit[lanes_at(m * CROPS + core, half), :] for m in range(2)], axis=0))
        proj = jnp.zeros((own, WIDTH), F32)
        proto = jnp.zeros((own, QUARTER_PAD), F32)
        for a in range(4):
            some = choose[a * PROJ : (a + 1) * PROJ, :]
            own_e = dot(d_embed[...], some).astype(BF16)
            column = [wide[b * rows : (b + 1) * rows, a * PART : (a + 1) * PART] for b in range(4)]
            proj = proj + dot_tn(own_e, jnp.concatenate(column, axis=1))
            for own_unit, d_scores in zip(units, (d_here, d_there)):
                own_u = dot(own_unit, some).astype(BF16)
                proto = proto + dot_tn(own_u, d_scores[:, a * QUARTER_PAD : (a + 1) * QUARTER_PAD])
        out[:, :WIDTH] = proj
        out[:, WIDTH:] = proto


def head_grads_kernel(place, pooled, d_pre, tail, out, parts):
    @pl.when(place[0] != SECTIONS - 1)
    def _():
        out[...] = jnp.zeros_like(out)

    @pl.when(place[0] == SECTIONS - 1)
    def _():
        own = out.shape[0]
        choose = own_columns(place, own)
        weave = interleave(PART)
        own_d = [dot(d_pre[:, q * WIDTH : (q + 1) * WIDTH], choose).astype(BF16) for q in range(4)]
        own_d = jnp.concatenate(own_d, axis=1)

        def product(b, carry):
            parts[:, lanes_at(b, WIDTH)] = dot_tn(own_d, pooled[:, lanes_at(b, WIDTH)]).astype(BF16)
            return carry

        lax.fori_loop(0, 4, product, 0)

        def mix(b, carry):
            mixed = []
            for j in range(4):
                lanes = pl.ds(pl.multiple_of(b * WIDTH + j * PART, PART), PART)
                four = [parts[q * own : (q + 1) * own, lanes] for q in range(4)]
                mixed.append(jnp.concatenate(four, axis=1))
            mixed = dot(jnp.concatenate(mixed, axis=0), weave)
            for j in range(4):
                lanes = pl.ds(pl.multiple_of((4 * b + j) * WIDTH, WIDTH), WIDTH)
                out[:, lanes] = mixed[j * own : (j + 1) * own, :]
            return carry

        lax.fori_loop(0, 4, mix, 0)
        out[:, FIRST:] = tail[:, : out.shape[1] - FIRST]


def finish_kernel(place, base, reduce, conv, expand, m1, m2, m3, out, buffer, sem):
    mixed = (None, m1, m2, m3)
    t = place[0]

    def write(lanes):
        copy = pltpu.make_async_copy(buffer.at[:, pl.ds(0, lanes)], out.at[:, pl.ds(0, lanes)], sem)
        copy.start()
        copy.wait()

    @pl.when(t == 0)
    def _():
        for u in range(SECTIONS):
            piece = reduce if u == 0 else mixed[u]
            buffer[:, u * WIDE : (u + 1) * WIDE] = piece[:, :WIDE].astype(F32)
        write(D)

    @pl.when(t == 1)
    def _():
        for u in range(SECTIONS):
            piece = conv if u == 1 else mixed[u ^ 1]
            for tap in range(9):
                at = tap * WIDTH + u * PART
                buffer[:, at : at + PART] = piece[:, tap * PART : (tap + 1) * PART].astype(F32)
        write(9 * WIDTH)

    @pl.when(t == 2)
    def _():
        four = [expand if u == 2 else mixed[u ^ 2] for u in range(SECTIONS)]
        weave = interleave(PART)
        for b in range(WIDTH // PART):
            lanes = slice(b * PART, (b + 1) * PART)
            row = jnp.concatenate([f[:, lanes] for f in four], axis=1)
            buffer[:, 4 * b * PART : 4 * (b + 1) * PART] = dot(row, weave)
        write(D)


def unpack_kernel(packed, out, buffer):
    rows = packed.shape[0]
    for b in range(4):
        buffer[b] = packed[:, b * PART : (b + 1) * PART].astype(F32)
    for q in range(4):
        for b in range(4):
            at = q * WIDTH + b * PART
            out[:, at : at + PART] = buffer[b, pl.ds(q, rows // 4, stride=4), :].astype(BF16)


def unpack(packed, rows):
    step = 1024
    return pl.pallas_call(
        unpack_kernel,
        name="unpack",
        out_shape=shape((rows // 4, 4 * WIDTH), BF16),
        grid=(rows // step,),
        in_specs=[pl.BlockSpec((step, WIDTH), lambda i: (i, 0))],
        out_specs=pl.BlockSpec((step // 4, 4 * WIDTH), lambda i: (i, 0)),
        scratch_shapes=[pltpu.VMEM((4, step, PART), F32)],
        compiler_params=pltpu.CompilerParams(vmem_limit_bytes=16 * 2**20),
        cost_estimate=cost(4),
    )(packed)


def pack_kernel(place, packed, norm, o0, o1, o2, o3, rows, buffer, sem):
    outs = (o0, o1, o2, o3)
    t, core = place[0], place[4]

    def run(copies):
        for copy in copies:
            copy.start()
        return copies

    def lanes_of(target, lanes):
        return pl.ds(target * lanes, lanes)

    @pl.when(t == 0)
    def _():
        half = D // 2
        copies = []
        for k, out in enumerate(outs):
            source = packed.at[pl.ds(pl.multiple_of(core * half, half), half), lanes_of(k, PART)]
            copies.append(pltpu.make_async_copy(source, out.at[pl.ds(16, half), :], sem.at[k]))
        run(copies)
        for k, out in enumerate(outs):
            out[:16, :] = tell_norm(norm, k * PART)
        for copy in copies:
            copy.wait()

    @pl.when(t == 1)
    def _():
        quarter = WIDTH // 4
        copies = []
        for k, out in enumerate(outs):
            for tap in range(9):
                at = pl.multiple_of(tap * WIDTH + place[8] * quarter, quarter)
                source = packed.at[pl.ds(at, quarter), lanes_of(1 ^ k, PART)]
                target = out.at[pl.ds(16 + tap * quarter, quarter), :]
                copies.append(pltpu.make_async_copy(source, target, sem.at[9 * k + tap]))
        run(copies)
        for k, out in enumerate(outs):
            out[:16, :] = tell_norm(norm, (1 ^ k) * PART)
        for copy in copies:
            copy.wait()

    @pl.when(t == 2)
    def _():
        size = rows.shape[0]
        copy = pltpu.make_async_copy(packed.at[pl.ds(pl.multiple_of(core * size, size), size), :], rows, sem.at[0])
        copy.start()
        copy.wait()
        for b in range(4):
            buffer[b] = rows[:, b * PART : (b + 1) * PART].astype(F32)
        for k, out in enumerate(outs):
            u = 2 ^ k
            for b in range(4):
                at = b * HALF_EXPAND
                lane = u * WIDE + b * PART
                out[at : at + 16, :] = tell_norm(norm, lane)
                out[at + 16 : at + HALF_EXPAND, :] = buffer[b, pl.ds(u, size // 4, stride=4), :].astype(BF16)


def pack(place, packed, norm):
    rows = 4 * (WIDTH // 2)
    return pl.pallas_call(
        pack_kernel,
        name="pack",
        out_shape=[shape((QUARTER_CONV, PART), BF16)] * 4,
        in_specs=[
            pl.BlockSpec(memory_space=pltpu.SMEM),
            pl.BlockSpec(memory_space=pltpu.HBM),
            pl.BlockSpec(memory_space=pltpu.VMEM),
        ],
        out_specs=[pl.BlockSpec(memory_space=pltpu.VMEM)] * 4,
        scratch_shapes=[
            pltpu.VMEM((rows, WIDTH), BF16), pltpu.VMEM((4, rows, PART), F32), pltpu.SemaphoreType.DMA((36,)),
        ],
        compiler_params=pltpu.CompilerParams(vmem_limit_bytes=12 * 2**20),
        cost_estimate=cost(2),
    )(place, hbm(packed), norm)


def multiple(value, step):
    return value if isinstance(value, int) else pl.multiple_of(value, step)


def pair_kernel(place, a, b, keep, out, full):
    full[...] = dot_tn(a[...], b[...])
    own = keep.shape[1]
    for z in range(keep.shape[0]):
        mine = (2 * z + place[4]) * own
        other = (2 * z + place[5]) * own
        keep[z] = full[pl.ds(pl.multiple_of(mine, own), own), :]
        out[z] = full[pl.ds(pl.multiple_of(other, own), own), :].astype(BF16)


def image_pair_kernel(place, d0, d1, d2, d3, image, keep, out, d_full, full):
    fill(place, (d0, d1, d2, d3), d_full)
    lanes = pl.ds(pl.multiple_of(place[0] * WIDE, WIDE), WIDE)
    pair_kernel(place, d_full, image.at[:, lanes], keep, out, full)


def cross_kernel(place, keep, came, own, o1, o2, o3):
    for k, o in enumerate((own, o1, o2, o3)):
        z = place[6] ^ k
        o[...] = (keep[z] + came[z].astype(F32)).astype(o.dtype)


def near_kernel(place, keep, came, kept, out):
    for j in range(2):
        mine, other = place[6] ^ (2 * j), place[6] ^ (2 * j + 1)
        kept[j] = keep[mine] + came[mine].astype(F32)
        out[j] = (keep[other] + came[other].astype(F32)).astype(BF16)


def far_kernel(keep, came, kept, out):
    kept[...] = keep[0] + came[0].astype(F32)
    out[...] = (keep[1] + came[1].astype(F32)).astype(BF16)


def last_kernel(keep, came, out):
    out[...] = (keep[...] + came[...].astype(F32)).astype(BF16)


def add_kernel(own, r1, r2, r3, out):
    out[...] = ((own[...] + r1[...].astype(F32)) + (r2[...].astype(F32) + r3[...].astype(F32))).astype(BF16)


def after(value, *others):
    return lax.optimization_barrier((value, *others))[0]


def body(image, section_weights, section_norms, queue, pairing):
    micro, images = image.shape[0], image.shape[2]
    ndp = lax.axis_size("dp")
    t = lax.axis_index("section")
    dp = lax.axis_index("dp")
    core = dp % 2
    place = jnp.stack([t ^ k for k in range(SECTIONS)] + [core, 1 - core, dp // 2, dp, dp % 4]).astype(jnp.int32)
    cells = CROPS * PLACES * images
    rows = micro * cells
    count = float(cells * ndp)
    packed = section_weights[0]
    norm3 = section_norms.transpose(1, 0, 2)
    param_rows = packed.shape[0]
    own = WIDTH // ndp
    k = functools.partial

    def pieces_of(width, dtype):
        return shape((rows, width), dtype)

    own_message, *messages = pack(place, packed, norm3)
    came = [own_message]
    for j in range(1, SECTIONS):
        came.append(lax.ppermute(messages[j - 1], "section", [(u, u ^ j) for u in range(3)]))
    flat = call(
        retile_kernel, shape((rows, D), BF16),
        image.transpose(0, 1, 3, 4, 2, 5).reshape(rows // images, images, D),
        us=2,
    )
    queue_size = CROPS * queue.shape[1]
    note = call(note_kernel, shape((queue_size + 16, PROJ), BF16), pairing, queue, us=0.5)
    steps = [1 << bit for bit in range(ndp.bit_length() - 1)]
    told, told_offsets = gather_dp(note, [(step,) for step in steps[:-1]])
    *came, flat, told[0] = lax.optimization_barrier((*came, flat, *told))[:6]
    told, told_offsets = [rows_of(told)], [sum(told_offsets, [])]
    conv_part, pair_part = call(
        pick_kernel,
        (shape((QUARTER_CONV, PART), BF16), shape((HALF_REDUCE + 4 * HALF_EXPAND, PART), BF16)),
        place, *came,
    )
    pair_parts = (pair_part, flip(pair_part, "dp", 1))
    conv_near = flip(conv_part, "dp", 2)
    sums_of = shape((8, PART), F32)
    pre0, part = call(
        k(reduce_kernel, micro), (pieces_of(PART, F32), sums_of), place, flat, *pair_parts, us=2
    )
    sums0 = sum_dp(part)
    active0 = call(k(active_kernel, micro, count), pieces_of(PART, BF16), pre0, sums0, pair_part, us=1)
    actives0 = gather_xor(active0, "section")

    conv_part = rows_of([conv_part, after(conv_near, active0)])
    w_conv = (conv_part, flip(conv_part, "dp", 1))
    told.append(flip(after(told[0], active0), "dp", steps[-1]))
    told_offsets.append([offset ^ steps[-1] for offset in told_offsets[0]])
    w_proj, table = pl.pallas_call(
        tables_kernel,
        name="tables",
        out_shape=(shape((D, PROJ), BF16), shape((QUARTER_PAD, WIDTH), BF16)),
        in_specs=[pl.BlockSpec(memory_space=pltpu.HBM)],
        out_specs=(pl.BlockSpec(memory_space=pltpu.VMEM), pl.BlockSpec(memory_space=pltpu.VMEM)),
        scratch_shapes=[
            pltpu.VMEM((THIRD - FIRST + 2, WIDTH), BF16), pltpu.VMEM((D, PROJ), F32), pltpu.SemaphoreType.DMA,
        ],
        compiler_params=pltpu.CompilerParams(vmem_limit_bytes=12 * 2**20),
        cost_estimate=cost(1.5),
    )(hbm(after(packed, active0)))
    taps = call(k(taps_kernel, images), pieces_of(9 * PART, BF16), active0, us=1.3)
    back_rows = 9 * PART // 2 + WIDE // 2
    back_own = call(
        back_parts_kernel, [shape((back_rows, PART), BF16)] * 4, place, *w_conv, *pair_parts, us=1
    )
    joined = lax.optimization_barrier((*actives0, table, taps, told[1], *back_own))
    actives0, (table, taps, told[1]), back_own = joined[:4], joined[4:7], joined[7:]
    pre1, part = call(
        k(conv_kernel, micro, images),
        (pieces_of(PART, F32), sums_of),
        place, *actives0, *w_conv,
        scratch=[pltpu.VMEM((rows, WIDTH), BF16), pltpu.VMEM((WIDTH, 9 * PART), BF16)],
        us=3,
    )
    sums1 = sum_dp(part)
    active1_own = call(k(active_kernel, micro, count), pieces_of(PART, BF16), pre1, sums1, conv_part, us=1)
    actives1 = gather_xor(active1_own, "section")
    natural = unpack(after(packed, active1_own), FIRST)
    head_rows = rows // PLACES * ndp
    lanes = 4 * QUARTER_PAD
    stages = dp_stages()
    head_stages = stages[1:] + stages[:1]
    offsets = [0]
    for steps in head_stages:
        offsets = offsets + [o ^ step for step in steps for o in offsets]
    small = head_rows <= 128 and images * ndp == 32 and queue.shape[1] * ndp <= 512
    if small:
        queued = ndp * queue.shape[1]
        mass, column, match = call(
            k(mass_kernel, micro, images, sum(told_offsets, [])),
            (
                shape((queued, lanes), BF16), shape((8, lanes), F32),
                shape((micro, images * ndp, images * ndp), BF16),
            ),
            place, after(table, active1_own), *told,
            scratch=[pltpu.VMEM((queued, PROJ), BF16), pltpu.VMEM((queued, lanes), F32)],
            vmem=16, us=5,
        )
    joined = lax.optimization_barrier((*actives1, natural, *([mass] if small else [])))
    actives1, natural = joined[:4], joined[4]
    mass = joined[5] if small else None
    active1, pre2, part, w_expand = call(
        k(expand_kernel, micro),
        (pieces_of(WIDTH, BF16), pieces_of(WIDE, F32), shape((8, WIDE), F32), shape((WIDTH, WIDE), BF16)),
        place, *actives1, *pair_parts,
        us=2,
    )
    back_own = lax.optimization_barrier((*back_own, part))[:4]
    back_came = [back_own[0]] + [flip(back_own[j], "section", j) for j in range(1, SECTIONS)]

    sums2 = sum_dp(part)
    pooled = call(
        k(pool_kernel, micro, images, count),
        shape((rows // PLACES, WIDE), BF16),
        place, pre2, sums2, pair_part, flat,
        us=1.6,
    )

    per_dp = rows // PLACES
    came_p = gather_xor(pooled, "section")[::-1]
    pooled_here = call(lanes_kernel, shape((per_dp, D), BF16), *came_p, us=0.3)
    parts, _ = gather_dp(pooled_here, head_stages)
    if small:
        all_pooled, active3, unit, d_scores, embed, *kept, said = call(
            k(head_kernel, micro, images, offsets),
            [
                shape((head_rows, D), BF16), shape((head_rows, D), BF16), shape((head_rows, PROJ), BF16),
                shape((head_rows // 2, lanes), BF16), shape((head_rows, PROJ), F32), shape((head_rows, D), F32),
                shape((head_rows, D), F32), shape((8, D), F32), shape((head_rows // 2 + 8, PROJ), F32),
            ],
            place, *parts, natural, w_proj, table, norm3, mass, column, match,
            scratch=[
                pltpu.VMEM((head_rows, lanes), F32), pltpu.VMEM((head_rows // 2, lanes), F32),
                pltpu.VMEM((micro, 8, lanes), F32), pltpu.VMEM((8, lanes), F32),
            ],
            vmem=15, us=12,
        )
        *d_pooled, notes3, d_embed, d_pre3 = call(
            k(head_back_kernel, micro, images, ndp),
            [shape((per_dp, WIDE), BF16)] * 4
            + [shape((8, D), F32), shape((head_rows, PROJ), BF16), shape((head_rows, D), BF16)],
            place, said, flip(said, "dp", 1), embed, w_proj, natural, norm3, *kept,
            scratch=[pltpu.VMEM((head_rows, PROJ), F32), pltpu.VMEM((per_dp, D), BF16)],
            us=5,
        )
    else:
        all_pooled = jnp.concatenate(parts)
        offset = jnp.array(offsets, jnp.int32)
        head_order = jnp.arange(head_rows, dtype=jnp.int32)
        block, inner = head_order // per_dp, head_order % per_dp
        group, single = inner // images, inner % images
        position = (group * ndp + (offset[block] ^ dp)) * images + single
        order = (position[None, :] == head_order[:, None]).astype(BF16)
        told = jnp.concatenate(told).reshape(ndp, queue_size + 16, PROJ)
        pairs = told[:, queue_size : queue_size + micro, :images].astype(jnp.int32)
        told_offset = jnp.array(sum(told_offsets, []), jnp.int32)
        pairs_dp = (told_offset ^ dp)[None, :] == jnp.arange(ndp, dtype=jnp.int32)[:, None]
        pairs = jnp.sum(jnp.where(pairs_dp[:, :, None, None], pairs[None], 0), axis=1)
        left = jnp.arange(images * ndp, dtype=jnp.int32)
        pairs = pairs.transpose(1, 0, 2).reshape(micro, ndp * images)
        match = ((left // images * images + pairs)[:, :, None] == left[None, None, :]).astype(F32)
        all_pooled = dot(order, all_pooled).astype(BF16)
        protos = jnp.concatenate([table[:, a * PROJ : (a + 1) * PROJ] for a in range(4)], axis=0)
        queue_all = told[:, :queue_size].reshape(ndp, CROPS, queue.shape[1], PROJ)
        queue_rows = queue_all.transpose(1, 0, 2, 3).reshape(CROPS, -1, PROJ)
        loss, grads3, active3, unit, d_scores, d_embed, d_pre3 = head(
            all_pooled, natural, w_proj, protos, norm3[:, 0], queue_rows, match, micro, images, dp
        )
        notes3 = jnp.concatenate([grads3, jnp.full((5, D), loss)])
        d_pooled = dot_nt(dot_tn(order[:, :per_dp], d_pre3).astype(BF16), natural).astype(BF16)
        d_pooled = [d_pooled[:, j * WIDE : (j + 1) * WIDE] for j in range(SECTIONS)]
        d_scores = d_scores.reshape(micro, CROPS, head_rows // 4, lanes)
        d_scores = lax.dynamic_index_in_dim(d_scores, 1 - core, 1, keepdims=False).reshape(-1, lanes)

    joined = lax.optimization_barrier((*d_pooled, *back_came))
    d_pooled, back_came = joined[:SECTIONS], joined[SECTIONS:]
    came_d = [flip(d_pooled[3 ^ j], "section", j) for j in range(1, SECTIONS)]
    back_half = call(stack_kernel, shape((SECTIONS, back_rows, PART), BF16), *back_came, us=0.6)
    back_halves = (back_half, flip(back_half, "dp", 1))
    d_z, part = call(
        k(out_back_kernel, micro, images, count),
        (pieces_of(WIDE, F32), shape((8, WIDE), F32)),
        place, pre2, sums2, pair_part, flat, d_pooled[3], *came_d,
        us=1.8,
    )
    back2 = sum_dp(part)
    d_pre2, *partial = call(
        k(expand_back_kernel, micro, count),
        [pieces_of(WIDE, BF16)] + [pieces_of(PART, BF16)] * 4,
        place, pre2, sums2, d_z, back2, pair_part, w_expand,
        scratch=[pltpu.VMEM((rows, WIDTH), F32)],
        us=2,
    )
    partial = [partial[0]] + [flip(partial[j], "section", j) for j in range(1, SECTIONS)]

    def scatter_start(a, b, width):
        if ndp != 8:
            return dot_tn(a, b)
        keep, out = call(
            pair_kernel,
            (shape((4, own, width), F32), shape((4, own, width), BF16)),
            place, a, b,
            scratch=[pltpu.VMEM((WIDTH, width), F32)],
            us=2.5,
        )
        return keep, flip(out, "dp", 1)

    def scatter_cross(started, *others):
        if ndp != 8:
            return [lax.psum_scatter(started.astype(BF16), "dp", scatter_dimension=0, tiled=True)]
        keep, came = started
        if others:
            keep = after(keep, *others)
        dims = keep.shape[1:]
        kept, *out = call(
            cross_kernel, [shape(dims, F32)] + [shape(dims, BF16)] * 3, place, keep, came
        )
        return [kept] + [flip(out[j], "dp", 2 * (j + 1)) for j in range(3)]

    def scatter_near(started, *others):
        if ndp != 8:
            return lax.psum_scatter(started.astype(BF16), "dp", scatter_dimension=0, tiled=True), None
        keep, came = started
        if others:
            keep = after(keep, *others)
        dims = (2, *keep.shape[1:])
        kept, out = call(near_kernel, (shape(dims, F32), shape(dims, BF16)), place, keep, came, us=0.7)
        return kept, flip(out, "dp", 2)

    def scatter_far(started, *others):
        if ndp != 8:
            return started
        keep, came = started
        if others:
            keep = after(keep, *others)
        dims = keep.shape[1:]
        kept, out = call(far_kernel, (shape(dims, F32), shape(dims, BF16)), keep, came, us=0.5)
        return kept, flip(out, "dp", 4)

    def scatter_last(started):
        if ndp != 8:
            return started[0].astype(BF16)
        return call(last_kernel, shape(started[0].shape, BF16), *started, us=0.4)

    def scatter_finish(crossed):
        if ndp != 8:
            return crossed[0].astype(BF16)
        return call(add_kernel, shape(crossed[0].shape, BF16), *crossed, us=0.6)

    expand_near = scatter_near(scatter_start(d_pre2, active1, WIDTH))
    tail = call(
        tail_grads_kernel,
        shape((own, WIDTH + QUARTER_PAD), F32),
        place, after(active3, d_pre2), unit, d_scores, flip(d_scores, "dp", 1), d_embed,
        us=3,
    )
    joined = lax.optimization_barrier((*partial, tail, *expand_near[: 2 if ndp == 8 else 1]))
    partial, tail, expand_near = joined[:SECTIONS], joined[SECTIONS], joined[SECTIONS + 1 :]

    d_y1, part = call(
        k(silu_back_kernel, micro, count),
        (pieces_of(PART, F32), sums_of),
        *partial, pre1, sums1, conv_part,
    )
    back1 = sum_dp(part)
    d_pre1_own = call(
        k(norm_back_kernel, micro, count), pieces_of(PART, BF16), d_y1, pre1, sums1, back1, conv_part
    )
    d_pre1s = gather_xor(d_pre1_own, "section")
    expand_far = scatter_far(expand_near, d_pre1_own)
    base = call(
        head_grads_kernel,
        shape((own, param_rows), F32),
        place, after(all_pooled, d_pre1_own), d_pre3, tail,
        scratch=[pltpu.VMEM((4 * own, D), BF16)],
        us=4,
    )
    joined = lax.optimization_barrier((*d_pre1s, base, *expand_far))
    d_pre1s, base, expand_far = joined[:SECTIONS], joined[SECTIONS], joined[SECTIONS + 1 :]
    d_pre1, d_y0, part = call(
        k(conv_back_kernel, micro, images, count),
        (pieces_of(WIDTH, BF16), pieces_of(PART, F32), sums_of),
        place, *d_pre1s, *back_halves, pre0, sums0, pair_part,
        scratch=[pltpu.VMEM((9 * PART, WIDTH), BF16)],
        us=3.5,
    )
    conv_started = scatter_start(d_pre1, taps, 9 * PART)
    back0 = sum_dp(part)
    d_pre0_own = call(
        k(last_norm_back_kernel, micro, count),
        shape((rows + NOTE_ROWS, PART), BF16),
        place, d_y0, pre0, sums0, back0, pair_part, back2, back1, notes3,
    )
    d_pre0s = gather_xor(d_pre0_own, "section")
    conv_near_sum = scatter_near(conv_started, d_pre0_own)
    joined = lax.optimization_barrier((*d_pre0s, conv_near_sum[0]))
    d_pre0s, conv_near_sum = joined[:SECTIONS], (joined[SECTIONS], conv_near_sum[1])
    conv_far = scatter_far(conv_near_sum)

    if ndp == 8:
        keep, out, d_pre0 = call(
            image_pair_kernel,
            (shape((4, own, WIDE), F32), shape((4, own, WIDE), BF16), pieces_of(WIDTH, BF16)),
            place, *d_pre0s, flat,
            scratch=[pltpu.VMEM((WIDTH, WIDE), F32)],
            us=2.5,
        )
        reduce_started = keep, flip(out, "dp", 1)
    else:
        d_pre0 = jnp.stack(d_pre0s)[place[:SECTIONS], :rows].transpose(1, 0, 2).reshape(rows, WIDTH)
        reduce_started = dot_tn(d_pre0, lax.dynamic_slice_in_dim(flat, t * WIDE, WIDE, 1))
    reduce_crossed = scatter_cross(reduce_started)
    grad_in = call(
        reduce_back_kernel,
        shape((rows // images, images, WIDE), F32),
        place, d_pre0, *back_halves, d_z,
        scratch=[pltpu.VMEM((WIDE, WIDTH), BF16)],
        us=2,
    )
    norm_grads, loss = call(
        told_kernel, (shape((3, 1, D), F32), shape((8, PROJ), F32)), place, *d_pre0s, notes3, us=0.5
    )
    g_conv = scatter_last(conv_far)
    g_expand = scatter_last(expand_far)
    joined = lax.optimization_barrier((*reduce_crossed, grad_in, norm_grads, g_conv, g_expand))
    *reduce_crossed, grad_in, norm_grads, g_conv, g_expand = joined
    g_reduce = scatter_finish(reduce_crossed)
    mixed = call(mixed_kernel, [shape(g_conv.shape, BF16)] * 3, place, g_reduce, g_conv, g_expand, us=0.3)
    mixed = [
        lax.ppermute(mixed[j - 1], "section", [(u ^ j, u) for u in range(3)]) for j in range(1, SECTIONS)
    ]
    weight_grads = pl.pallas_call(
        finish_kernel,
        name="finish",
        out_shape=shape((own, param_rows), F32),
        in_specs=[pl.BlockSpec(memory_space=pltpu.SMEM), pl.BlockSpec(memory_space=pltpu.HBM)]
        + [pl.BlockSpec(memory_space=pltpu.VMEM)] * 6,
        out_specs=pl.BlockSpec(memory_space=pltpu.HBM),
        scratch_shapes=[pltpu.VMEM((own, 9 * WIDTH), F32), pltpu.SemaphoreType.DMA],
        input_output_aliases={1: 0},
        compiler_params=pltpu.CompilerParams(vmem_limit_bytes=12 * 2**20),
        cost_estimate=cost(2),
    )(place, base, g_reduce, g_conv, g_expand, *mixed)
    grad_in = grad_in.reshape(micro, CROPS, SIDE, SIDE, images, WIDE).transpose(0, 1, 4, 2, 3, 5)
    return (loss[0, 0], grad_in, weight_grads.T[None], norm_grads.transpose(1, 0, 2))


def solution(mesh):
    in_specs = (
        P(None, None, "dp", None, None, None),
        P("section", None, None),
        P("section", None, None),
        P(None, "dp", None),
        P(None, "dp"),
    )
    out_specs = (
        P(),
        P(None, None, "dp", None, None, "section"),
        P("section", None, "dp"),
        P("section", None, None),
    )
    return jax.shard_map(body, mesh=mesh, in_specs=in_specs, out_specs=out_specs, check_vma=False)
```

```python
import functools

import jax
import jax.numpy as jnp
from jax import lax
from jax.experimental import pallas as pl
from jax.experimental.pallas import tpu as pltpu
from jax.sharding import PartitionSpec as P

D = 2048
WIDTH = 512
PROJ = 128
PROTOS = 3000
SIDE = 7
CROPS = 2
SECTIONS = 4
PART = WIDTH // SECTIONS
WIDE = D // SECTIONS
QUARTER = PROTOS // 4
QUARTER_PAD = 768
PLACES = SIDE * SIDE
FIRST = D * (D // WIDTH)
SECOND = FIRST + D * PROJ // WIDTH
THIRD = SECOND + PROTOS * PROJ // WIDTH
HALF_REDUCE = 16 + D // 2
HALF_EXPAND = 16 + WIDTH // 2
QUARTER_CONV = 16 + 9 * WIDTH // 4
NOTE_ROWS = 48

NORM_EPS = 1e-05
UNIT_EPS = 1e-06
SINK_EPS = 0.05
TEMPER = 0.1
HIGH = lax.Precision.HIGHEST
F32 = jnp.float32
BF16 = jnp.bfloat16
NT = (((1,), (1,)), ((), ()))
TN = (((0,), (0,)), ((), ()))


def dot(a, b):
    return jnp.dot(a, b, preferred_element_type=F32)


def dot_nt(a, b):
    return lax.dot_general(a, b, NT, preferred_element_type=F32)


def dot_tn(a, b):
    return lax.dot_general(a, b, TN, preferred_element_type=F32)


def flip(value, axis, step):
    count = lax.axis_size(axis)
    return lax.ppermute(value, axis, [(source, source ^ step) for source in range(count)])


def send(value, source, target):
    return lax.ppermute(value, "section", [(source, target)])


def sum_dp_steps(value):
    count = lax.axis_size("dp")
    value = pair = value + flip(value, "dp", 1)
    step = 2
    while step < count:
        if 2 * step < count:
            near = value + flip(value, "dp", step)
            far = flip(value, "dp", 2 * step) + flip(value, "dp", 3 * step)
            value = near + far
            step *= 4
        else:
            value = value + flip(value, "dp", step)
            step *= 2
    return value, pair


def sum_dp(value):
    return sum_dp_steps(value)[0]


def gather_xor(value, axis):
    return [value] + [flip(value, axis, step) for step in range(1, lax.axis_size(axis))]


def dp_stages():
    count = lax.axis_size("dp")
    stages, step = [(1,)], 2
    while step < count:
        if 2 * step < count:
            stages.append((step, 2 * step, 3 * step))
            step *= 4
        else:
            stages.append((step,))
            step *= 2
    return stages


def gather_dp(value, stages):
    arrays, offsets = [value], [[0]]
    for steps in stages:
        if len(arrays) > 1:
            arrays, offsets = [rows_of(arrays)], [sum(offsets, [])]
        first = offsets[0]
        for step in steps:
            arrays.append(flip(arrays[0], "dp", step))
            offsets.append([o ^ step for o in first])
    return arrays, offsets


def sigmoid(v):
    return 0.5 * jnp.tanh(0.5 * v) + 0.5


def slope(v):
    s = sigmoid(v)
    return s * (1.0 + v * (1.0 - s))


def cost(us):
    return pl.CostEstimate(flops=0, bytes_accessed=int(us * 3_000_000), transcendentals=0)


def hbm(value):
    return pltpu.with_memory_space_constraint(value, pltpu.HBM)


def call(kernel, out, *args, scratch=(), vmem=12, us=1.0, in_hbm=()):
    in_specs, ins = [], []
    for j, a in enumerate(args):
        space = pltpu.VMEM
        if jnp.issubdtype(a.dtype, jnp.integer):
            space = pltpu.SMEM
        elif j in in_hbm:
            space = pltpu.HBM
            a = hbm(a)
        in_specs.append(pl.BlockSpec(memory_space=space))
        ins.append(a)
    return pl.pallas_call(
        kernel,
        name=getattr(kernel, 'func', kernel).__name__,
        out_shape=out,
        in_specs=in_specs,
        out_specs=jax.tree.map(lambda _: pl.BlockSpec(memory_space=pltpu.VMEM), out),
        scratch_shapes=list(scratch),
        compiler_params=pltpu.CompilerParams(vmem_limit_bytes=vmem * 2**20),
        cost_estimate=cost(us),
    )(*ins)


def shape(dims, dtype):
    return jax.ShapeDtypeStruct(tuple(dims), dtype)


def retile_kernel(image, flat):
    flat[...] = image[...].reshape(flat.shape)


def note_kernel(place, pairing, queue, keep, send):
    size = queue.shape[1]
    row = lax.broadcasted_iota(jnp.int32, (16, PROJ), 0)
    lane = lax.broadcasted_iota(jnp.int32, (16, PROJ), 1)
    value = jnp.zeros((16, PROJ), F32)
    for m in range(pairing.shape[0]):
        for i in range(pairing.shape[1]):
            value = jnp.where((row == m) & (lane == i), pairing[m, i].astype(F32), value)
    for core, out in ((place[4], keep), (place[5], send)):
        out[:size, :] = queue[core]
        out[size:, :] = value.astype(BF16)


def rows_kernel(*refs):
    out, at = refs[-1], 0
    for ref in refs[:-1]:
        out[at : at + ref.shape[0], :] = ref[...]
        at += ref.shape[0]


def lanes_kernel(*refs):
    out, at = refs[-1], 0
    for ref in refs[:-1]:
        out[:, at : at + ref.shape[1]] = ref[...]
        at += ref.shape[1]


def rows_of(values, us=0.5):
    rows = sum(v.shape[0] for v in values)
    return call(rows_kernel, shape((rows, values[0].shape[1]), values[0].dtype), *values, us=us)


def split_sums(first, second, micro):
    width = first[0].shape[1]
    rows = [jnp.sum(v, axis=0, keepdims=True) for v in first]
    rows += [jnp.sum(v, axis=0, keepdims=True) for v in second]
    rows.append(jnp.zeros((8 - 2 * micro, width), F32))
    return jnp.concatenate(rows, axis=0)


def moments(sums, m, micro, count):
    mean = sums[m : m + 1] * (1.0 / count)
    square = sums[micro + m : micro + m + 1] * (1.0 / count)
    return mean, lax.rsqrt(square - mean * mean + NORM_EPS)


def per_micro(value, micro):
    rows = value.shape[0] // micro
    return [value[m * rows : (m + 1) * rows] for m in range(micro)]


def normalized(value, sums, micro, count):
    out = []
    for m, v in enumerate(per_micro(value, micro)):
        mean, rstd = moments(sums, m, micro, count)
        out.append(((v - mean) * rstd, rstd))
    return out


def join(parts):
    return jnp.concatenate(parts, axis=0)


def map_places(rows, images):
    row = lax.broadcasted_iota(jnp.int32, (rows, PART), 0).astype(F32)
    cell = jnp.floor((row + 0.5) * (1.0 / images))
    crop = jnp.floor((cell + 0.5) * (1.0 / PLACES))
    place = cell - crop * PLACES
    y = jnp.floor((place + 0.5) * (1.0 / SIDE))
    return y, place - y * SIDE


def tap_shift(value, images, tap, sign, y, x):
    rows = value.shape[0]
    down, right = sign * (tap // 3 - 1), sign * (tap % 3 - 1)
    offset = images * (SIDE * down + right)
    moved = value if offset == 0 else pltpu.roll(value, (-offset) % rows, 0)
    for step, at in ((down, y), (right, x)):
        if step < 0:
            moved = jnp.where(at > 0.5, moved, 0.0)
        elif step > 0:
            moved = jnp.where(at < SIDE - 1.5, moved, 0.0)
    return moved


def told_norm(message, at=0):
    rows = message[at : at + 16, :].astype(F32)
    return rows[0:1] + rows[1:2] + rows[2:3], rows[3:4] + rows[4:5] + rows[5:6]


def told_wide(message):
    parts = [told_norm(message, HALF_REDUCE + b * HALF_EXPAND) for b in range(4)]
    return tuple(jnp.concatenate(p, axis=1) for p in zip(*parts))


def terms(row):
    out = []
    for _ in range(3):
        term = row.astype(BF16).astype(F32)
        out.append(term)
        row = row - term
    return out


def tell_norm(norm, lane):
    out = []
    for r in range(2):
        out += terms(norm[r, :, lane : lane + PART])
    out.append(jnp.zeros((10, PART), F32))
    return jnp.concatenate(out, axis=0).astype(BF16)


def reduce_kernel(micro, place, image, w0, w1, pre, sums):
    half = D // 2
    first = pl.ds(pl.multiple_of(place[4] * half, half), half)
    second = pl.ds(pl.multiple_of(place[5] * half, half), half)
    value = dot(image[:, first], w0[16 : 16 + half, :]) + dot(image[:, second], w1[16 : 16 + half, :])
    pre[...] = value
    parts = per_micro(value, micro)
    sums[...] = split_sums(parts, [v * v for v in parts], micro)


def active_kernel(micro, count, pre, sums, told, active):
    gain, shift = told_norm(told)
    out = []
    for xhat, _ in normalized(pre[...], sums[...], micro, count):
        y = xhat * gain + shift
        out.append(y * sigmoid(y))
    active[...] = join(out).astype(BF16)


def fill(place, pieces, full):
    for k, piece in enumerate(pieces):
        full[:, pl.ds(pl.multiple_of(place[k] * PART, PART), PART)] = piece[: full.shape[0], :]


def quarter_of(place, j):
    return place[8] ^ (0, 2, 1, 3)[j]


def conv_kernel(micro, images, place, a0, a1, a2, a3, wa, wb, pre, sums, full, weight):
    fill(place, (a0, a1, a2, a3), full)
    quarter = WIDTH // 4
    for j in range(4):
        w = (wa, wb)[j // 2]
        at = pl.multiple_of(quarter_of(place, j) * quarter, quarter)
        for tap in range(9):
            lanes = slice(tap * PART, (tap + 1) * PART)
            first = (j % 2) * QUARTER_CONV + 16 + tap * quarter
            weight[pl.ds(at, quarter), lanes] = w[first : first + quarter, :]
    total = None
    y, x = map_places(full.shape[0], images)
    for first in range(0, 9, 2):
        taps = [tap for tap in (first, first + 1) if tap < 9]
        part = dot(full[...], weight[:, first * PART : (taps[-1] + 1) * PART])
        for j, tap in enumerate(taps):
            moved = tap_shift(part[:, j * PART : (j + 1) * PART], images, tap, 1, y, x)
            total = moved if total is None else total + moved
    pre[...] = total
    parts = per_micro(total, micro)
    sums[...] = split_sums(parts, [v * v for v in parts], micro)


def expand_kernel(micro, place, a0, a1, a2, a3, w0, w1, active, pre, sums, weight):
    fill(place, (a0, a1, a2, a3), active)
    half = WIDTH // 2
    for j, w in enumerate((w0, w1)):
        rows = pl.ds(pl.multiple_of(place[4 + j] * half, half), half)
        for b in range(4):
            at = HALF_REDUCE + b * HALF_EXPAND + 16
            weight[rows, b * PART : (b + 1) * PART] = w[at : at + half, :]
    value = dot(active[...], weight[...])
    pre[...] = value
    parts = per_micro(value, micro)
    sums[...] = split_sums(parts, [v * v for v in parts], micro)


def crop_rows(rows, images, transpose=False):
    shp = (rows // PLACES, rows)
    r = lax.broadcasted_iota(jnp.int32, shp, 1).astype(F32)
    q = lax.broadcasted_iota(jnp.int32, shp, 0).astype(F32)
    cell = jnp.floor((r + 0.5) * (1.0 / images))
    crop = jnp.floor((cell + 0.5) * (1.0 / PLACES))
    image = r - cell * images
    return (jnp.abs(crop * images + image - q) < 0.5).astype(F32).astype(BF16)


def pool_kernel(micro, images, count, place, pre, sums, told, image, pooled):
    lanes = pl.ds(pl.multiple_of(place[0] * WIDE, WIDE), WIDE)
    gain, shift = told_wide(told)
    out = []
    for xhat, _ in normalized(pre[...], sums[...], micro, count):
        out.append(xhat * gain + shift)
    z = join(out) + image[:, lanes].astype(F32)
    out = z * sigmoid(z)
    high = out.astype(BF16)
    low = (out - high.astype(F32)).astype(BF16)
    choose = crop_rows(pre.shape[0], images)
    pooled[...] = ((dot(choose, high) + dot(choose, low)) * (1.0 / PLACES)).astype(BF16)


def out_back_kernel(micro, images, count, place, pre, sums, told, image, own, r0, r1, r2, d_z, sums_out):
    lanes = pl.ds(pl.multiple_of(place[0] * WIDE, WIDE), WIDE)
    rows = pre.shape[0]
    gain, shift = told_wide(told)
    d_pooled = own[...].astype(F32)
    for k, came in enumerate((r0, r1, r2)):
        d_pooled = jnp.where(place[k + 1] == SECTIONS - 1, came[...].astype(F32), d_pooled)
    d_pooled = d_pooled.astype(BF16)
    spread = dot_tn(crop_rows(rows, images), d_pooled) * (1.0 / PLACES)
    xhats = [x for x, _ in normalized(pre[...], sums[...], micro, count)]
    z = join([x * gain + shift for x in xhats]) + image[:, lanes].astype(F32)
    value = spread * slope(z)
    d_z[...] = value
    parts = per_micro(value, micro)
    sums_out[...] = split_sums([v * x for v, x in zip(parts, xhats)], parts, micro)


def norm_back(value, pre, sums, back, gain, micro, count):
    out = []
    parts = per_micro(value, micro)
    for m, (xhat, rstd) in enumerate(normalized(pre, sums, micro, count)):
        by_x = back[m : m + 1] * (1.0 / count)
        plain = back[micro + m : micro + m + 1] * (1.0 / count)
        out.append(gain * rstd * (parts[m] - plain - xhat * by_x))
    return join(out)


def norm_back_kernel(micro, count, d_y, pre, sums, back, told, d_pre):
    gain, _ = told_norm(told)
    d_pre[...] = norm_back(d_y[...], pre[...], sums[...], back[...], gain, micro, count).astype(BF16)


def over_micro(back, micro):
    out = []
    for r in range(2):
        row = back[r * micro : r * micro + 1, :]
        for m in range(1, micro):
            row = row + back[r * micro + m : r * micro + m + 1, :]
        out.append(row)
    return out


def last_norm_back_kernel(micro, count, place, d_y, pre, sums, back, told, back2, back1, notes, d_pre):
    gain, _ = told_norm(told)
    rows = d_y.shape[0]
    d_pre[:rows, :] = norm_back(d_y[...], pre[...], sums[...], back[...], gain, micro, count).astype(BF16)
    said = []
    for row in over_micro(back2, micro):
        said += [row[:, b * PART : (b + 1) * PART] for b in range(4)]
    said += over_micro(back1, micro) + over_micro(back, micro)
    said.append(jnp.where(place[0] == SECTIONS - 1, notes[3:4, :PART], 0.0))
    said = sum([terms(row) for row in said], [])
    said.append(jnp.zeros((NOTE_ROWS - len(said), PART), F32))
    d_pre[rows:, :] = jnp.concatenate(said, axis=0).astype(BF16)


def expand_back_kernel(micro, count, place, pre, sums, d_z, back, told, weight, d_pre, q0, q1, q2, q3, full):
    gain, _ = told_wide(told)
    d_low = norm_back(d_z[...], pre[...], sums[...], back[...], gain, micro, count).astype(BF16)
    d_pre[...] = d_low
    full[...] = dot_nt(d_low, weight[...])
    for k, q in enumerate((q0, q1, q2, q3)):
        lanes = pl.ds(pl.multiple_of(place[k] * PART, PART), PART)
        q[...] = full[:, lanes].astype(BF16)


def finish_silu(micro, count, d_active, pre, sums, norm, d_y, sums_out):
    gain, shift = norm
    values, products = [], []
    parts = per_micro(d_active, micro)
    for m, (xhat, _) in enumerate(normalized(pre[...], sums[...], micro, count)):
        value = parts[m] * slope(xhat * gain + shift)
        values.append(value)
        products.append(value * xhat)
    d_y[...] = join(values)
    sums_out[...] = split_sums(products, values, micro)


def silu_back_kernel(micro, count, q0, q1, q2, q3, pre, sums, told, d_y, sums_out):
    total = (q0[...].astype(F32) + q1[...].astype(F32)) + (q2[...].astype(F32) + q3[...].astype(F32))
    d_active = total.astype(BF16).astype(F32)
    finish_silu(micro, count, d_active, pre, sums, told_norm(told), d_y, sums_out)


def conv_back_kernel(
    micro, images, count, place, d0, d1, d2, d3, back0, back1, pre, sums, told, d_full, d_y, sums_out, weight
):
    fill(place, (d0, d1, d2, d3), d_full)
    d_low = d_full[...]
    half = PART // 2
    for j, back in enumerate((back0, back1)):
        for k in range(SECTIONS):
            lanes = pl.ds(pl.multiple_of(place[k] * PART, PART), PART)
            for tap in range(9):
                rows = pl.ds(pl.multiple_of(tap * PART + place[4 + j] * half, half), half)
                weight[rows, lanes] = back[k, tap * half : (tap + 1) * half, :]
    total = None
    y, x = map_places(d_low.shape[0], images)
    for first in range(0, 9, 2):
        taps = [tap for tap in (first, first + 1) if tap < 9]
        part = dot_nt(d_low, weight[first * PART : (taps[-1] + 1) * PART, :])
        for j, tap in enumerate(taps):
            moved = tap_shift(part[:, j * PART : (j + 1) * PART], images, tap, -1, y, x)
            total = moved if total is None else total + moved
    d_active = total.astype(BF16).astype(F32)
    finish_silu(micro, count, d_active, pre, sums, told_norm(told), d_y, sums_out)


def reduce_back_kernel(place, d_full, back0, back1, d_z, grad_in, weight):
    half = WIDE // 2
    first = 9 * PART // 2
    for j, back in enumerate((back0, back1)):
        rows = pl.ds(pl.multiple_of(place[4 + j] * half, half), half)
        for k in range(SECTIONS):
            lanes = pl.ds(pl.multiple_of(place[k] * PART, PART), PART)
            weight[rows, lanes] = back[k, first : first + half, :]
    main = dot_nt(d_full[...], weight[...]).astype(BF16).astype(F32)
    value = main + d_z[...].astype(BF16).astype(F32)
    grad_in[...] = value.reshape(grad_in.shape)


def back_parts_kernel(place, conv_a, conv_b, reduce0, reduce1, *outs):
    half = PART // 2
    wide = WIDE // 2
    first = 9 * half
    quarter = WIDTH // 4
    for k, out in enumerate(outs):
        for core in range(2):
            for j in range(4):
                conv = (conv_a, conv_b)[j // 2]

                @pl.when((place[k] == quarter_of(place, j)) & (place[4] == core))
                def _():
                    for tap in range(9):
                        at = (j % 2) * QUARTER_CONV + 16 + tap * quarter + core * half
                        out[tap * half : (tap + 1) * half, :] = conv[at : at + half, :]

            for u in range(SECTIONS):
                reduce = (reduce0, reduce1)[core ^ (u // 2)]

                @pl.when((place[k] == u) & (place[4] == core))
                def _():
                    at = 16 + (u % 2) * WIDE + core * wide
                    out[first : first + wide, :] = reduce[at : at + wide, :]


def stack_kernel(*refs):
    out = refs[-1]
    rows = refs[0].shape[0]
    for j, ref in enumerate(refs[:-1]):
        if len(out.shape) == 3:
            out[j] = ref[...]
        else:
            out[j * rows : (j + 1) * rows, :] = ref[...]


def mixed_kernel(place, reduce, conv, expand, *outs):
    for k, out in enumerate(outs):
        target = place[k + 1]

        @pl.when(target == 0)
        def _():
            out[:, :WIDE] = reduce[...]

        @pl.when(target == 1)
        def _():
            out[...] = conv[...]

        @pl.when(target == 2)
        def _():
            out[:, :WIDE] = expand[...]


def told_kernel(place, n0, n1, n2, n3, notes, out, loss):
    t = place[0]
    out[...] = jnp.zeros_like(out)

    @pl.when(t == SECTIONS - 1)
    def _():
        for r in range(3):
            out[r] = notes[r : r + 1, :]

    total = None
    for k, note in enumerate((n0, n1, n2, n3)):
        u = place[k]
        rows = note[note.shape[0] - NOTE_ROWS :, :].astype(F32)

        def said(i):
            return (rows[3 * i : 3 * i + 1] + rows[3 * i + 1 : 3 * i + 2]) + rows[3 * i + 2 : 3 * i + 3]

        total = said(12) if total is None else total + said(12)

        @pl.when(t == 2)
        def _():
            for r in range(2):
                for b in range(4):
                    lanes = pl.ds(pl.multiple_of(u * WIDE + b * PART, PART), PART)
                    out[r, :, lanes] = said(4 * r + b)

        for section in range(2):

            @pl.when(t == section)
            def _():
                for r in range(2):
                    lanes = pl.ds(pl.multiple_of(u * PART, PART), PART)
                    out[r, :, lanes] = said((10, 8)[section] + r)

    loss[...] = jnp.broadcast_to(total, loss.shape)


def pick_kernel(place, p0, p1, p2, p3, conv, pair):
    for j, p in enumerate((p0, p1, p2, p3)):

        @pl.when(place[0] == j)
        def _():
            pair[:HALF_REDUCE, :] = p[:HALF_REDUCE, :]

        @pl.when(place[1] == j)
        def _():
            conv[...] = p[...]

        @pl.when(place[2] == j)
        def _():
            pair[HALF_REDUCE:, :] = p[: 4 * HALF_EXPAND, :]


def taps_kernel(images, active, out):
    value = active[...].astype(F32)
    y, x = map_places(value.shape[0], images)
    for tap in range(9):
        out[:, tap * PART : (tap + 1) * PART] = tap_shift(value, images, tap, 1, y, x).astype(BF16)


def head(pooled, w_head, w_proj, protos, norm, queue, match, micro, images, dp):
    rows = pooled.shape[0]
    group = rows // micro
    half = group // CROPS
    scale_all = 1.0 / (TEMPER * CROPS * half * micro)
    pre = dot(pooled, w_head)

    def by_micro(v):
        return v.reshape(micro, group, v.shape[-1])

    pre_m = by_micro(pre)
    mean = jnp.mean(pre_m, axis=1, keepdims=True)
    square = jnp.mean(pre_m * pre_m, axis=1, keepdims=True)
    rstd = lax.rsqrt(square - mean * mean + NORM_EPS)
    xhat = (pre_m - mean) * rstd
    y = xhat * norm[0] + norm[1]
    active = (y * sigmoid(y)).astype(BF16).reshape(rows, D)
    embed = dot(active, w_proj) + norm[2, :PROJ]
    recip = lax.rsqrt(jnp.sum(embed * embed, axis=1, keepdims=True) + UNIT_EPS)
    unit = (embed * recip).astype(BF16)
    scores = dot_nt(unit, protos)
    valid = lax.broadcasted_iota(jnp.int32, (1, 4, QUARTER_PAD), 2).reshape(1, 4 * QUARTER_PAD) < QUARTER
    own_mass = jnp.where(valid, jnp.exp(scores / SINK_EPS), 0.0).reshape(micro, CROPS, half, -1)
    queue_mass = jnp.where(valid, jnp.exp(jnp.einsum("cqp,kp->cqk", queue, protos, preferred_element_type=F32) / SINK_EPS), 0.0)
    codes = []
    for m in range(micro):
        for c in range(CROPS):
            a, b = queue_mass[c], own_mass[m, c]
            column = jnp.sum(a, axis=0, keepdims=True) + jnp.sum(b, axis=0, keepdims=True)
            once = jnp.where(valid, 1.0 / column, 0.0)
            a, b = a * once, b * once
            scale = valid.astype(F32)
            for turn in range(2):
                ra = 1.0 / jnp.sum(a * scale, axis=1, keepdims=True)
                rb = 1.0 / jnp.sum(b * scale, axis=1, keepdims=True)
                column = jnp.sum(a * ra, axis=0, keepdims=True) + jnp.sum(b * rb, axis=0, keepdims=True)
                scale = jnp.where(valid, 1.0 / column, 0.0)
            b = b * scale
            codes.append(b / jnp.sum(b, axis=1, keepdims=True))
    targets = []
    for m in range(micro):
        targets.append(jnp.dot(match[m], codes[m * CROPS + 1], precision=HIGH))
        targets.append(jnp.dot(match[m].T, codes[m * CROPS], precision=HIGH))
    target = jnp.concatenate(targets)
    logits = jnp.where(valid, scores / TEMPER, -1e30)
    logp = jax.nn.log_softmax(logits, axis=1)
    loss = -jnp.sum(jnp.where(valid, target * logp, 0.0)) * (TEMPER * scale_all)
    d_scores = ((jnp.exp(logp) * jnp.sum(target, axis=1, keepdims=True) - target) * scale_all).astype(BF16)
    d_unit = dot(d_scores, protos)
    d_embed = (
        recip * d_unit - embed * (recip * recip * recip) * jnp.sum(d_unit * embed, axis=1, keepdims=True)
    ).astype(BF16)
    d_active = dot_nt(d_embed, w_proj)
    d_y = by_micro(d_active) * slope(y)
    by_x = jnp.sum(d_y * xhat, axis=1, keepdims=True)
    plain = jnp.sum(d_y, axis=1, keepdims=True)
    d_pre = (norm[0] * rstd * (d_y - plain / group - xhat * by_x / group)).astype(BF16).reshape(rows, D)
    bias = jnp.pad(jnp.sum(d_embed.astype(F32), axis=0), (0, D - PROJ))
    grads = jnp.stack([jnp.sum(by_x, axis=(0, 1)), jnp.sum(plain, axis=(0, 1)), bias])
    return loss, grads, active, unit, d_scores, d_embed, d_pre


def valid_lanes():
    lane = lax.broadcasted_iota(jnp.int32, (1, 4 * QUARTER_PAD), 1).astype(F32)
    block = jnp.floor((lane + 0.5) * (1.0 / QUARTER_PAD))
    return lane - block * QUARTER_PAD < QUARTER - 0.5


def lanes_at(b, size):
    return pl.ds(pl.multiple_of(b * size, size), size)


def lanes_at(b, size):
    return pl.ds(pl.multiple_of(b * size, size), size)


def mass_kernel(micro, images, told_offsets, place, table, *refs):
    mass, column, match, rows_s, exps = refs[-5:]
    ndp = len(told_offsets)
    valid = valid_lanes()
    size = mass.shape[0] // ndp
    half = images * ndp
    at, said = 0, jnp.zeros((16, half), F32)
    row = lax.broadcasted_iota(jnp.int32, (PROJ, half), 0)
    lane = lax.broadcasted_iota(jnp.int32, (PROJ, half), 1)
    for ref in refs[:-5]:
        rows = size + 16
        for j in range(ref.shape[0] // rows):
            rows_s[lanes_at(place[7] ^ told_offsets[at], size), :] = ref[j * rows : j * rows + size, :]
            pairs = ref[(j + 1) * rows - 16 : (j + 1) * rows, :]
            spot_at = (place[7] ^ told_offsets[at]) * images
            spot = ((row < images) & (lane == row + spot_at)).astype(F32).astype(BF16)
            said = said + dot(pairs, spot)
            at += 1
    step = 128
    steps = mass.shape[0] // step

    def scored(i, sums):
        own = rows_s[lanes_at(i, step), :]
        out = []
        for a in range(4):
            lanes = slice(a * QUARTER_PAD, (a + 1) * QUARTER_PAD)
            value = jnp.exp(dot_nt(own, table[:, a * PROJ : (a + 1) * PROJ]) * (1.0 / SINK_EPS))
            value = jnp.where(valid[:, lanes], value, 0.0)
            exps[lanes_at(i, step), lanes] = value
            out.append(jnp.sum(value, axis=0, keepdims=True))
        return sums + jnp.concatenate(out, axis=1)

    sums = lax.fori_loop(0, steps, scored, jnp.zeros((1, 4 * QUARTER_PAD), F32))
    column[...] = jnp.broadcast_to(sums, column.shape)
    factor = jnp.where(valid & (sums > 1.18e-38), 1.0 / sums, 0.0)

    def divide(i, carry):
        mass[lanes_at(i, step), :] = (exps[lanes_at(i, step), :] * factor).astype(BF16)
        return carry

    lax.fori_loop(0, steps, divide, 0)

    def over(value, by):
        return jnp.floor((value + 0.5) * (1.0 / by))

    row = lax.broadcasted_iota(jnp.int32, (half, half), 0).astype(F32)
    lane = lax.broadcasted_iota(jnp.int32, (half, half), 1).astype(F32)
    block = over(row, images)
    for m in range(micro):
        same = (jnp.abs(block - over(lane, images)) < 0.5) & (jnp.abs(row - block * images - said[m : m + 1, :]) < 0.5)
        there = same.astype(F32)
        match[m] = jnp.where(place[4] == 0, there, there.T).astype(BF16)


def tables_kernel(packed, proj, table, rows, buffer, sem):
    size = THIRD - FIRST + 2
    copy = pltpu.make_async_copy(packed.at[pl.ds(FIRST, size), :], rows, sem)
    copy.start()
    copy.wait()
    wide = SECOND - FIRST
    for a in range(4):
        buffer[pl.ds(a, wide, stride=4), :] = rows[:wide, a * PROJ : (a + 1) * PROJ].astype(F32)
    proj[...] = buffer[...].astype(BF16)
    row = lax.broadcasted_iota(jnp.int32, (size - wide, WIDTH), 0)
    kept = jnp.where(row < QUARTER, rows[wide:, :].astype(F32), 0.0).astype(BF16)
    table[: size - wide, :] = kept
    table[size - wide :, :] = jnp.zeros((QUARTER_PAD - (size - wide), WIDTH), BF16)


def exact_dot(choose, value):
    parts, left = [], value
    for _ in range(3):
        term = left.astype(BF16)
        left = left - term.astype(F32)
        parts.append(term)
    return dot(jnp.concatenate([choose] * 3, axis=1), jnp.concatenate(parts, axis=0))


def by_micro_rows(value, ndp, micro):
    return value.reshape(ndp, micro, value.shape[0] // (ndp * micro), value.shape[1])


def total_of(value):
    return jnp.sum(jnp.sum(value, axis=0), axis=0, keepdims=True)


def regroup(rows, own, images, to_groups):
    ndp = rows // own
    row = lax.broadcasted_iota(jnp.int32, (rows, rows), 0).astype(F32)
    lane = lax.broadcasted_iota(jnp.int32, (rows, rows), 1).astype(F32)
    source, target = (lane, row) if to_groups else (row, lane)
    block = jnp.floor((source + 0.5) * (1.0 / own))
    inner = source - block * own
    part = jnp.floor((inner + 0.5) * (1.0 / images))
    moved = (part * ndp + block) * images + inner - part * images
    return (jnp.abs(moved - target) < 0.5).astype(F32).astype(BF16)


def head_kernel(
    micro, images, offsets, place, pooled_a, pooled_b, w_head, w_proj, table, norm, mass, column, match,
    pooled, active, unit, d_scores, embed, xhat_s, y_s, rstd_s, said,
    scores, own_mass, total, factor,
):
    ndp = len(offsets)
    rows = pooled.shape[0]
    group = rows // micro
    half = group // CROPS
    own = rows // ndp
    queued = mass.shape[0]
    scale_all = 1.0 / (TEMPER * CROPS * half * micro)
    chunk = WIDTH
    chunks = D // chunk
    core = place[4]
    for j, offset in enumerate(offsets):
        source = (pooled_a, pooled_b)[j * own // pooled_a.shape[0]]
        at = j * own % pooled_a.shape[0]
        pooled[lanes_at(place[7] ^ offset, own), :] = source[at : at + own, :]
    low = pooled[...]

    def forward(b, carry):
        lanes = lanes_at(b, chunk)
        pre = by_micro_rows(dot(low, w_head[:, lanes]), ndp, micro)
        gain, shift = norm[0, :, lanes], norm[1, :, lanes]
        xhats, ys = [], []
        for m in range(micro):
            v = pre[:, m]
            mean = total_of(v) * (1.0 / group)
            square = total_of(v * v) * (1.0 / group)
            rstd = lax.rsqrt(square - mean * mean + NORM_EPS)
            xhat = (v - mean) * rstd
            rstd_s[m : m + 1, lanes] = rstd
            xhats.append(xhat)
            ys.append(xhat * gain + shift)
        xhat_s[:, lanes] = jnp.stack(xhats, axis=1).reshape(rows, chunk)
        y = jnp.stack(ys, axis=1).reshape(rows, chunk)
        y_s[:, lanes] = y
        active[:, lanes] = (y * sigmoid(y)).astype(BF16)
        return carry

    lax.fori_loop(0, chunks, forward, 0)
    value = dot(active[...], w_proj[...]) + norm[2, :, :PROJ]
    embed[...] = value
    recip = lax.rsqrt(jnp.sum(value * value, axis=1, keepdims=True) + UNIT_EPS)
    unit_v = dot(regroup(rows, own, images, True), (value * recip).astype(BF16)).astype(BF16)
    unit[...] = unit_v
    valid = valid_lanes()
    for a in range(4):
        lanes = slice(a * QUARTER_PAD, (a + 1) * QUARTER_PAD)
        scores[:, lanes] = dot_nt(unit_v, table[:, a * PROJ : (a + 1) * PROJ])

    step = 128

    def divided(a):
        return a * (1.0 / jnp.sum(a, axis=1, keepdims=True))

    def folded(a):
        return jnp.sum(a.reshape(a.shape[0] // 8, 8, a.shape[1]), axis=0)

    def own_rows(m):
        return slice(m * half, (m + 1) * half)

    queue_sum = column[0:1, :]
    for m in range(micro):
        a = scores[lanes_at(m * CROPS + core, half), :]
        a = jnp.where(valid, jnp.exp(a * (1.0 / SINK_EPS)), 0.0)
        inverse = jnp.where(valid, 1.0 / (queue_sum + jnp.sum(a, axis=0, keepdims=True)), 0.0)
        factor[m : m + 1, :] = queue_sum * inverse
        factor[micro + m : micro + m + 1, :] = jnp.ones_like(inverse)
        own_mass[own_rows(m), :] = a * inverse

    def turn(i, carry):
        def block(i, carry):
            at = lanes_at(i, step)
            e_of = [mass[at, b * PART : (b + 1) * PART].astype(F32) for b in range(4 * QUARTER_PAD // PART)]
            rows_by = []
            for m in range(micro):
                sums = None
                for b, e in enumerate(e_of):
                    more = e * factor[m : m + 1, b * PART : (b + 1) * PART]
                    sums = more if sums is None else sums + more
                rows_by.append(1.0 / jnp.sum(sums, axis=1, keepdims=True))
            for b in range(4 * QUARTER_PAD // PART):
                lanes = slice(b * PART, (b + 1) * PART)
                e = mass[at, lanes].astype(F32)
                for m in range(micro):
                    total[m, :, lanes] += folded(e * rows_by[m])
            return carry

        total[...] = jnp.zeros_like(total)
        lax.fori_loop(0, queued // step, block, 0)
        for m in range(micro):
            scale = factor[micro + m : micro + m + 1, :]
            a = divided(own_mass[own_rows(m), :] * scale)
            sums = jnp.sum(total[m], axis=0, keepdims=True) * factor[m : m + 1, :]
            more = jnp.where(valid, 1.0 / (sums + jnp.sum(a, axis=0, keepdims=True)), 0.0)
            factor[m : m + 1, :] = factor[m : m + 1, :] * more
            factor[micro + m : micro + m + 1, :] = scale * more
        return carry

    lax.fori_loop(0, 2, turn, 0)

    def losses(m, loss):
        mine, there = lanes_at(m, half), lanes_at(m * CROPS + 1 - core, half)
        codes = divided(own_mass[mine, :] * factor[pl.ds(micro + m, 1), :])
        goal = exact_dot(match[m], codes)
        logits = jnp.where(valid, scores[there, :] * (1.0 / TEMPER), -1e30)
        logits = logits - jnp.max(logits, axis=1, keepdims=True)
        power = jnp.exp(logits)
        summed = jnp.sum(power, axis=1, keepdims=True)
        weight = jnp.sum(goal, axis=1, keepdims=True) / summed
        d_low = ((power * weight - goal) * scale_all).astype(BF16)
        d_scores[mine, :] = d_low
        d_unit = None
        for a in range(4):
            more = dot(d_low[:, a * QUARTER_PAD : (a + 1) * QUARTER_PAD], table[:, a * PROJ : (a + 1) * PROJ])
            d_unit = more if d_unit is None else d_unit + more
        said[mine, :] = d_unit
        return loss + jnp.sum(goal * (logits - jnp.log(summed)), axis=1, keepdims=True)

    loss = lax.fori_loop(0, micro, losses, jnp.zeros((half, 1), F32))
    loss = jnp.sum(loss, axis=0, keepdims=True) * (-TEMPER * scale_all)
    said[micro * half :, :] = jnp.broadcast_to(loss, (8, PROJ))


def head_back_kernel(
    micro, images, ndp, place, here, there, embed, w_proj, w_head, norm, xhat_s, y_s, rstd_s,
    d0, d1, d2, d3, notes, d_embed, d_pre, d_unit, d_own,
):
    rows = embed.shape[0]
    group = rows // micro
    half = group // CROPS
    own = rows // ndp
    chunk = WIDTH
    chunks = D // chunk
    for m in range(micro):
        d_unit[lanes_at(m * CROPS + place[5], half), :] = here[m * half : (m + 1) * half, :]
        d_unit[lanes_at(m * CROPS + place[4], half), :] = there[m * half : (m + 1) * half, :]
    value = embed[...]
    recip = lax.rsqrt(jnp.sum(value * value, axis=1, keepdims=True) + UNIT_EPS)
    d_back = exact_dot(regroup(rows, own, images, False), d_unit[...])
    along = jnp.sum(d_back * value, axis=1, keepdims=True)
    d_low = (recip * d_back - value * (recip * recip * recip) * along).astype(BF16)
    d_embed[...] = d_low
    notes[...] = jnp.zeros_like(notes)
    notes[2:3, :PROJ] = jnp.sum(d_low.astype(F32), axis=0, keepdims=True)
    loss = here[micro * half : micro * half + 1, :] + there[micro * half : micro * half + 1, :]
    notes[3:4, :PROJ] = loss

    def backward(b, carry):
        lanes = lanes_at(b, chunk)
        d_y = by_micro_rows(dot_nt(d_low, w_proj[lanes, :]) * slope(y_s[:, lanes]), ndp, micro)
        xhat = by_micro_rows(xhat_s[:, lanes], ndp, micro)
        gain = norm[0, :, lanes]
        values, by_xs, plains = [], None, None
        for m in range(micro):
            by_x = total_of(d_y[:, m] * xhat[:, m])
            plain = total_of(d_y[:, m])
            by_xs = by_x if by_xs is None else by_xs + by_x
            plains = plain if plains is None else plains + plain
            value = d_y[:, m] - plain * (1.0 / group) - xhat[:, m] * (by_x * (1.0 / group))
            values.append(gain * rstd_s[m : m + 1, lanes] * value)
        notes[0:1, lanes] = by_xs
        notes[1:2, lanes] = plains
        d_pre[:, lanes] = jnp.stack(values, axis=1).reshape(rows, chunk).astype(BF16)
        return carry

    lax.fori_loop(0, chunks, backward, 0)
    mine = d_pre[lanes_at(place[7], own), :]

    def to_pooled(b, carry):
        d_own[:, lanes_at(b, chunk)] = dot_nt(mine, w_head[lanes_at(b, chunk), :]).astype(BF16)
        return carry

    lax.fori_loop(0, chunks, to_pooled, 0)
    for j, out in enumerate((d0, d1, d2, d3)):
        out[...] = d_own[:, j * WIDE : (j + 1) * WIDE]


def interleave(width):
    row = lax.broadcasted_iota(jnp.int32, (4 * width, 4 * width), 0)
    column = lax.broadcasted_iota(jnp.int32, (4 * width, 4 * width), 1)
    return (column == 4 * (row & (width - 1)) + (row >> (width.bit_length() - 1))).astype(F32).astype(BF16)


def own_columns(place, own):
    row = lax.broadcasted_iota(jnp.int32, (WIDTH, own), 0)
    lane = lax.broadcasted_iota(jnp.int32, (WIDTH, own), 1)
    return (row == lane + place[7] * own).astype(F32).astype(BF16)


def tail_grads_kernel(place, active, unit, d_here, d_there, d_embed, out):
    @pl.when(place[0] == SECTIONS - 1)
    def _():
        own = out.shape[0]
        choose = own_columns(place, own)
        rows = active.shape[0]
        wide = jnp.concatenate([active[:, b * WIDTH : (b + 1) * WIDTH] for b in range(4)], axis=0)
        wide = dot_nt(wide, interleave(PART)).astype(BF16)
        half = d_here.shape[0] // 2
        units = []
        for core in (place[5], place[4]):
            units.append(jnp.concatenate([unit[lanes_at(m * CROPS + core, half), :] for m in range(2)], axis=0))
        proj = jnp.zeros((own, WIDTH), F32)
        proto = jnp.zeros((own, QUARTER_PAD), F32)
        for a in range(4):
            some = choose[a * PROJ : (a + 1) * PROJ, :]
            own_e = dot(d_embed[...], some).astype(BF16)
            column = [wide[b * rows : (b + 1) * rows, a * PART : (a + 1) * PART] for b in range(4)]
            proj = proj + dot_tn(own_e, jnp.concatenate(column, axis=1))
            for own_unit, d_scores in zip(units, (d_here, d_there)):
                own_u = dot(own_unit, some).astype(BF16)
                proto = proto + dot_tn(own_u, d_scores[:, a * QUARTER_PAD : (a + 1) * QUARTER_PAD])
        out[:, :WIDTH] = proj
        out[:, WIDTH:] = proto


def head_grads_kernel(place, pooled, d_pre, tail, out, parts):
    @pl.when(place[0] != SECTIONS - 1)
    def _():
        out[...] = jnp.zeros_like(out)

    @pl.when(place[0] == SECTIONS - 1)
    def _():
        own = out.shape[0]
        choose = own_columns(place, own)
        weave = interleave(PART)
        own_d = [dot(d_pre[:, q * WIDTH : (q + 1) * WIDTH], choose).astype(BF16) for q in range(4)]
        own_d = jnp.concatenate(own_d, axis=1)

        def product(b, carry):
            parts[:, lanes_at(b, WIDTH)] = dot_tn(own_d, pooled[:, lanes_at(b, WIDTH)]).astype(BF16)
            return carry

        lax.fori_loop(0, 4, product, 0)

        def mix(b, carry):
            mixed = []
            for j in range(4):
                lanes = pl.ds(pl.multiple_of(b * WIDTH + j * PART, PART), PART)
                four = [parts[q * own : (q + 1) * own, lanes] for q in range(4)]
                mixed.append(jnp.concatenate(four, axis=1))
            mixed = dot(jnp.concatenate(mixed, axis=0), weave)
            for j in range(4):
                lanes = pl.ds(pl.multiple_of((4 * b + j) * WIDTH, WIDTH), WIDTH)
                out[:, lanes] = mixed[j * own : (j + 1) * own, :]
            return carry

        lax.fori_loop(0, 4, mix, 0)
        out[:, FIRST:] = tail[:, : out.shape[1] - FIRST]


def finish_kernel(place, base, reduce, conv, expand, m1, m2, m3, out, buffer, sem):
    mixed = (None, m1, m2, m3)
    t = place[0]

    def write(lanes):
        copy = pltpu.make_async_copy(buffer.at[:, pl.ds(0, lanes)], out.at[:, pl.ds(0, lanes)], sem)
        copy.start()
        copy.wait()

    @pl.when(t == 0)
    def _():
        for u in range(SECTIONS):
            piece = reduce if u == 0 else mixed[u]
            buffer[:, u * WIDE : (u + 1) * WIDE] = piece[:, :WIDE].astype(F32)
        write(D)

    @pl.when(t == 1)
    def _():
        for u in range(SECTIONS):
            piece = conv if u == 1 else mixed[u ^ 1]
            for tap in range(9):
                at = tap * WIDTH + u * PART
                buffer[:, at : at + PART] = piece[:, tap * PART : (tap + 1) * PART].astype(F32)
        write(9 * WIDTH)

    @pl.when(t == 2)
    def _():
        four = [expand if u == 2 else mixed[u ^ 2] for u in range(SECTIONS)]
        weave = interleave(PART)
        for b in range(WIDTH // PART):
            lanes = slice(b * PART, (b + 1) * PART)
            row = jnp.concatenate([f[:, lanes] for f in four], axis=1)
            buffer[:, 4 * b * PART : 4 * (b + 1) * PART] = dot(row, weave)
        write(D)


def unpack_kernel(packed, out, buffer):
    rows = packed.shape[0]
    for b in range(4):
        buffer[b] = packed[:, b * PART : (b + 1) * PART].astype(F32)
    for q in range(4):
        for b in range(4):
            at = q * WIDTH + b * PART
            out[:, at : at + PART] = buffer[b, pl.ds(q, rows // 4, stride=4), :].astype(BF16)


def unpack(packed, rows):
    step = 1024
    return pl.pallas_call(
        unpack_kernel,
        name="unpack",
        out_shape=shape((rows // 4, 4 * WIDTH), BF16),
        grid=(rows // step,),
        in_specs=[pl.BlockSpec((step, WIDTH), lambda i: (i, 0))],
        out_specs=pl.BlockSpec((step // 4, 4 * WIDTH), lambda i: (i, 0)),
        scratch_shapes=[pltpu.VMEM((4, step, PART), F32)],
        compiler_params=pltpu.CompilerParams(vmem_limit_bytes=16 * 2**20),
        cost_estimate=cost(4),
    )(packed)


def pack_kernel(place, packed, norm, o0, o1, o2, o3, rows, buffer, sem):
    outs = (o0, o1, o2, o3)
    t, core = place[0], place[4]

    def run(copies):
        for copy in copies:
            copy.start()
        return copies

    def lanes_of(target, lanes):
        return pl.ds(target * lanes, lanes)

    @pl.when(t == 0)
    def _():
        half = D // 2
        copies = []
        for k, out in enumerate(outs):
            source = packed.at[pl.ds(pl.multiple_of(core * half, half), half), lanes_of(k, PART)]
            copies.append(pltpu.make_async_copy(source, out.at[pl.ds(16, half), :], sem.at[k]))
        run(copies)
        for k, out in enumerate(outs):
            out[:16, :] = tell_norm(norm, k * PART)
        for copy in copies:
            copy.wait()

    @pl.when(t == 1)
    def _():
        quarter = WIDTH // 4
        copies = []
        for k, out in enumerate(outs):
            for tap in range(9):
                at = pl.multiple_of(tap * WIDTH + place[8] * quarter, quarter)
                source = packed.at[pl.ds(at, quarter), lanes_of(1 ^ k, PART)]
                target = out.at[pl.ds(16 + tap * quarter, quarter), :]
                copies.append(pltpu.make_async_copy(source, target, sem.at[9 * k + tap]))
        run(copies)
        for k, out in enumerate(outs):
            out[:16, :] = tell_norm(norm, (1 ^ k) * PART)
        for copy in copies:
            copy.wait()

    @pl.when(t == 2)
    def _():
        size = rows.shape[0]
        copy = pltpu.make_async_copy(packed.at[pl.ds(pl.multiple_of(core * size, size), size), :], rows, sem.at[0])
        copy.start()
        copy.wait()
        for b in range(4):
            buffer[b] = rows[:, b * PART : (b + 1) * PART].astype(F32)
        for k, out in enumerate(outs):
            u = 2 ^ k
            for b in range(4):
                at = b * HALF_EXPAND
                lane = u * WIDE + b * PART
                out[at : at + 16, :] = tell_norm(norm, lane)
                out[at + 16 : at + HALF_EXPAND, :] = buffer[b, pl.ds(u, size // 4, stride=4), :].astype(BF16)


def pack(place, packed, norm):
    rows = 4 * (WIDTH // 2)
    return pl.pallas_call(
        pack_kernel,
        name="pack",
        out_shape=[shape((QUARTER_CONV, PART), BF16)] * 4,
        in_specs=[
            pl.BlockSpec(memory_space=pltpu.SMEM),
            pl.BlockSpec(memory_space=pltpu.HBM),
            pl.BlockSpec(memory_space=pltpu.VMEM),
        ],
        out_specs=[pl.BlockSpec(memory_space=pltpu.VMEM)] * 4,
        scratch_shapes=[
            pltpu.VMEM((rows, WIDTH), BF16), pltpu.VMEM((4, rows, PART), F32), pltpu.SemaphoreType.DMA((36,)),
        ],
        compiler_params=pltpu.CompilerParams(vmem_limit_bytes=12 * 2**20),
        cost_estimate=cost(2),
    )(place, hbm(packed), norm)


def multiple(value, step):
    return value if isinstance(value, int) else pl.multiple_of(value, step)


def pair_kernel(place, a, b, keep, out):
    full = dot_tn(a[...], b[...])
    own = keep.shape[1]
    first = place[4] == 0
    for z in range(keep.shape[0]):
        one = full[2 * z * own : (2 * z + 1) * own]
        two = full[(2 * z + 1) * own : (2 * z + 2) * own]
        keep[z] = jnp.where(first, one, two)
        out[z] = jnp.where(first, two, one).astype(BF16)


def image_pair_kernel(place, d0, d1, d2, d3, image, keep, out, d_full):
    fill(place, (d0, d1, d2, d3), d_full)
    lanes = pl.ds(pl.multiple_of(place[0] * WIDE, WIDE), WIDE)
    pair_kernel(place, d_full, image.at[:, lanes], keep, out)


def cross_kernel(place, keep, came, own, o1, o2, o3):
    for k, o in enumerate((own, o1, o2, o3)):
        z = place[6] ^ k
        o[...] = (keep[z] + came[z].astype(F32)).astype(o.dtype)


def far_kernel(place, keep, came, kept, out):
    for j in range(2):
        mine, other = place[6] ^ j, place[6] ^ (2 + j)
        kept[j] = keep[mine] + came[mine].astype(F32)
        out[j] = (keep[other] + came[other].astype(F32)).astype(BF16)


def near_kernel(keep, came, kept, out):
    kept[...] = keep[0] + came[0].astype(F32)
    out[...] = (keep[1] + came[1].astype(F32)).astype(BF16)


def last_kernel(keep, came, out):
    out[...] = (keep[...] + came[...].astype(F32)).astype(BF16)


def add_kernel(own, r1, r2, r3, out):
    out[...] = ((own[...] + r1[...].astype(F32)) + (r2[...].astype(F32) + r3[...].astype(F32))).astype(BF16)


def after(value, *others):
    return lax.optimization_barrier((value, *others))[0]


def body(image, section_weights, section_norms, queue, pairing):
    micro, images = image.shape[0], image.shape[2]
    ndp = lax.axis_size("dp")
    t = lax.axis_index("section")
    dp = lax.axis_index("dp")
    core = dp % 2
    place = jnp.stack([t ^ k for k in range(SECTIONS)] + [core, 1 - core, dp // 2, dp, dp % 4]).astype(jnp.int32)
    cells = CROPS * PLACES * images
    rows = micro * cells
    count = float(cells * ndp)
    packed = section_weights[0]
    norm3 = section_norms.transpose(1, 0, 2)
    param_rows = packed.shape[0]
    own = WIDTH // ndp
    k = functools.partial

    def pieces_of(width, dtype):
        return shape((rows, width), dtype)

    own_message, *messages = pack(place, packed, norm3)
    came = [own_message]
    for j in range(1, SECTIONS):
        came.append(lax.ppermute(messages[j - 1], "section", [(u, u ^ j) for u in range(3)]))
    flat = call(
        retile_kernel, shape((rows, D), BF16),
        image.transpose(0, 1, 3, 4, 2, 5).reshape(rows // images, images, D),
        us=2,
    )
    head_rows = rows // PLACES * ndp
    small = ndp == 8 and head_rows <= 128 and images == 4 and queue.shape[1] * ndp <= 512
    told, told_offsets = [flat], []
    if small:
        note = [shape((queue.shape[1] + 16, PROJ), BF16)] * 2
        keep, out = call(note_kernel, note, place, pairing, queue, us=0.5)
        told, told_offsets = [rows_of([keep, flip(out, "dp", 1)])], [0, 1]
        told = [rows_of([told[0], flip(told[0], "dp", 2)])]
        told_offsets = told_offsets + [offset ^ 2 for offset in told_offsets]
    natural = unpack(packed, FIRST)
    *came, flat, told[0], natural = lax.optimization_barrier((*came, flat, told[0], natural))
    conv_part, pair_part = call(
        pick_kernel,
        (shape((QUARTER_CONV, PART), BF16), shape((HALF_REDUCE + 4 * HALF_EXPAND, PART), BF16)),
        place, *came,
    )
    pair_parts = (pair_part, flip(pair_part, "dp", 1))
    conv_near = flip(conv_part, "dp", 2)
    sums_of = shape((8, PART), F32)
    pre0, part = call(
        k(reduce_kernel, micro), (pieces_of(PART, F32), sums_of), place, flat, *pair_parts, us=2
    )
    sums0 = sum_dp(part)
    active0 = call(k(active_kernel, micro, count), pieces_of(PART, BF16), pre0, sums0, pair_part, us=1)
    actives0 = gather_xor(active0, "section")

    conv_part = rows_of([conv_part, after(conv_near, active0)])
    w_conv = (conv_part, flip(conv_part, "dp", 1))
    if small:
        told.append(flip(after(told[0], active0), "dp", 4))
        told_offsets = told_offsets + [offset ^ 4 for offset in told_offsets]
    w_proj, table = pl.pallas_call(
        tables_kernel,
        name="tables",
        out_shape=(shape((D, PROJ), BF16), shape((QUARTER_PAD, WIDTH), BF16)),
        in_specs=[pl.BlockSpec(memory_space=pltpu.HBM)],
        out_specs=(pl.BlockSpec(memory_space=pltpu.VMEM), pl.BlockSpec(memory_space=pltpu.VMEM)),
        scratch_shapes=[
            pltpu.VMEM((THIRD - FIRST + 2, WIDTH), BF16), pltpu.VMEM((D, PROJ), F32), pltpu.SemaphoreType.DMA,
        ],
        compiler_params=pltpu.CompilerParams(vmem_limit_bytes=12 * 2**20),
        cost_estimate=cost(1.5),
    )(hbm(after(packed, active0)))
    taps = call(k(taps_kernel, images), pieces_of(9 * PART, BF16), active0, us=1.3)
    back_rows = 9 * PART // 2 + WIDE // 2
    back_own = call(
        back_parts_kernel, [shape((back_rows, PART), BF16)] * 4, place, *w_conv, *pair_parts, us=1
    )
    joined = lax.optimization_barrier((*actives0, table, taps, told[-1], *back_own))
    actives0, (table, taps, told[-1]), back_own = joined[:4], joined[4:7], joined[7:]
    pre1, part = call(
        k(conv_kernel, micro, images),
        (pieces_of(PART, F32), sums_of),
        place, *actives0, *w_conv,
        scratch=[pltpu.VMEM((rows, WIDTH), BF16), pltpu.VMEM((WIDTH, 9 * PART), BF16)],
        us=3,
    )
    sums1 = sum_dp(part)
    active1_own = call(k(active_kernel, micro, count), pieces_of(PART, BF16), pre1, sums1, conv_part, us=1)
    actives1 = gather_xor(active1_own, "section")
    lanes = 4 * QUARTER_PAD
    stages = dp_stages()
    head_stages = stages[1:] + stages[:1]
    offsets = [0]
    for steps in head_stages:
        offsets = offsets + [o ^ step for step in steps for o in offsets]
    if small:
        queued = ndp * queue.shape[1]
        mass, column, match = call(
            k(mass_kernel, micro, images, told_offsets),
            (
                shape((queued, lanes), BF16), shape((8, lanes), F32),
                shape((micro, images * ndp, images * ndp), BF16),
            ),
            place, after(table, active1_own), *told,
            scratch=[pltpu.VMEM((queued, PROJ), BF16), pltpu.VMEM((queued, lanes), F32)],
            vmem=16, us=5,
        )
    if small:
        *actives1, mass = lax.optimization_barrier((*actives1, mass))
    active1, pre2, part, w_expand = call(
        k(expand_kernel, micro),
        (pieces_of(WIDTH, BF16), pieces_of(WIDE, F32), shape((8, WIDE), F32), shape((WIDTH, WIDE), BF16)),
        place, *actives1, *pair_parts,
        us=2,
    )
    back_own = lax.optimization_barrier((*back_own, part))[:4]
    back_came = [back_own[0]] + [flip(back_own[j], "section", j) for j in range(1, SECTIONS)]

    sums2 = sum_dp(part)
    pooled = call(
        k(pool_kernel, micro, images, count),
        shape((rows // PLACES, WIDE), BF16),
        place, pre2, sums2, pair_part, flat,
        us=1.6,
    )

    per_dp = rows // PLACES
    came_p = gather_xor(pooled, "section")[::-1]
    pooled_here = call(lanes_kernel, shape((per_dp, D), BF16), *came_p, us=0.3)
    parts, _ = gather_dp(pooled_here, head_stages)
    if small:
        all_pooled, active3, unit, d_scores, embed, *kept, said = call(
            k(head_kernel, micro, images, offsets),
            [
                shape((head_rows, D), BF16), shape((head_rows, D), BF16), shape((head_rows, PROJ), BF16),
                shape((head_rows // 2, lanes), BF16), shape((head_rows, PROJ), F32), shape((head_rows, D), F32),
                shape((head_rows, D), F32), shape((8, D), F32), shape((head_rows // 2 + 8, PROJ), F32),
            ],
            place, *parts, natural, w_proj, table, norm3, mass, column, match,
            scratch=[
                pltpu.VMEM((head_rows, lanes), F32), pltpu.VMEM((head_rows // 2, lanes), F32),
                pltpu.VMEM((micro, 8, lanes), F32), pltpu.VMEM((8, lanes), F32),
            ],
            vmem=15, us=12,
        )
        *d_pooled, notes3, d_embed, d_pre3 = call(
            k(head_back_kernel, micro, images, ndp),
            [shape((per_dp, WIDE), BF16)] * 4
            + [shape((8, D), F32), shape((head_rows, PROJ), BF16), shape((head_rows, D), BF16)],
            place, said, flip(said, "dp", 1), embed, w_proj, natural, norm3, *kept,
            scratch=[pltpu.VMEM((head_rows, PROJ), F32), pltpu.VMEM((per_dp, D), BF16)],
            us=5,
        )
    else:
        all_pooled = jnp.concatenate(parts)
        offset = jnp.array(offsets, jnp.int32)
        head_order = jnp.arange(head_rows, dtype=jnp.int32)
        block, inner = head_order // per_dp, head_order % per_dp
        group, single = inner // images, inner % images
        position = (group * ndp + (offset[block] ^ dp)) * images + single
        order = (position[None, :] == head_order[:, None]).astype(BF16)
        pairs = lax.all_gather(pairing.astype(F32), "dp").astype(jnp.int32)
        left = jnp.arange(images * ndp, dtype=jnp.int32)
        pairs = pairs.transpose(1, 0, 2).reshape(micro, ndp * images)
        match = ((left // images * images + pairs)[:, :, None] == left[None, None, :]).astype(F32)
        all_pooled = dot(order, all_pooled).astype(BF16)
        protos = jnp.concatenate([table[:, a * PROJ : (a + 1) * PROJ] for a in range(4)], axis=0)
        queue_rows = lax.all_gather(queue, "dp", axis=1, tiled=True)
        loss, grads3, active3, unit, d_scores, d_embed, d_pre3 = head(
            all_pooled, natural, w_proj, protos, norm3[:, 0], queue_rows, match, micro, images, dp
        )
        notes3 = jnp.concatenate([grads3, jnp.full((5, D), loss)])
        d_pooled = dot_nt(dot_tn(order[:, :per_dp], d_pre3).astype(BF16), natural).astype(BF16)
        d_pooled = [d_pooled[:, j * WIDE : (j + 1) * WIDE] for j in range(SECTIONS)]
        d_scores = d_scores.reshape(micro, CROPS, head_rows // 4, lanes)
        d_scores = lax.dynamic_index_in_dim(d_scores, 1 - core, 1, keepdims=False).reshape(-1, lanes)

    joined = lax.optimization_barrier((*d_pooled, *back_came))
    d_pooled, back_came = joined[:SECTIONS], joined[SECTIONS:]
    came_d = [flip(d_pooled[3 ^ j], "section", j) for j in range(1, SECTIONS)]
    back_half = call(stack_kernel, shape((SECTIONS, back_rows, PART), BF16), *back_came, us=0.6)
    back_halves = (back_half, flip(back_half, "dp", 1))
    d_z, part = call(
        k(out_back_kernel, micro, images, count),
        (pieces_of(WIDE, F32), shape((8, WIDE), F32)),
        place, pre2, sums2, pair_part, flat, d_pooled[3], *came_d,
        us=1.8,
    )
    back2 = sum_dp(part)
    back2, *back_halves = lax.optimization_barrier((back2, *back_halves))
    d_pre2, *partial = call(
        k(expand_back_kernel, micro, count),
        [pieces_of(WIDE, BF16)] + [pieces_of(PART, BF16)] * 4,
        place, pre2, sums2, d_z, back2, pair_part, w_expand,
        scratch=[pltpu.VMEM((rows, WIDTH), F32)],
        us=2,
    )
    partial = [partial[0]] + [flip(partial[j], "section", j) for j in range(1, SECTIONS)]

    def scatter_start(a, b, width):
        if ndp != 8:
            return dot_tn(a, b)
        keep, out = call(
            pair_kernel,
            (shape((4, own, width), F32), shape((4, own, width), BF16)),
            place, a, b,
            us=2.5,
        )
        return keep, flip(out, "dp", 1)

    def scatter_cross(started, *others):
        if ndp != 8:
            return [lax.psum_scatter(started.astype(BF16), "dp", scatter_dimension=0, tiled=True)]
        keep, came = started
        if others:
            keep = after(keep, *others)
        dims = keep.shape[1:]
        kept, *out = call(
            cross_kernel, [shape(dims, F32)] + [shape(dims, BF16)] * 3, place, keep, came
        )
        return [kept] + [flip(out[j], "dp", 2 * (j + 1)) for j in range(3)]

    def scatter_far(started, *others):
        if ndp != 8:
            return lax.psum_scatter(started.astype(BF16), "dp", scatter_dimension=0, tiled=True), None
        keep, came = started
        if others:
            keep = after(keep, *others)
        dims = (2, *keep.shape[1:])
        kept, out = call(far_kernel, (shape(dims, F32), shape(dims, BF16)), place, keep, came, us=0.7)
        return kept, flip(out, "dp", 4)

    def scatter_near(started, *others):
        if ndp != 8:
            return started
        keep, came = started
        if others:
            keep = after(keep, *others)
        dims = keep.shape[1:]
        kept, out = call(near_kernel, (shape(dims, F32), shape(dims, BF16)), keep, came, us=0.5)
        return kept, flip(out, "dp", 2)

    def scatter_last(started):
        if ndp != 8:
            return started[0].astype(BF16)
        return call(last_kernel, shape(started[0].shape, BF16), *started, us=0.4)

    def scatter_finish(crossed):
        if ndp != 8:
            return crossed[0].astype(BF16)
        return call(add_kernel, shape(crossed[0].shape, BF16), *crossed, us=0.6)

    expand_half = scatter_far(scatter_start(d_pre2, active1, WIDTH))
    tail = call(
        tail_grads_kernel,
        shape((own, WIDTH + QUARTER_PAD), F32),
        place, after(active3, d_pre2), unit, d_scores, flip(d_scores, "dp", 1), d_embed,
        us=3,
    )
    joined = lax.optimization_barrier((*partial, tail, *expand_half[: 2 if ndp == 8 else 1]))
    partial, tail, expand_half = joined[:SECTIONS], joined[SECTIONS], joined[SECTIONS + 1 :]

    d_y1, part = call(
        k(silu_back_kernel, micro, count),
        (pieces_of(PART, F32), sums_of),
        *partial, pre1, sums1, conv_part,
    )
    back1 = sum_dp(part)
    d_pre1_own = call(
        k(norm_back_kernel, micro, count), pieces_of(PART, BF16), d_y1, pre1, sums1, back1, conv_part
    )
    d_pre1s = gather_xor(d_pre1_own, "section")
    expand_last = scatter_near(expand_half, d_pre1_own)
    base = call(
        head_grads_kernel,
        shape((own, param_rows), F32),
        place, after(all_pooled, d_pre1_own), d_pre3, tail,
        scratch=[pltpu.VMEM((4 * own, D), BF16)],
        us=4,
    )
    joined = lax.optimization_barrier((*d_pre1s, base, *expand_last))
    d_pre1s, base, expand_last = joined[:SECTIONS], joined[SECTIONS], joined[SECTIONS + 1 :]
    d_pre1, d_y0, part = call(
        k(conv_back_kernel, micro, images, count),
        (pieces_of(WIDTH, BF16), pieces_of(PART, F32), sums_of),
        place, *d_pre1s, *back_halves, pre0, sums0, pair_part,
        scratch=[pltpu.VMEM((9 * PART, WIDTH), BF16)],
        us=3.5,
    )
    conv_started = scatter_start(d_pre1, taps, 9 * PART)
    back0 = sum_dp(part)
    d_pre0_own = call(
        k(last_norm_back_kernel, micro, count),
        shape((rows + NOTE_ROWS, PART), BF16),
        place, d_y0, pre0, sums0, back0, pair_part, back2, back1, notes3,
    )
    d_pre0s = gather_xor(d_pre0_own, "section")
    conv_half = scatter_far(conv_started)
    joined = lax.optimization_barrier((*d_pre0s, conv_half[0]))
    d_pre0s, conv_half = joined[:SECTIONS], (joined[SECTIONS], conv_half[1])
    conv_last = scatter_near(conv_half)
    joined = lax.optimization_barrier((*d_pre0s, conv_last[0]))
    d_pre0s, conv_last = joined[:SECTIONS], (joined[SECTIONS], conv_last[1])

    if ndp == 8:
        keep, out, d_pre0 = call(
            image_pair_kernel,
            (shape((4, own, WIDE), F32), shape((4, own, WIDE), BF16), pieces_of(WIDTH, BF16)),
            place, *d_pre0s, flat,
            us=2.5,
        )
        reduce_started = keep, flip(out, "dp", 1)
    else:
        d_pre0 = jnp.stack(d_pre0s)[place[:SECTIONS], :rows].transpose(1, 0, 2).reshape(rows, WIDTH)
        reduce_started = dot_tn(d_pre0, lax.dynamic_slice_in_dim(flat, t * WIDE, WIDE, 1))
    reduce_crossed = scatter_cross(reduce_started)
    grad_in = call(
        reduce_back_kernel,
        shape((rows // images, images, WIDE), F32),
        place, d_pre0, *back_halves, d_z,
        scratch=[pltpu.VMEM((WIDE, WIDTH), BF16)],
        us=2,
    )
    norm_grads, loss = call(
        told_kernel, (shape((3, 1, D), F32), shape((8, PROJ), F32)), place, *d_pre0s, notes3, us=0.5
    )
    g_conv = scatter_last(conv_last)
    g_expand = scatter_last(expand_last)
    joined = lax.optimization_barrier((*reduce_crossed, grad_in, norm_grads, g_conv, g_expand))
    *reduce_crossed, grad_in, norm_grads, g_conv, g_expand = joined
    g_reduce = scatter_finish(reduce_crossed)
    mixed = call(mixed_kernel, [shape(g_conv.shape, BF16)] * 3, place, g_reduce, g_conv, g_expand, us=0.3)
    mixed = [
        lax.ppermute(mixed[j - 1], "section", [(u ^ j, u) for u in range(3)]) for j in range(1, SECTIONS)
    ]
    weight_grads = pl.pallas_call(
        finish_kernel,
        name="finish",
        out_shape=shape((own, param_rows), F32),
        in_specs=[pl.BlockSpec(memory_space=pltpu.SMEM), pl.BlockSpec(memory_space=pltpu.HBM)]
        + [pl.BlockSpec(memory_space=pltpu.VMEM)] * 6,
        out_specs=pl.BlockSpec(memory_space=pltpu.HBM),
        scratch_shapes=[pltpu.VMEM((own, 9 * WIDTH), F32), pltpu.SemaphoreType.DMA],
        input_output_aliases={1: 0},
        compiler_params=pltpu.CompilerParams(vmem_limit_bytes=12 * 2**20),
        cost_estimate=cost(2),
    )(place, base, g_reduce, g_conv, g_expand, *mixed)
    grad_in = grad_in.reshape(micro, CROPS, SIDE, SIDE, images, WIDE).transpose(0, 1, 4, 2, 3, 5)
    return (loss[0, 0], grad_in, weight_grads.T[None], norm_grads.transpose(1, 0, 2))


def solution(mesh):
    in_specs = (
        P(None, None, "dp", None, None, None),
        P("section", None, None),
        P("section", None, None),
        P(None, "dp", None),
        P(None, "dp"),
    )
    out_specs = (
        P(),
        P(None, None, "dp", None, None, "section"),
        P("section", None, "dp"),
        P("section", None, None),
    )
    return jax.shard_map(body, mesh=mesh, in_specs=in_specs, out_specs=out_specs, check_vma=False)
```

```python
import functools

import jax
import jax.numpy as jnp
from jax import lax
from jax.experimental import pallas as pl
from jax.experimental.pallas import tpu as pltpu
from jax.sharding import PartitionSpec as P

D = 2048
WIDTH = 512
PROJ = 128
PROTOS = 3000
SIDE = 7
CROPS = 2
SECTIONS = 4
PART = WIDTH // SECTIONS
WIDE = D // SECTIONS
QUARTER = PROTOS // 4
QUARTER_PAD = 768
PLACES = SIDE * SIDE
FIRST = D * (D // WIDTH)
SECOND = FIRST + D * PROJ // WIDTH
THIRD = SECOND + PROTOS * PROJ // WIDTH
HALF_REDUCE = 16 + D // 2
HALF_EXPAND = 16 + WIDTH // 2
QUARTER_CONV = 16 + 9 * WIDTH // 4
NOTE_ROWS = 48

NORM_EPS = 1e-05
UNIT_EPS = 1e-06
SINK_EPS = 0.05
TEMPER = 0.1
HIGH = lax.Precision.HIGHEST
F32 = jnp.float32
BF16 = jnp.bfloat16
NT = (((1,), (1,)), ((), ()))
TN = (((0,), (0,)), ((), ()))


def dot(a, b):
    return jnp.dot(a, b, preferred_element_type=F32)


def dot_nt(a, b):
    return lax.dot_general(a, b, NT, preferred_element_type=F32)


def dot_tn(a, b):
    return lax.dot_general(a, b, TN, preferred_element_type=F32)


def flip(value, axis, step):
    count = lax.axis_size(axis)
    return lax.ppermute(value, axis, [(source, source ^ step) for source in range(count)])


def send(value, source, target):
    return lax.ppermute(value, "section", [(source, target)])


def sum_dp_steps(value):
    count = lax.axis_size("dp")
    value = pair = value + flip(value, "dp", 1)
    step = 2
    while step < count:
        if 2 * step < count:
            near = value + flip(value, "dp", step)
            far = flip(value, "dp", 3 * step) + flip(value, "dp", 2 * step)
            value = near + far
            step *= 4
        else:
            value = value + flip(value, "dp", step)
            step *= 2
    return value, pair


def sum_dp(value):
    return sum_dp_steps(value)[0]


def gather_xor(value, axis):
    return [value] + [flip(value, axis, step) for step in range(1, lax.axis_size(axis))]


def dp_stages():
    count = lax.axis_size("dp")
    stages, step = [(1,)], 2
    while step < count:
        if 2 * step < count:
            stages.append((step, 2 * step, 3 * step))
            step *= 4
        else:
            stages.append((step,))
            step *= 2
    return stages


def gather_dp(value, stages):
    arrays, offsets = [value], [[0]]
    for steps in stages:
        if len(arrays) > 1:
            arrays, offsets = [rows_of(arrays)], [sum(offsets, [])]
        first = offsets[0]
        for step in steps:
            arrays.append(flip(arrays[0], "dp", step))
            offsets.append([o ^ step for o in first])
    return arrays, offsets


def sigmoid(v):
    return 0.5 * jnp.tanh(0.5 * v) + 0.5


def slope(v):
    s = sigmoid(v)
    return s * (1.0 + v * (1.0 - s))


def cost(us):
    return pl.CostEstimate(flops=0, bytes_accessed=int(us * 3_000_000), transcendentals=0)


def hbm(value):
    return pltpu.with_memory_space_constraint(value, pltpu.HBM)


def call(kernel, out, *args, scratch=(), vmem=12, us=1.0, in_hbm=()):
    in_specs, ins = [], []
    for j, a in enumerate(args):
        space = pltpu.VMEM
        if jnp.issubdtype(a.dtype, jnp.integer):
            space = pltpu.SMEM
        elif j in in_hbm:
            space = pltpu.HBM
            a = hbm(a)
        in_specs.append(pl.BlockSpec(memory_space=space))
        ins.append(a)
    return pl.pallas_call(
        kernel,
        name=getattr(kernel, 'func', kernel).__name__,
        out_shape=out,
        in_specs=in_specs,
        out_specs=jax.tree.map(lambda _: pl.BlockSpec(memory_space=pltpu.VMEM), out),
        scratch_shapes=list(scratch),
        compiler_params=pltpu.CompilerParams(vmem_limit_bytes=vmem * 2**20),
        cost_estimate=cost(us),
    )(*ins)


def shape(dims, dtype):
    return jax.ShapeDtypeStruct(tuple(dims), dtype)


def retile_kernel(image, flat):
    flat[...] = image[...].reshape(flat.shape)


def note_kernel(place, pairing, queue, keep, send):
    size = queue.shape[1]
    row = lax.broadcasted_iota(jnp.int32, (16, PROJ), 0)
    lane = lax.broadcasted_iota(jnp.int32, (16, PROJ), 1)
    value = jnp.zeros((16, PROJ), F32)
    for m in range(pairing.shape[0]):
        for i in range(pairing.shape[1]):
            value = jnp.where((row == m) & (lane == i), pairing[m, i].astype(F32), value)
    for core, out in ((place[4], keep), (place[5], send)):
        out[:size, :] = queue[core]
        out[size:, :] = value.astype(BF16)


def rows_kernel(*refs):
    out, at = refs[-1], 0
    for ref in refs[:-1]:
        out[at : at + ref.shape[0], :] = ref[...]
        at += ref.shape[0]


def lanes_kernel(*refs):
    out, at = refs[-1], 0
    for ref in refs[:-1]:
        out[:, at : at + ref.shape[1]] = ref[...]
        at += ref.shape[1]


def rows_of(values, us=0.5):
    rows = sum(v.shape[0] for v in values)
    return call(rows_kernel, shape((rows, values[0].shape[1]), values[0].dtype), *values, us=us)


def split_sums(first, second, micro):
    width = first[0].shape[1]
    rows = [jnp.sum(v, axis=0, keepdims=True) for v in first]
    rows += [jnp.sum(v, axis=0, keepdims=True) for v in second]
    rows.append(jnp.zeros((8 - 2 * micro, width), F32))
    return jnp.concatenate(rows, axis=0)


def moments(sums, m, micro, count):
    mean = sums[m : m + 1] * (1.0 / count)
    square = sums[micro + m : micro + m + 1] * (1.0 / count)
    return mean, lax.rsqrt(square - mean * mean + NORM_EPS)


def per_micro(value, micro):
    rows = value.shape[0] // micro
    return [value[m * rows : (m + 1) * rows] for m in range(micro)]


def normalized(value, sums, micro, count):
    out = []
    for m, v in enumerate(per_micro(value, micro)):
        mean, rstd = moments(sums, m, micro, count)
        out.append(((v - mean) * rstd, rstd))
    return out


def join(parts):
    return jnp.concatenate(parts, axis=0)


def map_places(rows, images):
    row = lax.broadcasted_iota(jnp.int32, (rows, PART), 0).astype(F32)
    cell = jnp.floor((row + 0.5) * (1.0 / images))
    crop = jnp.floor((cell + 0.5) * (1.0 / PLACES))
    place = cell - crop * PLACES
    y = jnp.floor((place + 0.5) * (1.0 / SIDE))
    return y, place - y * SIDE


def tap_shift(value, images, tap, sign, y, x):
    rows = value.shape[0]
    down, right = sign * (tap // 3 - 1), sign * (tap % 3 - 1)
    offset = images * (SIDE * down + right)
    moved = value if offset == 0 else pltpu.roll(value, (-offset) % rows, 0)
    for step, at in ((down, y), (right, x)):
        if step < 0:
            moved = jnp.where(at > 0.5, moved, 0.0)
        elif step > 0:
            moved = jnp.where(at < SIDE - 1.5, moved, 0.0)
    return moved


def told_norm(message, at=0):
    rows = message[at : at + 16, :].astype(F32)
    return rows[0:1] + rows[1:2] + rows[2:3], rows[3:4] + rows[4:5] + rows[5:6]


def told_wide(message):
    parts = [told_norm(message, HALF_REDUCE + b * HALF_EXPAND) for b in range(4)]
    return tuple(jnp.concatenate(p, axis=1) for p in zip(*parts))


def terms(row):
    out = []
    for _ in range(3):
        term = row.astype(BF16).astype(F32)
        out.append(term)
        row = row - term
    return out


def tell_norm(norm, lane):
    out = []
    for r in range(2):
        out += terms(norm[r, :, lane : lane + PART])
    out.append(jnp.zeros((10, PART), F32))
    return jnp.concatenate(out, axis=0).astype(BF16)


def reduce_kernel(micro, place, image, w0, w1, pre, sums):
    half = D // 2
    first = pl.ds(pl.multiple_of(place[4] * half, half), half)
    second = pl.ds(pl.multiple_of(place[5] * half, half), half)
    value = dot(image[:, first], w0[16 : 16 + half, :]) + dot(image[:, second], w1[16 : 16 + half, :])
    pre[...] = value
    parts = per_micro(value, micro)
    sums[...] = split_sums(parts, [v * v for v in parts], micro)


def active_kernel(micro, count, pre, sums, told, active):
    gain, shift = told_norm(told)
    out = []
    for xhat, _ in normalized(pre[...], sums[...], micro, count):
        y = xhat * gain + shift
        out.append(y * sigmoid(y))
    active[...] = join(out).astype(BF16)


def fill(place, pieces, full):
    for k, piece in enumerate(pieces):
        full[:, pl.ds(pl.multiple_of(place[k] * PART, PART), PART)] = piece[: full.shape[0], :]


def quarter_of(place, j):
    return place[8] ^ (0, 2, 1, 3)[j]


def conv_kernel(micro, images, place, a0, a1, a2, a3, wa, wb, pre, sums, full, weight):
    fill(place, (a0, a1, a2, a3), full)
    quarter = WIDTH // 4
    for j in range(4):
        w = (wa, wb)[j // 2]
        at = pl.multiple_of(quarter_of(place, j) * quarter, quarter)
        for tap in range(9):
            lanes = slice(tap * PART, (tap + 1) * PART)
            first = (j % 2) * QUARTER_CONV + 16 + tap * quarter
            weight[pl.ds(at, quarter), lanes] = w[first : first + quarter, :]
    total = None
    y, x = map_places(full.shape[0], images)
    for first in range(0, 9, 2):
        taps = [tap for tap in (first, first + 1) if tap < 9]
        part = dot(full[...], weight[:, first * PART : (taps[-1] + 1) * PART])
        for j, tap in enumerate(taps):
            moved = tap_shift(part[:, j * PART : (j + 1) * PART], images, tap, 1, y, x)
            total = moved if total is None else total + moved
    pre[...] = total
    parts = per_micro(total, micro)
    sums[...] = split_sums(parts, [v * v for v in parts], micro)


def expand_kernel(micro, place, a0, a1, a2, a3, w0, w1, active, pre, sums, weight):
    fill(place, (a0, a1, a2, a3), active)
    half = WIDTH // 2
    for j, w in enumerate((w0, w1)):
        rows = pl.ds(pl.multiple_of(place[4 + j] * half, half), half)
        for b in range(4):
            at = HALF_REDUCE + b * HALF_EXPAND + 16
            weight[rows, b * PART : (b + 1) * PART] = w[at : at + half, :]
    value = dot(active[...], weight[...])
    pre[...] = value
    parts = per_micro(value, micro)
    sums[...] = split_sums(parts, [v * v for v in parts], micro)


def crop_rows(rows, images, transpose=False):
    shp = (rows // PLACES, rows)
    r = lax.broadcasted_iota(jnp.int32, shp, 1).astype(F32)
    q = lax.broadcasted_iota(jnp.int32, shp, 0).astype(F32)
    cell = jnp.floor((r + 0.5) * (1.0 / images))
    crop = jnp.floor((cell + 0.5) * (1.0 / PLACES))
    image = r - cell * images
    return (jnp.abs(crop * images + image - q) < 0.5).astype(F32).astype(BF16)


def pool_kernel(micro, images, count, place, pre, sums, told, image, pooled):
    lanes = pl.ds(pl.multiple_of(place[0] * WIDE, WIDE), WIDE)
    gain, shift = told_wide(told)
    out = []
    for xhat, _ in normalized(pre[...], sums[...], micro, count):
        out.append(xhat * gain + shift)
    z = join(out) + image[:, lanes].astype(F32)
    out = z * sigmoid(z)
    high = out.astype(BF16)
    low = (out - high.astype(F32)).astype(BF16)
    choose = crop_rows(pre.shape[0], images)
    pooled[...] = ((dot(choose, high) + dot(choose, low)) * (1.0 / PLACES)).astype(BF16)


def out_back_kernel(micro, images, count, place, pre, sums, told, image, own, r0, r1, r2, d_z, sums_out):
    lanes = pl.ds(pl.multiple_of(place[0] * WIDE, WIDE), WIDE)
    rows = pre.shape[0]
    gain, shift = told_wide(told)
    d_pooled = own[...].astype(F32)
    for k, came in enumerate((r0, r1, r2)):
        d_pooled = jnp.where(place[k + 1] == SECTIONS - 1, came[...].astype(F32), d_pooled)
    d_pooled = d_pooled.astype(BF16)
    spread = dot_tn(crop_rows(rows, images), d_pooled) * (1.0 / PLACES)
    xhats = [x for x, _ in normalized(pre[...], sums[...], micro, count)]
    z = join([x * gain + shift for x in xhats]) + image[:, lanes].astype(F32)
    value = spread * slope(z)
    d_z[...] = value
    parts = per_micro(value, micro)
    sums_out[...] = split_sums([v * x for v, x in zip(parts, xhats)], parts, micro)


def norm_back(value, pre, sums, back, gain, micro, count):
    out = []
    parts = per_micro(value, micro)
    for m, (xhat, rstd) in enumerate(normalized(pre, sums, micro, count)):
        by_x = back[m : m + 1] * (1.0 / count)
        plain = back[micro + m : micro + m + 1] * (1.0 / count)
        out.append(gain * rstd * (parts[m] - plain - xhat * by_x))
    return join(out)


def norm_back_kernel(micro, count, d_y, pre, sums, back, told, d_pre):
    gain, _ = told_norm(told)
    d_pre[...] = norm_back(d_y[...], pre[...], sums[...], back[...], gain, micro, count).astype(BF16)


def over_micro(back, micro):
    out = []
    for r in range(2):
        row = back[r * micro : r * micro + 1, :]
        for m in range(1, micro):
            row = row + back[r * micro + m : r * micro + m + 1, :]
        out.append(row)
    return out


def last_norm_back_kernel(micro, count, place, d_y, pre, sums, back, told, back2, back1, notes, d_pre):
    gain, _ = told_norm(told)
    rows = d_y.shape[0]
    d_pre[:rows, :] = norm_back(d_y[...], pre[...], sums[...], back[...], gain, micro, count).astype(BF16)
    said = []
    for row in over_micro(back2, micro):
        said += [row[:, b * PART : (b + 1) * PART] for b in range(4)]
    said += over_micro(back1, micro) + over_micro(back, micro)
    said.append(jnp.where(place[0] == SECTIONS - 1, notes[3:4, :PART], 0.0))
    said = sum([terms(row) for row in said], [])
    said.append(jnp.zeros((NOTE_ROWS - len(said), PART), F32))
    d_pre[rows:, :] = jnp.concatenate(said, axis=0).astype(BF16)


def expand_back_kernel(micro, count, place, pre, sums, d_z, back, told, weight, d_pre, q0, q1, q2, q3, full):
    gain, _ = told_wide(told)
    d_low = norm_back(d_z[...], pre[...], sums[...], back[...], gain, micro, count).astype(BF16)
    d_pre[...] = d_low
    full[...] = dot_nt(d_low, weight[...])
    for k, q in enumerate((q0, q1, q2, q3)):
        lanes = pl.ds(pl.multiple_of(place[k] * PART, PART), PART)
        q[...] = full[:, lanes].astype(BF16)


def finish_silu(micro, count, d_active, pre, sums, norm, d_y, sums_out):
    gain, shift = norm
    values, products = [], []
    parts = per_micro(d_active, micro)
    for m, (xhat, _) in enumerate(normalized(pre[...], sums[...], micro, count)):
        value = parts[m] * slope(xhat * gain + shift)
        values.append(value)
        products.append(value * xhat)
    d_y[...] = join(values)
    sums_out[...] = split_sums(products, values, micro)


def silu_back_kernel(micro, count, q0, q1, q2, q3, pre, sums, told, d_y, sums_out):
    total = (q0[...].astype(F32) + q1[...].astype(F32)) + (q2[...].astype(F32) + q3[...].astype(F32))
    d_active = total.astype(BF16).astype(F32)
    finish_silu(micro, count, d_active, pre, sums, told_norm(told), d_y, sums_out)


def conv_back_kernel(
    micro, images, count, place, d0, d1, d2, d3, back0, back1, pre, sums, told, d_full, d_y, sums_out, weight
):
    fill(place, (d0, d1, d2, d3), d_full)
    d_low = d_full[...]
    half = PART // 2
    for j, back in enumerate((back0, back1)):
        for k in range(SECTIONS):
            lanes = pl.ds(pl.multiple_of(place[k] * PART, PART), PART)
            for tap in range(9):
                rows = pl.ds(pl.multiple_of(tap * PART + place[4 + j] * half, half), half)
                weight[rows, lanes] = back[k, tap * half : (tap + 1) * half, :]
    total = None
    y, x = map_places(d_low.shape[0], images)
    for first in range(0, 9, 2):
        taps = [tap for tap in (first, first + 1) if tap < 9]
        part = dot_nt(d_low, weight[first * PART : (taps[-1] + 1) * PART, :])
        for j, tap in enumerate(taps):
            moved = tap_shift(part[:, j * PART : (j + 1) * PART], images, tap, -1, y, x)
            total = moved if total is None else total + moved
    d_active = total.astype(BF16).astype(F32)
    finish_silu(micro, count, d_active, pre, sums, told_norm(told), d_y, sums_out)


def reduce_back_kernel(place, d_full, back0, back1, d_z, grad_in, weight):
    half = WIDE // 2
    first = 9 * PART // 2
    for j, back in enumerate((back0, back1)):
        rows = pl.ds(pl.multiple_of(place[4 + j] * half, half), half)
        for k in range(SECTIONS):
            lanes = pl.ds(pl.multiple_of(place[k] * PART, PART), PART)
            weight[rows, lanes] = back[k, first : first + half, :]
    main = dot_nt(d_full[...], weight[...]).astype(BF16).astype(F32)
    value = main + d_z[...].astype(BF16).astype(F32)
    grad_in[...] = value.reshape(grad_in.shape)


def back_parts_kernel(place, conv_a, conv_b, reduce0, reduce1, *outs):
    half = PART // 2
    wide = WIDE // 2
    first = 9 * half
    quarter = WIDTH // 4
    for k, out in enumerate(outs):
        for core in range(2):
            for j in range(4):
                conv = (conv_a, conv_b)[j // 2]

                @pl.when((place[k] == quarter_of(place, j)) & (place[4] == core))
                def _():
                    for tap in range(9):
                        at = (j % 2) * QUARTER_CONV + 16 + tap * quarter + core * half
                        out[tap * half : (tap + 1) * half, :] = conv[at : at + half, :]

            for u in range(SECTIONS):
                reduce = (reduce0, reduce1)[core ^ (u // 2)]

                @pl.when((place[k] == u) & (place[4] == core))
                def _():
                    at = 16 + (u % 2) * WIDE + core * wide
                    out[first : first + wide, :] = reduce[at : at + wide, :]


def stack_kernel(*refs):
    out = refs[-1]
    rows = refs[0].shape[0]
    for j, ref in enumerate(refs[:-1]):
        if len(out.shape) == 3:
            out[j] = ref[...]
        else:
            out[j * rows : (j + 1) * rows, :] = ref[...]


def mixed_kernel(place, own, r1, r2, r3, conv, expand, reduce, *outs):
    value = (own[...] + r1[...].astype(F32)) + (r2[...].astype(F32) + r3[...].astype(F32))
    reduce[...] = value.astype(BF16)
    for k, out in enumerate(outs):
        target = place[k + 1]

        @pl.when(target == 0)
        def _():
            out[:, :WIDE] = reduce[...]

        @pl.when(target == 1)
        def _():
            out[...] = conv[...]

        @pl.when(target == 2)
        def _():
            out[:, :WIDE] = expand[...]


def told_kernel(place, n0, n1, n2, n3, notes, out, loss):
    t = place[0]
    out[...] = jnp.zeros_like(out)

    @pl.when(t == SECTIONS - 1)
    def _():
        for r in range(3):
            out[r] = notes[r : r + 1, :]

    total = None
    for k, note in enumerate((n0, n1, n2, n3)):
        u = place[k]
        rows = note[note.shape[0] - NOTE_ROWS :, :].astype(F32)

        def said(i):
            return (rows[3 * i : 3 * i + 1] + rows[3 * i + 1 : 3 * i + 2]) + rows[3 * i + 2 : 3 * i + 3]

        total = said(12) if total is None else total + said(12)

        @pl.when(t == 2)
        def _():
            for r in range(2):
                for b in range(4):
                    lanes = pl.ds(pl.multiple_of(u * WIDE + b * PART, PART), PART)
                    out[r, :, lanes] = said(4 * r + b)

        for section in range(2):

            @pl.when(t == section)
            def _():
                for r in range(2):
                    lanes = pl.ds(pl.multiple_of(u * PART, PART), PART)
                    out[r, :, lanes] = said((10, 8)[section] + r)

    loss[...] = jnp.broadcast_to(total, loss.shape)


def pick_kernel(place, p0, p1, p2, p3, conv, pair):
    for j, p in enumerate((p0, p1, p2, p3)):

        @pl.when(place[0] == j)
        def _():
            pair[:HALF_REDUCE, :] = p[:HALF_REDUCE, :]

        @pl.when(place[1] == j)
        def _():
            conv[...] = p[...]

        @pl.when(place[2] == j)
        def _():
            pair[HALF_REDUCE:, :] = p[: 4 * HALF_EXPAND, :]


def taps_kernel(images, active, out):
    value = active[...].astype(F32)
    y, x = map_places(value.shape[0], images)
    for tap in range(9):
        out[:, tap * PART : (tap + 1) * PART] = tap_shift(value, images, tap, 1, y, x).astype(BF16)


def head(pooled, w_head, w_proj, protos, norm, queue, match, micro, images, dp):
    rows = pooled.shape[0]
    group = rows // micro
    half = group // CROPS
    scale_all = 1.0 / (TEMPER * CROPS * half * micro)
    pre = dot(pooled, w_head)

    def by_micro(v):
        return v.reshape(micro, group, v.shape[-1])

    pre_m = by_micro(pre)
    mean = jnp.mean(pre_m, axis=1, keepdims=True)
    square = jnp.mean(pre_m * pre_m, axis=1, keepdims=True)
    rstd = lax.rsqrt(square - mean * mean + NORM_EPS)
    xhat = (pre_m - mean) * rstd
    y = xhat * norm[0] + norm[1]
    active = (y * sigmoid(y)).astype(BF16).reshape(rows, D)
    embed = dot(active, w_proj) + norm[2, :PROJ]
    recip = lax.rsqrt(jnp.sum(embed * embed, axis=1, keepdims=True) + UNIT_EPS)
    unit = (embed * recip).astype(BF16)
    scores = dot_nt(unit, protos)
    valid = lax.broadcasted_iota(jnp.int32, (1, 4, QUARTER_PAD), 2).reshape(1, 4 * QUARTER_PAD) < QUARTER
    own_mass = jnp.where(valid, jnp.exp(scores / SINK_EPS), 0.0).reshape(micro, CROPS, half, -1)
    queue_mass = jnp.where(valid, jnp.exp(jnp.einsum("cqp,kp->cqk", queue, protos, preferred_element_type=F32) / SINK_EPS), 0.0)
    codes = []
    for m in range(micro):
        for c in range(CROPS):
            a, b = queue_mass[c], own_mass[m, c]
            column = jnp.sum(a, axis=0, keepdims=True) + jnp.sum(b, axis=0, keepdims=True)
            once = jnp.where(valid, 1.0 / column, 0.0)
            a, b = a * once, b * once
            scale = valid.astype(F32)
            for turn in range(2):
                ra = 1.0 / jnp.sum(a * scale, axis=1, keepdims=True)
                rb = 1.0 / jnp.sum(b * scale, axis=1, keepdims=True)
                column = jnp.sum(a * ra, axis=0, keepdims=True) + jnp.sum(b * rb, axis=0, keepdims=True)
                scale = jnp.where(valid, 1.0 / column, 0.0)
            b = b * scale
            codes.append(b / jnp.sum(b, axis=1, keepdims=True))
    targets = []
    for m in range(micro):
        targets.append(jnp.dot(match[m], codes[m * CROPS + 1], precision=HIGH))
        targets.append(jnp.dot(match[m].T, codes[m * CROPS], precision=HIGH))
    target = jnp.concatenate(targets)
    logits = jnp.where(valid, scores / TEMPER, -1e30)
    logp = jax.nn.log_softmax(logits, axis=1)
    loss = -jnp.sum(jnp.where(valid, target * logp, 0.0)) * (TEMPER * scale_all)
    d_scores = ((jnp.exp(logp) * jnp.sum(target, axis=1, keepdims=True) - target) * scale_all).astype(BF16)
    d_unit = dot(d_scores, protos)
    d_embed = (
        recip * d_unit - embed * (recip * recip * recip) * jnp.sum(d_unit * embed, axis=1, keepdims=True)
    ).astype(BF16)
    d_active = dot_nt(d_embed, w_proj)
    d_y = by_micro(d_active) * slope(y)
    by_x = jnp.sum(d_y * xhat, axis=1, keepdims=True)
    plain = jnp.sum(d_y, axis=1, keepdims=True)
    d_pre = (norm[0] * rstd * (d_y - plain / group - xhat * by_x / group)).astype(BF16).reshape(rows, D)
    bias = jnp.pad(jnp.sum(d_embed.astype(F32), axis=0), (0, D - PROJ))
    grads = jnp.stack([jnp.sum(by_x, axis=(0, 1)), jnp.sum(plain, axis=(0, 1)), bias])
    return loss, grads, active, unit, d_scores, d_embed, d_pre


def valid_lanes():
    lane = lax.broadcasted_iota(jnp.int32, (1, 4 * QUARTER_PAD), 1).astype(F32)
    block = jnp.floor((lane + 0.5) * (1.0 / QUARTER_PAD))
    return lane - block * QUARTER_PAD < QUARTER - 0.5


def lanes_at(b, size):
    return pl.ds(pl.multiple_of(b * size, size), size)


def lanes_at(b, size):
    return pl.ds(pl.multiple_of(b * size, size), size)


def mass_kernel(micro, images, told_offsets, place, table, *refs):
    mass, column, match, rows_s, exps = refs[-5:]
    ndp = len(told_offsets)
    valid = valid_lanes()
    size = mass.shape[0] // ndp
    half = images * ndp
    at, said = 0, jnp.zeros((16, half), F32)
    row = lax.broadcasted_iota(jnp.int32, (PROJ, half), 0)
    lane = lax.broadcasted_iota(jnp.int32, (PROJ, half), 1)
    for ref in refs[:-5]:
        rows = size + 16
        for j in range(ref.shape[0] // rows):
            rows_s[lanes_at(place[7] ^ told_offsets[at], size), :] = ref[j * rows : j * rows + size, :]
            pairs = ref[(j + 1) * rows - 16 : (j + 1) * rows, :]
            spot_at = (place[7] ^ told_offsets[at]) * images
            spot = ((row < images) & (lane == row + spot_at)).astype(F32).astype(BF16)
            said = said + dot(pairs, spot)
            at += 1
    step = 128
    steps = mass.shape[0] // step

    def scored(i, sums):
        own = rows_s[lanes_at(i, step), :]
        out = []
        for a in range(4):
            lanes = slice(a * QUARTER_PAD, (a + 1) * QUARTER_PAD)
            value = jnp.exp(dot_nt(own, table[:, a * PROJ : (a + 1) * PROJ]) * (1.0 / SINK_EPS))
            value = jnp.where(valid[:, lanes], value, 0.0)
            exps[lanes_at(i, step), lanes] = value
            out.append(jnp.sum(value, axis=0, keepdims=True))
        return sums + jnp.concatenate(out, axis=1)

    sums = lax.fori_loop(0, steps, scored, jnp.zeros((1, 4 * QUARTER_PAD), F32))
    column[...] = jnp.broadcast_to(sums, column.shape)
    factor = jnp.where(valid & (sums > 1.18e-38), 1.0 / sums, 0.0)

    def divide(i, carry):
        mass[lanes_at(i, step), :] = (exps[lanes_at(i, step), :] * factor).astype(BF16)
        return carry

    lax.fori_loop(0, steps, divide, 0)

    def over(value, by):
        return jnp.floor((value + 0.5) * (1.0 / by))

    row = lax.broadcasted_iota(jnp.int32, (half, half), 0).astype(F32)
    lane = lax.broadcasted_iota(jnp.int32, (half, half), 1).astype(F32)
    block = over(row, images)
    for m in range(micro):
        same = (jnp.abs(block - over(lane, images)) < 0.5) & (jnp.abs(row - block * images - said[m : m + 1, :]) < 0.5)
        there = same.astype(F32)
        match[m] = jnp.where(place[4] == 0, there, there.T).astype(BF16)


def tables_kernel(packed, proj, table, rows, buffer, sem):
    size = THIRD - FIRST + 2
    copy = pltpu.make_async_copy(packed.at[pl.ds(FIRST, size), :], rows, sem)
    copy.start()
    copy.wait()
    wide = SECOND - FIRST
    for a in range(4):
        buffer[pl.ds(a, wide, stride=4), :] = rows[:wide, a * PROJ : (a + 1) * PROJ].astype(F32)
    proj[...] = buffer[...].astype(BF16)
    row = lax.broadcasted_iota(jnp.int32, (size - wide, WIDTH), 0)
    kept = jnp.where(row < QUARTER, rows[wide:, :].astype(F32), 0.0).astype(BF16)
    table[: size - wide, :] = kept
    table[size - wide :, :] = jnp.zeros((QUARTER_PAD - (size - wide), WIDTH), BF16)


def exact_dot(choose, value):
    parts, left = [], value
    for _ in range(3):
        term = left.astype(BF16)
        left = left - term.astype(F32)
        parts.append(term)
    return dot(jnp.concatenate([choose] * 3, axis=1), jnp.concatenate(parts, axis=0))


def by_micro_rows(value, ndp, micro):
    return value.reshape(ndp, micro, value.shape[0] // (ndp * micro), value.shape[1])


def total_of(value):
    return jnp.sum(jnp.sum(value, axis=0), axis=0, keepdims=True)


def regroup(rows, own, images, to_groups):
    ndp = rows // own
    row = lax.broadcasted_iota(jnp.int32, (rows, rows), 0).astype(F32)
    lane = lax.broadcasted_iota(jnp.int32, (rows, rows), 1).astype(F32)
    source, target = (lane, row) if to_groups else (row, lane)
    block = jnp.floor((source + 0.5) * (1.0 / own))
    inner = source - block * own
    part = jnp.floor((inner + 0.5) * (1.0 / images))
    moved = (part * ndp + block) * images + inner - part * images
    return (jnp.abs(moved - target) < 0.5).astype(F32).astype(BF16)


def head_kernel(
    micro, images, offsets, place, pooled_a, pooled_b, w_head, w_proj, table, norm, mass, column, match,
    pooled, active, unit, d_scores, embed, xhat_s, y_s, rstd_s, said,
    scores, own_mass, total, factor,
):
    ndp = len(offsets)
    rows = pooled.shape[0]
    group = rows // micro
    half = group // CROPS
    own = rows // ndp
    queued = mass.shape[0]
    scale_all = 1.0 / (TEMPER * CROPS * half * micro)
    chunk = WIDTH
    chunks = D // chunk
    core = place[4]
    for j, offset in enumerate(offsets):
        source = (pooled_a, pooled_b)[j * own // pooled_a.shape[0]]
        at = j * own % pooled_a.shape[0]
        pooled[lanes_at(place[7] ^ offset, own), :] = source[at : at + own, :]
    low = pooled[...]

    def forward(b, carry):
        lanes = lanes_at(b, chunk)
        pre = by_micro_rows(dot(low, w_head[:, lanes]), ndp, micro)
        gain, shift = norm[0, :, lanes], norm[1, :, lanes]
        xhats, ys = [], []
        for m in range(micro):
            v = pre[:, m]
            mean = total_of(v) * (1.0 / group)
            square = total_of(v * v) * (1.0 / group)
            rstd = lax.rsqrt(square - mean * mean + NORM_EPS)
            xhat = (v - mean) * rstd
            rstd_s[m : m + 1, lanes] = rstd
            xhats.append(xhat)
            ys.append(xhat * gain + shift)
        xhat_s[:, lanes] = jnp.stack(xhats, axis=1).reshape(rows, chunk)
        y = jnp.stack(ys, axis=1).reshape(rows, chunk)
        y_s[:, lanes] = y
        active[:, lanes] = (y * sigmoid(y)).astype(BF16)
        return carry

    lax.fori_loop(0, chunks, forward, 0)
    value = dot(active[...], w_proj[...]) + norm[2, :, :PROJ]
    embed[...] = value
    recip = lax.rsqrt(jnp.sum(value * value, axis=1, keepdims=True) + UNIT_EPS)
    unit_v = dot(regroup(rows, own, images, True), (value * recip).astype(BF16)).astype(BF16)
    unit[...] = unit_v
    valid = valid_lanes()
    for a in range(4):
        lanes = slice(a * QUARTER_PAD, (a + 1) * QUARTER_PAD)
        scores[:, lanes] = dot_nt(unit_v, table[:, a * PROJ : (a + 1) * PROJ])

    step = 128

    def divided(a):
        return a * (1.0 / jnp.sum(a, axis=1, keepdims=True))

    def folded(a):
        return jnp.sum(a.reshape(a.shape[0] // 8, 8, a.shape[1]), axis=0)

    def own_rows(m):
        return slice(m * half, (m + 1) * half)

    queue_sum = column[0:1, :]
    for m in range(micro):
        a = scores[lanes_at(m * CROPS + core, half), :]
        a = jnp.where(valid, jnp.exp(a * (1.0 / SINK_EPS)), 0.0)
        inverse = jnp.where(valid, 1.0 / (queue_sum + jnp.sum(a, axis=0, keepdims=True)), 0.0)
        factor[m : m + 1, :] = queue_sum * inverse
        factor[micro + m : micro + m + 1, :] = jnp.ones_like(inverse)
        own_mass[own_rows(m), :] = a * inverse

    def turn(i, carry):
        def block(i, carry):
            at = lanes_at(i, step)
            e_of = [mass[at, b * PART : (b + 1) * PART].astype(F32) for b in range(4 * QUARTER_PAD // PART)]
            rows_by = []
            for m in range(micro):
                sums = None
                for b, e in enumerate(e_of):
                    more = e * factor[m : m + 1, b * PART : (b + 1) * PART]
                    sums = more if sums is None else sums + more
                rows_by.append(1.0 / jnp.sum(sums, axis=1, keepdims=True))
            for b in range(4 * QUARTER_PAD // PART):
                lanes = slice(b * PART, (b + 1) * PART)
                e = mass[at, lanes].astype(F32)
                for m in range(micro):
                    total[m, :, lanes] += folded(e * rows_by[m])
            return carry

        total[...] = jnp.zeros_like(total)
        lax.fori_loop(0, queued // step, block, 0)
        for m in range(micro):
            scale = factor[micro + m : micro + m + 1, :]
            a = divided(own_mass[own_rows(m), :] * scale)
            sums = jnp.sum(total[m], axis=0, keepdims=True) * factor[m : m + 1, :]
            more = jnp.where(valid, 1.0 / (sums + jnp.sum(a, axis=0, keepdims=True)), 0.0)
            factor[m : m + 1, :] = factor[m : m + 1, :] * more
            factor[micro + m : micro + m + 1, :] = scale * more
        return carry

    lax.fori_loop(0, 2, turn, 0)

    def losses(m, loss):
        mine, there = lanes_at(m, half), lanes_at(m * CROPS + 1 - core, half)
        codes = divided(own_mass[mine, :] * factor[pl.ds(micro + m, 1), :])
        goal = exact_dot(match[m], codes)
        logits = jnp.where(valid, scores[there, :] * (1.0 / TEMPER), -1e30)
        logits = logits - jnp.max(logits, axis=1, keepdims=True)
        power = jnp.exp(logits)
        summed = jnp.sum(power, axis=1, keepdims=True)
        weight = jnp.sum(goal, axis=1, keepdims=True) / summed
        d_low = ((power * weight - goal) * scale_all).astype(BF16)
        d_scores[mine, :] = d_low
        d_unit = None
        for a in range(4):
            more = dot(d_low[:, a * QUARTER_PAD : (a + 1) * QUARTER_PAD], table[:, a * PROJ : (a + 1) * PROJ])
            d_unit = more if d_unit is None else d_unit + more
        said[mine, :] = d_unit
        return loss + jnp.sum(goal * (logits - jnp.log(summed)), axis=1, keepdims=True)

    loss = lax.fori_loop(0, micro, losses, jnp.zeros((half, 1), F32))
    loss = jnp.sum(loss, axis=0, keepdims=True) * (-TEMPER * scale_all)
    said[micro * half :, :] = jnp.broadcast_to(loss, (8, PROJ))


def head_back_kernel(
    micro, images, ndp, place, here, there, embed, w_proj, w_head, norm, xhat_s, y_s, rstd_s,
    d0, d1, d2, d3, notes, d_embed, d_pre, d_unit, d_own,
):
    rows = embed.shape[0]
    group = rows // micro
    half = group // CROPS
    own = rows // ndp
    chunk = WIDTH
    chunks = D // chunk
    for m in range(micro):
        d_unit[lanes_at(m * CROPS + place[5], half), :] = here[m * half : (m + 1) * half, :]
        d_unit[lanes_at(m * CROPS + place[4], half), :] = there[m * half : (m + 1) * half, :]
    value = embed[...]
    recip = lax.rsqrt(jnp.sum(value * value, axis=1, keepdims=True) + UNIT_EPS)
    d_back = exact_dot(regroup(rows, own, images, False), d_unit[...])
    along = jnp.sum(d_back * value, axis=1, keepdims=True)
    d_low = (recip * d_back - value * (recip * recip * recip) * along).astype(BF16)
    d_embed[...] = d_low
    notes[...] = jnp.zeros_like(notes)
    notes[2:3, :PROJ] = jnp.sum(d_low.astype(F32), axis=0, keepdims=True)
    loss = here[micro * half : micro * half + 1, :] + there[micro * half : micro * half + 1, :]
    notes[3:4, :PROJ] = loss

    def backward(b, carry):
        lanes = lanes_at(b, chunk)
        d_y = by_micro_rows(dot_nt(d_low, w_proj[lanes, :]) * slope(y_s[:, lanes]), ndp, micro)
        xhat = by_micro_rows(xhat_s[:, lanes], ndp, micro)
        gain = norm[0, :, lanes]
        values, by_xs, plains = [], None, None
        for m in range(micro):
            by_x = total_of(d_y[:, m] * xhat[:, m])
            plain = total_of(d_y[:, m])
            by_xs = by_x if by_xs is None else by_xs + by_x
            plains = plain if plains is None else plains + plain
            value = d_y[:, m] - plain * (1.0 / group) - xhat[:, m] * (by_x * (1.0 / group))
            values.append(gain * rstd_s[m : m + 1, lanes] * value)
        notes[0:1, lanes] = by_xs
        notes[1:2, lanes] = plains
        d_pre[:, lanes] = jnp.stack(values, axis=1).reshape(rows, chunk).astype(BF16)
        return carry

    lax.fori_loop(0, chunks, backward, 0)
    mine = d_pre[lanes_at(place[7], own), :]

    def to_pooled(b, carry):
        d_own[:, lanes_at(b, chunk)] = dot_nt(mine, w_head[lanes_at(b, chunk), :]).astype(BF16)
        return carry

    lax.fori_loop(0, chunks, to_pooled, 0)
    for j, out in enumerate((d0, d1, d2, d3)):
        out[...] = d_own[:, j * WIDE : (j + 1) * WIDE]


def interleave(width):
    row = lax.broadcasted_iota(jnp.int32, (4 * width, 4 * width), 0)
    column = lax.broadcasted_iota(jnp.int32, (4 * width, 4 * width), 1)
    return (column == 4 * (row & (width - 1)) + (row >> (width.bit_length() - 1))).astype(F32).astype(BF16)


def own_columns(place, own):
    row = lax.broadcasted_iota(jnp.int32, (WIDTH, own), 0)
    lane = lax.broadcasted_iota(jnp.int32, (WIDTH, own), 1)
    return (row == lane + place[7] * own).astype(F32).astype(BF16)


def tail_grads_kernel(place, active, unit, d_here, d_there, d_embed, out):
    @pl.when(place[0] == SECTIONS - 1)
    def _():
        own = out.shape[0]
        choose = own_columns(place, own)
        rows = active.shape[0]
        wide = jnp.concatenate([active[:, b * WIDTH : (b + 1) * WIDTH] for b in range(4)], axis=0)
        wide = dot_nt(wide, interleave(PART)).astype(BF16)
        half = d_here.shape[0] // 2
        units = []
        for core in (place[5], place[4]):
            units.append(jnp.concatenate([unit[lanes_at(m * CROPS + core, half), :] for m in range(2)], axis=0))
        proj = jnp.zeros((own, WIDTH), F32)
        proto = jnp.zeros((own, QUARTER_PAD), F32)
        for a in range(4):
            some = choose[a * PROJ : (a + 1) * PROJ, :]
            own_e = dot(d_embed[...], some).astype(BF16)
            column = [wide[b * rows : (b + 1) * rows, a * PART : (a + 1) * PART] for b in range(4)]
            proj = proj + dot_tn(own_e, jnp.concatenate(column, axis=1))
            for own_unit, d_scores in zip(units, (d_here, d_there)):
                own_u = dot(own_unit, some).astype(BF16)
                proto = proto + dot_tn(own_u, d_scores[:, a * QUARTER_PAD : (a + 1) * QUARTER_PAD])
        out[:, :WIDTH] = proj
        out[:, WIDTH:] = proto


def head_grads_kernel(place, pooled, d_pre, tail, out, parts):
    @pl.when(place[0] != SECTIONS - 1)
    def _():
        out[...] = jnp.zeros_like(out)

    @pl.when(place[0] == SECTIONS - 1)
    def _():
        own = out.shape[0]
        choose = own_columns(place, own)
        weave = interleave(PART)
        own_d = [dot(d_pre[:, q * WIDTH : (q + 1) * WIDTH], choose).astype(BF16) for q in range(4)]
        own_d = jnp.concatenate(own_d, axis=1)

        def product(b, carry):
            parts[:, lanes_at(b, WIDTH)] = dot_tn(own_d, pooled[:, lanes_at(b, WIDTH)]).astype(BF16)
            return carry

        lax.fori_loop(0, 4, product, 0)

        def mix(b, carry):
            mixed = []
            for j in range(4):
                lanes = pl.ds(pl.multiple_of(b * WIDTH + j * PART, PART), PART)
                four = [parts[q * own : (q + 1) * own, lanes] for q in range(4)]
                mixed.append(jnp.concatenate(four, axis=1))
            mixed = dot(jnp.concatenate(mixed, axis=0), weave)
            for j in range(4):
                lanes = pl.ds(pl.multiple_of((4 * b + j) * WIDTH, WIDTH), WIDTH)
                out[:, lanes] = mixed[j * own : (j + 1) * own, :]
            return carry

        lax.fori_loop(0, 4, mix, 0)
        out[:, FIRST:] = tail[:, : out.shape[1] - FIRST]


def finish_kernel(place, base, reduce, conv, expand, m1, m2, m3, out, buffer, sem):
    mixed = (None, m1, m2, m3)
    t = place[0]

    def write(first, lanes):
        part = pl.ds(first, lanes)
        copy = pltpu.make_async_copy(buffer.at[:, part], out.at[:, part], sem.at[first // WIDE])
        copy.start()
        return copy

    @pl.when(t == 0)
    def _():
        copies = []
        for u in range(SECTIONS):
            piece = reduce if u == 0 else mixed[u]
            buffer[:, u * WIDE : (u + 1) * WIDE] = piece[:, :WIDE].astype(F32)
            copies.append(write(u * WIDE, WIDE))
        for copy in copies:
            copy.wait()

    @pl.when(t == 1)
    def _():
        for u in range(SECTIONS):
            piece = conv if u == 1 else mixed[u ^ 1]
            for tap in range(9):
                at = tap * WIDTH + u * PART
                buffer[:, at : at + PART] = piece[:, tap * PART : (tap + 1) * PART].astype(F32)
        write(0, 9 * WIDTH).wait()

    @pl.when(t == 2)
    def _():
        four = [expand if u == 2 else mixed[u ^ 2] for u in range(SECTIONS)]
        weave = interleave(PART)
        for b in range(WIDTH // PART):
            lanes = slice(b * PART, (b + 1) * PART)
            row = jnp.concatenate([f[:, lanes] for f in four], axis=1)
            buffer[:, 4 * b * PART : 4 * (b + 1) * PART] = dot(row, weave)
        write(0, D).wait()


def unpack_kernel(packed, out, buffer):
    rows = packed.shape[0]
    for b in range(4):
        buffer[b] = packed[:, b * PART : (b + 1) * PART].astype(F32)
    for q in range(4):
        for b in range(4):
            at = q * WIDTH + b * PART
            out[:, at : at + PART] = buffer[b, pl.ds(q, rows // 4, stride=4), :].astype(BF16)


def unpack(packed, rows):
    step = 1024
    return pl.pallas_call(
        unpack_kernel,
        name="unpack",
        out_shape=shape((rows // 4, 4 * WIDTH), BF16),
        grid=(rows // step,),
        in_specs=[pl.BlockSpec((step, WIDTH), lambda i: (i, 0))],
        out_specs=pl.BlockSpec((step // 4, 4 * WIDTH), lambda i: (i, 0)),
        scratch_shapes=[pltpu.VMEM((4, step, PART), F32)],
        compiler_params=pltpu.CompilerParams(vmem_limit_bytes=16 * 2**20),
        cost_estimate=cost(4),
    )(packed)


def pack_kernel(place, packed, norm, o0, o1, o2, o3, rows, buffer, sem):
    outs = (o0, o1, o2, o3)
    t, core = place[0], place[4]

    def run(copies):
        for copy in copies:
            copy.start()
        return copies

    def lanes_of(target, lanes):
        return pl.ds(target * lanes, lanes)

    @pl.when(t == 0)
    def _():
        half = D // 2
        copies = []
        for k, out in enumerate(outs):
            source = packed.at[pl.ds(pl.multiple_of(core * half, half), half), lanes_of(k, PART)]
            copies.append(pltpu.make_async_copy(source, out.at[pl.ds(16, half), :], sem.at[k]))
        run(copies)
        for k, out in enumerate(outs):
            out[:16, :] = tell_norm(norm, k * PART)
        for copy in copies:
            copy.wait()

    @pl.when(t == 1)
    def _():
        quarter = WIDTH // 4
        copies = []
        for k, out in enumerate(outs):
            for tap in range(9):
                at = pl.multiple_of(tap * WIDTH + place[8] * quarter, quarter)
                source = packed.at[pl.ds(at, quarter), lanes_of(1 ^ k, PART)]
                target = out.at[pl.ds(16 + tap * quarter, quarter), :]
                copies.append(pltpu.make_async_copy(source, target, sem.at[9 * k + tap]))
        run(copies)
        for k, out in enumerate(outs):
            out[:16, :] = tell_norm(norm, (1 ^ k) * PART)
        for copy in copies:
            copy.wait()

    @pl.when(t == 2)
    def _():
        size = rows.shape[0]
        copy = pltpu.make_async_copy(packed.at[pl.ds(pl.multiple_of(core * size, size), size), :], rows, sem.at[0])
        copy.start()
        copy.wait()
        for b in range(4):
            buffer[b] = rows[:, b * PART : (b + 1) * PART].astype(F32)
        for k, out in enumerate(outs):
            u = 2 ^ k
            for b in range(4):
                at = b * HALF_EXPAND
                lane = u * WIDE + b * PART
                out[at : at + 16, :] = tell_norm(norm, lane)
                out[at + 16 : at + HALF_EXPAND, :] = buffer[b, pl.ds(u, size // 4, stride=4), :].astype(BF16)


def pack(place, packed, norm):
    rows = 4 * (WIDTH // 2)
    return pl.pallas_call(
        pack_kernel,
        name="pack",
        out_shape=[shape((QUARTER_CONV, PART), BF16)] * 4,
        in_specs=[
            pl.BlockSpec(memory_space=pltpu.SMEM),
            pl.BlockSpec(memory_space=pltpu.HBM),
            pl.BlockSpec(memory_space=pltpu.VMEM),
        ],
        out_specs=[pl.BlockSpec(memory_space=pltpu.VMEM)] * 4,
        scratch_shapes=[
            pltpu.VMEM((rows, WIDTH), BF16), pltpu.VMEM((4, rows, PART), F32), pltpu.SemaphoreType.DMA((36,)),
        ],
        compiler_params=pltpu.CompilerParams(vmem_limit_bytes=12 * 2**20),
        cost_estimate=cost(2),
    )(place, hbm(packed), norm)


def multiple(value, step):
    return value if isinstance(value, int) else pl.multiple_of(value, step)


def pair_kernel(place, a, b, keep, out):
    full = dot_tn(a[...], b[...])
    own = keep.shape[1]
    first = place[4] == 0
    for z in range(keep.shape[0]):
        one = full[2 * z * own : (2 * z + 1) * own]
        two = full[(2 * z + 1) * own : (2 * z + 2) * own]
        keep[z] = jnp.where(first, one, two)
        out[z] = jnp.where(first, two, one).astype(BF16)


def image_pair_kernel(place, d0, d1, d2, d3, image, keep, out, d_full):
    fill(place, (d0, d1, d2, d3), d_full)
    lanes = pl.ds(pl.multiple_of(place[0] * WIDE, WIDE), WIDE)
    pair_kernel(place, d_full, image.at[:, lanes], keep, out)


def cross_kernel(place, keep, came, own, o1, o2, o3):
    for k, o in enumerate((own, o1, o2, o3)):
        z = place[6] ^ k
        o[...] = (keep[z] + came[z].astype(F32)).astype(o.dtype)


def far_kernel(place, keep, came, kept, out):
    for j in range(2):
        mine, other = place[6] ^ j, place[6] ^ (2 + j)
        kept[j] = keep[mine] + came[mine].astype(F32)
        out[j] = (keep[other] + came[other].astype(F32)).astype(BF16)


def near_kernel(keep, came, kept, out):
    kept[...] = keep[0] + came[0].astype(F32)
    out[...] = (keep[1] + came[1].astype(F32)).astype(BF16)


def last_kernel(keep, came, out):
    out[...] = (keep[...] + came[...].astype(F32)).astype(BF16)


def add_kernel(own, r1, r2, r3, out):
    out[...] = ((own[...] + r1[...].astype(F32)) + (r2[...].astype(F32) + r3[...].astype(F32))).astype(BF16)


def after(value, *others):
    return lax.optimization_barrier((value, *others))[0]


def body(image, section_weights, section_norms, queue, pairing):
    micro, images = image.shape[0], image.shape[2]
    ndp = lax.axis_size("dp")
    t = lax.axis_index("section")
    dp = lax.axis_index("dp")
    core = dp % 2
    place = jnp.stack([t ^ k for k in range(SECTIONS)] + [core, 1 - core, dp // 2, dp, dp % 4]).astype(jnp.int32)
    cells = CROPS * PLACES * images
    rows = micro * cells
    count = float(cells * ndp)
    packed = section_weights[0]
    norm3 = section_norms.transpose(1, 0, 2)
    param_rows = packed.shape[0]
    own = WIDTH // ndp
    k = functools.partial

    def pieces_of(width, dtype):
        return shape((rows, width), dtype)

    own_message, *messages = pack(place, packed, norm3)
    came = [own_message]
    for j in range(1, SECTIONS):
        came.append(lax.ppermute(messages[j - 1], "section", [(u, u ^ j) for u in range(3)]))
    flat = call(
        retile_kernel, shape((rows, D), BF16),
        image.transpose(0, 1, 3, 4, 2, 5).reshape(rows // images, images, D),
        us=2,
    )
    head_rows = rows // PLACES * ndp
    small = ndp == 8 and head_rows <= 128 and images == 4 and queue.shape[1] * ndp <= 512
    told, told_offsets = [flat], []
    if small:
        note = [shape((queue.shape[1] + 16, PROJ), BF16)] * 2
        keep, out = call(note_kernel, note, place, pairing, queue, us=0.5)
        told, told_offsets = [rows_of([keep, flip(out, "dp", 1)])], [0, 1]
        told = [rows_of([told[0], flip(told[0], "dp", 2)])]
        told_offsets = told_offsets + [offset ^ 2 for offset in told_offsets]
    natural = unpack(packed, FIRST)
    *came, flat, told[0], natural = lax.optimization_barrier((*came, flat, told[0], natural))
    conv_part, pair_part = call(
        pick_kernel,
        (shape((QUARTER_CONV, PART), BF16), shape((HALF_REDUCE + 4 * HALF_EXPAND, PART), BF16)),
        place, *came,
    )
    pair_parts = (pair_part, flip(pair_part, "dp", 1))
    conv_near = flip(conv_part, "dp", 2)
    sums_of = shape((8, PART), F32)
    pre0, part = call(
        k(reduce_kernel, micro), (pieces_of(PART, F32), sums_of), place, flat, *pair_parts, us=2
    )
    sums0 = sum_dp(part)
    active0 = call(k(active_kernel, micro, count), pieces_of(PART, BF16), pre0, sums0, pair_part, us=1)
    actives0 = gather_xor(active0, "section")

    conv_part = rows_of([conv_part, after(conv_near, active0)])
    w_conv = (conv_part, flip(conv_part, "dp", 1))
    if small:
        told.append(flip(after(told[0], active0), "dp", 4))
        told_offsets = told_offsets + [offset ^ 4 for offset in told_offsets]
    w_proj, table = pl.pallas_call(
        tables_kernel,
        name="tables",
        out_shape=(shape((D, PROJ), BF16), shape((QUARTER_PAD, WIDTH), BF16)),
        in_specs=[pl.BlockSpec(memory_space=pltpu.HBM)],
        out_specs=(pl.BlockSpec(memory_space=pltpu.VMEM), pl.BlockSpec(memory_space=pltpu.VMEM)),
        scratch_shapes=[
            pltpu.VMEM((THIRD - FIRST + 2, WIDTH), BF16), pltpu.VMEM((D, PROJ), F32), pltpu.SemaphoreType.DMA,
        ],
        compiler_params=pltpu.CompilerParams(vmem_limit_bytes=12 * 2**20),
        cost_estimate=cost(1.5),
    )(hbm(after(packed, active0)))
    taps = call(k(taps_kernel, images), pieces_of(9 * PART, BF16), active0, us=1.3)
    back_rows = 9 * PART // 2 + WIDE // 2
    back_own = call(
        back_parts_kernel, [shape((back_rows, PART), BF16)] * 4, place, *w_conv, *pair_parts, us=1
    )
    joined = lax.optimization_barrier((*actives0, table, taps, told[-1], *back_own))
    actives0, (table, taps, told[-1]), back_own = joined[:4], joined[4:7], joined[7:]
    pre1, part = call(
        k(conv_kernel, micro, images),
        (pieces_of(PART, F32), sums_of),
        place, *actives0, *w_conv,
        scratch=[pltpu.VMEM((rows, WIDTH), BF16), pltpu.VMEM((WIDTH, 9 * PART), BF16)],
        us=3,
    )
    sums1 = sum_dp(part)
    active1_own = call(k(active_kernel, micro, count), pieces_of(PART, BF16), pre1, sums1, conv_part, us=1)
    actives1 = gather_xor(active1_own, "section")
    lanes = 4 * QUARTER_PAD
    stages = dp_stages()
    head_stages = stages[1:] + stages[:1]
    offsets = [0]
    for steps in head_stages:
        offsets = offsets + [o ^ step for step in steps for o in offsets]
    if small:
        queued = ndp * queue.shape[1]
        mass, column, match = call(
            k(mass_kernel, micro, images, told_offsets),
            (
                shape((queued, lanes), BF16), shape((8, lanes), F32),
                shape((micro, images * ndp, images * ndp), BF16),
            ),
            place, after(table, active1_own), *told,
            scratch=[pltpu.VMEM((queued, PROJ), BF16), pltpu.VMEM((queued, lanes), F32)],
            vmem=16, us=5,
        )
    if small:
        *actives1, mass = lax.optimization_barrier((*actives1, mass))
    active1, pre2, part, w_expand = call(
        k(expand_kernel, micro),
        (pieces_of(WIDTH, BF16), pieces_of(WIDE, F32), shape((8, WIDE), F32), shape((WIDTH, WIDE), BF16)),
        place, *actives1, *pair_parts,
        us=2,
    )
    back_own = lax.optimization_barrier((*back_own, part))[:4]
    back_came = [back_own[0]] + [flip(back_own[j], "section", j) for j in range(1, SECTIONS)]

    sums2 = sum_dp(part)
    pooled = call(
        k(pool_kernel, micro, images, count),
        shape((rows // PLACES, WIDE), BF16),
        place, pre2, sums2, pair_part, flat,
        us=1.6,
    )

    per_dp = rows // PLACES
    came_p = gather_xor(pooled, "section")[::-1]
    pooled_here = call(lanes_kernel, shape((per_dp, D), BF16), *came_p, us=0.3)
    parts, _ = gather_dp(pooled_here, head_stages)
    if small:
        all_pooled, active3, unit, d_scores, embed, *kept, said = call(
            k(head_kernel, micro, images, offsets),
            [
                shape((head_rows, D), BF16), shape((head_rows, D), BF16), shape((head_rows, PROJ), BF16),
                shape((head_rows // 2, lanes), BF16), shape((head_rows, PROJ), F32), shape((head_rows, D), F32),
                shape((head_rows, D), F32), shape((8, D), F32), shape((head_rows // 2 + 8, PROJ), F32),
            ],
            place, *parts, natural, w_proj, table, norm3, mass, column, match,
            scratch=[
                pltpu.VMEM((head_rows, lanes), F32), pltpu.VMEM((head_rows // 2, lanes), F32),
                pltpu.VMEM((micro, 8, lanes), F32), pltpu.VMEM((8, lanes), F32),
            ],
            vmem=15, us=12,
        )
        *d_pooled, notes3, d_embed, d_pre3 = call(
            k(head_back_kernel, micro, images, ndp),
            [shape((per_dp, WIDE), BF16)] * 4
            + [shape((8, D), F32), shape((head_rows, PROJ), BF16), shape((head_rows, D), BF16)],
            place, said, flip(said, "dp", 1), embed, w_proj, natural, norm3, *kept,
            scratch=[pltpu.VMEM((head_rows, PROJ), F32), pltpu.VMEM((per_dp, D), BF16)],
            us=5,
        )
    else:
        all_pooled = jnp.concatenate(parts)
        offset = jnp.array(offsets, jnp.int32)
        head_order = jnp.arange(head_rows, dtype=jnp.int32)
        block, inner = head_order // per_dp, head_order % per_dp
        group, single = inner // images, inner % images
        position = (group * ndp + (offset[block] ^ dp)) * images + single
        order = (position[None, :] == head_order[:, None]).astype(BF16)
        pairs = lax.all_gather(pairing.astype(F32), "dp").astype(jnp.int32)
        left = jnp.arange(images * ndp, dtype=jnp.int32)
        pairs = pairs.transpose(1, 0, 2).reshape(micro, ndp * images)
        match = ((left // images * images + pairs)[:, :, None] == left[None, None, :]).astype(F32)
        all_pooled = dot(order, all_pooled).astype(BF16)
        protos = jnp.concatenate([table[:, a * PROJ : (a + 1) * PROJ] for a in range(4)], axis=0)
        queue_rows = lax.all_gather(queue, "dp", axis=1, tiled=True)
        loss, grads3, active3, unit, d_scores, d_embed, d_pre3 = head(
            all_pooled, natural, w_proj, protos, norm3[:, 0], queue_rows, match, micro, images, dp
        )
        notes3 = jnp.concatenate([grads3, jnp.full((5, D), loss)])
        d_pooled = dot_nt(dot_tn(order[:, :per_dp], d_pre3).astype(BF16), natural).astype(BF16)
        d_pooled = [d_pooled[:, j * WIDE : (j + 1) * WIDE] for j in range(SECTIONS)]
        d_scores = d_scores.reshape(micro, CROPS, head_rows // 4, lanes)
        d_scores = lax.dynamic_index_in_dim(d_scores, 1 - core, 1, keepdims=False).reshape(-1, lanes)

    joined = lax.optimization_barrier((*d_pooled, *back_came))
    d_pooled, back_came = joined[:SECTIONS], joined[SECTIONS:]
    came_d = [flip(d_pooled[3 ^ j], "section", j) for j in range(1, SECTIONS)]
    back_half = call(stack_kernel, shape((SECTIONS, back_rows, PART), BF16), *back_came, us=0.6)
    back_halves = (back_half, flip(back_half, "dp", 1))
    d_z, part = call(
        k(out_back_kernel, micro, images, count),
        (pieces_of(WIDE, F32), shape((8, WIDE), F32)),
        place, pre2, sums2, pair_part, flat, d_pooled[3], *came_d,
        us=1.8,
    )
    back2 = sum_dp(part)
    back2, *back_halves = lax.optimization_barrier((back2, *back_halves))
    d_pre2, *partial = call(
        k(expand_back_kernel, micro, count),
        [pieces_of(WIDE, BF16)] + [pieces_of(PART, BF16)] * 4,
        place, pre2, sums2, d_z, back2, pair_part, w_expand,
        scratch=[pltpu.VMEM((rows, WIDTH), F32)],
        us=2,
    )
    partial = [partial[0]] + [flip(partial[j], "section", j) for j in range(1, SECTIONS)]

    def scatter_start(a, b, width):
        if ndp != 8:
            return dot_tn(a, b)
        keep, out = call(
            pair_kernel,
            (shape((4, own, width), F32), shape((4, own, width), BF16)),
            place, a, b,
            us=2.5,
        )
        return keep, flip(out, "dp", 1)

    def scatter_cross(started, *others):
        if ndp != 8:
            return [lax.psum_scatter(started.astype(BF16), "dp", scatter_dimension=0, tiled=True)]
        keep, came = started
        if others:
            keep = after(keep, *others)
        dims = keep.shape[1:]
        kept, *out = call(
            cross_kernel, [shape(dims, F32)] + [shape(dims, BF16)] * 3, place, keep, came
        )
        return [kept] + [flip(out[j], "dp", 2 * (j + 1)) for j in range(3)]

    def scatter_far(started, *others):
        if ndp != 8:
            return lax.psum_scatter(started.astype(BF16), "dp", scatter_dimension=0, tiled=True), None
        keep, came = started
        if others:
            keep = after(keep, *others)
        dims = (2, *keep.shape[1:])
        kept, out = call(far_kernel, (shape(dims, F32), shape(dims, BF16)), place, keep, came, us=0.7)
        return kept, flip(out, "dp", 4)

    def scatter_near(started, *others):
        if ndp != 8:
            return started
        keep, came = started
        if others:
            keep = after(keep, *others)
        dims = keep.shape[1:]
        kept, out = call(near_kernel, (shape(dims, F32), shape(dims, BF16)), keep, came, us=0.5)
        return kept, flip(out, "dp", 2)

    def scatter_last(started):
        if ndp != 8:
            return started[0].astype(BF16)
        return call(last_kernel, shape(started[0].shape, BF16), *started, us=0.4)

    def scatter_finish(crossed):
        if ndp != 8:
            return crossed[0].astype(BF16)
        return call(add_kernel, shape(crossed[0].shape, BF16), *crossed, us=0.6)

    expand_half = scatter_far(scatter_start(d_pre2, active1, WIDTH))
    tail = call(
        tail_grads_kernel,
        shape((own, WIDTH + QUARTER_PAD), F32),
        place, after(active3, d_pre2), unit, d_scores, flip(d_scores, "dp", 1), d_embed,
        us=3,
    )
    joined = lax.optimization_barrier((*partial, tail, *expand_half[: 2 if ndp == 8 else 1]))
    partial, tail, expand_half = joined[:SECTIONS], joined[SECTIONS], joined[SECTIONS + 1 :]

    d_y1, part = call(
        k(silu_back_kernel, micro, count),
        (pieces_of(PART, F32), sums_of),
        *partial, pre1, sums1, conv_part,
    )
    back1 = sum_dp(part)
    d_pre1_own = call(
        k(norm_back_kernel, micro, count), pieces_of(PART, BF16), d_y1, pre1, sums1, back1, conv_part
    )
    d_pre1s = gather_xor(d_pre1_own, "section")
    expand_last = scatter_near(expand_half, d_pre1_own)
    base = call(
        head_grads_kernel,
        shape((own, param_rows), F32),
        place, after(all_pooled, d_pre1_own), d_pre3, tail,
        scratch=[pltpu.VMEM((4 * own, D), BF16)],
        us=4,
    )
    joined = lax.optimization_barrier((*d_pre1s, base, *expand_last))
    d_pre1s, base, expand_last = joined[:SECTIONS], joined[SECTIONS], joined[SECTIONS + 1 :]
    d_pre1, d_y0, part = call(
        k(conv_back_kernel, micro, images, count),
        (pieces_of(WIDTH, BF16), pieces_of(PART, F32), sums_of),
        place, *d_pre1s, *back_halves, pre0, sums0, pair_part,
        scratch=[pltpu.VMEM((9 * PART, WIDTH), BF16)],
        us=3.5,
    )
    conv_started = scatter_start(d_pre1, taps, 9 * PART)
    back0 = sum_dp(part)
    d_pre0_own = call(
        k(last_norm_back_kernel, micro, count),
        shape((rows + NOTE_ROWS, PART), BF16),
        place, d_y0, pre0, sums0, back0, pair_part, back2, back1, notes3,
    )
    d_pre0s = gather_xor(d_pre0_own, "section")
    conv_half = scatter_far(conv_started)
    joined = lax.optimization_barrier((*d_pre0s, conv_half[0]))
    d_pre0s, conv_half = joined[:SECTIONS], (joined[SECTIONS], conv_half[1])
    conv_last = scatter_near(conv_half)
    joined = lax.optimization_barrier((*d_pre0s, conv_last[0]))
    d_pre0s, conv_last = joined[:SECTIONS], (joined[SECTIONS], conv_last[1])

    if ndp == 8:
        keep, out, d_pre0 = call(
            image_pair_kernel,
            (shape((4, own, WIDE), F32), shape((4, own, WIDE), BF16), pieces_of(WIDTH, BF16)),
            place, *d_pre0s, flat,
            us=2.5,
        )
        reduce_started = keep, flip(out, "dp", 1)
    else:
        d_pre0 = jnp.stack(d_pre0s)[place[:SECTIONS], :rows].transpose(1, 0, 2).reshape(rows, WIDTH)
        reduce_started = dot_tn(d_pre0, lax.dynamic_slice_in_dim(flat, t * WIDE, WIDE, 1))
    reduce_crossed = scatter_cross(reduce_started)
    grad_in = call(
        reduce_back_kernel,
        shape((rows // images, images, WIDE), F32),
        place, d_pre0, *back_halves, d_z,
        scratch=[pltpu.VMEM((WIDE, WIDTH), BF16)],
        us=2,
    )
    norm_grads, loss = call(
        told_kernel, (shape((3, 1, D), F32), shape((8, PROJ), F32)), place, *d_pre0s, notes3, us=0.5
    )
    g_conv = scatter_last(conv_last)
    g_expand = scatter_last(expand_last)
    joined = lax.optimization_barrier((*reduce_crossed, grad_in, norm_grads, g_conv, g_expand))
    *reduce_crossed, grad_in, norm_grads, g_conv, g_expand = joined
    if ndp != 8:
        nothing = jnp.zeros(reduce_crossed[0].shape, BF16)
        reduce_crossed = [reduce_crossed[0].astype(F32), nothing, nothing, nothing]
    g_reduce, *mixed = call(
        mixed_kernel,
        [shape(reduce_crossed[0].shape, BF16)] + [shape(g_conv.shape, BF16)] * 3,
        place, *reduce_crossed, g_conv, g_expand,
        us=0.5,
    )
    mixed = [
        lax.ppermute(mixed[j - 1], "section", [(u ^ j, u) for u in range(3)]) for j in range(1, SECTIONS)
    ]
    weight_grads = pl.pallas_call(
        finish_kernel,
        name="finish",
        out_shape=shape((own, param_rows), F32),
        in_specs=[pl.BlockSpec(memory_space=pltpu.SMEM), pl.BlockSpec(memory_space=pltpu.HBM)]
        + [pl.BlockSpec(memory_space=pltpu.VMEM)] * 6,
        out_specs=pl.BlockSpec(memory_space=pltpu.HBM),
        scratch_shapes=[pltpu.VMEM((own, 9 * WIDTH), F32), pltpu.SemaphoreType.DMA((SECTIONS,))],
        input_output_aliases={1: 0},
        compiler_params=pltpu.CompilerParams(vmem_limit_bytes=12 * 2**20),
        cost_estimate=cost(2),
    )(place, base, g_reduce, g_conv, g_expand, *mixed)
    grad_in = grad_in.reshape(micro, CROPS, SIDE, SIDE, images, WIDE).transpose(0, 1, 4, 2, 3, 5)
    return (loss[0, 0], grad_in, weight_grads.T[None], norm_grads.transpose(1, 0, 2))


def solution(mesh):
    in_specs = (
        P(None, None, "dp", None, None, None),
        P("section", None, None),
        P("section", None, None),
        P(None, "dp", None),
        P(None, "dp"),
    )
    out_specs = (
        P(),
        P(None, None, "dp", None, None, "section"),
        P("section", None, "dp"),
        P("section", None, None),
    )
    return jax.shard_map(body, mesh=mesh, in_specs=in_specs, out_specs=out_specs, check_vma=False)
```

```python
import functools

import jax
import jax.numpy as jnp
from jax import lax
from jax.experimental import pallas as pl
from jax.experimental.pallas import tpu as pltpu
from jax.sharding import PartitionSpec as P

D = 2048
WIDTH = 512
PROJ = 128
PROTOS = 3000
SIDE = 7
CROPS = 2
SECTIONS = 4
PART = WIDTH // SECTIONS
WIDE = D // SECTIONS
QUARTER = PROTOS // 4
QUARTER_PAD = 768
PLACES = SIDE * SIDE
FIRST = D * (D // WIDTH)
SECOND = FIRST + D * PROJ // WIDTH
THIRD = SECOND + PROTOS * PROJ // WIDTH
HALF_REDUCE = 16 + D // 2
HALF_EXPAND = 16 + WIDTH // 2
QUARTER_CONV = 16 + 9 * WIDTH // 4
NOTE_ROWS = 48

NORM_EPS = 1e-05
UNIT_EPS = 1e-06
SINK_EPS = 0.05
TEMPER = 0.1
HIGH = lax.Precision.HIGHEST
F32 = jnp.float32
BF16 = jnp.bfloat16
NT = (((1,), (1,)), ((), ()))
TN = (((0,), (0,)), ((), ()))


def dot(a, b):
    return jnp.dot(a, b, preferred_element_type=F32)


def dot_nt(a, b):
    return lax.dot_general(a, b, NT, preferred_element_type=F32)


def dot_tn(a, b):
    return lax.dot_general(a, b, TN, preferred_element_type=F32)


def flip(value, axis, step):
    count = lax.axis_size(axis)
    return lax.ppermute(value, axis, [(source, source ^ step) for source in range(count)])


def send(value, source, target):
    return lax.ppermute(value, "section", [(source, target)])


def sum_dp_steps(value):
    count = lax.axis_size("dp")
    value = pair = value + flip(value, "dp", 1)
    step = 2
    while step < count:
        if 2 * step < count:
            near = value + flip(value, "dp", step)
            far = flip(value, "dp", 3 * step) + flip(value, "dp", 2 * step)
            value = near + far
            step *= 4
        else:
            value = value + flip(value, "dp", step)
            step *= 2
    return value, pair


def sum_dp(value):
    return sum_dp_steps(value)[0]


def gather_xor(value, axis):
    return [value] + [flip(value, axis, step) for step in range(1, lax.axis_size(axis))]


def dp_stages():
    count = lax.axis_size("dp")
    stages, step = [(1,)], 2
    while step < count:
        if 2 * step < count:
            stages.append((step, 2 * step, 3 * step))
            step *= 4
        else:
            stages.append((step,))
            step *= 2
    return stages


def gather_dp(value, stages):
    arrays, offsets = [value], [[0]]
    for steps in stages:
        if len(arrays) > 1:
            arrays, offsets = [rows_of(arrays)], [sum(offsets, [])]
        first = offsets[0]
        for step in steps:
            arrays.append(flip(arrays[0], "dp", step))
            offsets.append([o ^ step for o in first])
    return arrays, offsets


def sigmoid(v):
    return 0.5 * jnp.tanh(0.5 * v) + 0.5


def slope(v):
    s = sigmoid(v)
    return s * (1.0 + v * (1.0 - s))


def cost(us):
    return pl.CostEstimate(flops=0, bytes_accessed=int(us * 3_000_000), transcendentals=0)


def hbm(value):
    return pltpu.with_memory_space_constraint(value, pltpu.HBM)


def call(kernel, out, *args, scratch=(), vmem=12, us=1.0, in_hbm=()):
    in_specs, ins = [], []
    for j, a in enumerate(args):
        space = pltpu.VMEM
        if jnp.issubdtype(a.dtype, jnp.integer):
            space = pltpu.SMEM
        elif j in in_hbm:
            space = pltpu.HBM
            a = hbm(a)
        in_specs.append(pl.BlockSpec(memory_space=space))
        ins.append(a)
    return pl.pallas_call(
        kernel,
        name=getattr(kernel, 'func', kernel).__name__,
        out_shape=out,
        in_specs=in_specs,
        out_specs=jax.tree.map(lambda _: pl.BlockSpec(memory_space=pltpu.VMEM), out),
        scratch_shapes=list(scratch),
        compiler_params=pltpu.CompilerParams(vmem_limit_bytes=vmem * 2**20),
        cost_estimate=cost(us),
    )(*ins)


def shape(dims, dtype):
    return jax.ShapeDtypeStruct(tuple(dims), dtype)


def retile_kernel(image, flat):
    flat[...] = image[...].reshape(flat.shape)


def note_kernel(place, pairing, queue, keep, send):
    size = queue.shape[1]
    row = lax.broadcasted_iota(jnp.int32, (16, PROJ), 0)
    lane = lax.broadcasted_iota(jnp.int32, (16, PROJ), 1)
    value = jnp.zeros((16, PROJ), F32)
    for m in range(pairing.shape[0]):
        for i in range(pairing.shape[1]):
            value = jnp.where((row == m) & (lane == i), pairing[m, i].astype(F32), value)
    for core, out in ((place[4], keep), (place[5], send)):
        out[:size, :] = queue[core]
        out[size:, :] = value.astype(BF16)


def rows_kernel(*refs):
    out, at = refs[-1], 0
    for ref in refs[:-1]:
        out[at : at + ref.shape[0], :] = ref[...]
        at += ref.shape[0]


def lanes_kernel(*refs):
    out, at = refs[-1], 0
    for ref in refs[:-1]:
        out[:, at : at + ref.shape[1]] = ref[...]
        at += ref.shape[1]


def rows_of(values, us=0.5):
    rows = sum(v.shape[0] for v in values)
    return call(rows_kernel, shape((rows, values[0].shape[1]), values[0].dtype), *values, us=us)


def split_sums(first, second, micro):
    width = first[0].shape[1]
    rows = [jnp.sum(v, axis=0, keepdims=True) for v in first]
    rows += [jnp.sum(v, axis=0, keepdims=True) for v in second]
    rows.append(jnp.zeros((8 - 2 * micro, width), F32))
    return jnp.concatenate(rows, axis=0)


def moments(sums, m, micro, count):
    mean = sums[m : m + 1] * (1.0 / count)
    square = sums[micro + m : micro + m + 1] * (1.0 / count)
    return mean, lax.rsqrt(square - mean * mean + NORM_EPS)


def per_micro(value, micro):
    rows = value.shape[0] // micro
    return [value[m * rows : (m + 1) * rows] for m in range(micro)]


def normalized(value, sums, micro, count):
    out = []
    for m, v in enumerate(per_micro(value, micro)):
        mean, rstd = moments(sums, m, micro, count)
        out.append(((v - mean) * rstd, rstd))
    return out


def join(parts):
    return jnp.concatenate(parts, axis=0)


def map_places(rows, images):
    row = lax.broadcasted_iota(jnp.int32, (rows, PART), 0).astype(F32)
    cell = jnp.floor((row + 0.5) * (1.0 / images))
    crop = jnp.floor((cell + 0.5) * (1.0 / PLACES))
    place = cell - crop * PLACES
    y = jnp.floor((place + 0.5) * (1.0 / SIDE))
    return y, place - y * SIDE


def tap_shift(value, images, tap, sign, y, x):
    rows = value.shape[0]
    down, right = sign * (tap // 3 - 1), sign * (tap % 3 - 1)
    offset = images * (SIDE * down + right)
    moved = value if offset == 0 else pltpu.roll(value, (-offset) % rows, 0)
    for step, at in ((down, y), (right, x)):
        if step < 0:
            moved = jnp.where(at > 0.5, moved, 0.0)
        elif step > 0:
            moved = jnp.where(at < SIDE - 1.5, moved, 0.0)
    return moved


def told_norm(message, at=0):
    rows = message[at : at + 16, :].astype(F32)
    return rows[0:1] + rows[1:2] + rows[2:3], rows[3:4] + rows[4:5] + rows[5:6]


def told_wide(message):
    parts = [told_norm(message, HALF_REDUCE + b * HALF_EXPAND) for b in range(4)]
    return tuple(jnp.concatenate(p, axis=1) for p in zip(*parts))


def terms(row):
    out = []
    for _ in range(3):
        term = row.astype(BF16).astype(F32)
        out.append(term)
        row = row - term
    return out


def tell_norm(norm, lane):
    out = []
    for r in range(2):
        out += terms(norm[r, :, lane : lane + PART])
    out.append(jnp.zeros((10, PART), F32))
    return jnp.concatenate(out, axis=0).astype(BF16)


def reduce_kernel(micro, place, image, w0, w1, pre, sums):
    half = D // 2
    first = pl.ds(pl.multiple_of(place[4] * half, half), half)
    second = pl.ds(pl.multiple_of(place[5] * half, half), half)
    value = dot(image[:, first], w0[16 : 16 + half, :]) + dot(image[:, second], w1[16 : 16 + half, :])
    pre[...] = value
    parts = per_micro(value, micro)
    sums[...] = split_sums(parts, [v * v for v in parts], micro)


def active_kernel(micro, count, pre, sums, told, active):
    gain, shift = told_norm(told)
    out = []
    for xhat, _ in normalized(pre[...], sums[...], micro, count):
        y = xhat * gain + shift
        out.append(y * sigmoid(y))
    active[...] = join(out).astype(BF16)


def fill(place, pieces, full):
    for k, piece in enumerate(pieces):
        full[:, pl.ds(pl.multiple_of(place[k] * PART, PART), PART)] = piece[: full.shape[0], :]


def quarter_of(place, j):
    return place[8] ^ (0, 2, 1, 3)[j]


def conv_kernel(micro, images, place, a0, a2, a3, a1, wa, wb, pre, sums, full, weight):
    fill(place, (a0, a1, a2, a3), full)
    quarter = WIDTH // 4
    for j in range(4):
        w = (wa, wb)[j // 2]
        at = pl.multiple_of(quarter_of(place, j) * quarter, quarter)
        for tap in range(9):
            lanes = slice(tap * PART, (tap + 1) * PART)
            first = (j % 2) * QUARTER_CONV + 16 + tap * quarter
            weight[pl.ds(at, quarter), lanes] = w[first : first + quarter, :]
    total = None
    y, x = map_places(full.shape[0], images)
    for first in range(0, 9, 2):
        taps = [tap for tap in (first, first + 1) if tap < 9]
        part = dot(full[...], weight[:, first * PART : (taps[-1] + 1) * PART])
        for j, tap in enumerate(taps):
            moved = tap_shift(part[:, j * PART : (j + 1) * PART], images, tap, 1, y, x)
            total = moved if total is None else total + moved
    pre[...] = total
    parts = per_micro(total, micro)
    sums[...] = split_sums(parts, [v * v for v in parts], micro)


def expand_kernel(micro, place, a0, a2, a3, a1, w0, w1, active, pre, sums, weight):
    fill(place, (a0, a1, a2, a3), active)
    half = WIDTH // 2
    for j, w in enumerate((w0, w1)):
        rows = pl.ds(pl.multiple_of(place[4 + j] * half, half), half)
        for b in range(4):
            at = HALF_REDUCE + b * HALF_EXPAND + 16
            weight[rows, b * PART : (b + 1) * PART] = w[at : at + half, :]
    value = dot(active[...], weight[...])
    pre[...] = value
    parts = per_micro(value, micro)
    sums[...] = split_sums(parts, [v * v for v in parts], micro)


def crop_rows(rows, images, transpose=False):
    shp = (rows // PLACES, rows)
    r = lax.broadcasted_iota(jnp.int32, shp, 1).astype(F32)
    q = lax.broadcasted_iota(jnp.int32, shp, 0).astype(F32)
    cell = jnp.floor((r + 0.5) * (1.0 / images))
    crop = jnp.floor((cell + 0.5) * (1.0 / PLACES))
    image = r - cell * images
    return (jnp.abs(crop * images + image - q) < 0.5).astype(F32).astype(BF16)


def pool_kernel(micro, images, count, place, pre, sums, told, image, pooled):
    lanes = pl.ds(pl.multiple_of(place[0] * WIDE, WIDE), WIDE)
    gain, shift = told_wide(told)
    out = []
    for xhat, _ in normalized(pre[...], sums[...], micro, count):
        out.append(xhat * gain + shift)
    z = join(out) + image[:, lanes].astype(F32)
    out = z * sigmoid(z)
    high = out.astype(BF16)
    low = (out - high.astype(F32)).astype(BF16)
    choose = crop_rows(pre.shape[0], images)
    pooled[...] = ((dot(choose, high) + dot(choose, low)) * (1.0 / PLACES)).astype(BF16)


def out_back_kernel(micro, images, count, place, pre, sums, told, image, own, r0, r1, r2, d_z, sums_out):
    lanes = pl.ds(pl.multiple_of(place[0] * WIDE, WIDE), WIDE)
    rows = pre.shape[0]
    gain, shift = told_wide(told)
    d_pooled = own[...].astype(F32)
    for k, came in enumerate((r0, r1, r2)):
        d_pooled = jnp.where(place[k + 1] == SECTIONS - 1, came[...].astype(F32), d_pooled)
    d_pooled = d_pooled.astype(BF16)
    spread = dot_tn(crop_rows(rows, images), d_pooled) * (1.0 / PLACES)
    xhats = [x for x, _ in normalized(pre[...], sums[...], micro, count)]
    z = join([x * gain + shift for x in xhats]) + image[:, lanes].astype(F32)
    value = spread * slope(z)
    d_z[...] = value
    parts = per_micro(value, micro)
    sums_out[...] = split_sums([v * x for v, x in zip(parts, xhats)], parts, micro)


def norm_back(value, pre, sums, back, gain, micro, count):
    out = []
    parts = per_micro(value, micro)
    for m, (xhat, rstd) in enumerate(normalized(pre, sums, micro, count)):
        by_x = back[m : m + 1] * (1.0 / count)
        plain = back[micro + m : micro + m + 1] * (1.0 / count)
        out.append(gain * rstd * (parts[m] - plain - xhat * by_x))
    return join(out)


def norm_back_kernel(micro, count, d_y, pre, sums, back, told, d_pre):
    gain, _ = told_norm(told)
    d_pre[...] = norm_back(d_y[...], pre[...], sums[...], back[...], gain, micro, count).astype(BF16)


def over_micro(back, micro):
    out = []
    for r in range(2):
        row = back[r * micro : r * micro + 1, :]
        for m in range(1, micro):
            row = row + back[r * micro + m : r * micro + m + 1, :]
        out.append(row)
    return out


def last_norm_back_kernel(micro, count, place, d_y, pre, sums, back, told, back2, back1, notes, d_pre):
    gain, _ = told_norm(told)
    rows = d_y.shape[0]
    d_pre[:rows, :] = norm_back(d_y[...], pre[...], sums[...], back[...], gain, micro, count).astype(BF16)
    said = []
    for row in over_micro(back2, micro):
        said += [row[:, b * PART : (b + 1) * PART] for b in range(4)]
    said += over_micro(back1, micro) + over_micro(back, micro)
    said.append(jnp.where(place[0] == SECTIONS - 1, notes[3:4, :PART], 0.0))
    said = sum([terms(row) for row in said], [])
    said.append(jnp.zeros((NOTE_ROWS - len(said), PART), F32))
    d_pre[rows:, :] = jnp.concatenate(said, axis=0).astype(BF16)


def expand_back_kernel(micro, count, place, pre, sums, d_z, back, told, weight, d_pre, q0, q1, q2, q3, full):
    gain, _ = told_wide(told)
    d_low = norm_back(d_z[...], pre[...], sums[...], back[...], gain, micro, count).astype(BF16)
    d_pre[...] = d_low
    full[...] = dot_nt(d_low, weight[...])
    for k, q in enumerate((q0, q1, q2, q3)):
        lanes = pl.ds(pl.multiple_of(place[k] * PART, PART), PART)
        q[...] = full[:, lanes].astype(BF16)


def finish_silu(micro, count, d_active, pre, sums, norm, d_y, sums_out):
    gain, shift = norm
    values, products = [], []
    parts = per_micro(d_active, micro)
    for m, (xhat, _) in enumerate(normalized(pre[...], sums[...], micro, count)):
        value = parts[m] * slope(xhat * gain + shift)
        values.append(value)
        products.append(value * xhat)
    d_y[...] = join(values)
    sums_out[...] = split_sums(products, values, micro)


def silu_back_kernel(micro, count, q0, q1, q2, q3, pre, sums, told, d_y, sums_out):
    total = (q0[...].astype(F32) + q1[...].astype(F32)) + (q2[...].astype(F32) + q3[...].astype(F32))
    d_active = total.astype(BF16).astype(F32)
    finish_silu(micro, count, d_active, pre, sums, told_norm(told), d_y, sums_out)


def conv_back_kernel(
    micro, images, count, place, d0, d2, d3, d1, back0, back1, pre, sums, told, d_full, d_y, sums_out, weight
):
    fill(place, (d0, d1, d2, d3), d_full)
    d_low = d_full[...]
    half = PART // 2
    for j, back in enumerate((back0, back1)):
        for k in range(SECTIONS):
            lanes = pl.ds(pl.multiple_of(place[k] * PART, PART), PART)
            for tap in range(9):
                rows = pl.ds(pl.multiple_of(tap * PART + place[4 + j] * half, half), half)
                weight[rows, lanes] = back[k, tap * half : (tap + 1) * half, :]
    total = None
    y, x = map_places(d_low.shape[0], images)
    for first in range(0, 9, 2):
        taps = [tap for tap in (first, first + 1) if tap < 9]
        part = dot_nt(d_low, weight[first * PART : (taps[-1] + 1) * PART, :])
        for j, tap in enumerate(taps):
            moved = tap_shift(part[:, j * PART : (j + 1) * PART], images, tap, -1, y, x)
            total = moved if total is None else total + moved
    d_active = total.astype(BF16).astype(F32)
    finish_silu(micro, count, d_active, pre, sums, told_norm(told), d_y, sums_out)


def reduce_back_kernel(place, d_full, back0, back1, d_z, grad_in, weight):
    half = WIDE // 2
    first = 9 * PART // 2
    for j, back in enumerate((back0, back1)):
        rows = pl.ds(pl.multiple_of(place[4 + j] * half, half), half)
        for k in range(SECTIONS):
            lanes = pl.ds(pl.multiple_of(place[k] * PART, PART), PART)
            weight[rows, lanes] = back[k, first : first + half, :]
    main = dot_nt(d_full[...], weight[...]).astype(BF16).astype(F32)
    value = main + d_z[...].astype(BF16).astype(F32)
    grad_in[...] = value.reshape(grad_in.shape)


def back_parts_kernel(place, conv_a, conv_b, reduce0, reduce1, *outs):
    half = PART // 2
    wide = WIDE // 2
    first = 9 * half
    quarter = WIDTH // 4
    for k, out in enumerate(outs):
        for core in range(2):
            for j in range(4):
                conv = (conv_a, conv_b)[j // 2]

                @pl.when((place[k] == quarter_of(place, j)) & (place[4] == core))
                def _():
                    for tap in range(9):
                        at = (j % 2) * QUARTER_CONV + 16 + tap * quarter + core * half
                        out[tap * half : (tap + 1) * half, :] = conv[at : at + half, :]

            for u in range(SECTIONS):
                reduce = (reduce0, reduce1)[core ^ (u // 2)]

                @pl.when((place[k] == u) & (place[4] == core))
                def _():
                    at = 16 + (u % 2) * WIDE + core * wide
                    out[first : first + wide, :] = reduce[at : at + wide, :]


def stack_kernel(*refs):
    out = refs[-1]
    rows = refs[0].shape[0]
    for j, ref in enumerate(refs[:-1]):
        if len(out.shape) == 3:
            out[j] = ref[...]
        else:
            out[j * rows : (j + 1) * rows, :] = ref[...]


def mixed_kernel(place, own, r1, r2, r3, conv, expand, reduce, *outs):
    value = (own[...] + r1[...].astype(F32)) + (r2[...].astype(F32) + r3[...].astype(F32))
    reduce[...] = value.astype(BF16)
    for k, out in enumerate(outs):
        target = place[k + 1]

        @pl.when(target == 0)
        def _():
            out[:, :WIDE] = reduce[...]

        @pl.when(target == 1)
        def _():
            out[...] = conv[...]

        @pl.when(target == 2)
        def _():
            out[:, :WIDE] = expand[...]


def told_kernel(place, n0, n1, n2, n3, notes, out, loss):
    t = place[0]
    out[...] = jnp.zeros_like(out)

    @pl.when(t == SECTIONS - 1)
    def _():
        for r in range(3):
            out[r] = notes[r : r + 1, :]

    total = None
    for k, note in enumerate((n0, n1, n2, n3)):
        u = place[k]
        rows = note[note.shape[0] - NOTE_ROWS :, :].astype(F32)

        def said(i):
            return (rows[3 * i : 3 * i + 1] + rows[3 * i + 1 : 3 * i + 2]) + rows[3 * i + 2 : 3 * i + 3]

        total = said(12) if total is None else total + said(12)

        @pl.when(t == 2)
        def _():
            for r in range(2):
                for b in range(4):
                    lanes = pl.ds(pl.multiple_of(u * WIDE + b * PART, PART), PART)
                    out[r, :, lanes] = said(4 * r + b)

        for section in range(2):

            @pl.when(t == section)
            def _():
                for r in range(2):
                    lanes = pl.ds(pl.multiple_of(u * PART, PART), PART)
                    out[r, :, lanes] = said((10, 8)[section] + r)

    loss[...] = jnp.broadcast_to(total, loss.shape)


def pick_kernel(place, p0, p1, p2, p3, conv, pair):
    for j, p in enumerate((p0, p1, p2, p3)):

        @pl.when(place[0] == j)
        def _():
            pair[:HALF_REDUCE, :] = p[:HALF_REDUCE, :]

        @pl.when(place[1] == j)
        def _():
            conv[...] = p[...]

        @pl.when(place[2] == j)
        def _():
            pair[HALF_REDUCE:, :] = p[: 4 * HALF_EXPAND, :]


def taps_kernel(images, active, out):
    value = active[...].astype(F32)
    y, x = map_places(value.shape[0], images)
    for tap in range(9):
        out[:, tap * PART : (tap + 1) * PART] = tap_shift(value, images, tap, 1, y, x).astype(BF16)


def head(pooled, w_head, w_proj, protos, norm, queue, match, micro, images, dp):
    rows = pooled.shape[0]
    group = rows // micro
    half = group // CROPS
    scale_all = 1.0 / (TEMPER * CROPS * half * micro)
    pre = dot(pooled, w_head)

    def by_micro(v):
        return v.reshape(micro, group, v.shape[-1])

    pre_m = by_micro(pre)
    mean = jnp.mean(pre_m, axis=1, keepdims=True)
    square = jnp.mean(pre_m * pre_m, axis=1, keepdims=True)
    rstd = lax.rsqrt(square - mean * mean + NORM_EPS)
    xhat = (pre_m - mean) * rstd
    y = xhat * norm[0] + norm[1]
    active = (y * sigmoid(y)).astype(BF16).reshape(rows, D)
    embed = dot(active, w_proj) + norm[2, :PROJ]
    recip = lax.rsqrt(jnp.sum(embed * embed, axis=1, keepdims=True) + UNIT_EPS)
    unit = (embed * recip).astype(BF16)
    scores = dot_nt(unit, protos)
    valid = lax.broadcasted_iota(jnp.int32, (1, 4, QUARTER_PAD), 2).reshape(1, 4 * QUARTER_PAD) < QUARTER
    own_mass = jnp.where(valid, jnp.exp(scores / SINK_EPS), 0.0).reshape(micro, CROPS, half, -1)
    queue_mass = jnp.where(valid, jnp.exp(jnp.einsum("cqp,kp->cqk", queue, protos, preferred_element_type=F32) / SINK_EPS), 0.0)
    codes = []
    for m in range(micro):
        for c in range(CROPS):
            a, b = queue_mass[c], own_mass[m, c]
            column = jnp.sum(a, axis=0, keepdims=True) + jnp.sum(b, axis=0, keepdims=True)
            once = jnp.where(valid, 1.0 / column, 0.0)
            a, b = a * once, b * once
            scale = valid.astype(F32)
            for turn in range(2):
                ra = 1.0 / jnp.sum(a * scale, axis=1, keepdims=True)
                rb = 1.0 / jnp.sum(b * scale, axis=1, keepdims=True)
                column = jnp.sum(a * ra, axis=0, keepdims=True) + jnp.sum(b * rb, axis=0, keepdims=True)
                scale = jnp.where(valid, 1.0 / column, 0.0)
            b = b * scale
            codes.append(b / jnp.sum(b, axis=1, keepdims=True))
    targets = []
    for m in range(micro):
        targets.append(jnp.dot(match[m], codes[m * CROPS + 1], precision=HIGH))
        targets.append(jnp.dot(match[m].T, codes[m * CROPS], precision=HIGH))
    target = jnp.concatenate(targets)
    logits = jnp.where(valid, scores / TEMPER, -1e30)
    logp = jax.nn.log_softmax(logits, axis=1)
    loss = -jnp.sum(jnp.where(valid, target * logp, 0.0)) * (TEMPER * scale_all)
    d_scores = ((jnp.exp(logp) * jnp.sum(target, axis=1, keepdims=True) - target) * scale_all).astype(BF16)
    d_unit = dot(d_scores, protos)
    d_embed = (
        recip * d_unit - embed * (recip * recip * recip) * jnp.sum(d_unit * embed, axis=1, keepdims=True)
    ).astype(BF16)
    d_active = dot_nt(d_embed, w_proj)
    d_y = by_micro(d_active) * slope(y)
    by_x = jnp.sum(d_y * xhat, axis=1, keepdims=True)
    plain = jnp.sum(d_y, axis=1, keepdims=True)
    d_pre = (norm[0] * rstd * (d_y - plain / group - xhat * by_x / group)).astype(BF16).reshape(rows, D)
    bias = jnp.pad(jnp.sum(d_embed.astype(F32), axis=0), (0, D - PROJ))
    grads = jnp.stack([jnp.sum(by_x, axis=(0, 1)), jnp.sum(plain, axis=(0, 1)), bias])
    return loss, grads, active, unit, d_scores, d_embed, d_pre


def valid_lanes():
    lane = lax.broadcasted_iota(jnp.int32, (1, 4 * QUARTER_PAD), 1).astype(F32)
    block = jnp.floor((lane + 0.5) * (1.0 / QUARTER_PAD))
    return lane - block * QUARTER_PAD < QUARTER - 0.5


def lanes_at(b, size):
    return pl.ds(pl.multiple_of(b * size, size), size)


def lanes_at(b, size):
    return pl.ds(pl.multiple_of(b * size, size), size)


def mass_kernel(micro, images, told_offsets, place, table, *refs):
    mass, column, match, rows_s, exps = refs[-5:]
    ndp = len(told_offsets)
    valid = valid_lanes()
    size = mass.shape[0] // ndp
    half = images * ndp
    at, said = 0, jnp.zeros((16, half), F32)
    row = lax.broadcasted_iota(jnp.int32, (PROJ, half), 0)
    lane = lax.broadcasted_iota(jnp.int32, (PROJ, half), 1)
    for ref in refs[:-5]:
        rows = size + 16
        for j in range(ref.shape[0] // rows):
            rows_s[lanes_at(place[7] ^ told_offsets[at], size), :] = ref[j * rows : j * rows + size, :]
            pairs = ref[(j + 1) * rows - 16 : (j + 1) * rows, :]
            spot_at = (place[7] ^ told_offsets[at]) * images
            spot = ((row < images) & (lane == row + spot_at)).astype(F32).astype(BF16)
            said = said + dot(pairs, spot)
            at += 1
    step = 128
    steps = mass.shape[0] // step

    def scored(i, sums):
        own = rows_s[lanes_at(i, step), :]
        out = []
        for a in range(4):
            lanes = slice(a * QUARTER_PAD, (a + 1) * QUARTER_PAD)
            value = jnp.exp(dot_nt(own, table[:, a * PROJ : (a + 1) * PROJ]) * (1.0 / SINK_EPS))
            value = jnp.where(valid[:, lanes], value, 0.0)
            exps[lanes_at(i, step), lanes] = value
            out.append(jnp.sum(value, axis=0, keepdims=True))
        return sums + jnp.concatenate(out, axis=1)

    sums = lax.fori_loop(0, steps, scored, jnp.zeros((1, 4 * QUARTER_PAD), F32))
    column[...] = jnp.broadcast_to(sums, column.shape)
    factor = jnp.where(valid & (sums > 1.18e-38), 1.0 / sums, 0.0)

    def divide(i, carry):
        mass[lanes_at(i, step), :] = (exps[lanes_at(i, step), :] * factor).astype(BF16)
        return carry

    lax.fori_loop(0, steps, divide, 0)

    def over(value, by):
        return jnp.floor((value + 0.5) * (1.0 / by))

    row = lax.broadcasted_iota(jnp.int32, (half, half), 0).astype(F32)
    lane = lax.broadcasted_iota(jnp.int32, (half, half), 1).astype(F32)
    block = over(row, images)
    for m in range(micro):
        same = (jnp.abs(block - over(lane, images)) < 0.5) & (jnp.abs(row - block * images - said[m : m + 1, :]) < 0.5)
        there = same.astype(F32)
        match[m] = jnp.where(place[4] == 0, there, there.T).astype(BF16)


def tables_kernel(packed, proj, table, rows, buffer, sem):
    size = THIRD - FIRST + 2
    copy = pltpu.make_async_copy(packed.at[pl.ds(FIRST, size), :], rows, sem)
    copy.start()
    copy.wait()
    wide = SECOND - FIRST
    for a in range(4):
        buffer[pl.ds(a, wide, stride=4), :] = rows[:wide, a * PROJ : (a + 1) * PROJ].astype(F32)
    proj[...] = buffer[...].astype(BF16)
    row = lax.broadcasted_iota(jnp.int32, (size - wide, WIDTH), 0)
    kept = jnp.where(row < QUARTER, rows[wide:, :].astype(F32), 0.0).astype(BF16)
    table[: size - wide, :] = kept
    table[size - wide :, :] = jnp.zeros((QUARTER_PAD - (size - wide), WIDTH), BF16)


def exact_dot(choose, value):
    parts, left = [], value
    for _ in range(3):
        term = left.astype(BF16)
        left = left - term.astype(F32)
        parts.append(term)
    return dot(jnp.concatenate([choose] * 3, axis=1), jnp.concatenate(parts, axis=0))


def by_micro_rows(value, ndp, micro):
    return value.reshape(ndp, micro, value.shape[0] // (ndp * micro), value.shape[1])


def total_of(value):
    return jnp.sum(jnp.sum(value, axis=0), axis=0, keepdims=True)


def regroup(rows, own, images, to_groups):
    ndp = rows // own
    row = lax.broadcasted_iota(jnp.int32, (rows, rows), 0).astype(F32)
    lane = lax.broadcasted_iota(jnp.int32, (rows, rows), 1).astype(F32)
    source, target = (lane, row) if to_groups else (row, lane)
    block = jnp.floor((source + 0.5) * (1.0 / own))
    inner = source - block * own
    part = jnp.floor((inner + 0.5) * (1.0 / images))
    moved = (part * ndp + block) * images + inner - part * images
    return (jnp.abs(moved - target) < 0.5).astype(F32).astype(BF16)


def head_kernel(
    micro, images, offsets, place, pooled_a, pooled_b, w_head, w_proj, table, norm, mass, column, match,
    pooled, active, unit, d_scores, embed, xhat_s, y_s, rstd_s, said,
    scores, own_mass, total, factor,
):
    ndp = len(offsets)
    rows = pooled.shape[0]
    group = rows // micro
    half = group // CROPS
    own = rows // ndp
    queued = mass.shape[0]
    scale_all = 1.0 / (TEMPER * CROPS * half * micro)
    chunk = WIDTH
    chunks = D // chunk
    core = place[4]
    for j, offset in enumerate(offsets):
        source = (pooled_a, pooled_b)[j * own // pooled_a.shape[0]]
        at = j * own % pooled_a.shape[0]
        pooled[lanes_at(place[7] ^ offset, own), :] = source[at : at + own, :]
    low = pooled[...]

    def forward(b, carry):
        lanes = lanes_at(b, chunk)
        pre = by_micro_rows(dot(low, w_head[:, lanes]), ndp, micro)
        gain, shift = norm[0, :, lanes], norm[1, :, lanes]
        xhats, ys = [], []
        for m in range(micro):
            v = pre[:, m]
            mean = total_of(v) * (1.0 / group)
            square = total_of(v * v) * (1.0 / group)
            rstd = lax.rsqrt(square - mean * mean + NORM_EPS)
            xhat = (v - mean) * rstd
            rstd_s[m : m + 1, lanes] = rstd
            xhats.append(xhat)
            ys.append(xhat * gain + shift)
        xhat_s[:, lanes] = jnp.stack(xhats, axis=1).reshape(rows, chunk)
        y = jnp.stack(ys, axis=1).reshape(rows, chunk)
        y_s[:, lanes] = y
        active[:, lanes] = (y * sigmoid(y)).astype(BF16)
        return carry

    lax.fori_loop(0, chunks, forward, 0)
    value = dot(active[...], w_proj[...]) + norm[2, :, :PROJ]
    embed[...] = value
    recip = lax.rsqrt(jnp.sum(value * value, axis=1, keepdims=True) + UNIT_EPS)
    unit_v = dot(regroup(rows, own, images, True), (value * recip).astype(BF16)).astype(BF16)
    unit[...] = unit_v
    valid = valid_lanes()
    for a in range(4):
        lanes = slice(a * QUARTER_PAD, (a + 1) * QUARTER_PAD)
        scores[:, lanes] = dot_nt(unit_v, table[:, a * PROJ : (a + 1) * PROJ])

    step = 128

    def divided(a):
        return a * (1.0 / jnp.sum(a, axis=1, keepdims=True))

    def folded(a):
        return jnp.sum(a.reshape(a.shape[0] // 8, 8, a.shape[1]), axis=0)

    def own_rows(m):
        return slice(m * half, (m + 1) * half)

    queue_sum = column[0:1, :]
    for m in range(micro):
        a = scores[lanes_at(m * CROPS + core, half), :]
        a = jnp.where(valid, jnp.exp(a * (1.0 / SINK_EPS)), 0.0)
        inverse = jnp.where(valid, 1.0 / (queue_sum + jnp.sum(a, axis=0, keepdims=True)), 0.0)
        factor[m : m + 1, :] = queue_sum * inverse
        factor[micro + m : micro + m + 1, :] = jnp.ones_like(inverse)
        own_mass[own_rows(m), :] = a * inverse

    def turn(i, carry):
        def block(i, carry):
            at = lanes_at(i, step)
            e_of = [mass[at, b * PART : (b + 1) * PART].astype(F32) for b in range(4 * QUARTER_PAD // PART)]
            rows_by = []
            for m in range(micro):
                sums = None
                for b, e in enumerate(e_of):
                    more = e * factor[m : m + 1, b * PART : (b + 1) * PART]
                    sums = more if sums is None else sums + more
                rows_by.append(1.0 / jnp.sum(sums, axis=1, keepdims=True))
            for b in range(4 * QUARTER_PAD // PART):
                lanes = slice(b * PART, (b + 1) * PART)
                e = mass[at, lanes].astype(F32)
                for m in range(micro):
                    total[m, :, lanes] += folded(e * rows_by[m])
            return carry

        total[...] = jnp.zeros_like(total)
        lax.fori_loop(0, queued // step, block, 0)
        for m in range(micro):
            scale = factor[micro + m : micro + m + 1, :]
            a = divided(own_mass[own_rows(m), :] * scale)
            sums = jnp.sum(total[m], axis=0, keepdims=True) * factor[m : m + 1, :]
            more = jnp.where(valid, 1.0 / (sums + jnp.sum(a, axis=0, keepdims=True)), 0.0)
            factor[m : m + 1, :] = factor[m : m + 1, :] * more
            factor[micro + m : micro + m + 1, :] = scale * more
        return carry

    lax.fori_loop(0, 2, turn, 0)

    def losses(m, loss):
        mine, there = lanes_at(m, half), lanes_at(m * CROPS + 1 - core, half)
        codes = divided(own_mass[mine, :] * factor[pl.ds(micro + m, 1), :])
        goal = exact_dot(match[m], codes)
        logits = jnp.where(valid, scores[there, :] * (1.0 / TEMPER), -1e30)
        logits = logits - jnp.max(logits, axis=1, keepdims=True)
        power = jnp.exp(logits)
        summed = jnp.sum(power, axis=1, keepdims=True)
        weight = jnp.sum(goal, axis=1, keepdims=True) / summed
        d_low = ((power * weight - goal) * scale_all).astype(BF16)
        d_scores[mine, :] = d_low
        d_unit = None
        for a in range(4):
            more = dot(d_low[:, a * QUARTER_PAD : (a + 1) * QUARTER_PAD], table[:, a * PROJ : (a + 1) * PROJ])
            d_unit = more if d_unit is None else d_unit + more
        said[mine, :] = d_unit
        return loss + jnp.sum(goal * (logits - jnp.log(summed)), axis=1, keepdims=True)

    loss = lax.fori_loop(0, micro, losses, jnp.zeros((half, 1), F32))
    loss = jnp.sum(loss, axis=0, keepdims=True) * (-TEMPER * scale_all)
    said[micro * half :, :] = jnp.broadcast_to(loss, (8, PROJ))


def head_back_kernel(
    micro, images, ndp, place, here, there, embed, w_proj, w_head, norm, xhat_s, y_s, rstd_s,
    d0, d1, d2, d3, notes, d_embed, d_pre, d_unit, d_own,
):
    rows = embed.shape[0]
    group = rows // micro
    half = group // CROPS
    own = rows // ndp
    chunk = WIDTH
    chunks = D // chunk
    for m in range(micro):
        d_unit[lanes_at(m * CROPS + place[5], half), :] = here[m * half : (m + 1) * half, :]
        d_unit[lanes_at(m * CROPS + place[4], half), :] = there[m * half : (m + 1) * half, :]
    value = embed[...]
    recip = lax.rsqrt(jnp.sum(value * value, axis=1, keepdims=True) + UNIT_EPS)
    d_back = exact_dot(regroup(rows, own, images, False), d_unit[...])
    along = jnp.sum(d_back * value, axis=1, keepdims=True)
    d_low = (recip * d_back - value * (recip * recip * recip) * along).astype(BF16)
    d_embed[...] = d_low
    notes[...] = jnp.zeros_like(notes)
    notes[2:3, :PROJ] = jnp.sum(d_low.astype(F32), axis=0, keepdims=True)
    loss = here[micro * half : micro * half + 1, :] + there[micro * half : micro * half + 1, :]
    notes[3:4, :PROJ] = loss

    def backward(b, carry):
        lanes = lanes_at(b, chunk)
        d_y = by_micro_rows(dot_nt(d_low, w_proj[lanes, :]) * slope(y_s[:, lanes]), ndp, micro)
        xhat = by_micro_rows(xhat_s[:, lanes], ndp, micro)
        gain = norm[0, :, lanes]
        values, by_xs, plains = [], None, None
        for m in range(micro):
            by_x = total_of(d_y[:, m] * xhat[:, m])
            plain = total_of(d_y[:, m])
            by_xs = by_x if by_xs is None else by_xs + by_x
            plains = plain if plains is None else plains + plain
            value = d_y[:, m] - plain * (1.0 / group) - xhat[:, m] * (by_x * (1.0 / group))
            values.append(gain * rstd_s[m : m + 1, lanes] * value)
        notes[0:1, lanes] = by_xs
        notes[1:2, lanes] = plains
        d_pre[:, lanes] = jnp.stack(values, axis=1).reshape(rows, chunk).astype(BF16)
        return carry

    lax.fori_loop(0, chunks, backward, 0)
    mine = d_pre[lanes_at(place[7], own), :]

    def to_pooled(b, carry):
        d_own[:, lanes_at(b, chunk)] = dot_nt(mine, w_head[lanes_at(b, chunk), :]).astype(BF16)
        return carry

    lax.fori_loop(0, chunks, to_pooled, 0)
    for j, out in enumerate((d0, d1, d2, d3)):
        out[...] = d_own[:, j * WIDE : (j + 1) * WIDE]


def interleave(width):
    row = lax.broadcasted_iota(jnp.int32, (4 * width, 4 * width), 0)
    column = lax.broadcasted_iota(jnp.int32, (4 * width, 4 * width), 1)
    return (column == 4 * (row & (width - 1)) + (row >> (width.bit_length() - 1))).astype(F32).astype(BF16)


def own_columns(place, own):
    row = lax.broadcasted_iota(jnp.int32, (WIDTH, own), 0)
    lane = lax.broadcasted_iota(jnp.int32, (WIDTH, own), 1)
    return (row == lane + place[7] * own).astype(F32).astype(BF16)


def tail_grads_kernel(place, active, unit, d_here, d_there, d_embed, out):
    @pl.when(place[0] == SECTIONS - 1)
    def _():
        own = out.shape[0]
        choose = own_columns(place, own)
        rows = active.shape[0]
        wide = jnp.concatenate([active[:, b * WIDTH : (b + 1) * WIDTH] for b in range(4)], axis=0)
        wide = dot_nt(wide, interleave(PART)).astype(BF16)
        half = d_here.shape[0] // 2
        units = []
        for core in (place[5], place[4]):
            units.append(jnp.concatenate([unit[lanes_at(m * CROPS + core, half), :] for m in range(2)], axis=0))
        proj = jnp.zeros((own, WIDTH), F32)
        proto = jnp.zeros((own, QUARTER_PAD), F32)
        for a in range(4):
            some = choose[a * PROJ : (a + 1) * PROJ, :]
            own_e = dot(d_embed[...], some).astype(BF16)
            column = [wide[b * rows : (b + 1) * rows, a * PART : (a + 1) * PART] for b in range(4)]
            proj = proj + dot_tn(own_e, jnp.concatenate(column, axis=1))
            for own_unit, d_scores in zip(units, (d_here, d_there)):
                own_u = dot(own_unit, some).astype(BF16)
                proto = proto + dot_tn(own_u, d_scores[:, a * QUARTER_PAD : (a + 1) * QUARTER_PAD])
        out[:, :WIDTH] = proj
        out[:, WIDTH:] = proto


def head_grads_kernel(place, pooled, d_pre, tail, out, parts):
    @pl.when(place[0] != SECTIONS - 1)
    def _():
        out[...] = jnp.zeros_like(out)

    @pl.when(place[0] == SECTIONS - 1)
    def _():
        own = out.shape[0]
        choose = own_columns(place, own)
        weave = interleave(PART)
        own_d = [dot(d_pre[:, q * WIDTH : (q + 1) * WIDTH], choose).astype(BF16) for q in range(4)]
        own_d = jnp.concatenate(own_d, axis=1)

        def product(b, carry):
            parts[:, lanes_at(b, WIDTH)] = dot_tn(own_d, pooled[:, lanes_at(b, WIDTH)]).astype(BF16)
            return carry

        lax.fori_loop(0, 4, product, 0)

        def mix(b, carry):
            mixed = []
            for j in range(4):
                lanes = pl.ds(pl.multiple_of(b * WIDTH + j * PART, PART), PART)
                four = [parts[q * own : (q + 1) * own, lanes] for q in range(4)]
                mixed.append(jnp.concatenate(four, axis=1))
            mixed = dot(jnp.concatenate(mixed, axis=0), weave)
            for j in range(4):
                lanes = pl.ds(pl.multiple_of((4 * b + j) * WIDTH, WIDTH), WIDTH)
                out[:, lanes] = mixed[j * own : (j + 1) * own, :]
            return carry

        lax.fori_loop(0, 4, mix, 0)
        out[:, FIRST:] = tail[:, : out.shape[1] - FIRST]


def finish_kernel(place, base, reduce, conv, expand, m1, m2, m3, out, buffer, sem):
    mixed = (None, m1, m2, m3)
    t = place[0]

    def write(first, lanes):
        part = pl.ds(first, lanes)
        copy = pltpu.make_async_copy(buffer.at[:, part], out.at[:, part], sem.at[first // WIDE])
        copy.start()
        return copy

    @pl.when(t == 0)
    def _():
        copies = []
        for u in range(SECTIONS):
            piece = reduce if u == 0 else mixed[u]
            buffer[:, u * WIDE : (u + 1) * WIDE] = piece[:, :WIDE].astype(F32)
            copies.append(write(u * WIDE, WIDE))
        for copy in copies:
            copy.wait()

    @pl.when(t == 1)
    def _():
        for u in range(SECTIONS):
            piece = conv if u == 1 else mixed[u ^ 1]
            for tap in range(9):
                at = tap * WIDTH + u * PART
                buffer[:, at : at + PART] = piece[:, tap * PART : (tap + 1) * PART].astype(F32)
        write(0, 9 * WIDTH).wait()

    @pl.when(t == 2)
    def _():
        four = [expand if u == 2 else mixed[u ^ 2] for u in range(SECTIONS)]
        weave = interleave(PART)
        for b in range(WIDTH // PART):
            lanes = slice(b * PART, (b + 1) * PART)
            row = jnp.concatenate([f[:, lanes] for f in four], axis=1)
            buffer[:, 4 * b * PART : 4 * (b + 1) * PART] = dot(row, weave)
        write(0, D).wait()


def unpack_kernel(packed, out, buffer):
    rows = packed.shape[0]
    for b in range(4):
        buffer[b] = packed[:, b * PART : (b + 1) * PART].astype(F32)
    for q in range(4):
        for b in range(4):
            at = q * WIDTH + b * PART
            out[:, at : at + PART] = buffer[b, pl.ds(q, rows // 4, stride=4), :].astype(BF16)


def unpack(packed, rows):
    step = 1024
    return pl.pallas_call(
        unpack_kernel,
        name="unpack",
        out_shape=shape((rows // 4, 4 * WIDTH), BF16),
        grid=(rows // step,),
        in_specs=[pl.BlockSpec((step, WIDTH), lambda i: (i, 0))],
        out_specs=pl.BlockSpec((step // 4, 4 * WIDTH), lambda i: (i, 0)),
        scratch_shapes=[pltpu.VMEM((4, step, PART), F32)],
        compiler_params=pltpu.CompilerParams(vmem_limit_bytes=16 * 2**20),
        cost_estimate=cost(4),
    )(packed)


def pack_kernel(place, packed, norm, o0, o1, o2, o3, rows, buffer, sem):
    outs = (o0, o1, o2, o3)
    t, core = place[0], place[4]

    def run(copies):
        for copy in copies:
            copy.start()
        return copies

    def lanes_of(target, lanes):
        return pl.ds(target * lanes, lanes)

    @pl.when(t == 0)
    def _():
        half = D // 2
        copies = []
        for k, out in enumerate(outs):
            source = packed.at[pl.ds(pl.multiple_of(core * half, half), half), lanes_of(k, PART)]
            copies.append(pltpu.make_async_copy(source, out.at[pl.ds(16, half), :], sem.at[k]))
        run(copies)
        for k, out in enumerate(outs):
            out[:16, :] = tell_norm(norm, k * PART)
        for copy in copies:
            copy.wait()

    @pl.when(t == 1)
    def _():
        quarter = WIDTH // 4
        copies = []
        for k, out in enumerate(outs):
            for tap in range(9):
                at = pl.multiple_of(tap * WIDTH + place[8] * quarter, quarter)
                source = packed.at[pl.ds(at, quarter), lanes_of(1 ^ k, PART)]
                target = out.at[pl.ds(16 + tap * quarter, quarter), :]
                copies.append(pltpu.make_async_copy(source, target, sem.at[9 * k + tap]))
        run(copies)
        for k, out in enumerate(outs):
            out[:16, :] = tell_norm(norm, (1 ^ k) * PART)
        for copy in copies:
            copy.wait()

    @pl.when(t == 2)
    def _():
        size = rows.shape[0]
        copy = pltpu.make_async_copy(packed.at[pl.ds(pl.multiple_of(core * size, size), size), :], rows, sem.at[0])
        copy.start()
        copy.wait()
        for b in range(4):
            buffer[b] = rows[:, b * PART : (b + 1) * PART].astype(F32)
        for k, out in enumerate(outs):
            u = 2 ^ k
            for b in range(4):
                at = b * HALF_EXPAND
                lane = u * WIDE + b * PART
                out[at : at + 16, :] = tell_norm(norm, lane)
                out[at + 16 : at + HALF_EXPAND, :] = buffer[b, pl.ds(u, size // 4, stride=4), :].astype(BF16)


def pack(place, packed, norm):
    rows = 4 * (WIDTH // 2)
    return pl.pallas_call(
        pack_kernel,
        name="pack",
        out_shape=[shape((QUARTER_CONV, PART), BF16)] * 4,
        in_specs=[
            pl.BlockSpec(memory_space=pltpu.SMEM),
            pl.BlockSpec(memory_space=pltpu.HBM),
            pl.BlockSpec(memory_space=pltpu.VMEM),
        ],
        out_specs=[pl.BlockSpec(memory_space=pltpu.VMEM)] * 4,
        scratch_shapes=[
            pltpu.VMEM((rows, WIDTH), BF16), pltpu.VMEM((4, rows, PART), F32), pltpu.SemaphoreType.DMA((36,)),
        ],
        compiler_params=pltpu.CompilerParams(vmem_limit_bytes=12 * 2**20),
        cost_estimate=cost(2),
    )(place, hbm(packed), norm)


def multiple(value, step):
    return value if isinstance(value, int) else pl.multiple_of(value, step)


def pair_kernel(place, a, b, keep, out):
    full = dot_tn(a[...], b[...])
    own = keep.shape[1]
    first = place[4] == 0
    for z in range(keep.shape[0]):
        one = full[2 * z * own : (2 * z + 1) * own]
        two = full[(2 * z + 1) * own : (2 * z + 2) * own]
        keep[z] = jnp.where(first, one, two)
        out[z] = jnp.where(first, two, one).astype(BF16)


def image_pair_kernel(place, d0, d2, d3, d1, image, keep, out, d_full):
    fill(place, (d0, d1, d2, d3), d_full)
    lanes = pl.ds(pl.multiple_of(place[0] * WIDE, WIDE), WIDE)
    pair_kernel(place, d_full, image.at[:, lanes], keep, out)


def cross_kernel(place, keep, came, own, o1, o2, o3):
    for k, o in enumerate((own, o1, o2, o3)):
        z = place[6] ^ k
        o[...] = (keep[z] + came[z].astype(F32)).astype(o.dtype)


def far_kernel(place, keep, came, kept, out):
    for j in range(2):
        mine, other = place[6] ^ j, place[6] ^ (2 + j)
        kept[j] = keep[mine] + came[mine].astype(F32)
        out[j] = (keep[other] + came[other].astype(F32)).astype(BF16)


def near_kernel(keep, came, kept, out):
    kept[...] = keep[0] + came[0].astype(F32)
    out[...] = (keep[1] + came[1].astype(F32)).astype(BF16)


def last_kernel(keep, came, out):
    out[...] = (keep[...] + came[...].astype(F32)).astype(BF16)


def add_kernel(own, r1, r2, r3, out):
    out[...] = ((own[...] + r1[...].astype(F32)) + (r2[...].astype(F32) + r3[...].astype(F32))).astype(BF16)


def ordered(pieces):
    return [pieces[j] for j in (0, 2, 3, 1)]


def after(value, *others):
    return lax.optimization_barrier((value, *others))[0]


def body(image, section_weights, section_norms, queue, pairing):
    micro, images = image.shape[0], image.shape[2]
    ndp = lax.axis_size("dp")
    t = lax.axis_index("section")
    dp = lax.axis_index("dp")
    core = dp % 2
    place = jnp.stack([t ^ k for k in range(SECTIONS)] + [core, 1 - core, dp // 2, dp, dp % 4]).astype(jnp.int32)
    cells = CROPS * PLACES * images
    rows = micro * cells
    count = float(cells * ndp)
    packed = section_weights[0]
    norm3 = section_norms.transpose(1, 0, 2)
    param_rows = packed.shape[0]
    own = WIDTH // ndp
    k = functools.partial

    def pieces_of(width, dtype):
        return shape((rows, width), dtype)

    own_message, *messages = pack(place, packed, norm3)
    came = [own_message]
    for j in range(1, SECTIONS):
        came.append(lax.ppermute(messages[j - 1], "section", [(u, u ^ j) for u in range(3)]))
    flat = call(
        retile_kernel, shape((rows, D), BF16),
        image.transpose(0, 1, 3, 4, 2, 5).reshape(rows // images, images, D),
        us=2,
    )
    head_rows = rows // PLACES * ndp
    small = ndp == 8 and head_rows <= 128 and images == 4 and queue.shape[1] * ndp <= 512
    told, told_offsets = [flat], []
    if small:
        note = [shape((queue.shape[1] + 16, PROJ), BF16)] * 2
        keep, out = call(note_kernel, note, place, pairing, queue, us=0.5)
        told, told_offsets = [rows_of([keep, flip(out, "dp", 1)])], [0, 1]
        told = [rows_of([told[0], flip(told[0], "dp", 2)])]
        told_offsets = told_offsets + [offset ^ 2 for offset in told_offsets]
    natural = unpack(packed, FIRST)
    *came, flat, told[0], natural = lax.optimization_barrier((*came, flat, told[0], natural))
    conv_part, pair_part = call(
        pick_kernel,
        (shape((QUARTER_CONV, PART), BF16), shape((HALF_REDUCE + 4 * HALF_EXPAND, PART), BF16)),
        place, *came,
    )
    pair_parts = (pair_part, flip(pair_part, "dp", 1))
    conv_near = flip(conv_part, "dp", 2)
    sums_of = shape((8, PART), F32)
    pre0, part = call(
        k(reduce_kernel, micro), (pieces_of(PART, F32), sums_of), place, flat, *pair_parts, us=2
    )
    sums0 = sum_dp(part)
    active0 = call(k(active_kernel, micro, count), pieces_of(PART, BF16), pre0, sums0, pair_part, us=1)
    actives0 = gather_xor(active0, "section")

    conv_part = rows_of([conv_part, after(conv_near, active0)])
    w_conv = (conv_part, flip(conv_part, "dp", 1))
    if small:
        told.append(flip(after(told[0], active0), "dp", 4))
        told_offsets = told_offsets + [offset ^ 4 for offset in told_offsets]
    w_proj, table = pl.pallas_call(
        tables_kernel,
        name="tables",
        out_shape=(shape((D, PROJ), BF16), shape((QUARTER_PAD, WIDTH), BF16)),
        in_specs=[pl.BlockSpec(memory_space=pltpu.HBM)],
        out_specs=(pl.BlockSpec(memory_space=pltpu.VMEM), pl.BlockSpec(memory_space=pltpu.VMEM)),
        scratch_shapes=[
            pltpu.VMEM((THIRD - FIRST + 2, WIDTH), BF16), pltpu.VMEM((D, PROJ), F32), pltpu.SemaphoreType.DMA,
        ],
        compiler_params=pltpu.CompilerParams(vmem_limit_bytes=12 * 2**20),
        cost_estimate=cost(1.5),
    )(hbm(after(packed, active0)))
    taps = call(k(taps_kernel, images), pieces_of(9 * PART, BF16), active0, us=1.3)
    back_rows = 9 * PART // 2 + WIDE // 2
    back_own = call(
        back_parts_kernel, [shape((back_rows, PART), BF16)] * 4, place, *w_conv, *pair_parts, us=1
    )
    joined = lax.optimization_barrier((*actives0, table, taps, told[-1], *back_own))
    actives0, (table, taps, told[-1]), back_own = joined[:4], joined[4:7], joined[7:]
    pre1, part = call(
        k(conv_kernel, micro, images),
        (pieces_of(PART, F32), sums_of),
        place, *ordered(actives0), *w_conv,
        scratch=[pltpu.VMEM((rows, WIDTH), BF16), pltpu.VMEM((WIDTH, 9 * PART), BF16)],
        us=3,
    )
    sums1 = sum_dp(part)
    active1_own = call(k(active_kernel, micro, count), pieces_of(PART, BF16), pre1, sums1, conv_part, us=1)
    actives1 = gather_xor(active1_own, "section")
    lanes = 4 * QUARTER_PAD
    stages = dp_stages()
    head_stages = stages[1:] + stages[:1]
    offsets = [0]
    for steps in head_stages:
        offsets = offsets + [o ^ step for step in steps for o in offsets]
    if small:
        queued = ndp * queue.shape[1]
        mass, column, match = call(
            k(mass_kernel, micro, images, told_offsets),
            (
                shape((queued, lanes), BF16), shape((8, lanes), F32),
                shape((micro, images * ndp, images * ndp), BF16),
            ),
            place, after(table, active1_own), *told,
            scratch=[pltpu.VMEM((queued, PROJ), BF16), pltpu.VMEM((queued, lanes), F32)],
            vmem=16, us=5,
        )
    if small:
        *actives1, mass = lax.optimization_barrier((*actives1, mass))
    active1, pre2, part, w_expand = call(
        k(expand_kernel, micro),
        (pieces_of(WIDTH, BF16), pieces_of(WIDE, F32), shape((8, WIDE), F32), shape((WIDTH, WIDE), BF16)),
        place, *ordered(actives1), *pair_parts,
        us=2,
    )
    back_own = lax.optimization_barrier((*back_own, part))[:4]
    back_came = [back_own[0]] + [flip(back_own[j], "section", j) for j in range(1, SECTIONS)]

    sums2 = sum_dp(part)
    pooled = call(
        k(pool_kernel, micro, images, count),
        shape((rows // PLACES, WIDE), BF16),
        place, pre2, sums2, pair_part, flat,
        us=1.6,
    )

    per_dp = rows // PLACES
    came_p = gather_xor(pooled, "section")[::-1]
    pooled_here = call(lanes_kernel, shape((per_dp, D), BF16), *came_p, us=0.3)
    parts, _ = gather_dp(pooled_here, head_stages)
    if small:
        all_pooled, active3, unit, d_scores, embed, *kept, said = call(
            k(head_kernel, micro, images, offsets),
            [
                shape((head_rows, D), BF16), shape((head_rows, D), BF16), shape((head_rows, PROJ), BF16),
                shape((head_rows // 2, lanes), BF16), shape((head_rows, PROJ), F32), shape((head_rows, D), F32),
                shape((head_rows, D), F32), shape((8, D), F32), shape((head_rows // 2 + 8, PROJ), F32),
            ],
            place, *parts, natural, w_proj, table, norm3, mass, column, match,
            scratch=[
                pltpu.VMEM((head_rows, lanes), F32), pltpu.VMEM((head_rows // 2, lanes), F32),
                pltpu.VMEM((micro, 8, lanes), F32), pltpu.VMEM((8, lanes), F32),
            ],
            vmem=15, us=12,
        )
        *d_pooled, notes3, d_embed, d_pre3 = call(
            k(head_back_kernel, micro, images, ndp),
            [shape((per_dp, WIDE), BF16)] * 4
            + [shape((8, D), F32), shape((head_rows, PROJ), BF16), shape((head_rows, D), BF16)],
            place, said, flip(said, "dp", 1), embed, w_proj, natural, norm3, *kept,
            scratch=[pltpu.VMEM((head_rows, PROJ), F32), pltpu.VMEM((per_dp, D), BF16)],
            us=5,
        )
    else:
        all_pooled = jnp.concatenate(parts)
        offset = jnp.array(offsets, jnp.int32)
        head_order = jnp.arange(head_rows, dtype=jnp.int32)
        block, inner = head_order // per_dp, head_order % per_dp
        group, single = inner // images, inner % images
        position = (group * ndp + (offset[block] ^ dp)) * images + single
        order = (position[None, :] == head_order[:, None]).astype(BF16)
        pairs = lax.all_gather(pairing.astype(F32), "dp").astype(jnp.int32)
        left = jnp.arange(images * ndp, dtype=jnp.int32)
        pairs = pairs.transpose(1, 0, 2).reshape(micro, ndp * images)
        match = ((left // images * images + pairs)[:, :, None] == left[None, None, :]).astype(F32)
        all_pooled = dot(order, all_pooled).astype(BF16)
        protos = jnp.concatenate([table[:, a * PROJ : (a + 1) * PROJ] for a in range(4)], axis=0)
        queue_rows = lax.all_gather(queue, "dp", axis=1, tiled=True)
        loss, grads3, active3, unit, d_scores, d_embed, d_pre3 = head(
            all_pooled, natural, w_proj, protos, norm3[:, 0], queue_rows, match, micro, images, dp
        )
        notes3 = jnp.concatenate([grads3, jnp.full((5, D), loss)])
        d_pooled = dot_nt(dot_tn(order[:, :per_dp], d_pre3).astype(BF16), natural).astype(BF16)
        d_pooled = [d_pooled[:, j * WIDE : (j + 1) * WIDE] for j in range(SECTIONS)]
        d_scores = d_scores.reshape(micro, CROPS, head_rows // 4, lanes)
        d_scores = lax.dynamic_index_in_dim(d_scores, 1 - core, 1, keepdims=False).reshape(-1, lanes)

    joined = lax.optimization_barrier((*d_pooled, *back_came))
    d_pooled, back_came = joined[:SECTIONS], joined[SECTIONS:]
    came_d = [flip(d_pooled[3 ^ j], "section", j) for j in range(1, SECTIONS)]
    back_half = call(stack_kernel, shape((SECTIONS, back_rows, PART), BF16), *back_came, us=0.6)
    back_halves = (back_half, flip(back_half, "dp", 1))
    d_z, part = call(
        k(out_back_kernel, micro, images, count),
        (pieces_of(WIDE, F32), shape((8, WIDE), F32)),
        place, pre2, sums2, pair_part, flat, d_pooled[3], *came_d,
        us=1.8,
    )
    back2 = sum_dp(part)
    back2, *back_halves = lax.optimization_barrier((back2, *back_halves))
    d_pre2, *partial = call(
        k(expand_back_kernel, micro, count),
        [pieces_of(WIDE, BF16)] + [pieces_of(PART, BF16)] * 4,
        place, pre2, sums2, d_z, back2, pair_part, w_expand,
        scratch=[pltpu.VMEM((rows, WIDTH), F32)],
        us=2,
    )
    partial = [partial[0]] + [flip(partial[j], "section", j) for j in range(1, SECTIONS)]

    def scatter_start(a, b, width):
        if ndp != 8:
            return dot_tn(a, b)
        keep, out = call(
            pair_kernel,
            (shape((4, own, width), F32), shape((4, own, width), BF16)),
            place, a, b,
            us=2.5,
        )
        return keep, flip(out, "dp", 1)

    def scatter_cross(started, *others):
        if ndp != 8:
            return [lax.psum_scatter(started.astype(BF16), "dp", scatter_dimension=0, tiled=True)]
        keep, came = started
        if others:
            keep = after(keep, *others)
        dims = keep.shape[1:]
        kept, *out = call(
            cross_kernel, [shape(dims, F32)] + [shape(dims, BF16)] * 3, place, keep, came
        )
        return [kept] + [flip(out[j], "dp", 2 * (j + 1)) for j in range(3)]

    def scatter_far(started, *others):
        if ndp != 8:
            return lax.psum_scatter(started.astype(BF16), "dp", scatter_dimension=0, tiled=True), None
        keep, came = started
        if others:
            keep = after(keep, *others)
        dims = (2, *keep.shape[1:])
        kept, out = call(far_kernel, (shape(dims, F32), shape(dims, BF16)), place, keep, came, us=0.7)
        return kept, flip(out, "dp", 4)

    def scatter_near(started, *others):
        if ndp != 8:
            return started
        keep, came = started
        if others:
            keep = after(keep, *others)
        dims = keep.shape[1:]
        kept, out = call(near_kernel, (shape(dims, F32), shape(dims, BF16)), keep, came, us=0.5)
        return kept, flip(out, "dp", 2)

    def scatter_last(started):
        if ndp != 8:
            return started[0].astype(BF16)
        return call(last_kernel, shape(started[0].shape, BF16), *started, us=0.4)

    def scatter_finish(crossed):
        if ndp != 8:
            return crossed[0].astype(BF16)
        return call(add_kernel, shape(crossed[0].shape, BF16), *crossed, us=0.6)

    expand_half = scatter_far(scatter_start(d_pre2, active1, WIDTH))
    tail = call(
        tail_grads_kernel,
        shape((own, WIDTH + QUARTER_PAD), F32),
        place, after(active3, d_pre2), unit, d_scores, flip(d_scores, "dp", 1), d_embed,
        us=3,
    )
    joined = lax.optimization_barrier((*partial, tail, *expand_half[: 2 if ndp == 8 else 1]))
    partial, tail, expand_half = joined[:SECTIONS], joined[SECTIONS], joined[SECTIONS + 1 :]

    d_y1, part = call(
        k(silu_back_kernel, micro, count),
        (pieces_of(PART, F32), sums_of),
        *partial, pre1, sums1, conv_part,
    )
    back1 = sum_dp(part)
    d_pre1_own = call(
        k(norm_back_kernel, micro, count), pieces_of(PART, BF16), d_y1, pre1, sums1, back1, conv_part
    )
    d_pre1s = gather_xor(d_pre1_own, "section")
    expand_last = scatter_near(expand_half, d_pre1_own)
    base = call(
        head_grads_kernel,
        shape((own, param_rows), F32),
        place, after(all_pooled, d_pre1_own), d_pre3, tail,
        scratch=[pltpu.VMEM((4 * own, D), BF16)],
        us=4,
    )
    joined = lax.optimization_barrier((*d_pre1s, base, *expand_last))
    d_pre1s, base, expand_last = joined[:SECTIONS], joined[SECTIONS], joined[SECTIONS + 1 :]
    d_pre1, d_y0, part = call(
        k(conv_back_kernel, micro, images, count),
        (pieces_of(WIDTH, BF16), pieces_of(PART, F32), sums_of),
        place, *ordered(d_pre1s), *back_halves, pre0, sums0, pair_part,
        scratch=[pltpu.VMEM((9 * PART, WIDTH), BF16)],
        us=3.5,
    )
    conv_started = scatter_start(d_pre1, taps, 9 * PART)
    back0 = sum_dp(part)
    d_pre0_own = call(
        k(last_norm_back_kernel, micro, count),
        shape((rows + NOTE_ROWS, PART), BF16),
        place, d_y0, pre0, sums0, back0, pair_part, back2, back1, notes3,
    )
    d_pre0s = gather_xor(d_pre0_own, "section")
    conv_half = scatter_far(conv_started)
    joined = lax.optimization_barrier((*d_pre0s, conv_half[0]))
    d_pre0s, conv_half = joined[:SECTIONS], (joined[SECTIONS], conv_half[1])
    conv_last = scatter_near(conv_half)
    joined = lax.optimization_barrier((*d_pre0s, conv_last[0]))
    d_pre0s, conv_last = joined[:SECTIONS], (joined[SECTIONS], conv_last[1])

    if ndp == 8:
        keep, out, d_pre0 = call(
            image_pair_kernel,
            (shape((4, own, WIDE), F32), shape((4, own, WIDE), BF16), pieces_of(WIDTH, BF16)),
            place, *ordered(d_pre0s), flat,
            us=2.5,
        )
        reduce_started = keep, flip(out, "dp", 1)
    else:
        d_pre0 = jnp.stack(d_pre0s)[place[:SECTIONS], :rows].transpose(1, 0, 2).reshape(rows, WIDTH)
        reduce_started = dot_tn(d_pre0, lax.dynamic_slice_in_dim(flat, t * WIDE, WIDE, 1))
    reduce_crossed = scatter_cross(reduce_started)
    grad_in = call(
        reduce_back_kernel,
        shape((rows // images, images, WIDE), F32),
        place, d_pre0, *back_halves, d_z,
        scratch=[pltpu.VMEM((WIDE, WIDTH), BF16)],
        us=2,
    )
    norm_grads, loss = call(
        told_kernel, (shape((3, 1, D), F32), shape((8, PROJ), F32)), place, *d_pre0s, notes3, us=0.5
    )
    g_conv = scatter_last(conv_last)
    g_expand = scatter_last(expand_last)
    joined = lax.optimization_barrier((*reduce_crossed, grad_in, norm_grads, g_conv, g_expand))
    *reduce_crossed, grad_in, norm_grads, g_conv, g_expand = joined
    if ndp != 8:
        nothing = jnp.zeros(reduce_crossed[0].shape, BF16)
        reduce_crossed = [reduce_crossed[0].astype(F32), nothing, nothing, nothing]
    g_reduce, *mixed = call(
        mixed_kernel,
        [shape(reduce_crossed[0].shape, BF16)] + [shape(g_conv.shape, BF16)] * 3,
        place, *reduce_crossed, g_conv, g_expand,
        us=0.5,
    )
    mixed = [
        lax.ppermute(mixed[j - 1], "section", [(u ^ j, u) for u in range(3)]) for j in range(1, SECTIONS)
    ]
    weight_grads = pl.pallas_call(
        finish_kernel,
        name="finish",
        out_shape=shape((own, param_rows), F32),
        in_specs=[pl.BlockSpec(memory_space=pltpu.SMEM), pl.BlockSpec(memory_space=pltpu.HBM)]
        + [pl.BlockSpec(memory_space=pltpu.VMEM)] * 6,
        out_specs=pl.BlockSpec(memory_space=pltpu.HBM),
        scratch_shapes=[pltpu.VMEM((own, 9 * WIDTH), F32), pltpu.SemaphoreType.DMA((SECTIONS,))],
        input_output_aliases={1: 0},
        compiler_params=pltpu.CompilerParams(vmem_limit_bytes=12 * 2**20),
        cost_estimate=cost(2),
    )(place, base, g_reduce, g_conv, g_expand, *mixed)
    grad_in = grad_in.reshape(micro, CROPS, SIDE, SIDE, images, WIDE).transpose(0, 1, 4, 2, 3, 5)
    return (loss[0, 0], grad_in, weight_grads.T[None], norm_grads.transpose(1, 0, 2))


def solution(mesh):
    in_specs = (
        P(None, None, "dp", None, None, None),
        P("section", None, None),
        P("section", None, None),
        P(None, "dp", None),
        P(None, "dp"),
    )
    out_specs = (
        P(),
        P(None, None, "dp", None, None, "section"),
        P("section", None, "dp"),
        P("section", None, None),
    )
    return jax.shard_map(body, mesh=mesh, in_specs=in_specs, out_specs=out_specs, check_vma=False)
```
